128 devices in a mesh: shard: 4 (over y_lo, core), context: 8 (over y_hi, z), tensor: 4 (over x).
Axes of the slice: x: 4, y: 4 (y_hi: 2, y_lo: 2; y = y_hi * 2 + y_lo), z: 4, core: 2. Of those that a mesh axis runs over, the one named last changes fastest.
Arguments:
- inputs: bfloat16 [16, 1024, 2048], P('shard', 'context'), may hold values from -6 to 6
- cotangent: bfloat16 [16, 1024, 2048], P('shard', 'context'), may hold values from -6 to 6
- q_weight: bfloat16 [2048, 2048], P('shard', 'tensor'), may hold values from -0.125 to 0.125
- k_weight: bfloat16 [2048, 2048], P('shard', 'tensor'), may hold values from -0.125 to 0.125
- v_weight: bfloat16 [2048, 2048], P('shard', 'tensor'), may hold values from -0.125 to 0.125
- o_weight: bfloat16 [2048, 2048], P('tensor', 'shard'), may hold values from -2 to 2
- gate_weight: bfloat16 [2048, 8192], P('shard', 'tensor'), may hold values from -0.125 to 0.125
- up_weight: bfloat16 [2048, 8192], P('shard', 'tensor'), may hold values from -0.125 to 0.125
- down_weight: bfloat16 [8192, 2048], P('tensor', 'shard'), may hold values from -0.125 to 0.125
- attn_gain: bfloat16 [2048], P('shard'), may hold values from 0.099609375 to 1.8984375
- ffn_gain: bfloat16 [2048], P('shard'), may hold values from 0.099609375 to 1.8984375
- piece_starts: int32 [16, 2], P('shard'), may hold values from 0 to 768, as said below
- piece_ids: int32 [16, 2], P('shard'), may hold values from 0 to 1
- valid_mask: int32 [16, 1024], P('shard'), may hold values from 0 to 1, as said below
Outputs:
- output: bfloat16 [16, 1024, 2048], P('shard', 'context')
- input_grad: bfloat16 [16, 1024, 2048], P('shard', 'context')
- q_grad: float32 [2048, 2048], P('shard', 'tensor')
- k_grad: float32 [2048, 2048], P('shard', 'tensor')
- v_grad: float32 [2048, 2048], P('shard', 'tensor')
- o_grad: float32 [2048, 2048], P('tensor', 'shard')
- gate_grad: float32 [2048, 8192], P('shard', 'tensor')
- up_grad: float32 [2048, 8192], P('shard', 'tensor')
- down_grad: float32 [8192, 2048], P('tensor', 'shard')
- attn_gain_grad: float32 [2048], P(('shard', 'tensor'))
- ffn_gain_grad: float32 [2048], P(('shard', 'tensor'))
- branch_rms: float32 [3], replicated
The draws below stay inside these ranges and needn't reach their ends.
Inputs may be any that keep to these rules, and one draw needn't show every extreme that they name: `piece_starts`: the 2 pieces of a sequence do not intersection: piece p starts between p * 512 and (p + 1) * 512 - 256. `piece_ids`: pieces of one sequence with equal ids show one picture. `valid_mask`: the real tokens of a sequence are a prefix of 256 to 1024 tokens; both lengths occur in every draw.
All inputs are finite; a program needn't handle non-finite values.
Results may differ from the reference program's by a relative error of at most 0.03.
Values may be sent and summed in bfloat16 or wider, within the bound.
A program may use at most 256 MiB of HBM per device.

```python
import jax
import jax.numpy as jnp
from jax import lax

D = 2048
HEADS = 32
HEAD_DIM = 64
FF = 8192
LENGTH = 1024
PIECE = 256
PIECES = 2
SEQS = 16


def draw_piece_starts(key, part):
    own_key = jax.random.fold_in(key, 3)
    slot_len = LENGTH // PIECES
    room_len = slot_len - PIECE + 1
    offsets = jax.random.randint(own_key, (SEQS, PIECES), 0, room_len, dtype=jnp.int32)
    offsets = offsets.at[0, 0].set(0)
    offsets = offsets.at[SEQS - 1, PIECES - 1].set(room_len - 1)
    return (offsets + jnp.arange(PIECES, dtype=jnp.int32)[None, :] * slot_len).astype(jnp.int32)


def draw_valid_mask(key, part):
    own_key = jax.random.fold_in(key, 5)
    seq_lens = jax.random.randint(own_key, (SEQS,), LENGTH // 4, LENGTH + 1, dtype=jnp.int32)
    seq_lens = seq_lens.at[0].set(LENGTH)
    seq_lens = seq_lens.at[1].set(LENGTH // 4)
    seq_lens = jax.random.permutation(jax.random.fold_in(own_key, 17), seq_lens)
    return (jnp.arange(LENGTH, dtype=jnp.int32)[None, :] < seq_lens[:, None]).astype(jnp.int32)


def plant(values, rng, smallest, top_value):
    spot = [jax.random.randint(jax.random.fold_in(rng, axis), (), 0, length) for axis, length in enumerate(values.shape)]
    main_axis = values.shape.index(max(values.shape))
    neighbour = spot[:main_axis] + [(spot[main_axis] + 1) % values.shape[main_axis]] + spot[main_axis + 1:]
    return values.at[tuple(spot)].set(smallest).at[tuple(neighbour)].set(top_value)


def block_levels(rng, dims, cuts, smallest, top_value):
    factor_of = 1.0
    for position, shards_of in cuts:
        draws = jax.random.uniform(jax.random.fold_in(jax.random.fold_in(rng, 6), position), (shards_of,), jnp.float32, smallest / len(cuts), top_value / len(cuts))
        factor_of = factor_of * jnp.repeat(jnp.exp(draws), dims[position] // shards_of).reshape((-1,) + (1,) * (len(dims) - 1 - position))
    return factor_of


def gaussian(key, dims, scale, most, cuts=(), kind=jnp.bfloat16):
    gain = block_levels(key, dims, cuts, -0.22, 0.18) if cuts else 1.0
    drawn = jax.random.normal(key, dims, jnp.float32) * scale * gain
    return jnp.minimum(jnp.maximum(drawn, -most), most).astype(kind)


def setup_inputs(seed: int = 0) -> dict:
    arg_keys = jax.random.split(jax.random.key(seed), 15)
    return {
        "inputs": gaussian(arg_keys[0], (SEQS, LENGTH, D), 1.0, 6.0, ((0, 4), (1, 8))),
        "cotangent": gaussian(arg_keys[1], (SEQS, LENGTH, D), 1.0, 6.0, ((0, 4), (1, 8))),
        "q_weight": gaussian(arg_keys[2], (D, HEADS * HEAD_DIM), D ** -0.5, 0.125, ((0, 4), (1, 4))),
        "k_weight": gaussian(arg_keys[3], (D, HEADS * HEAD_DIM), D ** -0.5, 0.125, ((0, 4), (1, 4))),
        "v_weight": gaussian(arg_keys[4], (D, HEADS * HEAD_DIM), D ** -0.5, 0.125, ((0, 4), (1, 4))),
        "o_weight": gaussian(arg_keys[5], (HEADS * HEAD_DIM, D), (max(HEADS * HEAD_DIM // 256, 1)) ** -0.5, 2.0, ((0, 4), (1, 4))),
        "gate_weight": gaussian(arg_keys[6], (D, FF), D ** -0.5, 0.125, ((0, 4), (1, 4))),
        "up_weight": gaussian(arg_keys[7], (D, FF), D ** -0.5, 0.125, ((0, 4), (1, 4))),
        "down_weight": gaussian(arg_keys[8], (FF, D), (FF // 4) ** -0.5, 0.125, ((0, 4), (1, 4))),
        "attn_gain": jnp.clip(1.0 + 0.18 * jax.random.normal(arg_keys[9], (D,), jnp.float32), 0.099609375, 1.8984375).astype(jnp.bfloat16),
        "ffn_gain": jnp.clip(1.0 + 0.18 * jax.random.normal(arg_keys[10], (D,), jnp.float32), 0.099609375, 1.8984375).astype(jnp.bfloat16),
        "piece_starts": draw_piece_starts(jax.random.fold_in(arg_keys[14], 71), 0),
        "piece_ids": plant(jax.random.randint(arg_keys[12], (SEQS, PIECES), 0, PIECES), jax.random.fold_in(arg_keys[12], 1), 0, PIECES - 1).astype(jnp.int32),
        "valid_mask": draw_valid_mask(jax.random.fold_in(arg_keys[14], 71), 0),
    }


NORM_EPS = 1e-05
ROPE_BASE = 130000.0
MASK_FILL = -1e+30

@jax.custom_vjp
def low(v):
    return lax.optimization_barrier(v.astype(jnp.bfloat16)).astype(jnp.float32)

@jax.custom_vjp
def low_back(v):
    return v

def low_keep(v):
    return (low(v), None)

def low_pass(kept, grad):
    return (grad,)

def back_keep(v):
    return (v, None)

def back_low(kept, grad):
    return (low(grad),)
low.defvjp(low_keep, low_pass)
low_back.defvjp(back_keep, back_low)

def matmul_high(left, right):
    return jnp.dot(left, right, precision=lax.Precision.HIGHEST, preferred_element_type=jnp.float32)

def rope_tables(positions, head_size):
    half_dim = head_size // 2
    inv_freq = ROPE_BASE ** (-jnp.arange(half_dim, dtype=jnp.float32) * 2.0 / head_size)
    angles = positions.astype(jnp.float32)[:, None] * inv_freq[None, :]
    angles = jnp.concatenate([angles, angles], axis=1)
    return (jnp.cos(angles), jnp.sin(angles))

def rotate(values, cosine, sine_tab):
    row_count, col_count = values.shape
    head_size = cosine.shape[1]
    half_dim = head_size // 2
    split_heads = values.reshape(row_count, col_count // head_size, head_size)
    turned = jnp.concatenate([-split_heads[:, :, half_dim:], split_heads[:, :, :half_dim]], axis=2)
    return (split_heads * cosine[:, None, :] + turned * sine_tab[:, None, :]).reshape(row_count, col_count)

def piece_index(starts, piece_tags, positions):
    inside = (positions[None, :, None] >= starts[:, None, :]) & (positions[None, :, None] < starts[:, None, :] + PIECE)
    tagged = jnp.where(inside, piece_tags[:, None, :] + 1, 0)
    return (lax.optimization_barrier(jnp.sum(tagged, axis=2)) - 1).astype(jnp.int32)

def block_forward(seq_in, params, allowed, cosine, sine_tab):
    q_weight, k_weight, v_weight, o_weight, gate_weight, up_weight, down_weight, attn_gain, ffn_gain = params
    score_scale = HEAD_DIM ** (-0.5)
    normed_attn = seq_in * lax.rsqrt(lax.optimization_barrier(jnp.mean(seq_in * seq_in, axis=1, keepdims=True)) + NORM_EPS)
    attn_in = low(normed_attn * attn_gain)
    query_rot = low(rotate(low_back(matmul_high(attn_in, q_weight)), cosine, sine_tab))
    key_rot = low(rotate(low_back(matmul_high(attn_in, k_weight)), cosine, sine_tab))
    value_rows = low(low_back(matmul_high(attn_in, v_weight)))

    def by_heads(values):
        return values.reshape(LENGTH, HEADS, HEAD_DIM).transpose(1, 0, 2)

    def attend(head_item):
        query_h, key_h, value_h = head_item
        score = low_back(score_scale * matmul_high(query_h, key_h.T))
        score = jnp.where(allowed, score, MASK_FILL)
        row_total = jax.scipy.special.logsumexp(score, axis=1, keepdims=True)
        attn_prob = jnp.exp(score - row_total)
        return matmul_high(low(attn_prob), value_h)
    head_mix = lax.map(jax.checkpoint(attend), (by_heads(query_rot), by_heads(key_rot), by_heads(value_rows)))
    attended = low(low_back(head_mix.transpose(1, 0, 2).reshape(LENGTH, HEADS * HEAD_DIM)))
    attn_out = low_back(matmul_high(attended, o_weight))
    resid = seq_in + attn_out
    normed_ffn = resid * lax.rsqrt(lax.optimization_barrier(jnp.mean(resid * resid, axis=1, keepdims=True)) + NORM_EPS)
    ffn_in = low(normed_ffn * ffn_gain)
    gate_val = low_back(matmul_high(ffn_in, gate_weight))
    up_val = low_back(matmul_high(ffn_in, up_weight))
    hidden = low(jax.nn.silu(gate_val) * up_val)
    ffn_out = low_back(matmul_high(hidden, down_weight))
    final_out = resid + ffn_out
    return (final_out, (attn_out, ffn_out))

def add_pair(first, second):
    return first + second

def reference(inputs, cotangent, q_weight, k_weight, v_weight, o_weight, gate_weight, up_weight, down_weight, attn_gain, ffn_gain, piece_starts, piece_ids, valid_mask):
    params = tuple((w.astype(jnp.float32) for w in (q_weight, k_weight, v_weight, o_weight, gate_weight, up_weight, down_weight, attn_gain, ffn_gain)))
    positions = jnp.arange(LENGTH, dtype=jnp.int32)
    cosine, sine_tab = rope_tables(positions, HEAD_DIM)

    def seq_step(carry, seq_item):
        grad_sums, stat_sums = carry
        seq_in, seq_cot, starts, piece_tags, valid_row = seq_item
        piece_of = piece_index(starts[None, :], piece_tags[None, :], positions)[0]
        causal = positions[None, :] <= positions[:, None]
        same_pic = (piece_of[:, None] >= 0) & (piece_of[:, None] == piece_of[None, :])
        visible = (valid_row[None, :] > 0) | (positions[None, :] == positions[:, None])
        allowed = (causal | same_pic) & visible

        def run_block(seq_values, weights_now):
            return block_forward(seq_values, weights_now, allowed, cosine, sine_tab)
        final_out, pullback, branches = jax.vjp(run_block, seq_in.astype(jnp.float32), params, has_aux=True)
        grad_in, grad_params = pullback(seq_cot.astype(jnp.float32))
        attn_out, ffn_out = branches
        keep_rows = valid_row.astype(jnp.float32)[:, None]
        added = jnp.stack([jnp.sum(keep_rows), jnp.sum(keep_rows * attn_out * attn_out), jnp.sum(keep_rows * ffn_out * ffn_out), jnp.sum(keep_rows * final_out * final_out)])
        grad_sums = jax.tree.map(add_pair, grad_sums, grad_params)
        return ((grad_sums, stat_sums + added), (final_out.astype(jnp.bfloat16), grad_in.astype(jnp.bfloat16)))
    start_carry = (jax.tree.map(jnp.zeros_like, params), jnp.zeros((4,), jnp.float32))
    (grad_sums, stat_sums), (output, input_grad) = lax.scan(seq_step, start_carry, (inputs, cotangent, piece_starts, piece_ids, valid_mask))
    valid_count = jnp.maximum(stat_sums[0], 1.0)
    branch_rms = jnp.sqrt(stat_sums[1:] / (valid_count * D))
    return (output, input_grad, grad_sums[0], grad_sums[1], grad_sums[2], grad_sums[3], grad_sums[4], grad_sums[5], grad_sums[6], grad_sums[7], grad_sums[8], branch_rms)
```

```python
import functools

import jax
import jax.numpy as jnp
from jax import lax
from jax.experimental import pallas as pl
from jax.experimental.pallas import tpu as pltpu
from jax.sharding import PartitionSpec as P

HEAD_DIM = 64
PIECE = 256
NORM_EPS = 1e-05
ROPE_BASE = 130000.0
MASK_FILL = -1e30
BF = jnp.bfloat16
F32 = jnp.float32
ANY = pl.BlockSpec(memory_space=pl.ANY)
VM = pl.BlockSpec(memory_space=pltpu.VMEM)
DMA = pltpu.SemaphoreType.DMA
VMEM_LIMIT = 60 * 1024 * 1024
MODEL = 2048
BLOCK = 128
MESH_ID = pl.DeviceIdType.MESH


class Place:
    def __init__(self):
        self.s = lax.axis_index("shard")
        self.k = lax.axis_index("context")
        self.x = lax.axis_index("tensor")
        self.yl = self.s // 2
        self.c = self.s % 2
        self.y = (self.k // 4) * 2 + self.yl
        self.z = self.k % 4

    def dev(self, dx=0, dy=0, dz=0, core=None):
        x = (self.x + dx + 4) % 4
        y = (self.y + dy + 4) % 4
        z = (self.z + dz + 4) % 4
        c = self.c if core is None else core
        return {"shard": (y % 2) * 2 + c, "context": (y // 2) * 4 + z, "tensor": x}

    def member(self, k):
        return {"shard": self.s, "context": k, "tensor": self.x}

    def sib(self):
        return self.dev(core=1 - self.c)


def remote(src, dst, send_sem, recv_sem, device):
    return pltpu.make_async_remote_copy(
        src_ref=src,
        dst_ref=dst,
        send_sem=send_sem,
        recv_sem=recv_sem,
        device_id=device,
        device_id_type=MESH_ID,
    )


def greet(devices):
    barrier = pltpu.get_barrier_semaphore()
    for d in devices:
        pl.semaphore_signal(barrier, inc=1, device_id=d, device_id_type=MESH_ID)
    pl.semaphore_wait(barrier, len(devices))


def params(collective_id=None):
    if collective_id is None:
        return pltpu.CompilerParams(vmem_limit_bytes=VMEM_LIMIT)
    return pltpu.CompilerParams(
        vmem_limit_bytes=VMEM_LIMIT, collective_id=collective_id, has_side_effects=True
    )


def tiles(v):
    return v.reshape(*v.shape[:-2], v.shape[-2] // 8, 8, v.shape[-1])


def rows_of(v):
    return v.reshape(*v.shape[:-3], v.shape[-3] * 8, v.shape[-1])


def context_peers(p):
    return [p.member((p.k + d) % 8) for d in range(1, 8)]


def swap_halves(v):
    width = v.shape[1]
    lane = lax.broadcasted_iota(jnp.int32, v.shape, 1) % HEAD_DIM
    return jnp.where(
        lane < HEAD_DIM // 2,
        pltpu.roll(v, width - HEAD_DIM // 2, 1),
        pltpu.roll(v, HEAD_DIM // 2, 1),
    )


WEIGHTS = (
    (256, "row", 0, 0),
    (256, "row", 0, 256),
    (256, "row", 0, 512),
    (256, "col", 1, 0),
    (1024, "row", 2, 0),
    (1024, "row", 2, 1024),
    (1024, "col", 3, 0),
)


def start_kernel(
    x_ref,
    cot_ref,
    wq,
    wk,
    wv,
    wo,
    wg,
    wu,
    wd,
    gain_ref,
    meta_ref,
    cos_ref,
    sin_ref,
    wqkv_o,
    wo_o,
    wgu_o,
    wd_o,
    gains_o,
    meta_o,
    cot_o,
    attn_in_o,
    qkv_o,
    x_all,
    qkv_send,
    y_send,
    y_recv,
    z_send,
    z_recv,
    sib_send,
    sib_recv,
    loc,
    misc_send,
    misc_recv,
    gain_send,
    gain_recv,
    a2a_send,
    a2a_recv,
):
    p = Place()
    srcs = (wq, wk, wv, wo, wg, wu, wd)
    dsts = (wqkv_o, wo_o, wgu_o, wd_o)
    qa = 2 * (p.z % 2)

    def src_part(w, half, quarter):
        size, kind, _, _ = WEIGHTS[w]
        if kind == "row":
            rows = pl.ds(0, 64) if quarter is None else pl.ds(quarter * 16, 16)
            return srcs[w].at[rows, :, pl.ds(half * size, size)]
        size = size // 8
        if quarter is None:
            return srcs[w].at[pl.ds(half * size, size)]
        return srcs[w].at[pl.ds(half * size + quarter * (size // 4), size // 4)]

    def dst_part(w, block, quarter):
        size, kind, d, off = WEIGHTS[w]
        if kind == "row":
            rows = (
                pl.ds(block * 64, 64)
                if quarter is None
                else pl.ds(block * 64 + quarter * 16, 16)
            )
            return dsts[d].at[rows, :, pl.ds(off, size)]
        size = size // 8
        cols = pl.ds(block * 512, 512)
        if quarter is None:
            return dsts[d].at[:, :, cols]
        return dsts[d].at[pl.ds(quarter * (size // 4), size // 4), :, cols]

    def y_copy(w, side, core, block, target_half):
        quarter = qa + side
        return remote(
            src_part(w, target_half, quarter),
            dst_part(w, block, quarter),
            y_send.at[w, side, core],
            y_recv.at[w, side, p.c],
            p.dev(dy=-1 if side == 0 else 1, core=core),
        )

    def y_arrival(w, side, core):
        quarter = qa + side
        here = dst_part(w, (1 - p.yl) * 2 + core, quarter)
        return remote(
            here,
            here,
            y_send.at[w, side, core],
            y_recv.at[w, side, core],
            p.dev(dy=1 if side == 0 else -1, core=core),
        )

    def z_copy(w, side, core):
        here = dst_part(w, (1 - p.yl) * 2 + core, qa + side)
        return remote(
            here,
            here,
            z_send.at[w, side, core],
            z_recv.at[w, side, core],
            p.dev(dz=-1 if side == 0 else 1),
        )

    def z_arrival(w, side, core):
        here = dst_part(w, (1 - p.yl) * 2 + core, 2 - qa + side)
        return remote(
            here,
            here,
            z_send.at[w, side, core],
            z_recv.at[w, side, core],
            p.dev(dz=1 if side == 0 else -1),
        )

    def sib_copy(w):
        return remote(
            src_part(w, 1 - p.c, None),
            dst_part(w, p.s, None),
            sib_send.at[w],
            sib_recv.at[w],
            p.sib(),
        )

    def sib_arrival(w):
        here = dst_part(w, p.yl * 2 + 1 - p.c, None)
        return remote(here, here, sib_send.at[w], sib_recv.at[w], p.sib())

    def own_copy(w):
        return pltpu.make_async_copy(src_part(w, p.c, None), dst_part(w, p.s, None), loc.at[w])

    greet(
        [p.sib()]
        + [p.dev(dy=dy, core=core) for dy in (-1, 1) for core in (0, 1)]
        + context_peers(p)
    )

    def start_y(ws):
        for w in ws:
            for core in (0, 1):
                for side in (0, 1):
                    y_copy(w, side, core, p.s, core).start()

    gain_targets = [p.sib()] + [p.dev(dy=dy, core=core) for dy, core in ((1, 0), (1, 1))]
    gain_copies = [
        remote(gain_ref, gains_o.at[p.s], gain_send.at[i], gain_recv.at[i if i == 0 else 1 + p.c], d)
        for i, d in enumerate(gain_targets)
    ]
    for g in gain_copies:
        g.start()
    x_own = pltpu.make_async_copy(x_ref, x_all.at[:, 0], loc.at[7])
    x_own.start()
    x_out = remote(x_ref, x_all.at[:, 1], misc_send.at[0], misc_recv.at[0], p.sib())
    x_out.start()
    start_y((0, 1, 2))
    for w in (0, 1, 2):
        sib_copy(w).start()
        own_copy(w).start()
    gain_own = pltpu.make_async_copy(gain_ref, gains_o.at[p.s], loc.at[8])
    gain_own.start()
    meta_own = pltpu.make_async_copy(meta_ref, meta_o.at[p.c], loc.at[9])
    meta_own.start()
    meta_out = remote(meta_ref, meta_o.at[p.c], misc_send.at[1], misc_recv.at[1], p.sib())
    meta_out.start()
    cot_own = pltpu.make_async_copy(cot_ref, cot_o.at[:, 0], loc.at[10])
    cot_own.start()
    cot_out = remote(cot_ref, cot_o.at[:, 1], misc_send.at[2], misc_recv.at[2], p.sib())

    gain_own.wait()
    for i in range(3):
        block = p.yl * 2 + 1 - p.c if i == 0 else (1 - p.yl) * 2 + (i - 1)
        here = gains_o.at[block]
        remote(here, here, gain_send.at[i], gain_recv.at[i], p.sib()).wait_recv()
    x_own.wait()
    x_out.wait_recv()
    gain = jnp.concatenate([gains_o[b, 0:1, :] for b in range(4)], axis=1)

    def norm_step(i, carry):
        v = x_all[i // 2, i % 2].astype(F32).reshape(BLOCK, MODEL)
        r = lax.rsqrt(jnp.mean(v * v, axis=1, keepdims=True) + NORM_EPS)
        attn_in_o[i // 2, pl.ds((i % 2) * BLOCK, BLOCK), :] = (v * r * gain).astype(BF)
        return carry

    lax.fori_loop(0, 8, norm_step, 0)

    def pass_on(ws):
        for w in ws:
            for side in (0, 1):
                for core in (0, 1):
                    y_arrival(w, side, core).wait_recv()
                    z_copy(w, side, core).start()

    pass_on((0, 1, 2))
    start_y((3, 4, 5, 6))
    for w in (3, 4, 5, 6):
        sib_copy(w).start()
        own_copy(w).start()
    cot_out.start()
    for w in (0, 1, 2):
        for side in (0, 1):
            for core in (0, 1):
                z_arrival(w, side, core).wait_recv()
        sib_arrival(w).wait_recv()
        own_copy(w).wait()

    def send_block(j, q):
        other = p.c if q == 0 else 1 - p.c
        k = j * 2 + other
        slot = j * 2 + q
        return (
            k,
            remote(
                qkv_send.at[slot],
                qkv_o.at[p.k],
                a2a_send.at[slot],
                a2a_recv.at[p.k],
                p.member(k),
            ),
            pltpu.make_async_copy(qkv_send.at[slot], qkv_o.at[p.k], a2a_send.at[slot]),
        )

    def qkv_step(j, carry):
        a = attn_in_o[j]
        for part in range(3):
            cols = pl.ds(part * 256, 256)
            w = wqkv_o[:, :, cols].reshape(MODEL, 256)
            v = jnp.dot(a, w, preferred_element_type=F32)
            if part < 2:
                v = v * cos_ref[...] + swap_halves(v) * sin_ref[...]
            v = v.reshape(32, 8, 256).astype(BF)
            qkv_send[j * 2, :, :, cols] = v[:16]
            qkv_send[j * 2 + 1, :, :, cols] = v[16:]
        for q in (0, 1):
            k, out, here = send_block(j, q)

            @pl.when(k != p.k)
            def _():
                out.start()

            @pl.when(k == p.k)
            def _():
                here.start()

        return carry

    lax.fori_loop(0, 4, qkv_step, 0)
    pass_on((3, 4, 5, 6))
    for w in (3, 4, 5, 6):
        for side in (0, 1):
            for core in (0, 1):
                z_arrival(w, side, core).wait_recv()
        sib_arrival(w).wait_recv()
        own_copy(w).wait()
    for w in range(7):
        sib_copy(w).wait_send()
        for side in (0, 1):
            for core in (0, 1):
                y_copy(w, side, core, p.s, core).wait_send()
                z_copy(w, side, core).wait_send()
    x_out.wait_send()
    meta_own.wait()
    meta_out.wait_send()
    here = meta_o.at[1 - p.c]
    remote(here, here, misc_send.at[1], misc_recv.at[1], p.sib()).wait_recv()
    cot_own.wait()
    cot_out.wait()
    for g in gain_copies:
        g.wait_send()
    for j in range(4):
        for q in (0, 1):
            k, out, here = send_block(j, q)

            @pl.when(k != p.k)
            def _():
                out.wait_send()

            @pl.when(k == p.k)
            def _():
                here.wait()

    for i in range(8):

        @pl.when(i != p.k)
        def _():
            here = qkv_o.at[i]
            remote(here, here, a2a_send.at[i], a2a_recv.at[i], p.member(i)).wait_recv()


def start_call(x, cot, weights, gains, meta, cos_t, sin_t):
    shapes = (
        jax.ShapeDtypeStruct((256, 8, 768), BF),
        jax.ShapeDtypeStruct((32, 8, 2048), BF),
        jax.ShapeDtypeStruct((256, 8, 2048), BF),
        jax.ShapeDtypeStruct((128, 8, 2048), BF),
        jax.ShapeDtypeStruct((4, 8, 512), F32),
        jax.ShapeDtypeStruct((2, 8, 1024), jnp.int32),
        jax.ShapeDtypeStruct((4, 2, 16, 8, MODEL), BF),
        jax.ShapeDtypeStruct((4, 256, MODEL), BF),
        jax.ShapeDtypeStruct((8, 16, 8, 768), BF),
    )
    return pl.pallas_call(
        start_kernel,
        out_shape=shapes,
        in_specs=[ANY] * 9 + [VM, ANY, VM, VM],
        out_specs=[VM, ANY, ANY, ANY, VM, ANY, ANY, VM, ANY],
        scratch_shapes=[
            pltpu.VMEM((4, 2, 16, 8, MODEL), BF),
            pltpu.VMEM((8, 16, 8, 768), BF),
            DMA((7, 2, 2)),
            DMA((7, 2, 2)),
            DMA((7, 2, 2)),
            DMA((7, 2, 2)),
            DMA((7,)),
            DMA((7,)),
            DMA((11,)),
            DMA((3,)),
            DMA((3,)),
            DMA((3,)),
            DMA((3,)),
            DMA((8,)),
            DMA((8,)),
        ],
        compiler_params=params(1),
    )(tiles(x), tiles(cot), *[tiles(w) for w in weights], gains, meta, cos_t, sin_t)


def bias_rows(qb, rows, prow, vrow, pcol):
    i = qb * rows + lax.broadcasted_iota(jnp.int32, (rows, 1024), 0)
    j = lax.broadcasted_iota(jnp.int32, (rows, 1024), 1)
    same = (pcol >= 0) & (pcol == prow)
    ok = ((j <= i) | same) & ((vrow > 0) | (i == j))
    return jnp.where(ok, 0.0, MASK_FILL)


def attend_kernel(
    qkv, info, pcol, out_o, lse_o, o_send, a2a_send, a2a_recv
):
    p = Place()
    greet(context_peers(p))
    rows = 256

    def sends(i):
        return (
            remote(o_send.at[i], out_o.at[p.k], a2a_send.at[i], a2a_recv.at[p.k], p.member(i)),
            pltpu.make_async_copy(o_send.at[i], out_o.at[p.k], a2a_send.at[i]),
        )

    def step(qb, carry):
        at = pl.ds(pl.multiple_of(qb * rows, rows), rows)
        bias = bias_rows(qb, rows, info[0:1, :], info[1:2, :], pcol[at, 0:1])
        lane = lax.broadcasted_iota(jnp.int32, (rows, 128), 1)
        totals = jnp.zeros((rows, 128), F32)
        outs = []
        for h in range(4):
            q = qkv[at, pl.ds(h * 64, 64)]
            k = qkv[:, pl.ds(256 + h * 64, 64)]
            v = qkv[:, pl.ds(512 + h * 64, 64)]
            sc = lax.dot_general(q, k, (((1,), (1,)), ((), ())), preferred_element_type=F32)
            sc = sc * (HEAD_DIM**-0.5) + bias
            top = jnp.max(sc, axis=1, keepdims=True)
            e = jnp.exp(sc - top)
            total = jnp.sum(e, axis=1, keepdims=True)
            prob = (e * (1.0 / total)).astype(BF)
            totals = jnp.where(lane == h, top + jnp.log(total), totals)
            outs.append(jnp.dot(prob, v, preferred_element_type=F32))
        lse_o[at, :] = totals
        o = jnp.concatenate(outs, axis=1).reshape(32, 8, 256).astype(BF)
        for half in (0, 1):
            i = qb * 2 + half
            o_send[i] = o[half * 16 : (half + 1) * 16]
            out, here = sends(i)

            @pl.when(i != p.k)
            def _():
                out.start()

            @pl.when(i == p.k)
            def _():
                here.start()

        return carry

    lax.fori_loop(0, 4, step, 0)
    for i in range(8):
        out, here = sends(i)

        @pl.when(i != p.k)
        def _():
            out.wait_send()
            spot = out_o.at[i]
            remote(spot, spot, a2a_send.at[i], a2a_recv.at[i], p.member(i)).wait_recv()

        @pl.when(i == p.k)
        def _():
            here.wait()


def attend_call(qkv, info, pcol):
    return pl.pallas_call(
        attend_kernel,
        out_shape=(
            jax.ShapeDtypeStruct((8, 16, 8, 256), BF),
            jax.ShapeDtypeStruct((1024, 128), F32),
        ),
        in_specs=[VM] * 3,
        out_specs=[ANY, VM],
        scratch_shapes=[pltpu.VMEM((8, 16, 8, 256), BF), DMA((8,)), DMA((8,))],
        compiler_params=params(2),
    )(qkv, info, pcol)


def attend_back_kernel(
    g_ref,
    qkv,
    info,
    pcol,
    lse,
    cos_ref,
    sin_ref,
    out_o,
    g_all,
    d_send,
    dk,
    dv,
    g_send,
    g_recv,
    a2a_send,
    a2a_recv,
):
    p = Place()
    greet(context_peers(p))
    rows = 256

    def g_copy(j, q):
        other = p.c if q == 0 else 1 - p.c
        k = j * 2 + other
        slot = j * 2 + q
        return (
            k,
            remote(g_ref.at[slot], g_all.at[p.k], g_send.at[slot], g_recv.at[p.k], p.member(k)),
            pltpu.make_async_copy(g_ref.at[slot], g_all.at[p.k], g_send.at[slot]),
        )

    for j in range(4):
        for q in (0, 1):
            k, out, here = g_copy(j, q)

            @pl.when(k != p.k)
            def _():
                out.start()

            @pl.when(k == p.k)
            def _():
                here.start()

    dk[...] = jnp.zeros_like(dk)
    dv[...] = jnp.zeros_like(dv)
    for j in range(4):
        for q in (0, 1):
            k, out, here = g_copy(j, q)

            @pl.when(k != p.k)
            def _():
                out.wait_send()

            @pl.when(k == p.k)
            def _():
                here.wait()

    for i in range(8):

        @pl.when(i != p.k)
        def _():
            spot = g_all.at[i]
            remote(spot, spot, g_send.at[i], g_recv.at[i], p.member(i)).wait_recv()

    def sends(i):
        return (
            remote(d_send.at[i], out_o.at[p.k], a2a_send.at[i], a2a_recv.at[p.k], p.member(i)),
            pltpu.make_async_copy(d_send.at[i], out_o.at[p.k], a2a_send.at[i]),
        )

    scale = HEAD_DIM**-0.5

    def step(qb, carry):
        at = pl.ds(pl.multiple_of(qb * rows, rows), rows)
        bias = bias_rows(qb, rows, info[0:1, :], info[1:2, :], pcol[at, 0:1])
        g2 = g_all[pl.ds(qb * 2, 2)].astype(F32).reshape(rows, 256).astype(BF)
        dqs = []
        for h in range(4):
            lanes = pl.ds(h * 64, 64)
            q = qkv[at, lanes]
            k = qkv[:, pl.ds(256 + h * 64, 64)]
            v = qkv[:, pl.ds(512 + h * 64, 64)]
            g = g2[:, h * 64 : (h + 1) * 64]
            sc = lax.dot_general(q, k, (((1,), (1,)), ((), ())), preferred_element_type=F32)
            prob = jnp.exp(sc * scale + bias - lse[at, h : h + 1])
            gp = lax.dot_general(g, v, (((1,), (1,)), ((), ())), preferred_element_type=F32)
            inner = jnp.sum(prob * gp, axis=1, keepdims=True)
            gs = (prob * (gp - inner)).astype(BF)
            dqs.append(jnp.dot(gs, k, preferred_element_type=F32))
            dk[:, lanes] += lax.dot_general(
                gs, q, (((0,), (0,)), ((), ())), preferred_element_type=F32
            )
            dv[:, lanes] += lax.dot_general(
                prob.astype(BF), g, (((0,), (0,)), ((), ())), preferred_element_type=F32
            )
        dq = jnp.concatenate(dqs, axis=1) * scale
        dq = dq * cos_ref[at, :] - swap_halves(dq) * sin_ref[at, :]
        dq = dq.reshape(32, 8, 256).astype(BF)
        d_send[qb * 2, :, :, 0:256] = dq[:16]
        d_send[qb * 2 + 1, :, :, 0:256] = dq[16:]
        return carry

    lax.fori_loop(0, 4, step, 0)

    def finish(i, carry):
        at = pl.ds(pl.multiple_of(i * BLOCK, BLOCK), BLOCK)
        w = dk[at, :] * scale
        w = w * cos_ref[at, :] - swap_halves(w) * sin_ref[at, :]
        d_send[i, :, :, 256:512] = w.reshape(16, 8, 256).astype(BF)
        d_send[i, :, :, 512:768] = dv[at, :].reshape(16, 8, 256).astype(BF)
        out, here = sends(i)

        @pl.when(i != p.k)
        def _():
            out.start()

        @pl.when(i == p.k)
        def _():
            here.start()

        return carry

    lax.fori_loop(0, 8, finish, 0)
    for i in range(8):
        out, here = sends(i)

        @pl.when(i != p.k)
        def _():
            out.wait_send()
            spot = out_o.at[i]
            remote(spot, spot, a2a_send.at[i], a2a_recv.at[i], p.member(i)).wait_recv()

        @pl.when(i == p.k)
        def _():
            here.wait()


def attend_back_call(g, qkv, info, pcol, lse, cos_full, sin_full):
    return pl.pallas_call(
        attend_back_kernel,
        out_shape=jax.ShapeDtypeStruct((8, 16, 8, 768), BF),
        in_specs=[VM] * 7,
        out_specs=ANY,
        scratch_shapes=[
            pltpu.VMEM((8, 16, 8, 256), BF),
            pltpu.VMEM((8, 16, 8, 768), BF),
            pltpu.VMEM((1024, 256), F32),
            pltpu.VMEM((1024, 256), F32),
            DMA((8,)),
            DMA((8,)),
            DMA((8,)),
            DMA((8,)),
        ],
        compiler_params=params(5),
    )(tiles(g), qkv, info, pcol, lse, cos_full, sin_full)


RS_SCRATCH = [
    pltpu.VMEM((4, BLOCK, MODEL), F32),
    pltpu.VMEM((4, BLOCK, MODEL), BF),
    pltpu.VMEM((4, BLOCK, MODEL), BF),
    pltpu.VMEM((3, BLOCK, MODEL), BF),
    pltpu.VMEM((3, BLOCK, MODEL), BF),
    DMA((4,)),
    DMA((4,)),
    DMA((4,)),
    DMA((4,)),
]
AG_SCRATCH = [DMA((8,)), DMA((8,))]


def x_peers(p):
    return [p.sib(), p.dev(dx=1), p.dev(dx=-1)]


def reduce_scatter(p, lhs, rhs, transposed, scratch):
    acc, sib_out, sib_in, x_out, x_in, s_send, s_recv, x_send, x_recv = scratch
    tile = 256
    half = BLOCK // 2

    def sib_copy(r):
        return remote(sib_out.at[r], sib_in.at[r], s_send.at[r], s_recv.at[r], p.sib())

    def product(r):
        j = (p.x + r) % 4

        def step(n, carry):
            a = lhs[j]
            cols = pl.ds(pl.multiple_of(n * tile, tile), tile)
            if transposed:
                v = lax.dot_general(
                    a, rhs[cols, :], (((1,), (1,)), ((), ())), preferred_element_type=F32
                )
            else:
                v = jnp.dot(a, rhs[:, cols], preferred_element_type=F32)
            acc[r, :, cols] = v[:BLOCK]
            sib_out[r, :, cols] = v[BLOCK:].astype(BF)
            return carry

        lax.fori_loop(0, MODEL // tile, step, 0)
        sib_copy(r).start()

    far_right = remote(
        x_out.at[0, pl.ds(0, half)], x_in.at[0, pl.ds(0, half)], x_send.at[0], x_recv.at[0], p.dev(dx=1)
    )
    far_left = remote(
        x_out.at[0, pl.ds(half, half)],
        x_in.at[0, pl.ds(half, half)],
        x_send.at[1],
        x_recv.at[1],
        p.dev(dx=-1),
    )
    right = remote(x_out.at[1], x_in.at[1], x_send.at[2], x_recv.at[2], p.dev(dx=1))
    left = remote(x_out.at[2], x_in.at[2], x_send.at[3], x_recv.at[3], p.dev(dx=-1))
    product(2)
    product(1)
    sib_copy(2).wait_recv()
    x_out[0] = (acc[2] + sib_in[2].astype(F32)).astype(BF)
    far_right.start()
    far_left.start()
    product(3)
    sib_copy(1).wait_recv()
    far_right.wait_recv()
    x_out[1, 0:half] = (
        acc[1, 0:half] + sib_in[1, 0:half].astype(F32) + x_in[0, 0:half].astype(F32)
    ).astype(BF)
    x_out[1, half:] = (acc[1, half:] + sib_in[1, half:].astype(F32)).astype(BF)
    right.start()
    sib_copy(3).wait_recv()
    far_left.wait_recv()
    x_out[2, 0:half] = (acc[3, 0:half] + sib_in[3, 0:half].astype(F32)).astype(BF)
    x_out[2, half:] = (
        acc[3, half:] + sib_in[3, half:].astype(F32) + x_in[0, half:].astype(F32)
    ).astype(BF)
    left.start()
    product(0)
    sib_copy(0).wait_recv()
    right.wait_recv()
    left.wait_recv()
    total = acc[0] + sib_in[0].astype(F32) + x_in[1].astype(F32) + x_in[2].astype(F32)
    for r in range(4):
        sib_copy(r).wait_send()
    for c in (far_right, far_left, right, left):
        c.wait_send()
    return total


def all_gather(p, out, sems, both):
    send, recv = sems
    half = BLOCK // 2
    me, right, left, far = p.x, (p.x + 1) % 4, (p.x + 3) % 4, (p.x + 2) % 4

    def copy(n, j, rows, d):
        src = out.at[j, 0] if rows is None else out.at[j, 0, rows]
        return remote(src, src, send.at[n], recv.at[n], d)

    top, low = pl.ds(0, half), pl.ds(half, half)
    sent = []

    def go(c):
        c.start()
        sent.append(c)

    def sib_copy(n, j):
        return remote(out.at[j, 0], out.at[j, 1], send.at[n], recv.at[n], p.sib())

    go(copy(0, me, None, p.dev(dx=1)))
    go(copy(1, me, None, p.dev(dx=-1)))
    if both:
        go(sib_copy(4, me))
    copy(0, left, None, p.dev(dx=-1)).wait_recv()
    go(copy(2, left, top, p.dev(dx=1)))
    if both:
        go(sib_copy(5, left))
    copy(1, right, None, p.dev(dx=1)).wait_recv()
    go(copy(3, right, low, p.dev(dx=-1)))
    if both:
        go(sib_copy(6, right))
    copy(2, far, top, p.dev(dx=-1)).wait_recv()
    copy(3, far, low, p.dev(dx=1)).wait_recv()
    if both:
        go(sib_copy(7, far))
        for n, j in ((4, me), (5, left), (6, right), (7, far)):
            sib_copy(n, j).wait_recv()
    for c in sent:
        c.wait_send()


def rms(v):
    return lax.rsqrt(jnp.mean(v * v, axis=1, keepdims=True) + NORM_EPS)


def full_row(gains, row):
    return jnp.concatenate([gains[b, row : row + 1, :] for b in range(4)], axis=1)


def norm_back(grad, normed, gain, inv):
    w = grad * gain
    return inv * (w - normed * jnp.mean(w * normed, axis=1, keepdims=True))


def out_proj_kernel(lhs, rhs, x_own, keep, gains, ffn_in_o, resid_o, stat_o, *scratch):
    p = Place()
    greet(x_peers(p))
    attn_out = reduce_scatter(p, lhs, rhs, False, scratch[: len(RS_SCRATCH)])
    stat_o[...] = jnp.full((8, 128), jnp.sum(keep[:, 0:1] * attn_out * attn_out), F32)
    resid = x_own[...].astype(F32) + attn_out
    resid_o[...] = resid
    ffn_in_o[p.x, 0] = (resid * rms(resid) * full_row(gains, 1)).astype(BF)
    all_gather(p, ffn_in_o, scratch[len(RS_SCRATCH) :], True)


def out_proj_call(lhs, rhs, x_own, keep, gains):
    return pl.pallas_call(
        out_proj_kernel,
        out_shape=(
            jax.ShapeDtypeStruct((4, 2, BLOCK, MODEL), BF),
            jax.ShapeDtypeStruct((BLOCK, MODEL), F32),
            jax.ShapeDtypeStruct((8, 128), F32),
        ),
        in_specs=[VM] * 5,
        out_specs=[VM] * 3,
        scratch_shapes=RS_SCRATCH + AG_SCRATCH,
        compiler_params=params(3),
    )(lhs, rhs, x_own, keep, gains)


def ffn_out_kernel(lhs, rhs, resid, keep, out_o, stat_o, *scratch):
    p = Place()
    greet(x_peers(p))
    ffn_out = reduce_scatter(p, lhs, rhs, False, scratch[: len(RS_SCRATCH)])
    final = resid[...] + ffn_out
    k = keep[:, 0:1]
    stat_o[0] = jnp.full((8, 128), jnp.sum(k * ffn_out * ffn_out), F32)
    stat_o[1] = jnp.full((8, 128), jnp.sum(k * final * final), F32)
    out_o[p.x, 0] = final.astype(BF)
    all_gather(p, out_o, scratch[len(RS_SCRATCH) :], False)


def ffn_out_call(lhs, rhs, resid, keep):
    return pl.pallas_call(
        ffn_out_kernel,
        out_shape=(
            jax.ShapeDtypeStruct((4, 1, BLOCK, MODEL), BF),
            jax.ShapeDtypeStruct((2, 8, 128), F32),
        ),
        in_specs=[VM] * 4,
        out_specs=[VM] * 2,
        scratch_shapes=RS_SCRATCH + AG_SCRATCH,
        compiler_params=params(8),
    )(lhs, rhs, resid, keep)


def ffn_back_kernel(lhs, rhs, resid_ref, cot_own, gains, grad_o, resid_grad_o, gain_o, *scratch):
    p = Place()
    greet(x_peers(p))
    g = reduce_scatter(p, lhs, rhs, True, scratch[: len(RS_SCRATCH)])
    resid = resid_ref[...]
    inv = rms(resid)
    normed = resid * inv
    gain_o[...] = jnp.broadcast_to(jnp.sum(g * normed, axis=0, keepdims=True), (8, MODEL))
    grad_resid = cot_own[...].astype(F32) + norm_back(g, normed, full_row(gains, 1), inv)
    resid_grad_o[...] = grad_resid
    grad_o[p.x, 0] = grad_resid.astype(BF)
    all_gather(p, grad_o, scratch[len(RS_SCRATCH) :], True)


def ffn_back_call(lhs, rhs, resid, cot_own, gains):
    return pl.pallas_call(
        ffn_back_kernel,
        out_shape=(
            jax.ShapeDtypeStruct((4, 2, BLOCK, MODEL), BF),
            jax.ShapeDtypeStruct((BLOCK, MODEL), F32),
            jax.ShapeDtypeStruct((8, MODEL), F32),
        ),
        in_specs=[VM] * 5,
        out_specs=[VM] * 3,
        scratch_shapes=RS_SCRATCH + AG_SCRATCH,
        compiler_params=params(4),
    )(lhs, rhs, resid, cot_own, gains)


def attn_in_back_kernel(lhs, rhs, x_own, grad_resid, gains, out_o, gain_o, *scratch):
    p = Place()
    greet(x_peers(p))
    g = reduce_scatter(p, lhs, rhs, True, scratch[: len(RS_SCRATCH)])
    v = x_own[...].astype(F32)
    inv = rms(v)
    normed = v * inv
    gain_o[...] = jnp.broadcast_to(jnp.sum(g * normed, axis=0, keepdims=True), (8, MODEL))
    grad_in = grad_resid[...] + norm_back(g, normed, full_row(gains, 0), inv)
    out_o[p.x, 0] = grad_in.astype(BF)
    all_gather(p, out_o, scratch[len(RS_SCRATCH) :], False)


def attn_in_back_call(lhs, rhs, x_own, grad_resid, gains):
    return pl.pallas_call(
        attn_in_back_kernel,
        out_shape=(
            jax.ShapeDtypeStruct((4, 1, BLOCK, MODEL), BF),
            jax.ShapeDtypeStruct((8, MODEL), F32),
        ),
        in_specs=[VM] * 5,
        out_specs=[VM] * 2,
        scratch_shapes=RS_SCRATCH + AG_SCRATCH,
        compiler_params=params(6),
    )(lhs, rhs, x_own, grad_resid, gains)


UNITS = (
    (128, 512, 3, "col"),
    (64, 2048, 2, "row"),
    (32, 512, 1, "col"),
    (64, 768, 0, "row"),
)


def sum_kernel(*refs):
    nu = len(UNITS)
    srcs = refs[:4]
    outs = refs[4 : 4 + nu]
    at = 4 + nu
    own, yin, zout, zin, yhin = (refs[at + i * nu : at + (i + 1) * nu] for i in range(5))
    at += 5 * nu
    loc, send, recv = refs[at : at + 3]
    p = Place()
    greet(
        [p.sib(), p.dev(dy=1), p.dev(dy=-1), p.dev(dy=2), p.dev(dz=1), p.dev(dz=-1)]
    )

    def block_rows(u, block, rows):
        r, cols, src, kind = UNITS[u]
        if kind == "row":
            return srcs[src].at[pl.ds(block * r + rows[0], rows[1])]
        return srcs[src].at[pl.ds(rows[0], rows[1]), :, pl.ds(block * cols, cols)]

    def unit(u):
        rows, cols, _, _ = UNITS[u]
        part = rows // 8
        half = rows // 2
        waits = []

        def cp(n, src, dst, d):
            return remote(src, dst, send.at[u, n], recv.at[u, n], d)

        for core in (0, 1):
            for h in (0, 1):
                c = cp(
                    core * 2 + h,
                    block_rows(u, (1 - p.yl) * 2 + core, (h * half, half)),
                    yin[u].at[core, h],
                    p.dev(dy=1 if h == 0 else -1),
                )
                c.start()
                waits.append(c)
        local = []
        for core in (0, 1):
            for h in (0, 1):
                c = pltpu.make_async_copy(
                    block_rows(u, p.yl * 2 + core, (h * half, half)),
                    own[u].at[core, h],
                    loc.at[u, core * 2 + h],
                )
                c.start()
                local.append(c)
        yield
        for core in (0, 1):
            for h in (0, 1):
                local[core * 2 + h].wait()
                waits[core * 2 + h].wait_recv()
                own[u][core, h] = (
                    own[u][core, h].astype(F32) + yin[u][core, h].astype(F32)
                ).astype(BF)
        me, zr, zl, zf = p.z, (p.z + 1) % 4, (p.z + 3) % 4, (p.z + 2) % 4

        def chunk(ref, core, h, zc):
            return ref.at[core, h, pl.ds(zc * part, part)]

        far = []
        for core in (0, 1):
            for h in (0, 1):
                c = cp(
                    4 + core * 2 + h,
                    chunk(own[u], core, h, zf),
                    zin[u].at[0, core, h],
                    p.dev(dz=1 if h == 0 else -1),
                )
                c.start()
                far.append(c)
        yield
        near = []
        for side, zc in ((0, zr), (1, zl)):
            for core in (0, 1):
                for h in (0, 1):
                    v = own[u][core, h, pl.ds(zc * part, part)].astype(F32)
                    if h == side:
                        far[core * 2 + h].wait_recv()
                        v = v + zin[u][0, core, h].astype(F32)
                    zout[u][side, core, h] = v.astype(BF)
            c = cp(8 + side, zout[u].at[side], zin[u].at[1 + side], p.dev(dz=1 if side == 0 else -1))
            c.start()
            near.append(c)
        yield
        for c in near:
            c.wait_recv()
        for c in near:
            c.wait_send()
        for core in (0, 1):
            for h in (0, 1):
                v = own[u][core, h, pl.ds(me * part, part)].astype(F32)
                v = v + zin[u][1, core, h].astype(F32) + zin[u][2, core, h].astype(F32)
                zout[u][0, core, h] = v.astype(BF)
        yh = cp(10, zout[u].at[0], yhin[u], p.dev(dy=2))
        yh.start()
        for c in far:
            c.wait_send()
        yield
        yh.wait_recv()
        for core in (0, 1):
            for h in (0, 1):
                own[u][core, h, pl.ds(me * part, part)] = (
                    zout[u][0, core, h].astype(F32) + yhin[u][core, h].astype(F32)
                ).astype(BF)
        first = []
        for core in (0, 1):
            for h in (0, 1):
                for side in (0, 1):
                    here = chunk(own[u], core, h, me)
                    c = cp(
                        11 + core * 4 + h * 2 + side, here, here, p.dev(dz=1 if side == 0 else -1)
                    )
                    c.start()
                    first.append(c)
        yield
        second = []
        for core in (0, 1):
            for h in (0, 1):
                for side, zc in ((0, zl), (1, zr)):
                    here = chunk(own[u], core, h, zc)
                    n = 11 + core * 4 + h * 2 + side
                    cp(n, here, here, p.dev(dz=-1 if side == 0 else 1)).wait_recv()
                    if h == side:
                        c = cp(19 + core * 2 + h, here, here, p.dev(dz=1 if side == 0 else -1))
                        c.start()
                        second.append(c)
        yield
        for core in (0, 1):
            for h in (0, 1):
                here = chunk(own[u], core, h, zf)
                cp(19 + core * 2 + h, here, here, p.dev(dz=-1 if h == 0 else 1)).wait_recv()
        for c in first + second + waits + [yh]:
            c.wait_send()
        c = cp(23, own[u].at[1 - p.c], outs[u].at[1], p.sib())
        c.start()
        o = pltpu.make_async_copy(own[u].at[p.c], outs[u].at[0], loc.at[u, 4])
        o.start()
        yield
        c.wait()
        o.wait()

    todo = [unit(u) for u in range(nu)]
    alive = [True] * nu
    step = 0
    while any(alive):
        for u in range(nu):
            if alive[u] and step >= u:
                try:
                    next(todo[u])
                except StopIteration:
                    alive[u] = False
        step += 1


def sum_call(dqkv, do, dgu, dd):
    def bufs(shape):
        return [pltpu.VMEM(shape(r, c), BF) for r, c, _, _ in UNITS]

    return pl.pallas_call(
        sum_kernel,
        out_shape=tuple(
            jax.ShapeDtypeStruct((2, 2, r // 2, 8, c), BF) for r, c, _, _ in UNITS
        ),
        in_specs=[ANY] * 4,
        out_specs=[ANY] * len(UNITS),
        scratch_shapes=bufs(lambda r, c: (2, 2, r // 2, 8, c))
        + bufs(lambda r, c: (2, 2, r // 2, 8, c))
        + bufs(lambda r, c: (2, 2, 2, r // 8, 8, c))
        + bufs(lambda r, c: (3, 2, 2, r // 8, 8, c))
        + bufs(lambda r, c: (2, 2, r // 8, 8, c))
        + [DMA((len(UNITS), 5)), DMA((len(UNITS), 24)), DMA((len(UNITS), 24))],
        compiler_params=params(7),
    )(tiles(dqkv), tiles(do), tiles(dgu), tiles(dd))


def rope_tables(positions, head_size):
    half_dim = head_size // 2
    inv_freq = ROPE_BASE ** (-jnp.arange(half_dim, dtype=jnp.float32) * 2.0 / head_size)
    angles = positions.astype(jnp.float32)[:, None] * inv_freq[None, :]
    cosine, sine = jnp.cos(angles), jnp.sin(angles)
    return jnp.concatenate([cosine, cosine], axis=1), jnp.concatenate([-sine, sine], axis=1)


def piece_index(starts, piece_tags, positions):
    inside = (positions[None, :, None] >= starts[:, None, :]) & (
        positions[None, :, None] < starts[:, None, :] + PIECE
    )
    tagged = jnp.where(inside, piece_tags[:, None, :] + 1, 0)
    return jnp.sum(tagged, axis=2) - 1


def per_device(
    inputs,
    cotangent,
    q_weight,
    k_weight,
    v_weight,
    o_weight,
    gate_weight,
    up_weight,
    down_weight,
    attn_gain,
    ffn_gain,
    piece_starts,
    piece_ids,
    valid_mask,
):
    x_at = lax.axis_index("tensor")
    core = lax.axis_index("shard") % 2
    ctx = lax.axis_index("context")
    positions = jnp.arange(1024, dtype=jnp.int32)
    cos_t, sin_t = rope_tables(positions, HEAD_DIM)
    cos_full, sin_full = jnp.tile(cos_t, (1, 4)), jnp.tile(sin_t, (1, 4))
    cos_own = jnp.tile(lax.dynamic_slice_in_dim(cos_full, ctx * BLOCK, BLOCK, 0), (2, 1))
    sin_own = jnp.tile(lax.dynamic_slice_in_dim(sin_full, ctx * BLOCK, BLOCK, 0), (2, 1))
    meta = jnp.concatenate([piece_index(piece_starts, piece_ids, positions), valid_mask], axis=0)
    gains_own = jnp.concatenate(
        [
            attn_gain.astype(F32)[None],
            ffn_gain.astype(F32)[None],
            jnp.zeros((6, attn_gain.shape[0]), F32),
        ],
        axis=0,
    )
    wqkv, wo, wgu, wd, gains, meta_all, cot_all, attn_in, qkv = start_call(
        inputs,
        cotangent,
        (q_weight, k_weight, v_weight, o_weight, gate_weight, up_weight, down_weight),
        gains_own,
        meta,
        cos_own,
        sin_own,
    )
    seq = lax.dynamic_slice(meta_all, (ctx % 2, 0, 0), (1, 8, 1024))[0]
    piece_row = lax.dynamic_slice_in_dim(seq, ctx // 2, 1, 0)
    valid_row = lax.dynamic_slice_in_dim(seq, 4 + ctx // 2, 1, 0)
    info = jnp.concatenate([piece_row, valid_row, jnp.zeros((6, 1024), jnp.int32)], axis=0)
    pcol = jnp.broadcast_to(piece_row.reshape(1024, 1), (1024, 128))
    wqkv, wo, wgu, wd = rows_of(wqkv), rows_of(wo), rows_of(wgu), rows_of(wd)
    cot_all = rows_of(cot_all)
    qkv = qkv.reshape(1024, 768)
    attended_seq, lse = attend_call(qkv, info, pcol)
    slots = attended_seq.reshape(4, 2, BLOCK, 256)
    attended = jnp.where(core == 0, slots, slots[:, ::-1])
    x_own = lax.dynamic_index_in_dim(inputs, x_at, 0, keepdims=False)
    cot_own = lax.dynamic_index_in_dim(cotangent, x_at, 0, keepdims=False)
    keep_own = lax.dynamic_slice(valid_mask, (x_at, ctx * BLOCK), (1, BLOCK)).astype(F32)
    keep = jnp.broadcast_to(keep_own.reshape(BLOCK, 1), (BLOCK, 128))
    attended = attended.reshape(4, 256, 256)
    ffn_in, resid, stat_attn = out_proj_call(attended, wo, x_own, keep, gains)
    ffn_in = ffn_in.reshape(1024, MODEL)
    cot_rows = cot_all.reshape(1024, MODEL)
    gate_val = jnp.dot(ffn_in, wgu[:, :1024], preferred_element_type=F32)
    up_val = jnp.dot(ffn_in, wgu[:, 1024:], preferred_element_type=F32)
    grad_hidden = jnp.einsum("nd,fd->nf", cot_rows, wd, preferred_element_type=F32)
    gate_sig = jax.nn.sigmoid(gate_val)
    hidden = (gate_val * gate_sig * up_val).astype(BF)
    grad_gate = (grad_hidden * up_val * gate_sig * (1.0 + gate_val * (1.0 - gate_sig))).astype(BF)
    grad_up = (grad_hidden * gate_val * gate_sig).astype(BF)
    grad_gu = jnp.concatenate([grad_gate, grad_up], axis=1)
    grad_attn, grad_resid, ffn_gain_part = ffn_back_call(
        grad_gu.reshape(4, 256, 2048), wgu, resid, cot_own, gains
    )
    grad_attn = grad_attn.reshape(1024, MODEL)
    grad_att = jnp.einsum("nd,cd->nc", grad_attn, wo, preferred_element_type=F32).astype(BF)
    d_seq = attend_back_call(
        grad_att.reshape(8, BLOCK, 256), qkv, info, pcol, lse, cos_full, sin_full
    )
    slots = d_seq.reshape(4, 2, BLOCK, 768)
    dqkv = jnp.where(core == 0, slots, slots[:, ::-1]).reshape(4, 256, 768)
    input_grad, attn_gain_part = attn_in_back_call(dqkv, wqkv, x_own, grad_resid, gains)
    output, stat_ffn = ffn_out_call(hidden.reshape(4, 256, 1024), wd, resid, keep)

    def back(a, b):
        return jnp.einsum("nd,nf->df", a, b, preferred_element_type=F32).astype(BF)

    attn_rows = attn_in.reshape(1024, MODEL)
    dd = back(hidden, cot_rows)
    dgu = back(ffn_in, grad_gu)
    do = back(attended.reshape(1024, 256), grad_attn)
    dw = back(attn_rows, dqkv.reshape(1024, 768))
    sd, sgu, so, sqkv = sum_call(dw, do, dgu, dd)

    def halves(v, rows, cols):
        v = v.reshape(2, rows, cols).astype(F32)
        return jnp.where(core == 0, v, v[::-1])

    sd = halves(sd, 1024, 512).reshape(2048, 512)
    so = halves(so, 256, 512).reshape(512, 512)
    sgu = halves(sgu, 512, 2048)
    gate_grad = jnp.concatenate([sgu[0, :, :1024], sgu[1, :, :1024]], axis=1)
    up_grad = jnp.concatenate([sgu[0, :, 1024:], sgu[1, :, 1024:]], axis=1)
    sqkv = halves(sqkv, 512, 768)
    qkv_grads = [
        jnp.concatenate([sqkv[0, :, i * 256 : (i + 1) * 256], sqkv[1, :, i * 256 : (i + 1) * 256]], axis=1)
        for i in range(3)
    ]
    small = jnp.concatenate(
        [
            attn_gain_part[0],
            ffn_gain_part[0],
            jnp.stack(
                [jnp.sum(keep_own), stat_attn[0, 0], stat_ffn[0, 0, 0], stat_ffn[1, 0, 0]]
            ),
            jnp.zeros((124,), F32),
        ]
    )
    small = lax.psum(small, ("shard", "context", "tensor"))
    stat = small[2 * MODEL : 2 * MODEL + 4]
    branch_rms = jnp.sqrt(stat[1:] / (jnp.maximum(stat[0], 1.0) * MODEL))
    gain_start = (lax.axis_index("shard") * 4 + x_at) * BLOCK
    attn_gain_out = lax.dynamic_slice_in_dim(small, gain_start, BLOCK, 0)
    ffn_gain_out = lax.dynamic_slice_in_dim(small, MODEL + gain_start, BLOCK, 0)
    return (
        output.reshape(4, BLOCK, MODEL),
        input_grad.reshape(4, BLOCK, MODEL),
        *qkv_grads,
        so,
        gate_grad,
        up_grad,
        sd,
        attn_gain_out,
        ffn_gain_out,
        branch_rms,
    )


def solution(mesh):
    return jax.shard_map(
        per_device,
        mesh=mesh,
        in_specs=(
            P("shard", "context", None),
            P("shard", "context", None),
            P("shard", "tensor"),
            P("shard", "tensor"),
            P("shard", "tensor"),
            P("tensor", "shard"),
            P("shard", "tensor"),
            P("shard", "tensor"),
            P("tensor", "shard"),
            P("shard"),
            P("shard"),
            P("shard", None),
            P("shard", None),
            P("shard", None),
        ),
        out_specs=(
            P("shard", "context", None),
            P("shard", "context", None),
            P("shard", "tensor"),
            P("shard", "tensor"),
            P("shard", "tensor"),
            P("tensor", "shard"),
            P("shard", "tensor"),
            P("shard", "tensor"),
            P("tensor", "shard"),
            P(("shard", "tensor")),
            P(("shard", "tensor")),
            P(),
        ),
        check_vma=False,
    )
```

```python
import functools

import jax
import jax.numpy as jnp
from jax import lax
from jax.experimental import pallas as pl
from jax.experimental.pallas import tpu as pltpu
from jax.sharding import PartitionSpec as P

HEAD_DIM = 64
PIECE = 256
NORM_EPS = 1e-05
ROPE_BASE = 130000.0
MASK_FILL = -1e30
BF = jnp.bfloat16
F32 = jnp.float32
ANY = pl.BlockSpec(memory_space=pl.ANY)
VM = pl.BlockSpec(memory_space=pltpu.VMEM)
DMA = pltpu.SemaphoreType.DMA
PROJ_ORDER = "gxxxxxggxgxgxgxggx"
FFN_ORDER = "axbxxaxbxaxbabxababaxbxaxbxbba"
ATTEND_ORDER = "bxmxxaxbxmbaxabmabmbamamxxbaaxmxbamb"
LAST_ORDER = "abaadxxbbcaxdxxcdbaxcabdcbsdbsbcadxsabcxsadxxcsdccd"
FFN_TILE, FFN_ROWS, FFN_BACK = 256, 1024, 2048
VMEM_LIMIT = 60 * 1024 * 1024
MODEL = 2048
BLOCK = 128
MESH_ID = pl.DeviceIdType.MESH


class Place:
    def __init__(self):
        self.s = lax.axis_index("shard")
        self.k = lax.axis_index("context")
        self.x = lax.axis_index("tensor")
        self.yl = self.s // 2
        self.c = self.s % 2
        self.y = (self.k // 4) * 2 + self.yl
        self.z = self.k % 4

    def dev(self, dx=0, dy=0, dz=0, core=None):
        x = (self.x + dx + 4) % 4
        y = (self.y + dy + 4) % 4
        z = (self.z + dz + 4) % 4
        c = self.c if core is None else core
        return {"shard": (y % 2) * 2 + c, "context": (y // 2) * 4 + z, "tensor": x}

    def member(self, k):
        return {"shard": self.s, "context": k, "tensor": self.x}

    def sib(self):
        return self.dev(core=1 - self.c)


def remote(src, dst, send_sem, recv_sem, device):
    return pltpu.make_async_remote_copy(
        src_ref=src,
        dst_ref=dst,
        send_sem=send_sem,
        recv_sem=recv_sem,
        device_id=device,
        device_id_type=MESH_ID,
    )


def greet(devices):
    barrier = pltpu.get_barrier_semaphore()
    for d in devices:
        pl.semaphore_signal(barrier, inc=1, device_id=d, device_id_type=MESH_ID)
    pl.semaphore_wait(barrier, len(devices))


def params(collective_id=None):
    if collective_id is None:
        return pltpu.CompilerParams(vmem_limit_bytes=VMEM_LIMIT)
    return pltpu.CompilerParams(
        vmem_limit_bytes=VMEM_LIMIT, collective_id=collective_id, has_side_effects=True
    )


def tiles(v):
    return v.reshape(*v.shape[:-2], v.shape[-2] // 8, 8, v.shape[-1])


def rows_of(v):
    return v.reshape(*v.shape[:-3], v.shape[-3] * 8, v.shape[-1])


def context_peers(p):
    return [p.member((p.k + d) % 8) for d in range(1, 8)]


def swap_halves(v):
    width = v.shape[1]
    lane = lax.broadcasted_iota(jnp.int32, v.shape, 1) % HEAD_DIM
    return jnp.where(
        lane < HEAD_DIM // 2,
        pltpu.roll(v, width - HEAD_DIM // 2, 1),
        pltpu.roll(v, HEAD_DIM // 2, 1),
    )


WEIGHTS = (
    (256, "row", 0),
    (256, "row", 256),
    (256, "row", 512),
    (256, "col", 0),
    (1024, "row", 0),
    (1024, "row", 1024),
    (1024, "col", 0),
)


class Gather:
    def __init__(self, p, ws, srcs, dsts, stages, sems):
        self.p, self.ws, self.srcs, self.dsts, self.stages = p, ws, srcs, dsts, stages
        self.y_send, self.y_recv, self.z_send, self.z_recv, self.s_send, self.s_recv, self.loc = sems
        self.qa = 2 * (p.z % 2)

    @staticmethod
    def sems(n):
        return [DMA((n, 2, 2))] * 4 + [DMA((n,))] * 3

    @staticmethod
    def peers(p):
        return (
            [p.sib()]
            + [p.dev(dy=dy, core=core) for dy in (-1, 1) for core in (0, 1)]
            + [p.dev(dz=1), p.dev(dz=-1)]
        )

    def src(self, i, half, quarter):
        size, kind, _ = WEIGHTS[self.ws[i]]
        if kind == "row":
            rows = pl.ds(0, 64) if quarter is None else pl.ds(quarter * 16, 16)
            return self.srcs[i].at[rows, :, pl.ds(half * size, size)]
        size = size // 8
        if quarter is None:
            return self.srcs[i].at[pl.ds(half * size, size)]
        return self.srcs[i].at[pl.ds(half * size + quarter * (size // 4), size // 4)]

    def dst(self, i, block, quarter):
        size, kind, off = WEIGHTS[self.ws[i]]
        if kind == "row":
            rows = (
                pl.ds(block * 64, 64)
                if quarter is None
                else pl.ds(block * 64 + quarter * 16, 16)
            )
            return self.dsts[i].at[rows, :, pl.ds(off, size)]
        size = size // 8
        cols = pl.ds(block * 512, 512)
        if quarter is None:
            return self.dsts[i].at[:, :, cols]
        return self.dsts[i].at[pl.ds(quarter * (size // 4), size // 4), :, cols]

    def y_copy(self, i, side, core):
        p = self.p
        quarter = self.qa + side
        return remote(
            self.src(i, core, quarter),
            self.dst(i, p.s, quarter),
            self.y_send.at[i, side, core],
            self.y_recv.at[i, side, p.c],
            p.dev(dy=-1 if side == 0 else 1, core=core),
        )

    def y_arrival(self, i, side, core):
        p = self.p
        here = self.dst(i, (1 - p.yl) * 2 + core, self.qa + side)
        return remote(
            here,
            here,
            self.y_send.at[i, side, core],
            self.y_recv.at[i, side, core],
            p.dev(dy=1 if side == 0 else -1, core=core),
        )

    def z_copy(self, i, side, core, arrival=False):
        p = self.p
        quarter = 2 - self.qa + side if arrival else self.qa + side
        here = self.dst(i, (1 - p.yl) * 2 + core, quarter)
        return remote(
            here,
            here,
            self.z_send.at[i, side, core],
            self.z_recv.at[i, side, core],
            p.dev(dz=1 if (side == 0) == arrival else -1),
        )

    def sib_copy(self, i, arrival=False):
        p = self.p
        there = self.dst(i, p.yl * 2 + 1 - p.c if arrival else p.s, None)
        return remote(
            there if arrival else self.src(i, 1 - p.c, None),
            there,
            self.s_send.at[i],
            self.s_recv.at[i],
            p.sib(),
        )

    def own_copy(self, i, step):
        stage = self.stages[i]
        here = self.dst(i, self.p.s, None)
        if step == 1:
            return pltpu.make_async_copy(stage, here, self.loc.at[i])
        return pltpu.make_async_copy(
            self.src(i, self.p.c, None), here if stage is None else stage, self.loc.at[i]
        )

    def start(self):
        for i in range(len(self.ws)):
            for core in (0, 1):
                for side in (0, 1):
                    self.y_copy(i, side, core).start()
        for i in range(len(self.ws)):
            self.sib_copy(i).start()
            self.own_copy(i, 0).start()

    def pass_on(self, i):
        for side in (0, 1):
            for core in (0, 1):
                self.y_arrival(i, side, core).wait_recv()
                self.z_copy(i, side, core).start()
        if self.stages[i] is not None:
            self.own_copy(i, 0).wait()
            self.own_copy(i, 1).start()

    def arrive(self, i):
        for side in (0, 1):
            for core in (0, 1):
                self.z_copy(i, side, core, True).wait_recv()
        self.sib_copy(i, True).wait_recv()
        self.own_copy(i, 0 if self.stages[i] is None else 1).wait()

    def sent(self, i):
        self.sib_copy(i).wait_send()
        for side in (0, 1):
            for core in (0, 1):
                self.y_copy(i, side, core).wait_send()
                self.z_copy(i, side, core).wait_send()

    def steps(self):
        self.start()
        yield
        for i in range(len(self.ws)):
            self.pass_on(i)
            yield
        for i in range(len(self.ws)):
            self.arrive(i)
            self.sent(i)
            yield


def run(order, **gens):
    alive = dict(gens)

    def step(name):
        if name in alive:
            try:
                next(alive[name])
            except StopIteration:
                del alive[name]

    for name in order:
        step(name)
    while alive:
        for name in list(alive):
            step(name)


def start_kernel(
    x_ref,
    cot_ref,
    wq,
    wk,
    wv,
    wo,
    gain_ref,
    meta_ref,
    cos_ref,
    sin_ref,
    wqkv_o,
    wo_o,
    gains_o,
    meta_o,
    cot_o,
    attn_in_o,
    qkv_o,
    x_all,
    qkv_send,
    stage_o,
    stage_cot,
    loc,
    misc_send,
    misc_recv,
    gain_send,
    gain_recv,
    a2a_send,
    a2a_recv,
    *sems,
):
    p = Place()
    g = Gather(
        p,
        (0, 1, 2, 3),
        (wq, wk, wv, wo),
        (wqkv_o, wqkv_o, wqkv_o, wo_o),
        (None, None, None, stage_o),
        sems,
    )
    greet(
        [p.sib()]
        + [p.dev(dy=dy, core=core) for dy in (-1, 1) for core in (0, 1)]
        + context_peers(p)
    )
    gain_targets = [p.sib()] + [p.dev(dy=1, core=core) for core in (0, 1)]
    gain_copies = [
        remote(gain_ref, gains_o.at[p.s], gain_send.at[i], gain_recv.at[i if i == 0 else 1 + p.c], d)
        for i, d in enumerate(gain_targets)
    ]
    for c in gain_copies:
        c.start()
    x_own = pltpu.make_async_copy(x_ref, x_all.at[:, 0], loc.at[0])
    x_own.start()
    x_out = remote(x_ref, x_all.at[:, 1], misc_send.at[0], misc_recv.at[0], p.sib())
    x_out.start()
    g.start()
    gain_own = pltpu.make_async_copy(gain_ref, gains_o.at[p.s], loc.at[1])
    gain_own.start()
    meta_own = pltpu.make_async_copy(meta_ref, meta_o.at[p.c], loc.at[2])
    meta_own.start()
    meta_out = remote(meta_ref, meta_o.at[p.c], misc_send.at[1], misc_recv.at[1], p.sib())
    meta_out.start()
    cot_in = pltpu.make_async_copy(cot_ref, stage_cot, loc.at[3])
    cot_in.start()
    cot_own = pltpu.make_async_copy(stage_cot, cot_o.at[:, 0], loc.at[3])
    cot_out = remote(cot_ref, cot_o.at[:, 1], misc_send.at[2], misc_recv.at[2], p.sib())
    cot_out.start()

    gain_own.wait()
    for i in range(3):
        block = p.yl * 2 + 1 - p.c if i == 0 else (1 - p.yl) * 2 + (i - 1)
        here = gains_o.at[block]
        remote(here, here, gain_send.at[i], gain_recv.at[i], p.sib()).wait_recv()
    x_own.wait()
    x_out.wait_recv()
    gain = jnp.concatenate([gains_o[b, 0:1, :] for b in range(4)], axis=1)

    def norm_step(i, carry):
        v = x_all[i // 2, i % 2].astype(F32).reshape(BLOCK, MODEL)
        r = lax.rsqrt(jnp.mean(v * v, axis=1, keepdims=True) + NORM_EPS)
        attn_in_o[i // 2, pl.ds((i % 2) * BLOCK, BLOCK), :] = (v * r * gain).astype(BF)
        return carry

    lax.fori_loop(0, 8, norm_step, 0)
    for i in range(4):
        g.pass_on(i)
    cot_in.wait()
    cot_own.start()

    def send_block(j, q):
        other = p.c if q == 0 else 1 - p.c
        k = j * 2 + other
        slot = j * 2 + q
        return (
            k,
            remote(
                qkv_send.at[slot],
                qkv_o.at[p.k],
                a2a_send.at[slot],
                a2a_recv.at[p.k],
                p.member(k),
            ),
            pltpu.make_async_copy(qkv_send.at[slot], qkv_o.at[p.k], a2a_send.at[slot]),
        )

    for i in range(3):
        g.arrive(i)

    def qkv_step(j, carry):
        a = attn_in_o[j]
        for part in range(3):
            cols = pl.ds(part * 256, 256)
            w = wqkv_o[:, :, cols].reshape(MODEL, 256)
            v = jnp.dot(a, w, preferred_element_type=F32)
            if part < 2:
                v = v * cos_ref[...] + swap_halves(v) * sin_ref[...]
            v = v.reshape(32, 8, 256).astype(BF)
            qkv_send[j * 2, :, :, cols] = v[:16]
            qkv_send[j * 2 + 1, :, :, cols] = v[16:]
        for q in (0, 1):
            k, out, here = send_block(j, q)

            @pl.when(k != p.k)
            def _():
                out.start()

            @pl.when(k == p.k)
            def _():
                here.start()

        return carry

    lax.fori_loop(0, 4, qkv_step, 0)
    g.arrive(3)
    for i in range(4):
        g.sent(i)
    x_out.wait_send()
    meta_own.wait()
    meta_out.wait_send()
    here = meta_o.at[1 - p.c]
    remote(here, here, misc_send.at[1], misc_recv.at[1], p.sib()).wait_recv()
    cot_own.wait()
    cot_out.wait()
    for c in gain_copies:
        c.wait_send()
    for j in range(4):
        for q in (0, 1):
            k, out, here = send_block(j, q)

            @pl.when(k != p.k)
            def _():
                out.wait_send()

            @pl.when(k == p.k)
            def _():
                here.wait()

    for i in range(8):

        @pl.when(i != p.k)
        def _():
            here = qkv_o.at[i]
            remote(here, here, a2a_send.at[i], a2a_recv.at[i], p.member(i)).wait_recv()


def start_call(x, cot, weights, gains, meta, cos_t, sin_t):
    shapes = (
        jax.ShapeDtypeStruct((256, 8, 768), BF),
        jax.ShapeDtypeStruct((32, 8, 2048), BF),
        jax.ShapeDtypeStruct((4, 8, 512), F32),
        jax.ShapeDtypeStruct((2, 8, 1024), jnp.int32),
        jax.ShapeDtypeStruct((4, 2, 16, 8, MODEL), BF),
        jax.ShapeDtypeStruct((4, 256, MODEL), BF),
        jax.ShapeDtypeStruct((8, 16, 8, 768), BF),
    )
    return pl.pallas_call(
        start_kernel,
        out_shape=shapes,
        in_specs=[ANY] * 6 + [VM, ANY, VM, VM],
        out_specs=[VM, ANY, VM, ANY, ANY, VM, ANY],
        scratch_shapes=[
            pltpu.VMEM((4, 2, 16, 8, MODEL), BF),
            pltpu.VMEM((8, 16, 8, 768), BF),
            pltpu.VMEM((32, 8, 512), BF),
            pltpu.VMEM((4, 16, 8, MODEL), BF),
            DMA((4,)),
            DMA((3,)),
            DMA((3,)),
            DMA((3,)),
            DMA((3,)),
            DMA((8,)),
            DMA((8,)),
        ]
        + Gather.sems(4),
        compiler_params=params(1),
    )(tiles(x), tiles(cot), *[tiles(w) for w in weights], gains, meta, cos_t, sin_t)


def bias_rows(qb, rows, prow, vrow, pcol):
    i = qb * rows + lax.broadcasted_iota(jnp.int32, (rows, 1024), 0)
    j = lax.broadcasted_iota(jnp.int32, (rows, 1024), 1)
    same = (pcol >= 0) & (pcol == prow)
    ok = ((j <= i) | same) & ((vrow > 0) | (i == j))
    return jnp.where(ok, 0.0, MASK_FILL)


def attend_kernel(
    qkv, info, pcol, out_o, lse_o, o_send, a2a_send, a2a_recv
):
    p = Place()
    greet(context_peers(p))
    rows = 256

    def sends(i):
        return (
            remote(o_send.at[i], out_o.at[p.k], a2a_send.at[i], a2a_recv.at[p.k], p.member(i)),
            pltpu.make_async_copy(o_send.at[i], out_o.at[p.k], a2a_send.at[i]),
        )

    def step(qb, carry):
        at = pl.ds(pl.multiple_of(qb * rows, rows), rows)
        bias = bias_rows(qb, rows, info[0:1, :], info[1:2, :], pcol[at, 0:1])
        lane = lax.broadcasted_iota(jnp.int32, (rows, 128), 1)
        totals = jnp.zeros((rows, 128), F32)
        outs = []
        for h in range(4):
            q = qkv[at, pl.ds(h * 64, 64)]
            k = qkv[:, pl.ds(256 + h * 64, 64)]
            v = qkv[:, pl.ds(512 + h * 64, 64)]
            sc = lax.dot_general(q, k, (((1,), (1,)), ((), ())), preferred_element_type=F32)
            sc = sc * (HEAD_DIM**-0.5) + bias
            top = jnp.max(sc, axis=1, keepdims=True)
            e = jnp.exp(sc - top)
            total = jnp.sum(e, axis=1, keepdims=True)
            prob = (e * (1.0 / total)).astype(BF)
            totals = jnp.where(lane == h, top + jnp.log(total), totals)
            outs.append(jnp.dot(prob, v, preferred_element_type=F32))
        lse_o[at, :] = totals
        o = jnp.concatenate(outs, axis=1).reshape(32, 8, 256).astype(BF)
        for half in (0, 1):
            i = qb * 2 + half
            o_send[i] = o[half * 16 : (half + 1) * 16]
            out, here = sends(i)

            @pl.when(i != p.k)
            def _():
                out.start()

            @pl.when(i == p.k)
            def _():
                here.start()

        return carry

    lax.fori_loop(0, 4, step, 0)
    for i in range(8):
        out, here = sends(i)

        @pl.when(i != p.k)
        def _():
            out.wait_send()
            spot = out_o.at[i]
            remote(spot, spot, a2a_send.at[i], a2a_recv.at[i], p.member(i)).wait_recv()

        @pl.when(i == p.k)
        def _():
            here.wait()


def attend_call(qkv, info, pcol):
    return pl.pallas_call(
        attend_kernel,
        out_shape=(
            jax.ShapeDtypeStruct((8, 16, 8, 256), BF),
            jax.ShapeDtypeStruct((1024, 128), F32),
        ),
        in_specs=[VM] * 3,
        out_specs=[ANY, VM],
        scratch_shapes=[pltpu.VMEM((8, 16, 8, 256), BF), DMA((8,)), DMA((8,))],
        compiler_params=params(2),
    )(qkv, info, pcol)


X_SCRATCH = [
    pltpu.VMEM((4, BLOCK, MODEL), F32),
    pltpu.VMEM((4, BLOCK, MODEL), BF),
    pltpu.VMEM((4, BLOCK, MODEL), BF),
    pltpu.VMEM((3, BLOCK, MODEL), BF),
    pltpu.VMEM((3, BLOCK, MODEL), BF),
    DMA((4,)),
    DMA((4,)),
    DMA((6,)),
    DMA((6,)),
    DMA((10,)),
    DMA((10,)),
]


def x_peers(p):
    return [p.sib(), p.dev(dx=1), p.dev(dx=-1)]


def x_phase(p, lhs, rhs, transposed, scratch, out, both, finish):
    acc, sib_out, sib_in, x_out, x_in, s_send, s_recv, x_send, x_recv, g_send, g_recv = scratch
    tile = 256
    half = BLOCK // 2
    top, low = pl.ds(0, half), pl.ds(half, half)
    to_right, to_left = p.dev(dx=1), p.dev(dx=-1)

    def sib_copy(r):
        return remote(sib_out.at[r], sib_in.at[r], s_send.at[r], s_recv.at[r], p.sib())

    def product(r):
        j = (p.x + r) % 4

        def step(n, carry):
            cols = pl.ds(pl.multiple_of(n * tile, tile), tile)
            first = 0
            v = 0.0
            for part in lhs:
                depth = pl.ds(first, part.shape[2])
                first += part.shape[2]
                if transposed:
                    v += lax.dot_general(
                        part[j],
                        rhs[cols, depth],
                        (((1,), (1,)), ((), ())),
                        preferred_element_type=F32,
                    )
                else:
                    v += jnp.dot(part[j], rhs[depth, cols], preferred_element_type=F32)
            acc[r, :, cols] = v[:BLOCK]
            sib_out[r, :, cols] = v[BLOCK:].astype(BF)
            return carry

        lax.fori_loop(0, MODEL // tile, step, 0)
        sib_copy(r).start()

    def along(n, slot, rows, device):
        return remote(
            x_out.at[slot, rows], x_in.at[slot, rows], x_send.at[n], x_recv.at[n], device
        )

    far_right, far_left = along(0, 0, top, to_right), along(1, 0, low, to_left)
    right_low, right_top = along(2, 1, low, to_right), along(3, 1, top, to_right)
    left_top, left_low = along(4, 2, top, to_left), along(5, 2, low, to_left)
    product(2)
    yield
    product(1)
    sib_copy(2).wait_recv()
    x_out[0] = (acc[2] + sib_in[2].astype(F32)).astype(BF)
    far_right.start()
    far_left.start()
    yield
    product(3)
    sib_copy(1).wait_recv()
    x_out[1, half:] = (acc[1, half:] + sib_in[1, half:].astype(F32)).astype(BF)
    right_low.start()
    sib_copy(3).wait_recv()
    x_out[2, 0:half] = (acc[3, 0:half] + sib_in[3, 0:half].astype(F32)).astype(BF)
    left_top.start()
    yield
    product(0)
    yield
    far_right.wait_recv()
    x_out[1, 0:half] = (
        acc[1, 0:half] + sib_in[1, 0:half].astype(F32) + x_in[0, 0:half].astype(F32)
    ).astype(BF)
    right_top.start()
    far_left.wait_recv()
    x_out[2, half:] = (
        acc[3, half:] + sib_in[3, half:].astype(F32) + x_in[0, half:].astype(F32)
    ).astype(BF)
    left_low.start()
    yield
    sib_copy(0).wait_recv()
    acc[0] += sib_in[0].astype(F32)
    for c in (right_low, left_top, right_top, left_low):
        c.wait_recv()
    total = acc[0] + x_in[1].astype(F32) + x_in[2].astype(F32)
    for r in range(4):
        sib_copy(r).wait_send()
    for c in (far_right, far_left, right_low, right_top, left_top, left_low):
        c.wait_send()

    me, right, left, far = p.x, (p.x + 1) % 4, (p.x + 3) % 4, (p.x + 2) % 4
    out[me, 0] = finish(total)
    sent = []

    def copy(n, j, rows, d):
        src = out.at[j, 0, rows]
        return remote(src, src, g_send.at[n], g_recv.at[n], d)

    def go(c):
        c.start()
        sent.append(c)

    def to_sib(n, j):
        return remote(out.at[j, 0], out.at[j, 1], g_send.at[n], g_recv.at[n], p.sib())

    go(copy(0, me, top, to_right))
    go(copy(1, me, low, to_left))
    go(copy(2, me, low, to_right))
    go(copy(3, me, top, to_left))
    if both:
        go(to_sib(6, me))
    yield
    copy(0, left, top, to_left).wait_recv()
    go(copy(4, left, top, to_right))
    copy(1, right, low, to_right).wait_recv()
    go(copy(5, right, low, to_left))
    yield
    copy(2, left, low, to_left).wait_recv()
    copy(3, right, top, to_right).wait_recv()
    if both:
        go(to_sib(7, left))
        go(to_sib(8, right))
    yield
    copy(4, far, top, to_left).wait_recv()
    copy(5, far, low, to_right).wait_recv()
    if both:
        go(to_sib(9, far))
        yield
        for n, j in ((6, me), (7, left), (8, right), (9, far)):
            to_sib(n, j).wait_recv()
    for c in sent:
        c.wait_send()


def rms(v):
    return lax.rsqrt(jnp.mean(v * v, axis=1, keepdims=True) + NORM_EPS)


def full_row(gains, row):
    return jnp.concatenate([gains[b, row : row + 1, :] for b in range(4)], axis=1)


def norm_back(grad, normed, gain, inv):
    w = grad * gain
    return inv * (w - normed * jnp.mean(w * normed, axis=1, keepdims=True))


UNITS = {
    "down_a": (64, 512, "col", 0, ()),
    "down_b": (64, 512, "col", 64, ()),
    "gate_a": (64, 512, "row", 0, (1024,)),
    "gate_b": (64, 512, "row", 512, (1024,)),
    "up_a": (64, 512, "row", 0, (1024,)),
    "up_b": (64, 512, "row", 512, (1024,)),
    "out": (32, 512, "col", 0, ()),
    "qkv": (64, 768, "row", 0, (256, 256, 256)),
}
UNIT_SCRATCH = 8
DOWN_OUT = jax.ShapeDtypeStruct((2, 2, 2, 32, 8, 512), BF)
OUT_OUT = jax.ShapeDtypeStruct((2, 1, 2, 16, 8, 512), BF)
FFN_OUT = jax.ShapeDtypeStruct((2, 32, 8, 2048), BF)
QKV_OUT = jax.ShapeDtypeStruct((2, 32, 8, 512), BF)


def unit_scratch(name):
    r, c, _, _, _ = UNITS[name]
    return [
        pltpu.VMEM((2, 2, r // 2, 8, c), BF),
        pltpu.VMEM((2, 2, r // 2, 8, c), BF),
        pltpu.VMEM((2, 2, 2, r // 8, 8, c), BF),
        pltpu.VMEM((3, 2, 2, r // 8, 8, c), BF),
        pltpu.VMEM((2, 2, r // 8, 8, c), BF),
        DMA((4,)),
        DMA((18,)),
        DMA((18,)),
    ]


def unit_peers(p):
    return [p.sib(), p.dev(dy=1), p.dev(dy=-1), p.dev(dy=2), p.dev(dz=1), p.dev(dz=-1)]


def unit(p, name, src, outs, scratch):
    rows, cols, kind, first, widths = UNITS[name]
    own, yin, zout, zin, yhin, loc, send, recv = scratch
    part = rows // 8
    half = rows // 2
    z_of = {0: p.dev(dz=1), 1: p.dev(dz=-1)}
    me, zr, zl, zf = p.z, (p.z + 1) % 4, (p.z + 3) % 4, (p.z + 2) % 4

    def cp(n, src, dst, d):
        return remote(src, dst, send.at[n], recv.at[n], d)

    def fetch(yl, h, dst, make):
        if kind == "row":
            return [
                make(
                    h * 2,
                    src.at[pl.ds(yl * 2, 2), pl.ds(h * half, half), :, pl.ds(first, cols)],
                    dst.at[:, h],
                )
            ]
        return [
            make(
                h * 2 + core,
                src.at[pl.ds(first + h * half, half), :, pl.ds((yl * 2 + core) * cols, cols)],
                dst.at[core, h],
            )
            for core in (0, 1)
        ]

    along_y, local = [], []
    for h in (0, 1):
        d = p.dev(dy=1 if h == 0 else -1)
        along_y += fetch(1 - p.yl, h, yin, lambda n, a, b, d=d: cp(n, a, b, d))
        local += fetch(p.yl, h, own, lambda n, a, b: pltpu.make_async_copy(a, b, loc.at[n]))
    for c in along_y + local:
        c.start()
    yield
    for c in local:
        c.wait()
    for c in along_y:
        c.wait_recv()
    own[...] = (own[...].astype(F32) + yin[...].astype(F32)).astype(BF)

    def chunk(h, zc):
        return own.at[:, h, pl.ds(zc * part, part)]

    far = [cp(4 + h, chunk(h, zf), zin.at[0, :, h], z_of[h]) for h in (0, 1)]
    for c in far:
        c.start()
    yield
    for c in far:
        c.wait_send()
    near = []
    for side, zc in ((0, zr), (1, zl)):
        zout[side, :, 1 - side] = own[:, 1 - side, pl.ds(zc * part, part)]
        far[side].wait_recv()
        zout[side, :, side] = (
            own[:, side, pl.ds(zc * part, part)].astype(F32) + zin[0, :, side].astype(F32)
        ).astype(BF)
        c = cp(6 + side, zout.at[side], zin.at[1 + side], z_of[side])
        c.start()
        near.append(c)
    yield
    for c in near:
        c.wait_recv()
    for c in near:
        c.wait_send()
    v = own[:, :, pl.ds(me * part, part)].astype(F32)
    zout[0] = (v + zin[1].astype(F32) + zin[2].astype(F32)).astype(BF)
    yh = cp(8, zout.at[0], yhin, p.dev(dy=2))
    yh.start()
    yield
    yh.wait_recv()
    own[:, :, pl.ds(me * part, part)] = (zout[0].astype(F32) + yhin[...].astype(F32)).astype(BF)
    back = [cp(9 + side * 2 + h, chunk(h, me), chunk(h, me), z_of[side]) for side, h in ((0, 0), (1, 1), (0, 1), (1, 0))]
    for c in back:
        c.start()
    yield
    for side, zc in ((0, zl), (1, zr)):
        here = chunk(side, zc)
        cp(9 + side * 3, here, here, z_of[1 - side]).wait_recv()
        c = cp(13 + side, here, here, z_of[side])
        c.start()
        back.append(c)
    yield
    for side, zc in ((0, zl), (1, zr)):
        here = chunk(1 - side, zc)
        cp(9 + side * 2 + 1 - side, here, here, z_of[1 - side]).wait_recv()
    for h in (0, 1):
        here = chunk(h, zf)
        cp(13 + h, here, here, z_of[1 - h]).wait_recv()
    for c in back + along_y + [yh]:
        c.wait_send()
    done = []
    if kind == "col":
        spot = outs[0].at[p.c, first // rows]
        done.append(cp(15, own.at[1 - p.c], spot, p.sib()))
        done.append(pltpu.make_async_copy(own.at[p.c], spot, loc.at[0]))
    else:
        for i, width in enumerate(widths):
            take = min(cols, width)
            spot = outs[i].at[:, :, :, pl.ds(p.c * width + first, take)]
            piece = pl.ds(i * take, take)
            done.append(cp(15 + i, own.at[1 - p.c, :, :, :, piece], spot, p.sib()))
            done.append(pltpu.make_async_copy(own.at[p.c, :, :, :, piece], spot, loc.at[i]))
    for c in done:
        c.start()
    yield
    for c in done:
        c.wait()


def out_proj_kernel(
    lhs,
    rhs,
    x_own,
    keep,
    gains,
    wg,
    wu,
    wd,
    ffn_in_o,
    resid_o,
    stat_o,
    wgu_o,
    wd_o,
    stage_g,
    stage_u,
    stage_d,
    *scratch,
):
    p = Place()
    nx = len(X_SCRATCH)
    g = Gather(
        p,
        (4, 5, 6),
        (wg, wu, wd),
        (wgu_o, wgu_o, wd_o),
        (stage_g, stage_u, stage_d),
        scratch[nx:],
    )
    greet(Gather.peers(p) + [p.dev(dx=1), p.dev(dx=-1)])

    def finish(attn_out):
        stat_o[...] = jnp.full((8, 128), jnp.sum(keep[:, 0:1] * attn_out * attn_out), F32)
        resid = x_own[...].astype(F32) + attn_out
        resid_o[...] = resid
        return (resid * rms(resid) * full_row(gains, 1)).astype(BF)

    run(
        PROJ_ORDER,
        g=g.steps(),
        x=x_phase(p, (lhs,), rhs, False, scratch[:nx], ffn_in_o, True, finish),
    )


def out_proj_call(lhs, rhs, x_own, keep, gains, weights):
    return pl.pallas_call(
        out_proj_kernel,
        out_shape=(
            jax.ShapeDtypeStruct((4, 2, BLOCK, MODEL), BF),
            jax.ShapeDtypeStruct((BLOCK, MODEL), F32),
            jax.ShapeDtypeStruct((8, 128), F32),
            jax.ShapeDtypeStruct((256, 8, 2048), BF),
            jax.ShapeDtypeStruct((128, 8, 2048), BF),
        ),
        in_specs=[VM] * 5 + [ANY] * 3,
        out_specs=[VM] * 3 + [ANY] * 2,
        scratch_shapes=[
            pltpu.VMEM((64, 8, 1024), BF),
            pltpu.VMEM((64, 8, 1024), BF),
            pltpu.VMEM((128, 8, 512), BF),
        ]
        + X_SCRATCH
        + Gather.sems(3),
        compiler_params=params(3),
    )(lhs, rhs, x_own, keep, gains, *[tiles(w) for w in weights])


def ffn_kernel(a_ref, c_ref, wg, wu, wd, h_o, gg_o, gu_o, dd_o, dg_o, du_o, a_t):
    rows = FFN_ROWS

    @pl.when(pl.program_id(0) == 0)
    def _():
        def turn(i, carry):
            at = pl.ds(pl.multiple_of(i * 256, 256), 256)
            a_t[:, at] = a_ref[at, :].T
            return carry

        lax.fori_loop(0, 4, turn, 0)

    def step(i, carry):
        at = pl.ds(pl.multiple_of(i * rows, rows), rows)
        a = a_ref[at, :]
        gate = jnp.dot(a, wg[...], preferred_element_type=F32)
        up = jnp.dot(a, wu[...], preferred_element_type=F32)
        grad = lax.dot_general(
            c_ref[at, :], wd[...], (((1,), (1,)), ((), ())), preferred_element_type=F32
        )
        sig = 1.0 / (1.0 + jnp.exp(-gate))
        silu = gate * sig
        h_o[at, :] = (silu * up).astype(BF)
        gg_o[at, :] = (grad * up * sig * (1.0 + gate * (1.0 - sig))).astype(BF)
        gu_o[at, :] = (grad * silu).astype(BF)
        return carry

    lax.fori_loop(0, 1024 // rows, step, 0)
    h_t = h_o[...].T

    def down(n, carry):
        cols = pl.ds(pl.multiple_of(n * 256, 256), 256)
        dd_o[:, cols] = jnp.dot(h_t, c_ref[:, cols], preferred_element_type=F32).astype(BF)
        return carry

    lax.fori_loop(0, MODEL // 256, down, 0)

    def back(n, carry):
        at = pl.ds(pl.multiple_of(n * FFN_BACK, FFN_BACK), FFN_BACK)
        t = a_t[at, :]
        dg_o[at, :] = jnp.dot(t, gg_o[...], preferred_element_type=F32).astype(BF)
        du_o[at, :] = jnp.dot(t, gu_o[...], preferred_element_type=F32).astype(BF)
        return carry

    lax.fori_loop(0, MODEL // FFN_BACK, back, 0)


def ffn_call(ffn_in, cot, wgu, wd):
    tile = FFN_TILE
    n = 1024 // tile
    whole = pl.BlockSpec((1024, MODEL), lambda i: (0, 0), pipeline_mode=pl.Buffered(1))
    cols = pl.BlockSpec((1024, tile), lambda i: (0, i))
    tall = pl.BlockSpec((MODEL, tile), lambda i: (0, i))
    wide = pl.BlockSpec((tile, MODEL), lambda i: (i, 0))
    tokens = jax.ShapeDtypeStruct((1024, 1024), BF)
    grads = jax.ShapeDtypeStruct((MODEL, 1024), BF)
    return pl.pallas_call(
        ffn_kernel,
        grid=(n,),
        out_shape=(tokens, tokens, tokens, jax.ShapeDtypeStruct((1024, MODEL), BF), grads, grads),
        in_specs=[whole, whole, tall, pl.BlockSpec((MODEL, tile), lambda i: (0, i + n)), wide],
        out_specs=[cols, cols, cols, wide, tall, tall],
        scratch_shapes=[pltpu.VMEM((MODEL, 1024), BF)],
        compiler_params=params(),
    )(ffn_in, cot, wgu, wgu, wd)


def ffn_back_kernel(
    gate, up, rhs, resid_ref, cot_own, gains, dd, grad_o, resid_grad_o, gain_o, dd_o, *scratch
):
    p = Place()
    nx = len(X_SCRATCH)
    greet(unit_peers(p) + [p.dev(dx=1), p.dev(dx=-1)])

    def finish(g):
        resid = resid_ref[...]
        inv = rms(resid)
        normed = resid * inv
        gain_o[...] = jnp.broadcast_to(jnp.sum(g * normed, axis=0, keepdims=True), (8, MODEL))
        grad_resid = cot_own[...].astype(F32) + norm_back(g, normed, full_row(gains, 1), inv)
        resid_grad_o[...] = grad_resid
        return grad_resid.astype(BF)

    mid = nx + UNIT_SCRATCH
    run(
        FFN_ORDER,
        x=x_phase(p, (gate, up), rhs, True, scratch[:nx], grad_o, True, finish),
        a=unit(p, "down_a", dd, (dd_o,), scratch[nx:mid]),
        b=unit(p, "down_b", dd, (dd_o,), scratch[mid:]),
    )


def ffn_back_call(lhs, rhs, resid, cot_own, gains, dd):
    return pl.pallas_call(
        ffn_back_kernel,
        out_shape=(
            jax.ShapeDtypeStruct((4, 2, BLOCK, MODEL), BF),
            jax.ShapeDtypeStruct((BLOCK, MODEL), F32),
            jax.ShapeDtypeStruct((8, MODEL), F32),
            DOWN_OUT,
        ),
        in_specs=[VM] * 6 + [ANY],
        out_specs=[VM] * 3 + [ANY],
        scratch_shapes=X_SCRATCH + unit_scratch("down_a") + unit_scratch("down_b"),
        compiler_params=params(4),
    )(*lhs, rhs, resid, cot_own, gains, tiles(dd))


def attend_back_kernel(
    g_ref,
    qkv,
    info,
    pcol,
    lse,
    cos_ref,
    sin_ref,
    hidden,
    wd,
    resid,
    keep,
    dgate,
    out_o,
    final_o,
    stat_o,
    dgate_o,
    g_all,
    d_send,
    dk,
    dv,
    g_send,
    g_recv,
    a2a_send,
    a2a_recv,
    *scratch,
):
    p = Place()
    nx = len(X_SCRATCH)
    greet(context_peers(p) + x_peers(p) + [p.dev(dy=1), p.dev(dy=-1)])
    rows = 256

    def g_copy(j, q):
        other = p.c if q == 0 else 1 - p.c
        k = j * 2 + other
        slot = j * 2 + q
        return (
            k,
            remote(g_ref.at[slot], g_all.at[p.k], g_send.at[slot], g_recv.at[p.k], p.member(k)),
            pltpu.make_async_copy(g_ref.at[slot], g_all.at[p.k], g_send.at[slot]),
        )

    for j in range(4):
        for q in (0, 1):
            k, out, here = g_copy(j, q)

            @pl.when(k != p.k)
            def _():
                out.start()

            @pl.when(k == p.k)
            def _():
                here.start()

    def finish(ffn_out):
        final = resid[...] + ffn_out
        kp = keep[:, 0:1]
        stat_o[0] = jnp.full((8, 128), jnp.sum(kp * ffn_out * ffn_out), F32)
        stat_o[1] = jnp.full((8, 128), jnp.sum(kp * final * final), F32)
        return final.astype(BF)

    def main():
        dk[...] = jnp.zeros_like(dk)
        dv[...] = jnp.zeros_like(dv)
        yield
        for j in range(4):
            for q in (0, 1):
                k, out, here = g_copy(j, q)

                @pl.when(k != p.k)
                def _():
                    out.wait_send()

                @pl.when(k == p.k)
                def _():
                    here.wait()

        for i in range(8):

            @pl.when(i != p.k)
            def _():
                spot = g_all.at[i]
                remote(spot, spot, g_send.at[i], g_recv.at[i], p.member(i)).wait_recv()

        for qb in range(4):
            query_block(qb)
            yield
        lax.fori_loop(0, 8, give, 0)
        yield
        yield
        for i in range(8):
            out, here = sends(i)

            @pl.when(i != p.k)
            def _():
                out.wait_send()
                spot = out_o.at[i]
                remote(spot, spot, a2a_send.at[i], a2a_recv.at[i], p.member(i)).wait_recv()

            @pl.when(i == p.k)
            def _():
                here.wait()

    def sends(i):
        return (
            remote(d_send.at[i], out_o.at[p.k], a2a_send.at[i], a2a_recv.at[p.k], p.member(i)),
            pltpu.make_async_copy(d_send.at[i], out_o.at[p.k], a2a_send.at[i]),
        )

    scale = HEAD_DIM**-0.5

    def query_block(qb):
        at = pl.ds(qb * rows, rows)
        bias = bias_rows(qb, rows, info[0:1, :], info[1:2, :], pcol[at, 0:1])
        g2 = g_all[pl.ds(qb * 2, 2)].astype(F32).reshape(rows, 256).astype(BF)
        dqs = []
        for h in range(4):
            lanes = pl.ds(h * 64, 64)
            q = qkv[at, lanes]
            k = qkv[:, pl.ds(256 + h * 64, 64)]
            v = qkv[:, pl.ds(512 + h * 64, 64)]
            g = g2[:, h * 64 : (h + 1) * 64]
            sc = lax.dot_general(q, k, (((1,), (1,)), ((), ())), preferred_element_type=F32)
            prob = jnp.exp(sc * scale + bias - lse[at, h : h + 1])
            gp = lax.dot_general(g, v, (((1,), (1,)), ((), ())), preferred_element_type=F32)
            inner = jnp.sum(prob * gp, axis=1, keepdims=True)
            gs = (prob * (gp - inner)).astype(BF)
            dqs.append(jnp.dot(gs, k, preferred_element_type=F32))
            dk[:, lanes] += lax.dot_general(
                gs, q, (((0,), (0,)), ((), ())), preferred_element_type=F32
            )
            dv[:, lanes] += lax.dot_general(
                prob.astype(BF), g, (((0,), (0,)), ((), ())), preferred_element_type=F32
            )
        dq = jnp.concatenate(dqs, axis=1) * scale
        dq = dq * cos_ref[at, :] - swap_halves(dq) * sin_ref[at, :]
        dq = dq.reshape(32, 8, 256).astype(BF)
        d_send[qb * 2, :, :, 0:256] = dq[:16]
        d_send[qb * 2 + 1, :, :, 0:256] = dq[16:]

    def give(i, carry):
        at = pl.ds(pl.multiple_of(i * BLOCK, BLOCK), BLOCK)
        w = dk[at, :] * scale
        w = w * cos_ref[at, :] - swap_halves(w) * sin_ref[at, :]
        d_send[i, :, :, 256:512] = w.reshape(16, 8, 256).astype(BF)
        d_send[i, :, :, 512:768] = dv[at, :].reshape(16, 8, 256).astype(BF)
        out, here = sends(i)

        @pl.when(i != p.k)
        def _():
            out.start()

        @pl.when(i == p.k)
        def _():
            here.start()

        return carry

    mid = nx + UNIT_SCRATCH
    run(
        ATTEND_ORDER,
        m=main(),
        x=x_phase(p, (hidden,), wd, False, scratch[:nx], final_o, False, finish),
        a=unit(p, "gate_a", dgate, (dgate_o,), scratch[nx:mid]),
        b=unit(p, "gate_b", dgate, (dgate_o,), scratch[mid:]),
    )


def attend_back_call(g, qkv, info, pcol, lse, cos_full, sin_full, hidden, wd, resid, keep, dgate):
    return pl.pallas_call(
        attend_back_kernel,
        out_shape=(
            jax.ShapeDtypeStruct((8, 16, 8, 768), BF),
            jax.ShapeDtypeStruct((4, 1, BLOCK, MODEL), BF),
            jax.ShapeDtypeStruct((2, 8, 128), F32),
            FFN_OUT,
        ),
        in_specs=[VM] * 11 + [ANY],
        out_specs=[ANY, VM, VM, ANY],
        scratch_shapes=[
            pltpu.VMEM((8, 16, 8, 256), BF),
            pltpu.VMEM((8, 16, 8, 768), BF),
            pltpu.VMEM((1024, 256), F32),
            pltpu.VMEM((1024, 256), F32),
            DMA((8,)),
            DMA((8,)),
            DMA((8,)),
            DMA((8,)),
        ]
        + X_SCRATCH
        + unit_scratch("gate_a")
        + unit_scratch("gate_b"),
        compiler_params=params(5),
    )(
        tiles(g),
        qkv,
        info,
        pcol,
        lse,
        cos_full,
        sin_full,
        hidden,
        wd,
        resid,
        keep,
        tiles(dgate).reshape(4, 64, 8, 1024),
    )


LAST = ("up_a", "up_b", "out", "qkv")


def last_kernel(lhs, rhs, x_own, grad_resid, gains, extra, dup, do, dw, *refs):
    out_o, small_o, up_o, do_o = refs[:4]
    qkv_o = refs[4:7]
    at = 7
    nx = len(X_SCRATCH)
    xs = refs[at : at + nx]
    at += nx
    us = []
    for _ in LAST:
        us.append(refs[at : at + UNIT_SCRATCH])
        at += UNIT_SCRATCH
    core_in, ring_in, s_send, s_recv = refs[at:]
    p = Place()
    greet(unit_peers(p) + [p.dev(dx=1), p.dev(dx=-1), p.dev(dx=2), p.dev(dz=2)])

    def finish(g):
        v = x_own[...].astype(F32)
        inv = rms(v)
        normed = v * inv
        small_o[...] = extra[...]
        small_o[0:1, :] = jnp.sum(g * normed, axis=0, keepdims=True)
        grad_in = grad_resid[...] + norm_back(g, normed, full_row(gains, 0), inv)
        return grad_in.astype(BF)

    def small():
        core_in[p.c] = small_o[...]
        c = remote(core_in.at[p.c], core_in.at[p.c], s_send.at[0], s_recv.at[0], p.sib())
        c.start()
        yield
        here = core_in.at[1 - p.c]
        remote(here, here, s_send.at[0], s_recv.at[0], p.sib()).wait_recv()
        c.wait_send()
        total = core_in[0] + core_in[1]
        for axis, me, move in (
            (0, p.x, lambda d: p.dev(dx=d)),
            (1, p.y, lambda d: p.dev(dy=d)),
            (2, p.z, lambda d: p.dev(dz=d)),
        ):
            ring_in[axis, me] = total
            here = ring_in.at[axis, me]
            out = [
                remote(
                    here, here, s_send.at[axis * 3 + d], s_recv.at[axis * 3 + d], move(d)
                )
                for d in (1, 2, 3)
            ]
            for c in out:
                c.start()
            yield
            for d in (1, 2, 3):
                there = ring_in.at[axis, (me + 4 - d) % 4]
                remote(
                    there, there, s_send.at[axis * 3 + d], s_recv.at[axis * 3 + d], move(4 - d)
                ).wait_recv()
            for c in out:
                c.wait_send()
            total = (ring_in[axis, 0] + ring_in[axis, 1]) + (ring_in[axis, 2] + ring_in[axis, 3])
        small_o[...] = total

    run(
        LAST_ORDER,
        x=x_phase(p, (lhs,), rhs, True, xs, out_o, False, finish),
        a=unit(p, LAST[0], dup, (up_o,), us[0]),
        b=unit(p, LAST[1], dup, (up_o,), us[1]),
        c=unit(p, LAST[2], do, (do_o,), us[2]),
        d=unit(p, LAST[3], dw, qkv_o, us[3]),
        s=small(),
    )


def last_call(lhs, rhs, x_own, grad_resid, gains, extra, dup, do, dw):
    scratch = list(X_SCRATCH)
    for name in LAST:
        scratch += unit_scratch(name)
    outs = [FFN_OUT, OUT_OUT, QKV_OUT, QKV_OUT, QKV_OUT]
    return pl.pallas_call(
        last_kernel,
        out_shape=(
            jax.ShapeDtypeStruct((4, 1, BLOCK, MODEL), BF),
            jax.ShapeDtypeStruct((8, MODEL), F32),
            *outs,
        ),
        in_specs=[VM] * 6 + [ANY] * 3,
        out_specs=[VM] * 2 + [ANY] * len(outs),
        scratch_shapes=scratch
        + [
            pltpu.VMEM((2, 8, MODEL), F32),
            pltpu.VMEM((3, 4, 8, MODEL), F32),
            DMA((10,)),
            DMA((10,)),
        ],
        compiler_params=params(6),
    )(
        lhs,
        rhs,
        x_own,
        grad_resid,
        gains,
        extra,
        tiles(dup).reshape(4, 64, 8, 1024),
        tiles(do),
        tiles(dw).reshape(4, 64, 8, 768),
    )


def rope_tables(positions, head_size):
    half_dim = head_size // 2
    inv_freq = ROPE_BASE ** (-jnp.arange(half_dim, dtype=jnp.float32) * 2.0 / head_size)
    angles = positions.astype(jnp.float32)[:, None] * inv_freq[None, :]
    cosine, sine = jnp.cos(angles), jnp.sin(angles)
    return jnp.concatenate([cosine, cosine], axis=1), jnp.concatenate([-sine, sine], axis=1)


def piece_index(starts, piece_tags, positions):
    inside = (positions[None, :, None] >= starts[:, None, :]) & (
        positions[None, :, None] < starts[:, None, :] + PIECE
    )
    tagged = jnp.where(inside, piece_tags[:, None, :] + 1, 0)
    return jnp.sum(tagged, axis=2) - 1


def per_device(
    inputs,
    cotangent,
    q_weight,
    k_weight,
    v_weight,
    o_weight,
    gate_weight,
    up_weight,
    down_weight,
    attn_gain,
    ffn_gain,
    piece_starts,
    piece_ids,
    valid_mask,
):
    x_at = lax.axis_index("tensor")
    core = lax.axis_index("shard") % 2
    ctx = lax.axis_index("context")
    positions = jnp.arange(1024, dtype=jnp.int32)
    cos_t, sin_t = rope_tables(positions, HEAD_DIM)
    cos_full, sin_full = jnp.tile(cos_t, (1, 4)), jnp.tile(sin_t, (1, 4))
    cos_own = jnp.tile(lax.dynamic_slice_in_dim(cos_full, ctx * BLOCK, BLOCK, 0), (2, 1))
    sin_own = jnp.tile(lax.dynamic_slice_in_dim(sin_full, ctx * BLOCK, BLOCK, 0), (2, 1))
    meta = jnp.concatenate([piece_index(piece_starts, piece_ids, positions), valid_mask], axis=0)
    gains_own = jnp.concatenate(
        [
            attn_gain.astype(F32)[None],
            ffn_gain.astype(F32)[None],
            jnp.zeros((6, attn_gain.shape[0]), F32),
        ],
        axis=0,
    )
    wqkv, wo, gains, meta_all, cot_all, attn_in, qkv = start_call(
        inputs,
        cotangent,
        (q_weight, k_weight, v_weight, o_weight),
        gains_own,
        meta,
        cos_own,
        sin_own,
    )
    seq = lax.dynamic_slice(meta_all, (ctx % 2, 0, 0), (1, 8, 1024))[0]
    piece_row = lax.dynamic_slice_in_dim(seq, ctx // 2, 1, 0)
    valid_row = lax.dynamic_slice_in_dim(seq, 4 + ctx // 2, 1, 0)
    info = jnp.concatenate([piece_row, valid_row, jnp.zeros((6, 1024), jnp.int32)], axis=0)
    pcol = jnp.broadcast_to(piece_row.reshape(1024, 1), (1024, 128))
    wqkv, wo = rows_of(wqkv), rows_of(wo)
    cot_all = rows_of(cot_all)
    qkv = qkv.reshape(1024, 768)
    attended_seq, lse = attend_call(qkv, info, pcol)
    slots = attended_seq.reshape(4, 2, BLOCK, 256)
    attended = jnp.where(core == 0, slots, slots[:, ::-1])
    x_own = lax.dynamic_index_in_dim(inputs, x_at, 0, keepdims=False)
    cot_own = lax.dynamic_index_in_dim(cotangent, x_at, 0, keepdims=False)
    keep_own = lax.dynamic_slice(valid_mask, (x_at, ctx * BLOCK), (1, BLOCK)).astype(F32)
    keep = jnp.broadcast_to(keep_own.reshape(BLOCK, 1), (BLOCK, 128))
    attended = attended.reshape(4, 256, 256)
    ffn_in, resid, stat_attn, wgu, wd = out_proj_call(
        attended, wo, x_own, keep, gains, (gate_weight, up_weight, down_weight)
    )
    wgu, wd = rows_of(wgu), rows_of(wd)
    ffn_in = ffn_in.reshape(1024, MODEL)
    cot_rows = cot_all.reshape(1024, MODEL)
    hidden, grad_gate, grad_up, dd, dgate, dup = ffn_call(ffn_in, cot_rows, wgu, wd)

    def back(a, b):
        return jnp.einsum("nd,nf->df", a, b, preferred_element_type=F32).astype(BF)

    grad_attn, grad_resid, ffn_gain_part, sd = ffn_back_call(
        (grad_gate.reshape(4, 256, 1024), grad_up.reshape(4, 256, 1024)),
        wgu,
        resid,
        cot_own,
        gains,
        dd,
    )
    grad_attn = grad_attn.reshape(1024, MODEL)
    grad_att = jnp.einsum("nd,cd->nc", grad_attn, wo, preferred_element_type=F32).astype(BF)
    d_seq, output, stat_ffn, sgate = attend_back_call(
        grad_att.reshape(8, BLOCK, 256),
        qkv,
        info,
        pcol,
        lse,
        cos_full,
        sin_full,
        hidden.reshape(4, 256, 1024),
        wd,
        resid,
        keep,
        dgate,
    )
    slots = d_seq.reshape(4, 2, BLOCK, 768)
    dqkv = jnp.where(core == 0, slots, slots[:, ::-1]).reshape(4, 256, 768)
    do = back(attended.reshape(1024, 256), grad_attn)
    dw = back(attn_in.reshape(1024, MODEL), dqkv.reshape(1024, 768))
    stats = jnp.stack([jnp.sum(keep_own), stat_attn[0, 0], stat_ffn[0, 0, 0], stat_ffn[1, 0, 0]])
    extra = jnp.concatenate(
        [
            jnp.zeros((1, MODEL), F32),
            ffn_gain_part[0:1],
            jnp.pad(stats, (0, MODEL - 4))[None],
            jnp.zeros((5, MODEL), F32),
        ],
        axis=0,
    )
    input_grad, small, sup, so, sq, sk, sv = last_call(
        dqkv, wqkv, x_own, grad_resid, gains, extra, dup, do, dw
    )
    grads = [v.reshape(-1, v.shape[-1]).astype(F32) for v in (sq, sk, sv, so, sgate, sup, sd)]
    branch_rms = jnp.sqrt(small[2, 1:4] / (jnp.maximum(small[2, 0], 1.0) * MODEL))
    gain_start = (lax.axis_index("shard") * 4 + x_at) * BLOCK
    attn_gain_out = lax.dynamic_slice(small, (0, gain_start), (1, BLOCK))[0]
    ffn_gain_out = lax.dynamic_slice(small, (1, gain_start), (1, BLOCK))[0]
    return (
        output.reshape(4, BLOCK, MODEL),
        input_grad.reshape(4, BLOCK, MODEL),
        *grads,
        attn_gain_out,
        ffn_gain_out,
        branch_rms,
    )


def solution(mesh):
    return jax.shard_map(
        per_device,
        mesh=mesh,
        in_specs=(
            P("shard", "context", None),
            P("shard", "context", None),
            P("shard", "tensor"),
            P("shard", "tensor"),
            P("shard", "tensor"),
            P("tensor", "shard"),
            P("shard", "tensor"),
            P("shard", "tensor"),
            P("tensor", "shard"),
            P("shard"),
            P("shard"),
            P("shard", None),
            P("shard", None),
            P("shard", None),
        ),
        out_specs=(
            P("shard", "context", None),
            P("shard", "context", None),
            P("shard", "tensor"),
            P("shard", "tensor"),
            P("shard", "tensor"),
            P("tensor", "shard"),
            P("shard", "tensor"),
            P("shard", "tensor"),
            P("tensor", "shard"),
            P(("shard", "tensor")),
            P(("shard", "tensor")),
            P(),
        ),
        check_vma=False,
    )
```

```python
import functools

import jax
import jax.numpy as jnp
import numpy as np
from jax import lax
from jax.experimental import pallas as pl
from jax.experimental.pallas import tpu as pltpu
from jax.sharding import PartitionSpec as P

HEAD_DIM = 64
PIECE = 256
NORM_EPS = 1e-05
ROPE_BASE = 130000.0
MASK_FILL = -1e30
BF = jnp.bfloat16
F32 = jnp.float32
ANY = pl.BlockSpec(memory_space=pl.ANY)
VM = pl.BlockSpec(memory_space=pltpu.VMEM)
DMA = pltpu.SemaphoreType.DMA
PROJ_ORDER = "gxxxxxggxgxgxgxggx"
MID_ORDER = "amcmmammbacmcdbambmdcmbmdxacxxbdmxamdxbmdxcmmxcdbaxdbcaxmbammmxx"
ATTEND_ROWS = 256
LAST_ORDER = "bxaxdbxxbxabaxcdxbcdxacsbadsbxsaxdadccaabdcbscddscc"
FFN_TILE, FFN_ROWS, FFN_BACK = 256, 1024, 2048
VMEM_LIMIT = 60 * 1024 * 1024
MODEL = 2048
TILE = 256
BLOCK = 128
MESH_ID = pl.DeviceIdType.MESH


class Place:
    def __init__(self):
        self.s = lax.axis_index("shard")
        self.k = lax.axis_index("context")
        self.x = lax.axis_index("tensor")
        self.yl = self.s // 2
        self.c = self.s % 2
        self.y = (self.k // 4) * 2 + self.yl
        self.z = self.k % 4

    def dev(self, dx=0, dy=0, dz=0, core=None):
        x = (self.x + dx + 4) % 4
        y = (self.y + dy + 4) % 4
        z = (self.z + dz + 4) % 4
        c = self.c if core is None else core
        return {"shard": (y % 2) * 2 + c, "context": (y // 2) * 4 + z, "tensor": x}

    def member(self, k):
        return {"shard": self.s, "context": k, "tensor": self.x}

    def slot(self, k):
        return (k // 2) * 2 + (k % 2 + self.c) % 2

    def sib(self):
        return self.dev(core=1 - self.c)


def remote(src, dst, send_sem, recv_sem, device):
    return pltpu.make_async_remote_copy(
        src_ref=src,
        dst_ref=dst,
        send_sem=send_sem,
        recv_sem=recv_sem,
        device_id=device,
        device_id_type=MESH_ID,
    )


def greet(devices):
    barrier = pltpu.get_barrier_semaphore()
    for d in devices:
        pl.semaphore_signal(barrier, inc=1, device_id=d, device_id_type=MESH_ID)
    pl.semaphore_wait(barrier, len(devices))


def params(collective_id=None):
    if collective_id is None:
        return pltpu.CompilerParams(vmem_limit_bytes=VMEM_LIMIT)
    return pltpu.CompilerParams(
        vmem_limit_bytes=VMEM_LIMIT, collective_id=collective_id, has_side_effects=True
    )


def tiles(v):
    return v.reshape(*v.shape[:-2], v.shape[-2] // 8, 8, v.shape[-1])


def rows_of(v):
    return v.reshape(*v.shape[:-3], v.shape[-3] * 8, v.shape[-1])


def context_peers(p):
    return [p.member((p.k + d) % 8) for d in range(1, 8)]


def swap_halves(v):
    width = v.shape[1]
    lane = lax.broadcasted_iota(jnp.int32, v.shape, 1) % HEAD_DIM
    return jnp.where(
        lane < HEAD_DIM // 2,
        pltpu.roll(v, width - HEAD_DIM // 2, 1),
        pltpu.roll(v, HEAD_DIM // 2, 1),
    )


WEIGHTS = (
    (256, "row", 0),
    (256, "row", 256),
    (256, "row", 512),
    (256, "col", 0),
    (1024, "row", 0),
    (1024, "row", 1024),
    (1024, "col", 0),
)


class Gather:
    def __init__(self, p, ws, srcs, dsts, stages, sems):
        self.p, self.ws, self.srcs, self.dsts, self.stages = p, ws, srcs, dsts, stages
        self.y_send, self.y_recv, self.z_send, self.z_recv, self.s_send, self.s_recv, self.loc = sems
        self.qa = 2 * (p.z % 2)

    @staticmethod
    def sems(n):
        return [DMA((n, 2, 2))] * 4 + [DMA((n,))] * 3

    @staticmethod
    def peers(p):
        return (
            [p.sib()]
            + [p.dev(dy=dy, core=core) for dy in (-1, 1) for core in (0, 1)]
            + [p.dev(dz=1), p.dev(dz=-1)]
        )

    def src(self, i, half, quarter):
        size, kind, _ = WEIGHTS[self.ws[i]]
        if kind == "row":
            rows = pl.ds(0, 64) if quarter is None else pl.ds(quarter * 16, 16)
            return self.srcs[i].at[rows, :, pl.ds(half * size, size)]
        size = size // 8
        if quarter is None:
            return self.srcs[i].at[pl.ds(half * size, size)]
        return self.srcs[i].at[pl.ds(half * size + quarter * (size // 4), size // 4)]

    def dst(self, i, block, quarter):
        size, kind, off = WEIGHTS[self.ws[i]]
        if kind == "row":
            rows = (
                pl.ds(block * 64, 64)
                if quarter is None
                else pl.ds(block * 64 + quarter * 16, 16)
            )
            return self.dsts[i].at[rows, :, pl.ds(off, size)]
        size = size // 8
        cols = pl.ds(block * 512, 512)
        if quarter is None:
            return self.dsts[i].at[:, :, cols]
        return self.dsts[i].at[pl.ds(quarter * (size // 4), size // 4), :, cols]

    def y_copy(self, i, side, core):
        p = self.p
        quarter = self.qa + side
        return remote(
            self.src(i, core, quarter),
            self.dst(i, p.s, quarter),
            self.y_send.at[i, side, core],
            self.y_recv.at[i, side, p.c],
            p.dev(dy=-1 if side == 0 else 1, core=core),
        )

    def y_arrival(self, i, side, core):
        p = self.p
        here = self.dst(i, (1 - p.yl) * 2 + core, self.qa + side)
        return remote(
            here,
            here,
            self.y_send.at[i, side, core],
            self.y_recv.at[i, side, core],
            p.dev(dy=1 if side == 0 else -1, core=core),
        )

    def z_copy(self, i, side, core, arrival=False):
        p = self.p
        quarter = 2 - self.qa + side if arrival else self.qa + side
        here = self.dst(i, (1 - p.yl) * 2 + core, quarter)
        return remote(
            here,
            here,
            self.z_send.at[i, side, core],
            self.z_recv.at[i, side, core],
            p.dev(dz=1 if (side == 0) == arrival else -1),
        )

    def sib_copy(self, i, arrival=False):
        p = self.p
        there = self.dst(i, p.yl * 2 + 1 - p.c if arrival else p.s, None)
        return remote(
            there if arrival else self.src(i, 1 - p.c, None),
            there,
            self.s_send.at[i],
            self.s_recv.at[i],
            p.sib(),
        )

    def own_copy(self, i, step):
        stage = self.stages[i]
        here = self.dst(i, self.p.s, None)
        if step == 1:
            return pltpu.make_async_copy(stage, here, self.loc.at[i])
        return pltpu.make_async_copy(
            self.src(i, self.p.c, None), here if stage is None else stage, self.loc.at[i]
        )

    def start(self):
        for i in range(len(self.ws)):
            for core in (0, 1):
                for side in (0, 1):
                    self.y_copy(i, side, core).start()
        for i in range(len(self.ws)):
            self.sib_copy(i).start()
            self.own_copy(i, 0).start()

    def pass_on(self, i):
        for side in (0, 1):
            for core in (0, 1):
                self.y_arrival(i, side, core).wait_recv()
                self.z_copy(i, side, core).start()
        if self.stages[i] is not None:
            self.own_copy(i, 0).wait()
            self.own_copy(i, 1).start()

    def arrive(self, i):
        for side in (0, 1):
            for core in (0, 1):
                self.z_copy(i, side, core, True).wait_recv()
        self.sib_copy(i, True).wait_recv()
        self.own_copy(i, 0 if self.stages[i] is None else 1).wait()

    def sent(self, i):
        self.sib_copy(i).wait_send()
        for side in (0, 1):
            for core in (0, 1):
                self.y_copy(i, side, core).wait_send()
                self.z_copy(i, side, core).wait_send()

    def steps(self):
        self.start()
        yield
        for i in range(len(self.ws)):
            self.pass_on(i)
            yield
        for i in range(len(self.ws)):
            self.arrive(i)
            self.sent(i)
            yield


def run(order, **gens):
    alive = dict(gens)

    def step(name):
        if name in alive:
            try:
                next(alive[name])
            except StopIteration:
                del alive[name]

    for name in order:
        step(name)
    while alive:
        for name in list(alive):
            step(name)


def start_kernel(
    x_ref,
    cot_ref,
    wq,
    wk,
    wv,
    wo,
    gain_ref,
    meta_ref,
    rope_ref,
    wqkv_o,
    wo_o,
    gains_o,
    meta_o,
    cot_o,
    attn_in_t_o,
    qkv_o,
    attn_in,
    x_all,
    qkv_send,
    stage_o,
    stage_cot,
    loc,
    misc_send,
    misc_recv,
    gain_send,
    gain_recv,
    a2a_send,
    a2a_recv,
    *sems,
):
    p = Place()
    g = Gather(
        p,
        (0, 1, 2, 3),
        (wq, wk, wv, wo),
        (wqkv_o, wqkv_o, wqkv_o, wo_o),
        (None, None, None, stage_o),
        sems,
    )
    greet(
        [p.sib()]
        + [p.dev(dy=dy, core=core) for dy in (-1, 1) for core in (0, 1)]
        + context_peers(p)
    )
    gain_targets = [p.sib()] + [p.dev(dy=1, core=core) for core in (0, 1)]
    gain_copies = [
        remote(gain_ref, gains_o.at[p.s], gain_send.at[i], gain_recv.at[i if i == 0 else 1 + p.c], d)
        for i, d in enumerate(gain_targets)
    ]
    for c in gain_copies:
        c.start()
    x_own = pltpu.make_async_copy(x_ref, x_all.at[:, 0], loc.at[0])
    x_own.start()
    x_out = remote(x_ref, x_all.at[:, 1], misc_send.at[0], misc_recv.at[0], p.sib())
    x_out.start()
    g.start()
    gain_own = pltpu.make_async_copy(gain_ref, gains_o.at[p.s], loc.at[1])
    gain_own.start()
    meta_own = pltpu.make_async_copy(meta_ref, meta_o.at[p.c], loc.at[2])
    meta_own.start()
    meta_out = remote(meta_ref, meta_o.at[p.c], misc_send.at[1], misc_recv.at[1], p.sib())
    meta_out.start()
    cot_in = pltpu.make_async_copy(cot_ref, stage_cot, loc.at[3])
    cot_in.start()
    cot_own = pltpu.make_async_copy(stage_cot, cot_o.at[:, 0], loc.at[3])
    cot_out = remote(cot_ref, cot_o.at[:, 1], misc_send.at[2], misc_recv.at[2], p.sib())
    cot_out.start()

    gain_own.wait()
    for i in range(3):
        block = p.yl * 2 + 1 - p.c if i == 0 else (1 - p.yl) * 2 + (i - 1)
        here = gains_o.at[block]
        remote(here, here, gain_send.at[i], gain_recv.at[i], p.sib()).wait_recv()
    x_own.wait()
    x_out.wait_recv()
    gain = jnp.concatenate([gains_o[b, 0:1, :] for b in range(4)], axis=1)

    def norm_step(i, carry):
        v = x_all[i // 2, i % 2].astype(F32).reshape(BLOCK, MODEL)
        r = lax.rsqrt(jnp.mean(v * v, axis=1, keepdims=True) + NORM_EPS)
        v = (v * r * gain).astype(BF)
        attn_in[i // 2, pl.ds((i % 2) * BLOCK, BLOCK), :] = v
        attn_in_t_o[:, pl.ds(pl.multiple_of(i * BLOCK, BLOCK), BLOCK)] = v.T
        return carry

    lax.fori_loop(0, 8, norm_step, 0)
    for i in range(4):
        g.pass_on(i)
    cot_in.wait()
    cot_own.start()

    def send_block(j, q):
        other = p.c if q == 0 else 1 - p.c
        k = j * 2 + other
        slot = j * 2 + q
        return (
            k,
            remote(
                qkv_send.at[slot],
                qkv_o.at[p.k],
                a2a_send.at[slot],
                a2a_recv.at[p.k],
                p.member(k),
            ),
            pltpu.make_async_copy(qkv_send.at[slot], qkv_o.at[p.k], a2a_send.at[slot]),
        )

    for i in range(3):
        g.arrive(i)

    def wide(v):
        v = jnp.concatenate([v, v], axis=1)
        return jnp.concatenate([v, v], axis=0)

    def qkv_step(j, carry):
        a = attn_in[j]
        for part in range(3):
            cols = pl.ds(part * 256, 256)
            w = wqkv_o[:, :, cols].reshape(MODEL, 256)
            v = jnp.dot(a, w, preferred_element_type=F32)
            if part < 2:
                v = v * wide(rope_ref[0]) + swap_halves(v) * wide(rope_ref[1])
            v = v.reshape(32, 8, 256).astype(BF)
            qkv_send[j * 2, :, :, cols] = v[:16]
            qkv_send[j * 2 + 1, :, :, cols] = v[16:]
        for q in (0, 1):
            k, out, here = send_block(j, q)

            @pl.when(k != p.k)
            def _():
                out.start()

            @pl.when(k == p.k)
            def _():
                here.start()

        return carry

    lax.fori_loop(0, 4, qkv_step, 0)
    g.arrive(3)
    for i in range(4):
        g.sent(i)
    x_out.wait_send()
    meta_own.wait()
    meta_out.wait_send()
    here = meta_o.at[1 - p.c]
    remote(here, here, misc_send.at[1], misc_recv.at[1], p.sib()).wait_recv()
    cot_own.wait()
    cot_out.wait()
    for c in gain_copies:
        c.wait_send()
    for j in range(4):
        for q in (0, 1):
            k, out, here = send_block(j, q)

            @pl.when(k != p.k)
            def _():
                out.wait_send()

            @pl.when(k == p.k)
            def _():
                here.wait()

    for i in range(8):

        @pl.when(i != p.k)
        def _():
            here = qkv_o.at[i]
            remote(here, here, a2a_send.at[i], a2a_recv.at[i], p.member(i)).wait_recv()


def start_call(x, cot, weights, gains, meta, rope_own):
    shapes = (
        jax.ShapeDtypeStruct((256, 8, 768), BF),
        jax.ShapeDtypeStruct((32, 8, 2048), BF),
        jax.ShapeDtypeStruct((4, 8, 512), F32),
        jax.ShapeDtypeStruct((2, 8, 1024), jnp.int32),
        jax.ShapeDtypeStruct((4, 2, 16, 8, MODEL), BF),
        jax.ShapeDtypeStruct((MODEL, 1024), BF),
        jax.ShapeDtypeStruct((8, 16, 8, 768), BF),
    )
    return pl.pallas_call(
        start_kernel,
        out_shape=shapes,
        in_specs=[ANY] * 6 + [VM, ANY, VM],
        out_specs=[VM, ANY, VM, ANY, ANY, VM, ANY],
        scratch_shapes=[
            pltpu.VMEM((4, 256, MODEL), BF),
            pltpu.VMEM((4, 2, 16, 8, MODEL), BF),
            pltpu.VMEM((8, 16, 8, 768), BF),
            pltpu.VMEM((32, 8, 512), BF),
            pltpu.VMEM((4, 16, 8, MODEL), BF),
            DMA((4,)),
            DMA((3,)),
            DMA((3,)),
            DMA((3,)),
            DMA((3,)),
            DMA((8,)),
            DMA((8,)),
        ]
        + Gather.sems(4),
        compiler_params=params(1),
    )(tiles(x), tiles(cot), *[tiles(w) for w in weights], gains, meta, rope_own)


def bias_rows(qb, rows, prow, vrow, pcol):
    i = qb * rows + lax.broadcasted_iota(jnp.int32, (rows, 1024), 0)
    j = lax.broadcasted_iota(jnp.int32, (rows, 1024), 1)
    same = (pcol >= 0) & (pcol == prow)
    ok = ((j <= i) | same) & ((vrow > 0) | (i == j))
    return jnp.where(ok, 0.0, MASK_FILL)


def attend_kernel(
    qkv, info, pcol, out_o, lse_o, o_send, a2a_send, a2a_recv
):
    p = Place()
    greet(context_peers(p))
    mine = p.slot(p.k)
    rows = 256

    def sends(i):
        return (
            remote(o_send.at[i], out_o.at[mine], a2a_send.at[i], a2a_recv.at[p.k], p.member(i)),
            pltpu.make_async_copy(o_send.at[i], out_o.at[mine], a2a_send.at[i]),
        )

    def step(qb, carry):
        at = pl.ds(pl.multiple_of(qb * rows, rows), rows)
        bias = bias_rows(qb, rows, info[0:1, :], info[1:2, :], pcol[at, 0:1])
        lane = lax.broadcasted_iota(jnp.int32, (rows, 128), 1)
        totals = jnp.zeros((rows, 128), F32)
        outs = []
        for h in range(4):
            q = qkv[at, pl.ds(h * 64, 64)]
            k = qkv[:, pl.ds(256 + h * 64, 64)]
            v = qkv[:, pl.ds(512 + h * 64, 64)]
            sc = lax.dot_general(q, k, (((1,), (1,)), ((), ())), preferred_element_type=F32)
            sc = sc * (HEAD_DIM**-0.5) + bias
            top = jnp.max(sc, axis=1, keepdims=True)
            e = jnp.exp(sc - top)
            total = jnp.sum(e, axis=1, keepdims=True)
            prob = (e * (1.0 / total)).astype(BF)
            totals = jnp.where(lane == h, top + jnp.log(total), totals)
            outs.append(jnp.dot(prob, v, preferred_element_type=F32))
        lse_o[at, :] = totals
        o = jnp.concatenate(outs, axis=1).reshape(32, 8, 256).astype(BF)
        for half in (0, 1):
            i = qb * 2 + half
            o_send[i] = o[half * 16 : (half + 1) * 16]
            out, here = sends(i)

            @pl.when(i != p.k)
            def _():
                out.start()

            @pl.when(i == p.k)
            def _():
                here.start()

        return carry

    lax.fori_loop(0, 4, step, 0)
    for i in range(8):
        out, here = sends(i)

        @pl.when(i != p.k)
        def _():
            out.wait_send()
            spot = out_o.at[p.slot(i)]
            remote(spot, spot, a2a_send.at[i], a2a_recv.at[i], p.member(i)).wait_recv()

        @pl.when(i == p.k)
        def _():
            here.wait()


def attend_call(qkv, info, pcol):
    return pl.pallas_call(
        attend_kernel,
        out_shape=(
            jax.ShapeDtypeStruct((8, 16, 8, 256), BF),
            jax.ShapeDtypeStruct((1024, 128), F32),
        ),
        in_specs=[VM] * 3,
        out_specs=[ANY, VM],
        scratch_shapes=[pltpu.VMEM((8, 16, 8, 256), BF), DMA((8,)), DMA((8,))],
        compiler_params=params(2),
    )(qkv, info, pcol)


X_SCRATCH = [
    pltpu.VMEM((4, BLOCK, MODEL), F32),
    pltpu.VMEM((4, BLOCK, MODEL), BF),
    pltpu.VMEM((4, BLOCK, MODEL), BF),
    pltpu.VMEM((3, BLOCK, MODEL), BF),
    pltpu.VMEM((3, BLOCK, MODEL), BF),
    DMA((4,)),
    DMA((4,)),
    DMA((6,)),
    DMA((6,)),
    DMA((10,)),
    DMA((10,)),
]


def x_peers(p):
    return [p.sib(), p.dev(dx=1), p.dev(dx=-1)]


def multiplier(lhs, rhs, transposed):
    def multiply(n, j, first):
        cols = pl.ds(pl.multiple_of(first, TILE), TILE)
        if transposed:
            return lax.dot_general(
                lhs[j], rhs[cols, :], (((1,), (1,)), ((), ())), preferred_element_type=F32
            )
        return jnp.dot(lhs[j], rhs[:, cols], preferred_element_type=F32)

    return multiply


def x_phase(p, multiply, scratch, out, both, finish, prepare=None, arrived=None):
    acc, sib_out, sib_in, x_out, x_in, s_send, s_recv, x_send, x_recv, g_send, g_recv = scratch
    half = BLOCK // 2
    top, low = pl.ds(0, half), pl.ds(half, half)
    to_right, to_left = p.dev(dx=1), p.dev(dx=-1)

    def sib_copy(r):
        return remote(sib_out.at[r], sib_in.at[r], s_send.at[r], s_recv.at[r], p.sib())

    def product(r):
        j = (p.x + r) % 4
        n = (2, 1, 3, 0).index(r)
        if prepare is not None:
            prepare(n, j)

        def step(i, carry):
            cols = pl.ds(pl.multiple_of(i * TILE, TILE), TILE)
            v = multiply(n, j, i * TILE)
            acc[r, :, cols] = v[:BLOCK]
            sib_out[r, :, cols] = v[BLOCK:].astype(BF)
            return carry

        lax.fori_loop(0, MODEL // TILE, step, 0)
        sib_copy(r).start()

    def along(n, slot, rows, device):
        return remote(
            x_out.at[slot, rows], x_in.at[slot, rows], x_send.at[n], x_recv.at[n], device
        )

    far_right, far_left = along(0, 0, top, to_right), along(1, 0, low, to_left)
    right_low, right_top = along(2, 1, low, to_right), along(3, 1, top, to_right)
    left_top, left_low = along(4, 2, top, to_left), along(5, 2, low, to_left)
    product(2)
    yield
    product(1)
    sib_copy(2).wait_recv()
    x_out[0] = (acc[2] + sib_in[2].astype(F32)).astype(BF)
    far_right.start()
    far_left.start()
    yield
    product(3)
    sib_copy(1).wait_recv()
    x_out[1, half:] = (acc[1, half:] + sib_in[1, half:].astype(F32)).astype(BF)
    right_low.start()
    sib_copy(3).wait_recv()
    x_out[2, 0:half] = (acc[3, 0:half] + sib_in[3, 0:half].astype(F32)).astype(BF)
    left_top.start()
    yield
    product(0)
    yield
    far_right.wait_recv()
    x_out[1, 0:half] = (
        acc[1, 0:half] + sib_in[1, 0:half].astype(F32) + x_in[0, 0:half].astype(F32)
    ).astype(BF)
    right_top.start()
    far_left.wait_recv()
    x_out[2, half:] = (
        acc[3, half:] + sib_in[3, half:].astype(F32) + x_in[0, half:].astype(F32)
    ).astype(BF)
    left_low.start()
    yield
    sib_copy(0).wait_recv()
    acc[0] += sib_in[0].astype(F32)
    for c in (right_low, left_top, right_top, left_low):
        c.wait_recv()
    total = acc[0] + x_in[1].astype(F32) + x_in[2].astype(F32)
    for r in range(4):
        sib_copy(r).wait_send()
    for c in (far_right, far_left, right_low, right_top, left_top, left_low):
        c.wait_send()

    me, right, left, far = p.x, (p.x + 1) % 4, (p.x + 3) % 4, (p.x + 2) % 4
    out[me, 0] = finish(total)
    sent = []

    def copy(n, j, rows, d):
        src = out.at[j, 0, rows]
        return remote(src, src, g_send.at[n], g_recv.at[n], d)

    def go(c):
        c.start()
        sent.append(c)

    def to_sib(n, j):
        return remote(out.at[j, 0], out.at[j, 1], g_send.at[n], g_recv.at[n], p.sib())

    go(copy(0, me, top, to_right))
    go(copy(1, me, low, to_left))
    go(copy(2, me, low, to_right))
    go(copy(3, me, top, to_left))
    if both:
        go(to_sib(6, me))
    yield
    copy(0, left, top, to_left).wait_recv()
    go(copy(4, left, top, to_right))
    copy(1, right, low, to_right).wait_recv()
    go(copy(5, right, low, to_left))
    yield
    copy(2, left, low, to_left).wait_recv()
    copy(3, right, top, to_right).wait_recv()
    if both:
        go(to_sib(7, left))
        go(to_sib(8, right))
    yield
    copy(4, far, top, to_left).wait_recv()
    copy(5, far, low, to_right).wait_recv()
    if both:
        go(to_sib(9, far))
        yield
        for n, j in ((6, me), (7, left), (8, right), (9, far)):
            to_sib(n, j).wait_recv()
            if arrived is not None:
                arrived(j)
    for c in sent:
        c.wait_send()


def rms(v):
    return lax.rsqrt(jnp.mean(v * v, axis=1, keepdims=True) + NORM_EPS)


def full_row(gains, row):
    return jnp.concatenate([gains[b, row : row + 1, :] for b in range(4)], axis=1)


def norm_back(grad, normed, gain, inv):
    w = grad * gain
    return inv * (w - normed * jnp.mean(w * normed, axis=1, keepdims=True))


UNITS = {
    "down_a": (64, 512, "col", 0, ()),
    "down_b": (64, 512, "col", 64, ()),
    "gate_a": (64, 512, "row", 0, (1024,)),
    "gate_b": (64, 512, "row", 512, (1024,)),
    "up_a": (64, 512, "row", 0, (1024,)),
    "up_b": (64, 512, "row", 512, (1024,)),
    "out": (32, 512, "col", 0, ()),
    "qkv": (64, 768, "row", 0, (256, 256, 256)),
}
UNIT_SCRATCH = 8
DOWN_OUT = jax.ShapeDtypeStruct((2, 2, 2, 32, 8, 512), BF)
OUT_OUT = jax.ShapeDtypeStruct((2, 1, 2, 16, 8, 512), BF)
FFN_OUT = jax.ShapeDtypeStruct((2, 32, 8, 2048), BF)
QKV_OUT = jax.ShapeDtypeStruct((2, 32, 8, 512), BF)


def unit_scratch(name):
    r, c, _, _, _ = UNITS[name]
    return [
        pltpu.VMEM((2, 2, r // 2, 8, c), BF),
        pltpu.VMEM((2, 2, r // 2, 8, c), BF),
        pltpu.VMEM((2, 2, 2, r // 8, 8, c), BF),
        pltpu.VMEM((3, 2, 2, r // 8, 8, c), BF),
        pltpu.VMEM((2, 2, r // 8, 8, c), BF),
        DMA((4,)),
        DMA((18,)),
        DMA((18,)),
    ]


def unit_peers(p):
    return [p.sib(), p.dev(dy=1), p.dev(dy=-1), p.dev(dy=2), p.dev(dz=1), p.dev(dz=-1)]


def unit(p, name, src, outs, scratch):
    rows, cols, kind, first, widths = UNITS[name]
    own, yin, zout, zin, yhin, loc, send, recv = scratch
    part = rows // 8
    half = rows // 2
    z_of = {0: p.dev(dz=1), 1: p.dev(dz=-1)}
    me, zr, zl, zf = p.z, (p.z + 1) % 4, (p.z + 3) % 4, (p.z + 2) % 4

    def cp(n, src, dst, d):
        return remote(src, dst, send.at[n], recv.at[n], d)

    def fetch(yl, h, dst, make):
        if kind == "row":
            return [
                make(
                    h * 2,
                    src.at[pl.ds(yl * 2, 2), pl.ds(h * half, half), :, pl.ds(first, cols)],
                    dst.at[:, h],
                )
            ]
        return [
            make(
                h * 2 + core,
                src.at[pl.ds(first + h * half, half), :, pl.ds((yl * 2 + core) * cols, cols)],
                dst.at[core, h],
            )
            for core in (0, 1)
        ]

    along_y, local = [], []
    for h in (0, 1):
        d = p.dev(dy=1 if h == 0 else -1)
        along_y += fetch(1 - p.yl, h, yin, lambda n, a, b, d=d: cp(n, a, b, d))
        local += fetch(p.yl, h, own, lambda n, a, b: pltpu.make_async_copy(a, b, loc.at[n]))
    for c in along_y + local:
        c.start()
    yield
    for c in local:
        c.wait()
    for c in along_y:
        c.wait_recv()
    own[...] = (own[...].astype(F32) + yin[...].astype(F32)).astype(BF)

    def chunk(h, zc):
        return own.at[:, h, pl.ds(zc * part, part)]

    far = [cp(4 + h, chunk(h, zf), zin.at[0, :, h], z_of[h]) for h in (0, 1)]
    for c in far:
        c.start()
    yield
    for c in far:
        c.wait_send()
    near = []
    for side, zc in ((0, zr), (1, zl)):
        zout[side, :, 1 - side] = own[:, 1 - side, pl.ds(zc * part, part)]
        far[side].wait_recv()
        zout[side, :, side] = (
            own[:, side, pl.ds(zc * part, part)].astype(F32) + zin[0, :, side].astype(F32)
        ).astype(BF)
        c = cp(6 + side, zout.at[side], zin.at[1 + side], z_of[side])
        c.start()
        near.append(c)
    yield
    for c in near:
        c.wait_recv()
    for c in near:
        c.wait_send()
    v = own[:, :, pl.ds(me * part, part)].astype(F32)
    zout[0] = (v + zin[1].astype(F32) + zin[2].astype(F32)).astype(BF)
    yh = cp(8, zout.at[0], yhin, p.dev(dy=2))
    yh.start()
    yield
    yh.wait_recv()
    own[:, :, pl.ds(me * part, part)] = (zout[0].astype(F32) + yhin[...].astype(F32)).astype(BF)
    back = [cp(9 + side * 2 + h, chunk(h, me), chunk(h, me), z_of[side]) for side, h in ((0, 0), (1, 1), (0, 1), (1, 0))]
    for c in back:
        c.start()
    yield
    for side, zc in ((0, zl), (1, zr)):
        here = chunk(side, zc)
        cp(9 + side * 3, here, here, z_of[1 - side]).wait_recv()
        c = cp(13 + side, here, here, z_of[side])
        c.start()
        back.append(c)
    yield
    for side, zc in ((0, zl), (1, zr)):
        here = chunk(1 - side, zc)
        cp(9 + side * 2 + 1 - side, here, here, z_of[1 - side]).wait_recv()
    for h in (0, 1):
        here = chunk(h, zf)
        cp(13 + h, here, here, z_of[1 - h]).wait_recv()
    for c in back + along_y + [yh]:
        c.wait_send()
    done = []
    if kind == "col":
        spot = outs[0].at[p.c, first // rows]
        done.append(cp(15, own.at[1 - p.c], spot, p.sib()))
        done.append(pltpu.make_async_copy(own.at[p.c], spot, loc.at[0]))
    else:
        for i, width in enumerate(widths):
            take = min(cols, width)
            spot = outs[i].at[:, :, :, pl.ds(p.c * width + first, take)]
            piece = pl.ds(i * take, take)
            done.append(cp(15 + i, own.at[1 - p.c, :, :, :, piece], spot, p.sib()))
            done.append(pltpu.make_async_copy(own.at[p.c, :, :, :, piece], spot, loc.at[i]))
    for c in done:
        c.start()
    yield
    for c in done:
        c.wait()


def out_proj_kernel(
    lhs,
    rhs,
    x_own,
    keep,
    gains,
    wg,
    wu,
    wd,
    ffn_in_o,
    resid_o,
    stat_o,
    wgu_o,
    wd_o,
    stage_g,
    stage_u,
    stage_d,
    *scratch,
):
    p = Place()
    nx = len(X_SCRATCH)
    g = Gather(
        p,
        (4, 5, 6),
        (wg, wu, wd),
        (wgu_o, wgu_o, wd_o),
        (stage_g, stage_u, stage_d),
        scratch[nx:],
    )
    greet(Gather.peers(p) + [p.dev(dx=1), p.dev(dx=-1)])

    def finish(attn_out):
        stat_o[...] = jnp.full((8, 128), jnp.sum(keep[:, 0:1] * attn_out * attn_out), F32)
        resid = x_own[...].astype(F32) + attn_out
        resid_o[...] = resid
        return (resid * rms(resid) * full_row(gains, 1)).astype(BF)

    run(
        PROJ_ORDER,
        g=g.steps(),
        x=x_phase(p, multiplier(lhs, rhs, False), scratch[:nx], ffn_in_o, True, finish),
    )


def out_proj_call(lhs, rhs, x_own, keep, gains, weights):
    return pl.pallas_call(
        out_proj_kernel,
        out_shape=(
            jax.ShapeDtypeStruct((4, 2, BLOCK, MODEL), BF),
            jax.ShapeDtypeStruct((BLOCK, MODEL), F32),
            jax.ShapeDtypeStruct((8, 128), F32),
            jax.ShapeDtypeStruct((256, 8, 2048), BF),
            jax.ShapeDtypeStruct((128, 8, 2048), BF),
        ),
        in_specs=[VM] * 5 + [ANY] * 3,
        out_specs=[VM] * 3 + [ANY] * 2,
        scratch_shapes=[
            pltpu.VMEM((64, 8, 1024), BF),
            pltpu.VMEM((64, 8, 1024), BF),
            pltpu.VMEM((128, 8, 512), BF),
        ]
        + X_SCRATCH
        + Gather.sems(3),
        compiler_params=params(3),
    )(lhs, rhs, x_own, keep, gains, *[tiles(w) for w in weights])


def ffn_kernel(a_ref, c_ref, wg, wu, wd, h_o, gg_o, gu_o, dd_o, dg_o, du_o, a_t):
    rows = FFN_ROWS

    @pl.when(pl.program_id(0) == 0)
    def _():
        def turn(i, carry):
            at = pl.ds(pl.multiple_of(i * 256, 256), 256)
            a_t[:, at] = a_ref[at, :].T
            return carry

        lax.fori_loop(0, 4, turn, 0)

    def step(i, carry):
        at = pl.ds(pl.multiple_of(i * rows, rows), rows)
        a = a_ref[at, :]
        gate = jnp.dot(a, wg[...], preferred_element_type=F32)
        up = jnp.dot(a, wu[...], preferred_element_type=F32)
        grad = lax.dot_general(
            c_ref[at, :], wd[...], (((1,), (1,)), ((), ())), preferred_element_type=F32
        )
        sig = 1.0 / (1.0 + jnp.exp(-gate))
        silu = gate * sig
        h_o[at, :] = (silu * up).astype(BF)
        gg_o[at, :] = (grad * up * sig * (1.0 + gate * (1.0 - sig))).astype(BF)
        gu_o[at, :] = (grad * silu).astype(BF)
        return carry

    lax.fori_loop(0, 1024 // rows, step, 0)
    h_t = h_o[...].T

    def down(n, carry):
        cols = pl.ds(pl.multiple_of(n * 256, 256), 256)
        dd_o[:, cols] = jnp.dot(h_t, c_ref[:, cols], preferred_element_type=F32).astype(BF)
        return carry

    lax.fori_loop(0, MODEL // 256, down, 0)

    def back(n, carry):
        at = pl.ds(pl.multiple_of(n * FFN_BACK, FFN_BACK), FFN_BACK)
        t = a_t[at, :]
        dg_o[at, :] = jnp.dot(t, gg_o[...], preferred_element_type=F32).astype(BF)
        du_o[at, :] = jnp.dot(t, gu_o[...], preferred_element_type=F32).astype(BF)
        return carry

    lax.fori_loop(0, MODEL // FFN_BACK, back, 0)


def ffn_call(ffn_in, cot, wgu, wd):
    tile = FFN_TILE
    n = 1024 // tile
    whole = pl.BlockSpec((1024, MODEL), lambda i: (0, 0), pipeline_mode=pl.Buffered(1))
    cols = pl.BlockSpec((1024, tile), lambda i: (0, i))
    tall = pl.BlockSpec((MODEL, tile), lambda i: (0, i))
    wide = pl.BlockSpec((tile, MODEL), lambda i: (i, 0))
    tokens = jax.ShapeDtypeStruct((1024, 1024), BF)
    grads = jax.ShapeDtypeStruct((MODEL, 1024), BF)
    return pl.pallas_call(
        ffn_kernel,
        grid=(n,),
        out_shape=(tokens, tokens, tokens, jax.ShapeDtypeStruct((1024, MODEL), BF), grads, grads),
        in_specs=[whole, whole, tall, pl.BlockSpec((MODEL, tile), lambda i: (0, i + n)), wide],
        out_specs=[cols, cols, cols, wide, tall, tall],
        scratch_shapes=[pltpu.VMEM((MODEL, 1024), BF)],
        compiler_params=params(),
    )(ffn_in, cot, wgu, wgu, wd)


MID = ("down_a", "down_b", "gate_a", "gate_b")


def mid_kernel(*refs):
    gate, up, hidden, wgu, wd, dd, dgate = refs[:7]
    wo, resid_ref, cot_own, gains, keep, qkv, info, pcol, lse, rope = refs[7:17]
    grad_o, resid_grad_o, gain_o, final_o, stat_o, d_o, dd_o, dgate_o = refs[17:25]
    lhs, rhs, g_out, g_in, d_out, dk, dv = refs[25:32]
    loc, g_send, g_recv, a2a_send, a2a_recv = refs[32:37]
    at = 37
    nx = len(X_SCRATCH)
    xs = refs[at : at + nx]
    at += nx
    us = [refs[at + i * UNIT_SCRATCH : at + (i + 1) * UNIT_SCRATCH] for i in range(len(MID))]
    p = Place()
    greet(context_peers(p) + x_peers(p) + [p.dev(dy=1), p.dev(dy=-1)])
    rows = ATTEND_ROWS
    each = rows // 8
    scale = HEAD_DIM**-0.5
    mine = p.slot(p.k)

    def fetch(n, sources):
        j = (p.x + (2, 1, 3, 0)[n]) % 4
        return [
            pltpu.make_async_copy(v.at[j], lhs.at[n % 2, i], loc.at[(n % 2) * 2 + i])
            for i, v in enumerate(sources)
        ]

    def preparer(sources, right):
        def prepare(n, j):
            if n == 0:
                for c in fetch(0, sources):
                    c.start()
            if n < 3:
                for c in fetch(n + 1, sources):
                    c.start()
            if n == 0:
                right.wait()
            for c in fetch(n, sources):
                c.wait()

        return prepare

    def flat(v):
        return v.reshape(v.shape[0] * 8, v.shape[2])

    wgu_in = pltpu.make_async_copy(wgu, rhs, loc.at[4])
    wgu_in.start()
    wd_in = pltpu.make_async_copy(wd, rhs.at[pl.ds(0, 128)], loc.at[4])

    def multiply_back(n, j, first):
        v = 0.0
        for i in (0, 1):
            w = rhs[pl.ds(first // 8, TILE // 8), :, pl.ds(i * 1024, 1024)]
            v += lax.dot_general(
                flat(lhs[n % 2, i]), flat(w), (((1,), (1,)), ((), ())), preferred_element_type=F32
            )
        return v

    def multiply_out(n, j, first):
        w = rhs[pl.ds(0, 128), :, pl.ds(pl.multiple_of(first, TILE), TILE)]
        return jnp.dot(flat(lhs[n % 2, 0]), flat(w), preferred_element_type=F32)

    def finish_back(g):
        wd_in.start()
        resid = resid_ref[...]
        inv = rms(resid)
        normed = resid * inv
        gain_o[...] = jnp.broadcast_to(jnp.sum(g * normed, axis=0, keepdims=True), (8, MODEL))
        grad_resid = cot_own[...].astype(F32) + norm_back(g, normed, full_row(gains, 1), inv)
        resid_grad_o[...] = grad_resid
        return grad_resid.astype(BF)

    def finish_out(ffn_out):
        final = resid_ref[...] + ffn_out
        kp = keep[:, 0:1]
        stat_o[0] = jnp.full((8, 128), jnp.sum(kp * ffn_out * ffn_out), F32)
        stat_o[1] = jnp.full((8, 128), jnp.sum(kp * final * final), F32)
        return final.astype(BF)

    def g_copy(j, q):
        k = j * 2 + (p.c if q == 0 else 1 - p.c)
        slot = j * 2 + q
        return (
            k,
            remote(g_out.at[slot], g_in.at[p.k], g_send.at[slot], g_recv.at[p.k], p.member(k)),
            pltpu.make_async_copy(g_out.at[slot], g_in.at[p.k], g_send.at[slot]),
        )

    def arrived(j):
        v = lax.dot_general(
            grad_o[j].reshape(256, MODEL), wo[...], (((1,), (1,)), ((), ())), preferred_element_type=F32
        )
        v = v.reshape(32, 8, 256).astype(BF)
        for q in (0, 1):
            g_out[j * 2 + q] = v[q * 16 : (q + 1) * 16]
            k, out, here = g_copy(j, q)

            @pl.when(k != p.k)
            def _():
                out.start()

            @pl.when(k == p.k)
            def _():
                here.start()

    def sends(i):
        return (
            remote(d_out.at[i], d_o.at[mine], a2a_send.at[i], a2a_recv.at[p.k], p.member(i)),
            pltpu.make_async_copy(d_out.at[i], d_o.at[mine], a2a_send.at[i]),
        )

    def wide(v):
        return jnp.concatenate([v, v], axis=1)

    def query_block(qb):
        spot = pl.ds(qb * rows, rows)
        bias = bias_rows(qb, rows, info[0:1, :], info[1:2, :], pcol[spot, 0:1])
        blocks = pl.ds(qb * (rows // BLOCK), rows // BLOCK)
        g2 = g_in[blocks].astype(F32).reshape(rows, 256).astype(BF)
        dqs = []
        for h in range(4):
            lanes = pl.ds(h * 64, 64)
            q = qkv[spot, lanes]
            k = qkv[:, pl.ds(256 + h * 64, 64)]
            v = qkv[:, pl.ds(512 + h * 64, 64)]
            g = g2[:, h * 64 : (h + 1) * 64]
            sc = lax.dot_general(q, k, (((1,), (1,)), ((), ())), preferred_element_type=F32)
            prob = jnp.exp(sc * scale + bias - lse[spot, h : h + 1])
            gp = lax.dot_general(g, v, (((1,), (1,)), ((), ())), preferred_element_type=F32)
            inner = jnp.sum(prob * gp, axis=1, keepdims=True)
            gs = (prob * (gp - inner)).astype(BF)
            dqs.append(jnp.dot(gs, k, preferred_element_type=F32))
            dk[:, lanes] += lax.dot_general(
                gs, q, (((0,), (0,)), ((), ())), preferred_element_type=F32
            )
            dv[:, lanes] += lax.dot_general(
                prob.astype(BF), g, (((0,), (0,)), ((), ())), preferred_element_type=F32
            )
        dq = jnp.concatenate(dqs, axis=1) * scale
        dq = dq * wide(rope[0, spot]) - swap_halves(dq) * wide(rope[1, spot])
        dq = dq.reshape(each, 8, 256).astype(BF)
        for b in range(rows // BLOCK):
            d_out[qb * (rows // BLOCK) + b, :, :, 0:256] = dq[b * 16 : (b + 1) * 16]

    def give(i, carry):
        spot = pl.ds(pl.multiple_of(i * BLOCK, BLOCK), BLOCK)
        w = dk[spot, :] * scale
        w = w * wide(rope[0, spot]) - swap_halves(w) * wide(rope[1, spot])
        d_out[i, :, :, 256:512] = w.reshape(16, 8, 256).astype(BF)
        d_out[i, :, :, 512:768] = dv[spot, :].reshape(16, 8, 256).astype(BF)
        out, here = sends(i)

        @pl.when(i != p.k)
        def _():
            out.start()

        @pl.when(i == p.k)
        def _():
            here.start()

        return carry

    def main():
        yield from x_phase(
            p,
            multiply_back,
            xs,
            grad_o,
            True,
            finish_back,
            preparer((gate, up), wgu_in),
            arrived,
        )
        dk[...] = jnp.zeros_like(dk)
        dv[...] = jnp.zeros_like(dv)
        yield
        for j in range(4):
            for q in (0, 1):
                k, out, here = g_copy(j, q)

                @pl.when(k != p.k)
                def _():
                    out.wait_send()

                @pl.when(k == p.k)
                def _():
                    here.wait()

        for i in range(8):

            @pl.when(i != p.k)
            def _():
                spot = g_in.at[i]
                remote(spot, spot, g_send.at[i], g_recv.at[i], p.member(i)).wait_recv()

        for qb in range(1024 // rows):
            query_block(qb)
            yield
        lax.fori_loop(0, 8, give, 0)
        yield
        for i in range(8):
            out, here = sends(i)

            @pl.when(i != p.k)
            def _():
                out.wait_send()
                spot = d_o.at[p.slot(i)]
                remote(spot, spot, a2a_send.at[i], a2a_recv.at[i], p.member(i)).wait_recv()

            @pl.when(i == p.k)
            def _():
                here.wait()

    x = x_phase(
        p, multiply_out, xs, final_o, False, finish_out, preparer((hidden,), wd_in)
    )
    a, b, c, d = [
        unit(p, name, src, (o,), scr)
        for name, src, o, scr in zip(MID, (dd, dd, dgate, dgate), (dd_o, dd_o, dgate_o, dgate_o), us)
    ]
    run(MID_ORDER, m=main(), x=x, a=a, b=b, c=c, d=d)


def mid_call(gate, up, hidden, wgu, wd, dd, dgate, wo, *rest):
    scratch = list(X_SCRATCH)
    for name in MID:
        scratch += unit_scratch(name)
    blocks = [tiles(v.reshape(4, 256, 1024)) for v in (gate, up, hidden)]
    return pl.pallas_call(
        mid_kernel,
        out_shape=(
            jax.ShapeDtypeStruct((4, 2, BLOCK, MODEL), BF),
            jax.ShapeDtypeStruct((BLOCK, MODEL), F32),
            jax.ShapeDtypeStruct((8, MODEL), F32),
            jax.ShapeDtypeStruct((4, 1, BLOCK, MODEL), BF),
            jax.ShapeDtypeStruct((2, 8, 128), F32),
            jax.ShapeDtypeStruct((8, 16, 8, 768), BF),
            DOWN_OUT,
            FFN_OUT,
        ),
        in_specs=[ANY] * 7 + [VM] * 10,
        out_specs=[VM] * 5 + [ANY] * 3,
        scratch_shapes=[
            pltpu.VMEM((2, 2, 32, 8, 1024), BF),
            pltpu.VMEM((256, 8, 2048), BF),
            pltpu.VMEM((8, 16, 8, 256), BF),
            pltpu.VMEM((8, 16, 8, 256), BF),
            pltpu.VMEM((8, 16, 8, 768), BF),
            pltpu.VMEM((1024, 256), F32),
            pltpu.VMEM((1024, 256), F32),
            DMA((5,)),
            DMA((8,)),
            DMA((8,)),
            DMA((8,)),
            DMA((8,)),
        ]
        + scratch,
        compiler_params=params(5),
    )(*blocks, wgu, wd, tiles(dd), tiles(dgate).reshape(4, 64, 8, 1024), wo, *rest)


LAST = ("up_a", "up_b", "out", "qkv")


def last_kernel(
    lhs,
    rhs,
    x_own,
    grad_resid,
    gains,
    ffn_gain,
    stat_attn,
    stat_ffn,
    keep,
    attn_in_t,
    attended,
    grad_attn,
    dup,
    *refs,
):
    out_o, small_o, up_o, do_o = refs[:4]
    qkv_o = refs[4:7]
    at = 7
    nx = len(X_SCRATCH)
    xs = refs[at : at + nx]
    at += nx
    us = []
    for _ in LAST:
        us.append(refs[at : at + UNIT_SCRATCH])
        at += UNIT_SCRATCH
    core_in, ring_in, s_send, s_recv, do, dw = refs[at:]
    p = Place()
    greet(unit_peers(p) + [p.dev(dx=1), p.dev(dx=-1), p.dev(dx=2), p.dev(dz=2)])

    def finish(g):
        v = x_own[...].astype(F32)
        inv = rms(v)
        normed = v * inv
        few = slice(0, 128)
        small_o[...] = jnp.zeros_like(small_o)
        small_o[0:1, :] = jnp.sum(g * normed, axis=0, keepdims=True)
        small_o[1:2, :] = ffn_gain[0:1, :]
        small_o[2:3, few] = jnp.sum(keep[...], axis=0, keepdims=True)
        small_o[3:4, few] = stat_attn[0:1, :]
        small_o[4:5, few] = stat_ffn[0, 0:1, :]
        small_o[5:6, few] = stat_ffn[1, 0:1, :]
        grad_in = grad_resid[...] + norm_back(g, normed, full_row(gains, 0), inv)
        return grad_in.astype(BF)

    def small():
        core_in[p.c] = small_o[...]
        c = remote(core_in.at[p.c], core_in.at[p.c], s_send.at[0], s_recv.at[0], p.sib())
        c.start()
        yield
        here = core_in.at[1 - p.c]
        remote(here, here, s_send.at[0], s_recv.at[0], p.sib()).wait_recv()
        c.wait_send()
        total = core_in[0] + core_in[1]
        for axis, me, move in (
            (0, p.x, lambda d: p.dev(dx=d)),
            (1, p.y, lambda d: p.dev(dy=d)),
            (2, p.z, lambda d: p.dev(dz=d)),
        ):
            ring_in[axis, me] = total
            here = ring_in.at[axis, me]
            out = [
                remote(
                    here, here, s_send.at[axis * 3 + d], s_recv.at[axis * 3 + d], move(d)
                )
                for d in (1, 2, 3)
            ]
            for c in out:
                c.start()
            yield
            for d in (1, 2, 3):
                there = ring_in.at[axis, (me + 4 - d) % 4]
                remote(
                    there, there, s_send.at[axis * 3 + d], s_recv.at[axis * 3 + d], move(4 - d)
                ).wait_recv()
            for c in out:
                c.wait_send()
            total = (ring_in[axis, 0] + ring_in[axis, 1]) + (ring_in[axis, 2] + ring_in[axis, 3])
        small_o[...] = total

    def out_unit():
        left = attended[...].reshape(1024, 256).T

        def step(n, carry):
            cols = pl.ds(pl.multiple_of(n * 512, 512), 512)
            v = jnp.dot(left, grad_attn[:, cols], preferred_element_type=F32)
            do[:, :, cols] = v.reshape(32, 8, 512).astype(BF)
            return carry

        lax.fori_loop(0, 4, step, 0)
        yield from unit(p, LAST[2], do, (do_o,), us[2])

    def qkv_unit():
        def step(n, carry):
            v = jnp.dot(
                attn_in_t[pl.ds(pl.multiple_of(n * 512, 512), 512), :],
                lhs[...].reshape(1024, 768),
                preferred_element_type=F32,
            )
            dw[n] = v.reshape(64, 8, 768).astype(BF)
            return carry

        lax.fori_loop(0, 4, step, 0)
        yield from unit(p, LAST[3], dw, qkv_o, us[3])

    run(
        LAST_ORDER,
        x=x_phase(p, multiplier(lhs, rhs, True), xs, out_o, False, finish),
        a=unit(p, LAST[0], dup, (up_o,), us[0]),
        b=unit(p, LAST[1], dup, (up_o,), us[1]),
        c=out_unit(),
        d=qkv_unit(),
        s=small(),
    )


def last_call(lhs, rhs, x_own, grad_resid, gains, small_parts, attn_in_t, attended, grad_attn, dup):
    scratch = list(X_SCRATCH)
    for name in LAST:
        scratch += unit_scratch(name)
    outs = [FFN_OUT, OUT_OUT, QKV_OUT, QKV_OUT, QKV_OUT]
    return pl.pallas_call(
        last_kernel,
        out_shape=(
            jax.ShapeDtypeStruct((4, 1, BLOCK, MODEL), BF),
            jax.ShapeDtypeStruct((8, MODEL), F32),
            *outs,
        ),
        in_specs=[VM] * 12 + [ANY],
        out_specs=[VM] * 2 + [ANY] * len(outs),
        scratch_shapes=scratch
        + [
            pltpu.VMEM((2, 8, MODEL), F32),
            pltpu.VMEM((3, 4, 8, MODEL), F32),
            DMA((10,)),
            DMA((10,)),
            pltpu.VMEM((32, 8, MODEL), BF),
            pltpu.VMEM((4, 64, 8, 768), BF),
        ],
        compiler_params=params(6),
    )(
        lhs,
        rhs,
        x_own,
        grad_resid,
        gains,
        *small_parts,
        attn_in_t,
        attended,
        grad_attn,
        tiles(dup).reshape(4, 64, 8, 1024),
    )


def rope_table():
    half_dim = HEAD_DIM // 2
    inv_freq = ROPE_BASE ** (-np.arange(half_dim) * 2.0 / HEAD_DIM)
    angles = np.arange(1024)[:, None] * inv_freq[None, :]
    cosine, sine = np.cos(angles), np.sin(angles)
    cosine = np.concatenate([cosine, cosine], axis=1)
    sine = np.concatenate([-sine, sine], axis=1)
    return np.stack([np.tile(cosine, (1, 2)), np.tile(sine, (1, 2))]).astype(np.float32)


def piece_index(starts, piece_tags, positions):
    inside = (positions[None, :, None] >= starts[:, None, :]) & (
        positions[None, :, None] < starts[:, None, :] + PIECE
    )
    tagged = jnp.where(inside, piece_tags[:, None, :] + 1, 0)
    return jnp.sum(tagged, axis=2) - 1


def per_device(
    inputs,
    cotangent,
    q_weight,
    k_weight,
    v_weight,
    o_weight,
    gate_weight,
    up_weight,
    down_weight,
    attn_gain,
    ffn_gain,
    piece_starts,
    piece_ids,
    valid_mask,
):
    x_at = lax.axis_index("tensor")
    ctx = lax.axis_index("context")
    positions = jnp.arange(1024, dtype=jnp.int32)
    rope = jnp.asarray(rope_table())
    rope_own = lax.dynamic_slice_in_dim(rope, ctx * BLOCK, BLOCK, 1)
    meta = jnp.concatenate([piece_index(piece_starts, piece_ids, positions), valid_mask], axis=0)
    gains_own = jnp.concatenate(
        [
            attn_gain.astype(F32)[None],
            ffn_gain.astype(F32)[None],
            jnp.zeros((6, attn_gain.shape[0]), F32),
        ],
        axis=0,
    )
    wqkv, wo, gains, meta_all, cot_all, attn_in_t, qkv = start_call(
        inputs,
        cotangent,
        (q_weight, k_weight, v_weight, o_weight),
        gains_own,
        meta,
        rope_own,
    )
    seq = lax.dynamic_slice(meta_all, (ctx % 2, 0, 0), (1, 8, 1024))[0]
    piece_row = lax.dynamic_slice_in_dim(seq, ctx // 2, 1, 0)
    valid_row = lax.dynamic_slice_in_dim(seq, 4 + ctx // 2, 1, 0)
    info = jnp.concatenate([piece_row, valid_row, jnp.zeros((6, 1024), jnp.int32)], axis=0)
    pcol = jnp.broadcast_to(piece_row.reshape(1024, 1), (1024, 128))
    wqkv, wo = rows_of(wqkv), rows_of(wo)
    cot_all = rows_of(cot_all)
    qkv = qkv.reshape(1024, 768)
    attended, lse = attend_call(qkv, info, pcol)
    x_own = lax.dynamic_index_in_dim(inputs, x_at, 0, keepdims=False)
    cot_own = lax.dynamic_index_in_dim(cotangent, x_at, 0, keepdims=False)
    keep_own = lax.dynamic_slice(valid_mask, (x_at, ctx * BLOCK), (1, BLOCK)).astype(F32)
    keep = jnp.broadcast_to(keep_own.reshape(BLOCK, 1), (BLOCK, 128))
    attended = attended.reshape(4, 256, 256)
    ffn_in, resid, stat_attn, wgu, wd = out_proj_call(
        attended, wo, x_own, keep, gains, (gate_weight, up_weight, down_weight)
    )
    ffn_in = ffn_in.reshape(1024, MODEL)
    cot_rows = cot_all.reshape(1024, MODEL)
    hidden, grad_gate, grad_up, dd, dgate, dup = ffn_call(
        ffn_in, cot_rows, rows_of(wgu), rows_of(wd)
    )

    grad_attn, grad_resid, ffn_gain_part, output, stat_ffn, d_seq, sd, sgate = mid_call(
        grad_gate,
        grad_up,
        hidden,
        wgu,
        wd,
        dd,
        dgate,
        wo,
        resid,
        cot_own,
        gains,
        keep,
        qkv,
        info,
        pcol,
        lse,
        rope,
    )
    dqkv = d_seq.reshape(4, 256, 768)
    input_grad, small, sup, so, sq, sk, sv = last_call(
        dqkv,
        wqkv,
        x_own,
        grad_resid,
        gains,
        (ffn_gain_part, stat_attn, stat_ffn, keep),
        attn_in_t,
        attended,
        grad_attn.reshape(1024, MODEL),
        dup,
    )
    grads = [v.reshape(-1, v.shape[-1]).astype(F32) for v in (sq, sk, sv, so, sgate, sup, sd)]
    branch_rms = jnp.sqrt(small[3:6, 0] / (jnp.maximum(small[2, 0], 1.0) * MODEL))
    gain_start = (lax.axis_index("shard") * 4 + x_at) * BLOCK
    attn_gain_out = lax.dynamic_slice(small, (0, gain_start), (1, BLOCK))[0]
    ffn_gain_out = lax.dynamic_slice(small, (1, gain_start), (1, BLOCK))[0]
    return (
        output.reshape(4, BLOCK, MODEL),
        input_grad.reshape(4, BLOCK, MODEL),
        *grads,
        attn_gain_out,
        ffn_gain_out,
        branch_rms,
    )


def solution(mesh):
    return jax.shard_map(
        per_device,
        mesh=mesh,
        in_specs=(
            P("shard", "context", None),
            P("shard", "context", None),
            P("shard", "tensor"),
            P("shard", "tensor"),
            P("shard", "tensor"),
            P("tensor", "shard"),
            P("shard", "tensor"),
            P("shard", "tensor"),
            P("tensor", "shard"),
            P("shard"),
            P("shard"),
            P("shard", None),
            P("shard", None),
            P("shard", None),
        ),
        out_specs=(
            P("shard", "context", None),
            P("shard", "context", None),
            P("shard", "tensor"),
            P("shard", "tensor"),
            P("shard", "tensor"),
            P("tensor", "shard"),
            P("shard", "tensor"),
            P("shard", "tensor"),
            P("tensor", "shard"),
            P(("shard", "tensor")),
            P(("shard", "tensor")),
            P(),
        ),
        check_vma=False,
    )
```

```python
import functools

import jax
import jax.numpy as jnp
import numpy as np
from jax import lax
from jax.experimental import pallas as pl
from jax.experimental.pallas import tpu as pltpu
from jax.sharding import PartitionSpec as P

HEAD_DIM = 64
PIECE = 256
NORM_EPS = 1e-05
ROPE_BASE = 130000.0
MASK_FILL = -1e30
BF = jnp.bfloat16
F32 = jnp.float32
ANY = pl.BlockSpec(memory_space=pl.ANY)
VM = pl.BlockSpec(memory_space=pltpu.VMEM)
DMA = pltpu.SemaphoreType.DMA
PROJ_ORDER = "gxxxxxggxgxgxgxggx"
MID_ORDER = (
    "amemmcbmmaemadcemmbacmebmxcxdbaxdmeaxxdcmbe"
    "mcxdbmdmxcabdxecxabdmexdxmbcamme"
)
ATTEND_ROWS = 256
LAST_ORDER = "bxdxxbxcbdxbdcbxdbcdscbsbxcxdscbsxdcsxdccd"
FFN_TILE, FFN_ROWS, FFN_BACK = 512, 1024, 2048
VMEM_LIMIT = 60 * 1024 * 1024
MODEL = 2048
TILE = 256
BLOCK = 128
MESH_ID = pl.DeviceIdType.MESH


class Place:
    def __init__(self):
        self.s = lax.axis_index("shard")
        self.k = lax.axis_index("context")
        self.x = lax.axis_index("tensor")
        self.yl = self.s // 2
        self.c = self.s % 2
        self.y = (self.k // 4) * 2 + self.yl
        self.z = self.k % 4

    def dev(self, dx=0, dy=0, dz=0, core=None):
        x = (self.x + dx + 4) % 4
        y = (self.y + dy + 4) % 4
        z = (self.z + dz + 4) % 4
        c = self.c if core is None else core
        return {"shard": (y % 2) * 2 + c, "context": (y // 2) * 4 + z, "tensor": x}

    def member(self, k):
        return {"shard": self.s, "context": k, "tensor": self.x}

    def slot(self, k):
        return (k // 2) * 2 + (k % 2 + self.c) % 2

    def sib(self):
        return self.dev(core=1 - self.c)


def remote(src, dst, send_sem, recv_sem, device):
    return pltpu.make_async_remote_copy(
        src_ref=src,
        dst_ref=dst,
        send_sem=send_sem,
        recv_sem=recv_sem,
        device_id=device,
        device_id_type=MESH_ID,
    )


def greet(devices):
    barrier = pltpu.get_barrier_semaphore()
    for d in devices:
        pl.semaphore_signal(barrier, inc=1, device_id=d, device_id_type=MESH_ID)
    pl.semaphore_wait(barrier, len(devices))


def params(collective_id=None):
    if collective_id is None:
        return pltpu.CompilerParams(vmem_limit_bytes=VMEM_LIMIT)
    return pltpu.CompilerParams(
        vmem_limit_bytes=VMEM_LIMIT, collective_id=collective_id, has_side_effects=True
    )


def tiles(v):
    return v.reshape(*v.shape[:-2], v.shape[-2] // 8, 8, v.shape[-1])


def rows_of(v):
    return v.reshape(*v.shape[:-3], v.shape[-3] * 8, v.shape[-1])


def context_peers(p):
    return [p.member((p.k + d) % 8) for d in range(1, 8)]


def swap_halves(v):
    width = v.shape[1]
    lane = lax.broadcasted_iota(jnp.int32, v.shape, 1) % HEAD_DIM
    return jnp.where(
        lane < HEAD_DIM // 2,
        pltpu.roll(v, width - HEAD_DIM // 2, 1),
        pltpu.roll(v, HEAD_DIM // 2, 1),
    )


WEIGHTS = (
    (256, "row", 0),
    (256, "row", 256),
    (256, "row", 512),
    (256, "col", 0),
    (1024, "row", 0),
    (1024, "row", 1024),
    (1024, "col", 0),
)


OWN_ROWS = [pltpu.VMEM((16, 8, MODEL), BF), DMA((1,))]


def own_rows(p, ref, scratch):
    rows, sem = scratch
    copy = pltpu.make_async_copy(ref.at[p.x], rows, sem.at[0])
    copy.start()

    def read():
        copy.wait()
        return rows[...].astype(F32).reshape(BLOCK, MODEL)

    return read


class Gather:
    def __init__(self, p, ws, srcs, dsts, stages, sems):
        self.p, self.ws, self.srcs, self.dsts, self.stages = p, ws, srcs, dsts, stages
        self.y_send, self.y_recv, self.z_send, self.z_recv, self.s_send, self.s_recv, self.loc = sems
        self.qa = 2 * (p.z % 2)

    @staticmethod
    def sems(n):
        return [DMA((n, 2, 2))] * 4 + [DMA((n,))] * 3

    @staticmethod
    def peers(p):
        return (
            [p.sib()]
            + [p.dev(dy=dy, core=core) for dy in (-1, 1) for core in (0, 1)]
            + [p.dev(dz=1), p.dev(dz=-1)]
        )

    def src(self, i, half, quarter):
        size, kind, _ = WEIGHTS[self.ws[i]]
        if kind == "row":
            rows = pl.ds(0, 64) if quarter is None else pl.ds(quarter * 16, 16)
            return self.srcs[i].at[rows, :, pl.ds(half * size, size)]
        size = size // 8
        if quarter is None:
            return self.srcs[i].at[pl.ds(half * size, size)]
        return self.srcs[i].at[pl.ds(half * size + quarter * (size // 4), size // 4)]

    def dst(self, i, block, quarter):
        size, kind, off = WEIGHTS[self.ws[i]]
        if kind == "row":
            rows = (
                pl.ds(block * 64, 64)
                if quarter is None
                else pl.ds(block * 64 + quarter * 16, 16)
            )
            return self.dsts[i].at[rows, :, pl.ds(off, size)]
        size = size // 8
        cols = pl.ds(block * 512, 512)
        if quarter is None:
            return self.dsts[i].at[:, :, cols]
        return self.dsts[i].at[pl.ds(quarter * (size // 4), size // 4), :, cols]

    def y_copy(self, i, side, core):
        p = self.p
        quarter = self.qa + side
        return remote(
            self.src(i, core, quarter),
            self.dst(i, p.s, quarter),
            self.y_send.at[i, side, core],
            self.y_recv.at[i, side, p.c],
            p.dev(dy=-1 if side == 0 else 1, core=core),
        )

    def y_arrival(self, i, side, core):
        p = self.p
        here = self.dst(i, (1 - p.yl) * 2 + core, self.qa + side)
        return remote(
            here,
            here,
            self.y_send.at[i, side, core],
            self.y_recv.at[i, side, core],
            p.dev(dy=1 if side == 0 else -1, core=core),
        )

    def z_copy(self, i, side, core, arrival=False):
        p = self.p
        quarter = 2 - self.qa + side if arrival else self.qa + side
        here = self.dst(i, (1 - p.yl) * 2 + core, quarter)
        return remote(
            here,
            here,
            self.z_send.at[i, side, core],
            self.z_recv.at[i, side, core],
            p.dev(dz=1 if (side == 0) == arrival else -1),
        )

    def sib_copy(self, i, arrival=False):
        p = self.p
        there = self.dst(i, p.yl * 2 + 1 - p.c if arrival else p.s, None)
        return remote(
            there if arrival else self.src(i, 1 - p.c, None),
            there,
            self.s_send.at[i],
            self.s_recv.at[i],
            p.sib(),
        )

    def own_copy(self, i, step):
        stage = self.stages[i]
        here = self.dst(i, self.p.s, None)
        if step == 1:
            return pltpu.make_async_copy(stage, here, self.loc.at[i])
        return pltpu.make_async_copy(
            self.src(i, self.p.c, None), here if stage is None else stage, self.loc.at[i]
        )

    def start(self):
        for i in range(len(self.ws)):
            for core in (0, 1):
                for side in (0, 1):
                    self.y_copy(i, side, core).start()
        for i in range(len(self.ws)):
            self.sib_copy(i).start()
            self.own_copy(i, 0).start()

    def pass_on(self, i):
        for side in (0, 1):
            for core in (0, 1):
                self.y_arrival(i, side, core).wait_recv()
                self.z_copy(i, side, core).start()
        if self.stages[i] is not None:
            self.own_copy(i, 0).wait()
            self.own_copy(i, 1).start()

    def arrive(self, i):
        for side in (0, 1):
            for core in (0, 1):
                self.z_copy(i, side, core, True).wait_recv()
        self.sib_copy(i, True).wait_recv()
        self.own_copy(i, 0 if self.stages[i] is None else 1).wait()

    def sent(self, i):
        self.sib_copy(i).wait_send()
        for side in (0, 1):
            for core in (0, 1):
                self.y_copy(i, side, core).wait_send()
                self.z_copy(i, side, core).wait_send()

    def steps(self):
        self.start()
        yield
        for i in range(len(self.ws)):
            self.pass_on(i)
            yield
        for i in range(len(self.ws)):
            self.arrive(i)
            self.sent(i)
            yield


def run(order, **gens):
    alive = dict(gens)

    def step(name):
        if name in alive:
            try:
                next(alive[name])
            except StopIteration:
                del alive[name]

    for name in order:
        step(name)
    while alive:
        for name in list(alive):
            step(name)


def start_kernel(
    x_ref,
    cot_ref,
    wq,
    wk,
    wv,
    wo,
    gain_ref,
    meta_ref,
    rope_ref,
    wqkv_o,
    wo_o,
    gains_o,
    meta_o,
    cot_o,
    attn_in_t_o,
    qkv_o,
    attn_in,
    rope_own,
    x_all,
    qkv_send,
    stage_o,
    stage_cot,
    loc,
    misc_send,
    misc_recv,
    gain_send,
    gain_recv,
    a2a_send,
    a2a_recv,
    *sems,
):
    p = Place()
    g = Gather(
        p,
        (0, 1, 2, 3),
        (wq, wk, wv, wo),
        (wqkv_o, wqkv_o, wqkv_o, wo_o),
        (None, None, None, stage_o),
        sems,
    )
    greet(
        [p.sib()]
        + [p.dev(dy=dy, core=core) for dy in (-1, 1) for core in (0, 1)]
        + context_peers(p)
    )
    gain_targets = [p.sib()] + [p.dev(dy=1, core=core) for core in (0, 1)]
    gain_copies = [
        remote(gain_ref, gains_o.at[p.s], gain_send.at[i], gain_recv.at[i if i == 0 else 1 + p.c], d)
        for i, d in enumerate(gain_targets)
    ]
    for c in gain_copies:
        c.start()
    x_own = pltpu.make_async_copy(x_ref, x_all.at[:, 0], loc.at[0])
    x_own.start()
    x_out = remote(x_ref, x_all.at[:, 1], misc_send.at[0], misc_recv.at[0], p.sib())
    x_out.start()
    g.start()
    rope_in = pltpu.make_async_copy(
        rope_ref.at[:, pl.ds(pl.multiple_of(p.k * BLOCK, BLOCK), BLOCK)], rope_own, loc.at[4]
    )
    rope_in.start()
    gain_own = pltpu.make_async_copy(gain_ref, gains_o.at[p.s], loc.at[1])
    gain_own.start()
    meta_own = pltpu.make_async_copy(meta_ref, meta_o.at[p.c], loc.at[2])
    meta_own.start()
    meta_out = remote(meta_ref, meta_o.at[p.c], misc_send.at[1], misc_recv.at[1], p.sib())
    meta_out.start()
    cot_in = pltpu.make_async_copy(cot_ref, stage_cot, loc.at[3])
    cot_in.start()
    cot_own = pltpu.make_async_copy(stage_cot, cot_o.at[:, 0], loc.at[3])
    cot_out = remote(cot_ref, cot_o.at[:, 1], misc_send.at[2], misc_recv.at[2], p.sib())
    cot_out.start()

    gain_own.wait()
    for i in range(3):
        block = p.yl * 2 + 1 - p.c if i == 0 else (1 - p.yl) * 2 + (i - 1)
        here = gains_o.at[block]
        remote(here, here, gain_send.at[i], gain_recv.at[i], p.sib()).wait_recv()
    x_own.wait()
    x_out.wait_recv()
    gain = jnp.concatenate([gains_o[b, 0:1, :] for b in range(4)], axis=1)

    def norm_step(i, carry):
        v = x_all[i // 2, i % 2].astype(F32).reshape(BLOCK, MODEL)
        r = lax.rsqrt(jnp.mean(v * v, axis=1, keepdims=True) + NORM_EPS)
        v = (v * r * gain).astype(BF)
        attn_in[i // 2, pl.ds((i % 2) * BLOCK, BLOCK), :] = v
        attn_in_t_o[:, pl.ds(pl.multiple_of(i * BLOCK, BLOCK), BLOCK)] = v.T
        return carry

    lax.fori_loop(0, 8, norm_step, 0)
    rope_in.wait()
    for i in range(4):
        g.pass_on(i)
    cot_in.wait()
    cot_own.start()

    def send_block(j, q):
        other = p.c if q == 0 else 1 - p.c
        k = j * 2 + other
        slot = j * 2 + q
        return (
            k,
            remote(
                qkv_send.at[slot],
                qkv_o.at[p.k],
                a2a_send.at[slot],
                a2a_recv.at[p.k],
                p.member(k),
            ),
            pltpu.make_async_copy(qkv_send.at[slot], qkv_o.at[p.k], a2a_send.at[slot]),
        )

    for i in range(3):
        g.arrive(i)

    def wide(v):
        v = jnp.concatenate([v, v], axis=1)
        return jnp.concatenate([v, v], axis=0)

    def qkv_step(j, carry):
        a = attn_in[j]
        for part in range(3):
            cols = pl.ds(part * 256, 256)
            w = wqkv_o[:, :, cols].reshape(MODEL, 256)
            v = jnp.dot(a, w, preferred_element_type=F32)
            if part < 2:
                v = v * wide(rope_own[0]) + swap_halves(v) * wide(rope_own[1])
            v = v.reshape(32, 8, 256).astype(BF)
            qkv_send[j * 2, :, :, cols] = v[:16]
            qkv_send[j * 2 + 1, :, :, cols] = v[16:]
        for q in (0, 1):
            k, out, here = send_block(j, q)

            @pl.when(k != p.k)
            def _():
                out.start()

            @pl.when(k == p.k)
            def _():
                here.start()

        return carry

    lax.fori_loop(0, 4, qkv_step, 0)
    g.arrive(3)
    for i in range(4):
        g.sent(i)
    x_out.wait_send()
    meta_own.wait()
    meta_out.wait_send()
    here = meta_o.at[1 - p.c]
    remote(here, here, misc_send.at[1], misc_recv.at[1], p.sib()).wait_recv()
    cot_own.wait()
    cot_out.wait()
    for c in gain_copies:
        c.wait_send()
    for j in range(4):
        for q in (0, 1):
            k, out, here = send_block(j, q)

            @pl.when(k != p.k)
            def _():
                out.wait_send()

            @pl.when(k == p.k)
            def _():
                here.wait()

    for i in range(8):

        @pl.when(i != p.k)
        def _():
            here = qkv_o.at[i]
            remote(here, here, a2a_send.at[i], a2a_recv.at[i], p.member(i)).wait_recv()


def start_call(x, cot, weights, gains, meta, rope):
    shapes = (
        jax.ShapeDtypeStruct((256, 8, 768), BF),
        jax.ShapeDtypeStruct((32, 8, 2048), BF),
        jax.ShapeDtypeStruct((4, 8, 512), F32),
        jax.ShapeDtypeStruct((2, 8, 1024), jnp.int32),
        jax.ShapeDtypeStruct((4, 2, 16, 8, MODEL), BF),
        jax.ShapeDtypeStruct((MODEL, 1024), BF),
        jax.ShapeDtypeStruct((8, 16, 8, 768), BF),
    )
    return pl.pallas_call(
        start_kernel,
        out_shape=shapes,
        in_specs=[ANY] * 6 + [VM, ANY, ANY],
        out_specs=[VM, ANY, VM, ANY, ANY, VM, ANY],
        scratch_shapes=[
            pltpu.VMEM((4, 256, MODEL), BF),
            pltpu.VMEM((2, BLOCK, 128), F32),
            pltpu.VMEM((4, 2, 16, 8, MODEL), BF),
            pltpu.VMEM((8, 16, 8, 768), BF),
            pltpu.VMEM((32, 8, 512), BF),
            pltpu.VMEM((4, 16, 8, MODEL), BF),
            DMA((5,)),
            DMA((3,)),
            DMA((3,)),
            DMA((3,)),
            DMA((3,)),
            DMA((8,)),
            DMA((8,)),
        ]
        + Gather.sems(4),
        compiler_params=params(1),
    )(tiles(x), tiles(cot), *[tiles(w) for w in weights], gains, meta, rope)


def bias_rows(qb, rows, prow, vrow, pcol):
    i = qb * rows + lax.broadcasted_iota(jnp.int32, (rows, 1024), 0)
    j = lax.broadcasted_iota(jnp.int32, (rows, 1024), 1)
    same = (pcol >= 0) & (pcol == prow)
    ok = ((j <= i) | same) & ((vrow > 0) | (i == j))
    return jnp.where(ok, 0.0, MASK_FILL)


def attend_kernel(
    qkv, info, pcol, out_o, lse_o, o_send, a2a_send, a2a_recv
):
    p = Place()
    greet(context_peers(p))
    mine = p.slot(p.k)
    rows = 256

    def sends(i):
        return (
            remote(o_send.at[i], out_o.at[mine], a2a_send.at[i], a2a_recv.at[p.k], p.member(i)),
            pltpu.make_async_copy(o_send.at[i], out_o.at[mine], a2a_send.at[i]),
        )

    def step(qb, carry):
        at = pl.ds(pl.multiple_of(qb * rows, rows), rows)
        bias = bias_rows(qb, rows, info[0:1, :], info[1:2, :], pcol[at, 0:1])
        lane = lax.broadcasted_iota(jnp.int32, (rows, 128), 1)
        totals = jnp.zeros((rows, 128), F32)
        outs = []
        for h in range(4):
            q = qkv[at, pl.ds(h * 64, 64)]
            k = qkv[:, pl.ds(256 + h * 64, 64)]
            v = qkv[:, pl.ds(512 + h * 64, 64)]
            sc = lax.dot_general(q, k, (((1,), (1,)), ((), ())), preferred_element_type=F32)
            sc = sc * (HEAD_DIM**-0.5) + bias
            top = jnp.max(sc, axis=1, keepdims=True)
            e = jnp.exp(sc - top)
            total = jnp.sum(e, axis=1, keepdims=True)
            prob = (e * (1.0 / total)).astype(BF)
            totals = jnp.where(lane == h, top + jnp.log(total), totals)
            outs.append(jnp.dot(prob, v, preferred_element_type=F32))
        lse_o[at, :] = totals
        o = jnp.concatenate(outs, axis=1).reshape(32, 8, 256).astype(BF)
        for half in (0, 1):
            i = qb * 2 + half
            o_send[i] = o[half * 16 : (half + 1) * 16]
            out, here = sends(i)

            @pl.when(i != p.k)
            def _():
                out.start()

            @pl.when(i == p.k)
            def _():
                here.start()

        return carry

    lax.fori_loop(0, 4, step, 0)
    for i in range(8):
        out, here = sends(i)

        @pl.when(i != p.k)
        def _():
            out.wait_send()
            spot = out_o.at[p.slot(i)]
            remote(spot, spot, a2a_send.at[i], a2a_recv.at[i], p.member(i)).wait_recv()

        @pl.when(i == p.k)
        def _():
            here.wait()


def attend_call(qkv, info, pcol):
    return pl.pallas_call(
        attend_kernel,
        out_shape=(
            jax.ShapeDtypeStruct((8, 16, 8, 256), BF),
            jax.ShapeDtypeStruct((1024, 128), F32),
        ),
        in_specs=[VM] * 3,
        out_specs=[ANY, VM],
        scratch_shapes=[pltpu.VMEM((8, 16, 8, 256), BF), DMA((8,)), DMA((8,))],
        compiler_params=params(2),
    )(qkv, info, pcol)


X_SCRATCH = [
    pltpu.VMEM((4, BLOCK, MODEL), F32),
    pltpu.VMEM((4, BLOCK, MODEL), BF),
    pltpu.VMEM((4, BLOCK, MODEL), BF),
    pltpu.VMEM((3, BLOCK, MODEL), BF),
    pltpu.VMEM((3, BLOCK, MODEL), BF),
    DMA((4,)),
    DMA((4,)),
    DMA((6,)),
    DMA((6,)),
    DMA((10,)),
    DMA((10,)),
]


def x_peers(p):
    return [p.sib(), p.dev(dx=1), p.dev(dx=-1)]


def multiplier(lhs, rhs, transposed):
    def multiply(n, j, first):
        cols = pl.ds(pl.multiple_of(first, TILE), TILE)
        if transposed:
            return lax.dot_general(
                lhs[j], rhs[cols, :], (((1,), (1,)), ((), ())), preferred_element_type=F32
            )
        return jnp.dot(lhs[j], rhs[:, cols], preferred_element_type=F32)

    return multiply


def x_phase(p, multiply, scratch, out, both, finish, prepare=None, arrived=None):
    acc, sib_out, sib_in, x_out, x_in, s_send, s_recv, x_send, x_recv, g_send, g_recv = scratch
    half = BLOCK // 2
    top, low = pl.ds(0, half), pl.ds(half, half)
    to_right, to_left = p.dev(dx=1), p.dev(dx=-1)

    def sib_copy(r):
        return remote(sib_out.at[r], sib_in.at[r], s_send.at[r], s_recv.at[r], p.sib())

    def product(r):
        j = (p.x + r) % 4
        n = (2, 1, 3, 0).index(r)
        if prepare is not None:
            prepare(n, j)

        def step(i, carry):
            cols = pl.ds(pl.multiple_of(i * TILE, TILE), TILE)
            v = multiply(n, j, i * TILE)
            acc[r, :, cols] = v[:BLOCK]
            sib_out[r, :, cols] = v[BLOCK:].astype(BF)
            return carry

        lax.fori_loop(0, MODEL // TILE, step, 0)
        sib_copy(r).start()

    def along(n, slot, rows, device):
        return remote(
            x_out.at[slot, rows], x_in.at[slot, rows], x_send.at[n], x_recv.at[n], device
        )

    far_right, far_left = along(0, 0, top, to_right), along(1, 0, low, to_left)
    right_low, right_top = along(2, 1, low, to_right), along(3, 1, top, to_right)
    left_top, left_low = along(4, 2, top, to_left), along(5, 2, low, to_left)
    product(2)
    yield
    product(1)
    sib_copy(2).wait_recv()
    x_out[0] = (acc[2] + sib_in[2].astype(F32)).astype(BF)
    far_right.start()
    far_left.start()
    yield
    product(3)
    sib_copy(1).wait_recv()
    x_out[1, half:] = (acc[1, half:] + sib_in[1, half:].astype(F32)).astype(BF)
    right_low.start()
    sib_copy(3).wait_recv()
    x_out[2, 0:half] = (acc[3, 0:half] + sib_in[3, 0:half].astype(F32)).astype(BF)
    left_top.start()
    yield
    product(0)
    yield
    far_right.wait_recv()
    x_out[1, 0:half] = (
        acc[1, 0:half] + sib_in[1, 0:half].astype(F32) + x_in[0, 0:half].astype(F32)
    ).astype(BF)
    right_top.start()
    far_left.wait_recv()
    x_out[2, half:] = (
        acc[3, half:] + sib_in[3, half:].astype(F32) + x_in[0, half:].astype(F32)
    ).astype(BF)
    left_low.start()
    yield
    sib_copy(0).wait_recv()
    acc[0] += sib_in[0].astype(F32)
    for c in (right_low, left_top, right_top, left_low):
        c.wait_recv()
    total = acc[0] + x_in[1].astype(F32) + x_in[2].astype(F32)
    for r in range(4):
        sib_copy(r).wait_send()
    for c in (far_right, far_left, right_low, right_top, left_top, left_low):
        c.wait_send()

    me, right, left, far = p.x, (p.x + 1) % 4, (p.x + 3) % 4, (p.x + 2) % 4
    out[me, 0] = finish(total)
    sent = []

    def copy(n, j, rows, d):
        src = out.at[j, 0, rows]
        return remote(src, src, g_send.at[n], g_recv.at[n], d)

    def go(c):
        c.start()
        sent.append(c)

    def to_sib(n, j):
        return remote(out.at[j, 0], out.at[j, 1], g_send.at[n], g_recv.at[n], p.sib())

    go(copy(0, me, top, to_right))
    go(copy(1, me, low, to_left))
    go(copy(2, me, low, to_right))
    go(copy(3, me, top, to_left))
    if both:
        go(to_sib(6, me))
    yield
    copy(0, left, top, to_left).wait_recv()
    go(copy(4, left, top, to_right))
    copy(1, right, low, to_right).wait_recv()
    go(copy(5, right, low, to_left))
    yield
    copy(2, left, low, to_left).wait_recv()
    copy(3, right, top, to_right).wait_recv()
    if both:
        go(to_sib(7, left))
        go(to_sib(8, right))
    yield
    copy(4, far, top, to_left).wait_recv()
    copy(5, far, low, to_right).wait_recv()
    if both:
        go(to_sib(9, far))
        yield
        for n, j in ((6, me), (7, left), (8, right), (9, far)):
            to_sib(n, j).wait_recv()
            if arrived is not None:
                arrived(j)
    for c in sent:
        c.wait_send()


def rms(v):
    return lax.rsqrt(jnp.mean(v * v, axis=1, keepdims=True) + NORM_EPS)


def full_row(gains, row):
    return jnp.concatenate([gains[b, row : row + 1, :] for b in range(4)], axis=1)


def norm_back(grad, normed, gain, inv):
    w = grad * gain
    return inv * (w - normed * jnp.mean(w * normed, axis=1, keepdims=True))


UNITS = {
    "down_a": (64, 512, "col", 0, ()),
    "down_b": (64, 512, "col", 64, ()),
    "gate_a": (64, 512, "row", 0, (1024,)),
    "gate_b": (64, 512, "row", 512, (1024,)),
    "up_a": (64, 512, "row", 0, (512,)),
    "up_b": (64, 512, "row", 512, (512,)),
    "out": (32, 512, "col", 0, ()),
    "qkv": (64, 768, "row", 0, (256, 256, 256)),
}
UNIT_SCRATCH = 8
DOWN_OUT = jax.ShapeDtypeStruct((2, 2, 2, 32, 8, 512), BF)
OUT_OUT = jax.ShapeDtypeStruct((2, 1, 2, 16, 8, 512), BF)
FFN_OUT = jax.ShapeDtypeStruct((2, 32, 8, 2048), BF)
UP_OUT = jax.ShapeDtypeStruct((2, 32, 8, 1024), BF)
QKV_OUT = jax.ShapeDtypeStruct((2, 32, 8, 512), BF)


def unit_scratch(name):
    r, c, _, _, _ = UNITS[name]
    return [
        pltpu.VMEM((2, 2, r // 2, 8, c), BF),
        pltpu.VMEM((2, 2, r // 2, 8, c), BF),
        pltpu.VMEM((2, 2, 2, r // 8, 8, c), BF),
        pltpu.VMEM((3, 2, 2, r // 8, 8, c), BF),
        pltpu.VMEM((2, 2, r // 8, 8, c), BF),
        DMA((4,)),
        DMA((18,)),
        DMA((18,)),
    ]


def unit_peers(p):
    return [p.sib(), p.dev(dy=1), p.dev(dy=-1), p.dev(dy=2), p.dev(dz=1), p.dev(dz=-1)]


def unit(p, name, src, outs, scratch):
    rows, cols, kind, first, widths = UNITS[name]
    own, yin, zout, zin, yhin, loc, send, recv = scratch
    part = rows // 8
    half = rows // 2
    z_of = {0: p.dev(dz=1), 1: p.dev(dz=-1)}
    me, zr, zl, zf = p.z, (p.z + 1) % 4, (p.z + 3) % 4, (p.z + 2) % 4

    def cp(n, src, dst, d):
        return remote(src, dst, send.at[n], recv.at[n], d)

    def fetch(yl, h, dst, make):
        if kind == "row":
            return [
                make(
                    h * 2,
                    src.at[pl.ds(yl * 2, 2), pl.ds(h * half, half), :, pl.ds(first, cols)],
                    dst.at[:, h],
                )
            ]
        return [
            make(
                h * 2 + core,
                src.at[pl.ds(first + h * half, half), :, pl.ds((yl * 2 + core) * cols, cols)],
                dst.at[core, h],
            )
            for core in (0, 1)
        ]

    along_y, local = [], []
    for h in (0, 1):
        d = p.dev(dy=1 if h == 0 else -1)
        along_y += fetch(1 - p.yl, h, yin, lambda n, a, b, d=d: cp(n, a, b, d))
        local += fetch(p.yl, h, own, lambda n, a, b: pltpu.make_async_copy(a, b, loc.at[n]))
    for c in along_y + local:
        c.start()
    yield
    for c in local:
        c.wait()
    for c in along_y:
        c.wait_recv()
    own[...] = (own[...].astype(F32) + yin[...].astype(F32)).astype(BF)

    def chunk(h, zc):
        return own.at[:, h, pl.ds(zc * part, part)]

    far = [cp(4 + h, chunk(h, zf), zin.at[0, :, h], z_of[h]) for h in (0, 1)]
    for c in far:
        c.start()
    yield
    for c in far:
        c.wait_send()
    near = []
    for side, zc in ((0, zr), (1, zl)):
        zout[side, :, 1 - side] = own[:, 1 - side, pl.ds(zc * part, part)]
        far[side].wait_recv()
        zout[side, :, side] = (
            own[:, side, pl.ds(zc * part, part)].astype(F32) + zin[0, :, side].astype(F32)
        ).astype(BF)
        c = cp(6 + side, zout.at[side], zin.at[1 + side], z_of[side])
        c.start()
        near.append(c)
    yield
    for c in near:
        c.wait_recv()
    for c in near:
        c.wait_send()
    v = own[:, :, pl.ds(me * part, part)].astype(F32)
    zout[0] = (v + zin[1].astype(F32) + zin[2].astype(F32)).astype(BF)
    yh = cp(8, zout.at[0], yhin, p.dev(dy=2))
    yh.start()
    yield
    yh.wait_recv()
    own[:, :, pl.ds(me * part, part)] = (zout[0].astype(F32) + yhin[...].astype(F32)).astype(BF)
    back = [cp(9 + side * 2 + h, chunk(h, me), chunk(h, me), z_of[side]) for side, h in ((0, 0), (1, 1), (0, 1), (1, 0))]
    for c in back:
        c.start()
    yield
    for side, zc in ((0, zl), (1, zr)):
        here = chunk(side, zc)
        cp(9 + side * 3, here, here, z_of[1 - side]).wait_recv()
        c = cp(13 + side, here, here, z_of[side])
        c.start()
        back.append(c)
    yield
    for side, zc in ((0, zl), (1, zr)):
        here = chunk(1 - side, zc)
        cp(9 + side * 2 + 1 - side, here, here, z_of[1 - side]).wait_recv()
    for h in (0, 1):
        here = chunk(h, zf)
        cp(13 + h, here, here, z_of[1 - h]).wait_recv()
    for c in back + along_y + [yh]:
        c.wait_send()
    done = []
    if kind == "col":
        spot = outs[0].at[p.c, first // rows]
        done.append(cp(15, own.at[1 - p.c], spot, p.sib()))
        done.append(pltpu.make_async_copy(own.at[p.c], spot, loc.at[0]))
    else:
        for i, width in enumerate(widths):
            take = min(cols, width)
            spot = outs[i].at[:, :, :, pl.ds(p.c * width + (first if width > cols else 0), take)]
            piece = pl.ds(i * take, take)
            done.append(cp(15 + i, own.at[1 - p.c, :, :, :, piece], spot, p.sib()))
            done.append(pltpu.make_async_copy(own.at[p.c, :, :, :, piece], spot, loc.at[i]))
    for c in done:
        c.start()
    yield
    for c in done:
        c.wait()


def out_proj_kernel(
    lhs,
    rhs,
    keep,
    gains,
    x_ref,
    wg,
    wu,
    wd,
    ffn_in_o,
    resid_o,
    stat_o,
    wgu_o,
    wd_o,
    stage_g,
    stage_u,
    stage_d,
    x_rows,
    x_sem,
    *scratch,
):
    p = Place()
    nx = len(X_SCRATCH)
    g = Gather(
        p,
        (4, 5, 6),
        (wg, wu, wd),
        (wgu_o, wgu_o, wd_o),
        (stage_g, stage_u, stage_d),
        scratch[nx:],
    )
    greet(Gather.peers(p) + [p.dev(dx=1), p.dev(dx=-1)])
    x_read = own_rows(p, x_ref, (x_rows, x_sem))

    def finish(attn_out):
        stat_o[...] = jnp.full((8, 128), jnp.sum(keep[:, 0:1] * attn_out * attn_out), F32)
        resid = x_read() + attn_out
        resid_o[...] = resid
        return (resid * rms(resid) * full_row(gains, 1)).astype(BF)

    run(
        PROJ_ORDER,
        g=g.steps(),
        x=x_phase(p, multiplier(lhs, rhs, False), scratch[:nx], ffn_in_o, True, finish),
    )


def out_proj_call(lhs, rhs, keep, gains, x, weights):
    return pl.pallas_call(
        out_proj_kernel,
        out_shape=(
            jax.ShapeDtypeStruct((4, 2, BLOCK, MODEL), BF),
            jax.ShapeDtypeStruct((BLOCK, MODEL), F32),
            jax.ShapeDtypeStruct((8, 128), F32),
            jax.ShapeDtypeStruct((256, 8, 2048), BF),
            jax.ShapeDtypeStruct((128, 8, 2048), BF),
        ),
        in_specs=[VM] * 4 + [ANY] * 4,
        out_specs=[VM] * 3 + [ANY] * 2,
        scratch_shapes=[
            pltpu.VMEM((64, 8, 1024), BF),
            pltpu.VMEM((64, 8, 1024), BF),
            pltpu.VMEM((128, 8, 512), BF),
        ]
        + OWN_ROWS
        + X_SCRATCH
        + Gather.sems(3),
        compiler_params=params(3),
    )(lhs, rhs, keep, gains, tiles(x), *[tiles(w) for w in weights])


def ffn_kernel(a_ref, c_ref, wg, wu, wd, h_o, gg_o, gu_o, dd_o, dg_o, du_o, a_t):
    rows = FFN_ROWS

    @pl.when(pl.program_id(0) == 0)
    def _():
        def turn(i, carry):
            at = pl.ds(pl.multiple_of(i * 256, 256), 256)
            a_t[:, at] = a_ref[at, :].T
            return carry

        lax.fori_loop(0, 4, turn, 0)

    def step(i, carry):
        at = pl.ds(pl.multiple_of(i * rows, rows), rows)
        a = a_ref[at, :]
        gate = jnp.dot(a, wg[...], preferred_element_type=F32)
        up = jnp.dot(a, wu[...], preferred_element_type=F32)
        grad = lax.dot_general(
            c_ref[at, :], wd[...], (((1,), (1,)), ((), ())), preferred_element_type=F32
        )
        sig = 1.0 / (1.0 + jnp.exp(-gate))
        silu = gate * sig
        h_o[at, :] = (silu * up).astype(BF)
        gg_o[at, :] = (grad * up * sig * (1.0 + gate * (1.0 - sig))).astype(BF)
        gu_o[at, :] = (grad * silu).astype(BF)
        return carry

    lax.fori_loop(0, 1024 // rows, step, 0)
    h_t = h_o[...].T

    def down(n, carry):
        cols = pl.ds(pl.multiple_of(n * 256, 256), 256)
        dd_o[:, cols] = jnp.dot(h_t, c_ref[:, cols], preferred_element_type=F32).astype(BF)
        return carry

    lax.fori_loop(0, MODEL // 256, down, 0)

    def back(n, carry):
        at = pl.ds(pl.multiple_of(n * FFN_BACK, FFN_BACK), FFN_BACK)
        t = a_t[at, :]
        dg_o[at, :] = jnp.dot(t, gg_o[...], preferred_element_type=F32).astype(BF)
        du_o[at, :] = jnp.dot(t, gu_o[...], preferred_element_type=F32).astype(BF)
        return carry

    lax.fori_loop(0, MODEL // FFN_BACK, back, 0)


def ffn_call(ffn_in, cot, wgu, wd):
    tile = FFN_TILE
    n = 1024 // tile
    whole = pl.BlockSpec((1024, MODEL), lambda i: (0, 0), pipeline_mode=pl.Buffered(1))
    cols = pl.BlockSpec((1024, tile), lambda i: (0, i))
    tall = pl.BlockSpec((MODEL, tile), lambda i: (0, i))
    wide = pl.BlockSpec((tile, MODEL), lambda i: (i, 0))
    tokens = jax.ShapeDtypeStruct((1024, 1024), BF)
    grads = jax.ShapeDtypeStruct((MODEL, 1024), BF)
    return pl.pallas_call(
        ffn_kernel,
        grid=(n,),
        out_shape=(tokens, tokens, tokens, jax.ShapeDtypeStruct((1024, MODEL), BF), grads, grads),
        in_specs=[whole, whole, tall, pl.BlockSpec((MODEL, tile), lambda i: (0, i + n)), wide],
        out_specs=[cols, cols, cols, wide, tall, tall],
        scratch_shapes=[pltpu.VMEM((MODEL, 1024), BF)],
        compiler_params=params(),
    )(ffn_in, cot, wgu, wgu, wd)


MID = ("down_a", "down_b", "gate_a", "gate_b", "up_a")


def mid_kernel(*refs):
    gate, up, hidden, wgu, wd, dd, dgate, dup, cot_ref = refs[:9]
    wo, resid_ref, gains, keep, qkv, info, pcol, lse, rope = refs[9:18]
    grad_o, resid_grad_o, gain_o, final_o, stat_o, d_o, dd_o, dgate_o, dup_o = refs[18:27]
    lhs, rhs, g_out, g_in, d_out, dk, dv = refs[27:34]
    loc, g_send, g_recv, a2a_send, a2a_recv = refs[34:39]
    cot_scratch = refs[39:41]
    at = 41
    nx = len(X_SCRATCH)
    xs = refs[at : at + nx]
    at += nx
    us = [refs[at + i * UNIT_SCRATCH : at + (i + 1) * UNIT_SCRATCH] for i in range(len(MID))]
    p = Place()
    greet(context_peers(p) + x_peers(p) + [p.dev(dy=1), p.dev(dy=-1)])
    rows = ATTEND_ROWS
    each = rows // 8
    scale = HEAD_DIM**-0.5
    mine = p.slot(p.k)
    cot_read = own_rows(p, cot_ref, cot_scratch)

    def fetch(n, sources):
        j = (p.x + (2, 1, 3, 0)[n]) % 4
        return [
            pltpu.make_async_copy(v.at[j], lhs.at[n % 2, i], loc.at[(n % 2) * 2 + i])
            for i, v in enumerate(sources)
        ]

    def preparer(sources, right):
        def prepare(n, j):
            if n == 0:
                for c in fetch(0, sources):
                    c.start()
            if n < 3:
                for c in fetch(n + 1, sources):
                    c.start()
            if n == 0:
                right.wait()
            for c in fetch(n, sources):
                c.wait()

        return prepare

    def flat(v):
        return v.reshape(v.shape[0] * 8, v.shape[2])

    wgu_in = pltpu.make_async_copy(wgu, rhs, loc.at[4])
    wgu_in.start()
    wd_in = pltpu.make_async_copy(wd, rhs.at[pl.ds(0, 128)], loc.at[4])

    def multiply_back(n, j, first):
        v = 0.0
        for i in (0, 1):
            w = rhs[pl.ds(first // 8, TILE // 8), :, pl.ds(i * 1024, 1024)]
            v += lax.dot_general(
                flat(lhs[n % 2, i]), flat(w), (((1,), (1,)), ((), ())), preferred_element_type=F32
            )
        return v

    def multiply_out(n, j, first):
        w = rhs[pl.ds(0, 128), :, pl.ds(pl.multiple_of(first, TILE), TILE)]
        return jnp.dot(flat(lhs[n % 2, 0]), flat(w), preferred_element_type=F32)

    def finish_back(g):
        wd_in.start()
        resid = resid_ref[...]
        inv = rms(resid)
        normed = resid * inv
        gain_o[...] = jnp.broadcast_to(jnp.sum(g * normed, axis=0, keepdims=True), (8, MODEL))
        grad_resid = cot_read() + norm_back(g, normed, full_row(gains, 1), inv)
        resid_grad_o[...] = grad_resid
        return grad_resid.astype(BF)

    def finish_out(ffn_out):
        final = resid_ref[...] + ffn_out
        kp = keep[:, 0:1]
        stat_o[0] = jnp.full((8, 128), jnp.sum(kp * ffn_out * ffn_out), F32)
        stat_o[1] = jnp.full((8, 128), jnp.sum(kp * final * final), F32)
        return final.astype(BF)

    def g_copy(j, q):
        k = j * 2 + (p.c if q == 0 else 1 - p.c)
        slot = j * 2 + q
        return (
            k,
            remote(g_out.at[slot], g_in.at[p.k], g_send.at[slot], g_recv.at[p.k], p.member(k)),
            pltpu.make_async_copy(g_out.at[slot], g_in.at[p.k], g_send.at[slot]),
        )

    def arrived(j):
        v = lax.dot_general(
            grad_o[j].reshape(256, MODEL), wo[...], (((1,), (1,)), ((), ())), preferred_element_type=F32
        )
        v = v.reshape(32, 8, 256).astype(BF)
        for q in (0, 1):
            g_out[j * 2 + q] = v[q * 16 : (q + 1) * 16]
            k, out, here = g_copy(j, q)

            @pl.when(k != p.k)
            def _():
                out.start()

            @pl.when(k == p.k)
            def _():
                here.start()

    def sends(i):
        return (
            remote(d_out.at[i], d_o.at[mine], a2a_send.at[i], a2a_recv.at[p.k], p.member(i)),
            pltpu.make_async_copy(d_out.at[i], d_o.at[mine], a2a_send.at[i]),
        )

    def wide(v):
        return jnp.concatenate([v, v], axis=1)

    def query_block(qb):
        spot = pl.ds(qb * rows, rows)
        bias = bias_rows(qb, rows, info[0:1, :], info[1:2, :], pcol[spot, 0:1])
        blocks = pl.ds(qb * (rows // BLOCK), rows // BLOCK)
        g2 = g_in[blocks].astype(F32).reshape(rows, 256).astype(BF)
        dqs = []
        for h in range(4):
            lanes = pl.ds(h * 64, 64)
            q = qkv[spot, lanes]
            k = qkv[:, pl.ds(256 + h * 64, 64)]
            v = qkv[:, pl.ds(512 + h * 64, 64)]
            g = g2[:, h * 64 : (h + 1) * 64]
            sc = lax.dot_general(q, k, (((1,), (1,)), ((), ())), preferred_element_type=F32)
            prob = jnp.exp(sc * scale + bias - lse[spot, h : h + 1])
            gp = lax.dot_general(g, v, (((1,), (1,)), ((), ())), preferred_element_type=F32)
            inner = jnp.sum(prob * gp, axis=1, keepdims=True)
            gs = (prob * (gp - inner)).astype(BF)
            dqs.append(jnp.dot(gs, k, preferred_element_type=F32))
            dk[:, lanes] += lax.dot_general(
                gs, q, (((0,), (0,)), ((), ())), preferred_element_type=F32
            )
            dv[:, lanes] += lax.dot_general(
                prob.astype(BF), g, (((0,), (0,)), ((), ())), preferred_element_type=F32
            )
        dq = jnp.concatenate(dqs, axis=1) * scale
        dq = dq * wide(rope[0, spot]) - swap_halves(dq) * wide(rope[1, spot])
        dq = dq.reshape(each, 8, 256).astype(BF)
        for b in range(rows // BLOCK):
            d_out[qb * (rows // BLOCK) + b, :, :, 0:256] = dq[b * 16 : (b + 1) * 16]

    def give(i, carry):
        spot = pl.ds(pl.multiple_of(i * BLOCK, BLOCK), BLOCK)
        w = dk[spot, :] * scale
        w = w * wide(rope[0, spot]) - swap_halves(w) * wide(rope[1, spot])
        d_out[i, :, :, 256:512] = w.reshape(16, 8, 256).astype(BF)
        d_out[i, :, :, 512:768] = dv[spot, :].reshape(16, 8, 256).astype(BF)
        out, here = sends(i)

        @pl.when(i != p.k)
        def _():
            out.start()

        @pl.when(i == p.k)
        def _():
            here.start()

        return carry

    def main():
        yield from x_phase(
            p,
            multiply_back,
            xs,
            grad_o,
            True,
            finish_back,
            preparer((gate, up), wgu_in),
            arrived,
        )
        dk[...] = jnp.zeros_like(dk)
        dv[...] = jnp.zeros_like(dv)
        yield
        for j in range(4):
            for q in (0, 1):
                k, out, here = g_copy(j, q)

                @pl.when(k != p.k)
                def _():
                    out.wait_send()

                @pl.when(k == p.k)
                def _():
                    here.wait()

        for i in range(8):

            @pl.when(i != p.k)
            def _():
                spot = g_in.at[i]
                remote(spot, spot, g_send.at[i], g_recv.at[i], p.member(i)).wait_recv()

        for qb in range(1024 // rows):
            query_block(qb)
            yield
        lax.fori_loop(0, 8, give, 0)
        yield
        for i in range(8):
            out, here = sends(i)

            @pl.when(i != p.k)
            def _():
                out.wait_send()
                spot = d_o.at[p.slot(i)]
                remote(spot, spot, a2a_send.at[i], a2a_recv.at[i], p.member(i)).wait_recv()

            @pl.when(i == p.k)
            def _():
                here.wait()

    x = x_phase(
        p, multiply_out, xs, final_o, False, finish_out, preparer((hidden,), wd_in)
    )
    sources = (dd, dd, dgate, dgate, dup)
    results = (dd_o, dd_o, dgate_o, dgate_o, dup_o)
    a, b, c, d, e = [
        unit(p, name, src, (o,), scr) for name, src, o, scr in zip(MID, sources, results, us)
    ]
    run(MID_ORDER, m=main(), x=x, a=a, b=b, c=c, d=d, e=e)


def mid_call(gate, up, hidden, wgu, wd, dd, dgate, dup, cot, wo, *rest):
    scratch = list(X_SCRATCH)
    for name in MID:
        scratch += unit_scratch(name)
    blocks = [tiles(v.reshape(4, 256, 1024)) for v in (gate, up, hidden)]
    return pl.pallas_call(
        mid_kernel,
        out_shape=(
            jax.ShapeDtypeStruct((4, 2, BLOCK, MODEL), BF),
            jax.ShapeDtypeStruct((BLOCK, MODEL), F32),
            jax.ShapeDtypeStruct((8, MODEL), F32),
            jax.ShapeDtypeStruct((4, 1, BLOCK, MODEL), BF),
            jax.ShapeDtypeStruct((2, 8, 128), F32),
            jax.ShapeDtypeStruct((8, 16, 8, 768), BF),
            DOWN_OUT,
            FFN_OUT,
            UP_OUT,
        ),
        in_specs=[ANY] * 9 + [VM] * 9,
        out_specs=[VM] * 5 + [ANY] * 4,
        scratch_shapes=[
            pltpu.VMEM((2, 2, 32, 8, 1024), BF),
            pltpu.VMEM((256, 8, 2048), BF),
            pltpu.VMEM((8, 16, 8, 256), BF),
            pltpu.VMEM((8, 16, 8, 256), BF),
            pltpu.VMEM((8, 16, 8, 768), BF),
            pltpu.VMEM((1024, 256), F32),
            pltpu.VMEM((1024, 256), F32),
            DMA((5,)),
            DMA((8,)),
            DMA((8,)),
            DMA((8,)),
            DMA((8,)),
        ]
        + OWN_ROWS
        + scratch,
        compiler_params=params(5),
    )(
        *blocks,
        wgu,
        wd,
        tiles(dd),
        tiles(dgate).reshape(4, 64, 8, 1024),
        tiles(dup).reshape(4, 64, 8, 1024),
        tiles(cot),
        wo,
        *rest,
    )


LAST = ("up_b", "out", "qkv")


def last_kernel(
    lhs,
    rhs,
    grad_resid,
    gains,
    ffn_gain,
    stat_attn,
    stat_ffn,
    keep,
    attn_in_t,
    attended,
    grad_attn,
    dup,
    x_ref,
    *refs,
):
    out_o, small_o, up_o, do_o = refs[:4]
    qkv_o = refs[4:7]
    at = 7
    nx = len(X_SCRATCH)
    xs = refs[at : at + nx]
    at += nx
    us = []
    for _ in LAST:
        us.append(refs[at : at + UNIT_SCRATCH])
        at += UNIT_SCRATCH
    core_in, ring_in, s_send, s_recv, do, dw = refs[at : at + 6]
    x_scratch = refs[at + 6 :]
    p = Place()
    greet(unit_peers(p) + [p.dev(dx=1), p.dev(dx=-1), p.dev(dx=2), p.dev(dz=2)])
    x_read = own_rows(p, x_ref, x_scratch)

    def finish(g):
        v = x_read()
        inv = rms(v)
        normed = v * inv
        few = slice(0, 128)
        small_o[...] = jnp.zeros_like(small_o)
        small_o[0:1, :] = jnp.sum(g * normed, axis=0, keepdims=True)
        small_o[1:2, :] = ffn_gain[0:1, :]
        small_o[2:3, few] = jnp.sum(keep[...], axis=0, keepdims=True)
        small_o[3:4, few] = stat_attn[0:1, :]
        small_o[4:5, few] = stat_ffn[0, 0:1, :]
        small_o[5:6, few] = stat_ffn[1, 0:1, :]
        grad_in = grad_resid[...] + norm_back(g, normed, full_row(gains, 0), inv)
        return grad_in.astype(BF)

    def small():
        core_in[p.c] = small_o[...]
        c = remote(core_in.at[p.c], core_in.at[p.c], s_send.at[0], s_recv.at[0], p.sib())
        c.start()
        yield
        here = core_in.at[1 - p.c]
        remote(here, here, s_send.at[0], s_recv.at[0], p.sib()).wait_recv()
        c.wait_send()
        total = core_in[0] + core_in[1]
        for axis, me, move in (
            (0, p.x, lambda d: p.dev(dx=d)),
            (1, p.y, lambda d: p.dev(dy=d)),
            (2, p.z, lambda d: p.dev(dz=d)),
        ):
            ring_in[axis, me] = total
            here = ring_in.at[axis, me]
            out = [
                remote(
                    here, here, s_send.at[axis * 3 + d], s_recv.at[axis * 3 + d], move(d)
                )
                for d in (1, 2, 3)
            ]
            for c in out:
                c.start()
            yield
            for d in (1, 2, 3):
                there = ring_in.at[axis, (me + 4 - d) % 4]
                remote(
                    there, there, s_send.at[axis * 3 + d], s_recv.at[axis * 3 + d], move(4 - d)
                ).wait_recv()
            for c in out:
                c.wait_send()
            total = (ring_in[axis, 0] + ring_in[axis, 1]) + (ring_in[axis, 2] + ring_in[axis, 3])
        small_o[...] = total

    def out_unit():
        left = attended[...].reshape(1024, 256).T

        def step(n, carry):
            cols = pl.ds(pl.multiple_of(n * 512, 512), 512)
            v = jnp.dot(left, grad_attn[:, cols], preferred_element_type=F32)
            do[:, :, cols] = v.reshape(32, 8, 512).astype(BF)
            return carry

        lax.fori_loop(0, 4, step, 0)
        yield from unit(p, LAST[1], do, (do_o,), us[1])

    def qkv_unit():
        def step(n, carry):
            v = jnp.dot(
                attn_in_t[pl.ds(pl.multiple_of(n * 512, 512), 512), :],
                lhs[...].reshape(1024, 768),
                preferred_element_type=F32,
            )
            dw[n] = v.reshape(64, 8, 768).astype(BF)
            return carry

        lax.fori_loop(0, 4, step, 0)
        yield from unit(p, LAST[2], dw, qkv_o, us[2])

    run(
        LAST_ORDER,
        x=x_phase(p, multiplier(lhs, rhs, True), xs, out_o, False, finish),
        b=unit(p, LAST[0], dup, (up_o,), us[0]),
        c=out_unit(),
        d=qkv_unit(),
        s=small(),
    )


def last_call(lhs, rhs, grad_resid, gains, small_parts, attn_in_t, attended, grad_attn, dup, x):
    scratch = list(X_SCRATCH)
    for name in LAST:
        scratch += unit_scratch(name)
    outs = [UP_OUT, OUT_OUT, QKV_OUT, QKV_OUT, QKV_OUT]
    return pl.pallas_call(
        last_kernel,
        out_shape=(
            jax.ShapeDtypeStruct((4, 1, BLOCK, MODEL), BF),
            jax.ShapeDtypeStruct((8, MODEL), F32),
            *outs,
        ),
        in_specs=[VM] * 11 + [ANY] * 2,
        out_specs=[VM] * 2 + [ANY] * len(outs),
        scratch_shapes=scratch
        + [
            pltpu.VMEM((2, 8, MODEL), F32),
            pltpu.VMEM((3, 4, 8, MODEL), F32),
            DMA((10,)),
            DMA((10,)),
            pltpu.VMEM((32, 8, MODEL), BF),
            pltpu.VMEM((4, 64, 8, 768), BF),
        ]
        + OWN_ROWS,
        compiler_params=params(6),
    )(
        lhs,
        rhs,
        grad_resid,
        gains,
        *small_parts,
        attn_in_t,
        attended,
        grad_attn,
        tiles(dup).reshape(4, 64, 8, 1024),
        tiles(x),
    )


def results_kernel(output, grad, q, k, v, o, gate, up_a, up_b, down, *outs):
    for src, dst in zip((output, grad, q, k, v, o, gate), outs[:7]):
        dst[...] = src[...].astype(dst.dtype)
    for h in (0, 1):
        here = slice(h * 512, (h + 1) * 512)
        outs[7][:, h * 1024 : h * 1024 + 512] = up_a[:, here].astype(F32)
        outs[7][:, h * 1024 + 512 : (h + 1) * 1024] = up_b[:, here].astype(F32)
    outs[8][...] = down[...].astype(F32)


def results_call(*arrays):
    arrays = [a.reshape(-1, a.shape[-1]) for a in arrays]
    steps = 4

    def block(shape):
        return pl.BlockSpec((shape[0] // steps, shape[1]), lambda i: (i, 0))

    types = [BF, BF] + [F32] * 7
    shapes = [(512, 2048)] * 2 + [(512, 512)] * 4 + [(512, 2048)] * 2 + [(2048, 512)]
    return pl.pallas_call(
        results_kernel,
        grid=(steps,),
        out_shape=[jax.ShapeDtypeStruct(sh, t) for sh, t in zip(shapes, types)],
        in_specs=[block(a.shape) for a in arrays],
        out_specs=[block(sh) for sh in shapes],
        compiler_params=params(),
    )(*arrays)


def rope_table():
    half_dim = HEAD_DIM // 2
    inv_freq = ROPE_BASE ** (-np.arange(half_dim) * 2.0 / HEAD_DIM)
    angles = np.arange(1024)[:, None] * inv_freq[None, :]
    cosine, sine = np.cos(angles), np.sin(angles)
    cosine = np.concatenate([cosine, cosine], axis=1)
    sine = np.concatenate([-sine, sine], axis=1)
    return np.stack([np.tile(cosine, (1, 2)), np.tile(sine, (1, 2))]).astype(np.float32)


def piece_index(starts, piece_tags, positions):
    inside = (positions[None, :, None] >= starts[:, None, :]) & (
        positions[None, :, None] < starts[:, None, :] + PIECE
    )
    tagged = jnp.where(inside, piece_tags[:, None, :] + 1, 0)
    return jnp.sum(tagged, axis=2) - 1


def per_device(
    inputs,
    cotangent,
    q_weight,
    k_weight,
    v_weight,
    o_weight,
    gate_weight,
    up_weight,
    down_weight,
    attn_gain,
    ffn_gain,
    piece_starts,
    piece_ids,
    valid_mask,
):
    x_at = lax.axis_index("tensor")
    ctx = lax.axis_index("context")
    positions = jnp.arange(1024, dtype=jnp.int32)
    rope = jnp.asarray(rope_table())
    meta = jnp.concatenate([piece_index(piece_starts, piece_ids, positions), valid_mask], axis=0)
    gains_own = jnp.concatenate(
        [
            attn_gain.astype(F32)[None],
            ffn_gain.astype(F32)[None],
            jnp.zeros((6, attn_gain.shape[0]), F32),
        ],
        axis=0,
    )
    wqkv, wo, gains, meta_all, cot_all, attn_in_t, qkv = start_call(
        inputs,
        cotangent,
        (q_weight, k_weight, v_weight, o_weight),
        gains_own,
        meta,
        rope,
    )
    seq = lax.dynamic_slice(meta_all, (ctx % 2, 0, 0), (1, 8, 1024))[0]
    piece_row = lax.dynamic_slice_in_dim(seq, ctx // 2, 1, 0)
    valid_row = lax.dynamic_slice_in_dim(seq, 4 + ctx // 2, 1, 0)
    info = jnp.concatenate([piece_row, valid_row, jnp.zeros((6, 1024), jnp.int32)], axis=0)
    pcol = jnp.broadcast_to(piece_row.reshape(1024, 1), (1024, 128))
    wqkv, wo = rows_of(wqkv), rows_of(wo)
    cot_all = rows_of(cot_all)
    qkv = qkv.reshape(1024, 768)
    attended, lse = attend_call(qkv, info, pcol)
    keep_own = lax.dynamic_slice(valid_mask, (x_at, ctx * BLOCK), (1, BLOCK)).astype(F32)
    keep = jnp.broadcast_to(keep_own.reshape(BLOCK, 1), (BLOCK, 128))
    attended = attended.reshape(4, 256, 256)
    ffn_in, resid, stat_attn, wgu, wd = out_proj_call(
        attended, wo, keep, gains, inputs, (gate_weight, up_weight, down_weight)
    )
    ffn_in = ffn_in.reshape(1024, MODEL)
    cot_rows = cot_all.reshape(1024, MODEL)
    hidden, grad_gate, grad_up, dd, dgate, dup = ffn_call(
        ffn_in, cot_rows, rows_of(wgu), rows_of(wd)
    )

    grad_attn, grad_resid, ffn_gain_part, output, stat_ffn, d_seq, sd, sgate, sup_a = mid_call(
        grad_gate,
        grad_up,
        hidden,
        wgu,
        wd,
        dd,
        dgate,
        dup,
        cotangent,
        wo,
        resid,
        gains,
        keep,
        qkv,
        info,
        pcol,
        lse,
        rope,
    )
    dqkv = d_seq.reshape(4, 256, 768)
    input_grad, small, sup_b, so, sq, sk, sv = last_call(
        dqkv,
        wqkv,
        grad_resid,
        gains,
        (ffn_gain_part, stat_attn, stat_ffn, keep),
        attn_in_t,
        attended,
        grad_attn.reshape(1024, MODEL),
        dup,
        inputs,
    )
    output, input_grad, *grads = results_call(
        output, input_grad, sq, sk, sv, so, sgate, sup_a, sup_b, sd
    )
    branch_rms = jnp.sqrt(small[3:6, 0] / (jnp.maximum(small[2, 0], 1.0) * MODEL))
    gain_start = (lax.axis_index("shard") * 4 + x_at) * BLOCK
    attn_gain_out = lax.dynamic_slice(small, (0, gain_start), (1, BLOCK))[0]
    ffn_gain_out = lax.dynamic_slice(small, (1, gain_start), (1, BLOCK))[0]
    return (
        output.reshape(4, BLOCK, MODEL),
        input_grad.reshape(4, BLOCK, MODEL),
        *grads,
        attn_gain_out,
        ffn_gain_out,
        branch_rms,
    )


def solution(mesh):
    return jax.shard_map(
        per_device,
        mesh=mesh,
        in_specs=(
            P("shard", "context", None),
            P("shard", "context", None),
            P("shard", "tensor"),
            P("shard", "tensor"),
            P("shard", "tensor"),
            P("tensor", "shard"),
            P("shard", "tensor"),
            P("shard", "tensor"),
            P("tensor", "shard"),
            P("shard"),
            P("shard"),
            P("shard", None),
            P("shard", None),
            P("shard", None),
        ),
        out_specs=(
            P("shard", "context", None),
            P("shard", "context", None),
            P("shard", "tensor"),
            P("shard", "tensor"),
            P("shard", "tensor"),
            P("tensor", "shard"),
            P("shard", "tensor"),
            P("shard", "tensor"),
            P("tensor", "shard"),
            P(("shard", "tensor")),
            P(("shard", "tensor")),
            P(),
        ),
        check_vma=False,
    )
```

```python
import functools

import jax
import jax.numpy as jnp
import numpy as np
from jax import lax
from jax.experimental import pallas as pl
from jax.experimental.pallas import tpu as pltpu
from jax.sharding import PartitionSpec as P

HEAD_DIM = 64
PIECE = 256
NORM_EPS = 1e-05
ROPE_BASE = 130000.0
MASK_FILL = -1e30
BF = jnp.bfloat16
F32 = jnp.float32
ANY = pl.BlockSpec(memory_space=pl.ANY)
VM = pl.BlockSpec(memory_space=pltpu.VMEM)
DMA = pltpu.SemaphoreType.DMA
PROJ_ORDER = "gxxxxxggxgxgxgxggx"
MID_ORDER = (
    "amemmcbmmaemadcemmbacmebmxcxdbaxdmeaxxdcmbe"
    "mcxdbmdmxcabdxecxabdmexdxmbcamme"
)
ATTEND_ROWS = 256
LAST_ORDER = "bxdxxbxcbdxbdcbxdbcdscbsbxcxdscbsxdcsxdccd"
FFN_TILE, FFN_ROWS, FFN_BACK = 512, 1024, 2048
VMEM_LIMIT = 60 * 1024 * 1024
MODEL = 2048
TILE = 256
BLOCK = 128
MESH_ID = pl.DeviceIdType.MESH


class Place:
    def __init__(self):
        self.s = lax.axis_index("shard")
        self.k = lax.axis_index("context")
        self.x = lax.axis_index("tensor")
        self.yl = self.s // 2
        self.c = self.s % 2
        self.y = (self.k // 4) * 2 + self.yl
        self.z = self.k % 4

    def dev(self, dx=0, dy=0, dz=0, core=None):
        x = (self.x + dx + 4) % 4
        y = (self.y + dy + 4) % 4
        z = (self.z + dz + 4) % 4
        c = self.c if core is None else core
        return {"shard": (y % 2) * 2 + c, "context": (y // 2) * 4 + z, "tensor": x}

    def member(self, k):
        return {"shard": self.s, "context": k, "tensor": self.x}

    def slot(self, k):
        return (k // 2) * 2 + (k % 2 + self.c) % 2

    def sib(self):
        return self.dev(core=1 - self.c)


def remote(src, dst, send_sem, recv_sem, device):
    return pltpu.make_async_remote_copy(
        src_ref=src,
        dst_ref=dst,
        send_sem=send_sem,
        recv_sem=recv_sem,
        device_id=device,
        device_id_type=MESH_ID,
    )


def greet(devices):
    barrier = pltpu.get_barrier_semaphore()
    for d in devices:
        pl.semaphore_signal(barrier, inc=1, device_id=d, device_id_type=MESH_ID)
    pl.semaphore_wait(barrier, len(devices))


def params(collective_id=None):
    if collective_id is None:
        return pltpu.CompilerParams(vmem_limit_bytes=VMEM_LIMIT)
    return pltpu.CompilerParams(
        vmem_limit_bytes=VMEM_LIMIT, collective_id=collective_id, has_side_effects=True
    )


def tiles(v):
    return v.reshape(*v.shape[:-2], v.shape[-2] // 8, 8, v.shape[-1])


def rows_of(v):
    return v.reshape(*v.shape[:-3], v.shape[-3] * 8, v.shape[-1])


def context_peers(p):
    return [p.member((p.k + d) % 8) for d in range(1, 8)]


def swap_halves(v):
    width = v.shape[1]
    lane = lax.broadcasted_iota(jnp.int32, v.shape, 1) % HEAD_DIM
    return jnp.where(
        lane < HEAD_DIM // 2,
        pltpu.roll(v, width - HEAD_DIM // 2, 1),
        pltpu.roll(v, HEAD_DIM // 2, 1),
    )


WEIGHTS = (
    (256, "row", 0),
    (256, "row", 256),
    (256, "row", 512),
    (256, "col", 0),
    (1024, "row", 0),
    (1024, "row", 1024),
    (1024, "col", 0),
)


OWN_ROWS = [pltpu.VMEM((16, 8, MODEL), BF), DMA((1,))]


def own_rows(p, ref, scratch):
    rows, sem = scratch
    copy = pltpu.make_async_copy(ref.at[p.x], rows, sem.at[0])
    copy.start()

    def read():
        copy.wait()
        return rows[...].astype(F32).reshape(BLOCK, MODEL)

    return read


class Gather:
    def __init__(self, p, ws, srcs, dsts, stages, sems):
        self.p, self.ws, self.srcs, self.dsts, self.stages = p, ws, srcs, dsts, stages
        self.y_send, self.y_recv, self.z_send, self.z_recv, self.s_send, self.s_recv, self.loc = sems
        self.qa = 2 * (p.z % 2)

    @staticmethod
    def sems(n):
        return [DMA((n, 2, 2))] * 4 + [DMA((n,))] * 3

    @staticmethod
    def peers(p):
        return (
            [p.sib()]
            + [p.dev(dy=dy, core=core) for dy in (-1, 1) for core in (0, 1)]
            + [p.dev(dz=1), p.dev(dz=-1)]
        )

    def src(self, i, half, quarter):
        size, kind, _ = WEIGHTS[self.ws[i]]
        if kind == "row":
            rows = pl.ds(0, 64) if quarter is None else pl.ds(quarter * 16, 16)
            return self.srcs[i].at[rows, :, pl.ds(half * size, size)]
        size = size // 8
        if quarter is None:
            return self.srcs[i].at[pl.ds(half * size, size)]
        return self.srcs[i].at[pl.ds(half * size + quarter * (size // 4), size // 4)]

    def dst(self, i, block, quarter):
        size, kind, off = WEIGHTS[self.ws[i]]
        if kind == "row":
            rows = (
                pl.ds(block * 64, 64)
                if quarter is None
                else pl.ds(block * 64 + quarter * 16, 16)
            )
            return self.dsts[i].at[rows, :, pl.ds(off, size)]
        size = size // 8
        cols = pl.ds(block * 512, 512)
        if quarter is None:
            return self.dsts[i].at[:, :, cols]
        return self.dsts[i].at[pl.ds(quarter * (size // 4), size // 4), :, cols]

    def y_copy(self, i, side, core):
        p = self.p
        quarter = self.qa + side
        return remote(
            self.src(i, core, quarter),
            self.dst(i, p.s, quarter),
            self.y_send.at[i, side, core],
            self.y_recv.at[i, side, p.c],
            p.dev(dy=-1 if side == 0 else 1, core=core),
        )

    def y_arrival(self, i, side, core):
        p = self.p
        here = self.dst(i, (1 - p.yl) * 2 + core, self.qa + side)
        return remote(
            here,
            here,
            self.y_send.at[i, side, core],
            self.y_recv.at[i, side, core],
            p.dev(dy=1 if side == 0 else -1, core=core),
        )

    def z_copy(self, i, side, core, arrival=False):
        p = self.p
        quarter = 2 - self.qa + side if arrival else self.qa + side
        here = self.dst(i, (1 - p.yl) * 2 + core, quarter)
        return remote(
            here,
            here,
            self.z_send.at[i, side, core],
            self.z_recv.at[i, side, core],
            p.dev(dz=1 if (side == 0) == arrival else -1),
        )

    def sib_copy(self, i, arrival=False):
        p = self.p
        there = self.dst(i, p.yl * 2 + 1 - p.c if arrival else p.s, None)
        return remote(
            there if arrival else self.src(i, 1 - p.c, None),
            there,
            self.s_send.at[i],
            self.s_recv.at[i],
            p.sib(),
        )

    def own_copy(self, i, step):
        stage = self.stages[i]
        here = self.dst(i, self.p.s, None)
        if step == 1:
            return pltpu.make_async_copy(stage, here, self.loc.at[i])
        return pltpu.make_async_copy(
            self.src(i, self.p.c, None), here if stage is None else stage, self.loc.at[i]
        )

    def start(self):
        for i in range(len(self.ws)):
            for core in (0, 1):
                for side in (0, 1):
                    self.y_copy(i, side, core).start()
        for i in range(len(self.ws)):
            self.sib_copy(i).start()
            self.own_copy(i, 0).start()

    def pass_on(self, i):
        for side in (0, 1):
            for core in (0, 1):
                self.y_arrival(i, side, core).wait_recv()
                self.z_copy(i, side, core).start()
        if self.stages[i] is not None:
            self.own_copy(i, 0).wait()
            self.own_copy(i, 1).start()

    def arrive(self, i):
        for side in (0, 1):
            for core in (0, 1):
                self.z_copy(i, side, core, True).wait_recv()
        self.sib_copy(i, True).wait_recv()
        self.own_copy(i, 0 if self.stages[i] is None else 1).wait()

    def sent(self, i):
        self.sib_copy(i).wait_send()
        for side in (0, 1):
            for core in (0, 1):
                self.y_copy(i, side, core).wait_send()
                self.z_copy(i, side, core).wait_send()

    def steps(self):
        self.start()
        yield
        for i in range(len(self.ws)):
            self.pass_on(i)
            yield
        for i in range(len(self.ws)):
            self.arrive(i)
            self.sent(i)
            yield


def run(order, **gens):
    alive = dict(gens)

    def step(name):
        if name in alive:
            try:
                next(alive[name])
            except StopIteration:
                del alive[name]

    for name in order:
        step(name)
    while alive:
        for name in list(alive):
            step(name)


def start_kernel(
    x_ref,
    cot_ref,
    wq,
    wk,
    wv,
    wo,
    attn_gain,
    ffn_gain,
    starts,
    ids,
    valid,
    rope_ref,
    wqkv_o,
    wo_o,
    gains_o,
    info_o,
    pcol_o,
    keep_o,
    cot_o,
    attn_in_t_o,
    qkv_o,
    attn_in,
    rope_own,
    gain_ref,
    meta,
    x_all,
    qkv_send,
    stage_o,
    stage_cot,
    loc,
    misc_send,
    misc_recv,
    gain_send,
    gain_recv,
    a2a_send,
    a2a_recv,
    *sems,
):
    p = Place()
    g = Gather(
        p,
        (0, 1, 2, 3),
        (wq, wk, wv, wo),
        (wqkv_o, wqkv_o, wqkv_o, wo_o),
        (None, None, None, stage_o),
        sems,
    )
    greet(
        [p.sib()]
        + [p.dev(dy=dy, core=core) for dy in (-1, 1) for core in (0, 1)]
        + context_peers(p)
    )
    gain_ref[...] = jnp.zeros_like(gain_ref)
    gain_ref[0:1, :] = attn_gain[...].astype(F32)
    gain_ref[1:2, :] = ffn_gain[...].astype(F32)
    gain_targets = [p.sib()] + [p.dev(dy=1, core=core) for core in (0, 1)]
    gain_copies = [
        remote(gain_ref, gains_o.at[p.s], gain_send.at[i], gain_recv.at[i if i == 0 else 1 + p.c], d)
        for i, d in enumerate(gain_targets)
    ]
    for c in gain_copies:
        c.start()
    x_own = pltpu.make_async_copy(x_ref, x_all.at[:, 0], loc.at[0])
    x_own.start()
    x_out = remote(x_ref, x_all.at[:, 1], misc_send.at[0], misc_recv.at[0], p.sib())
    x_out.start()
    g.start()
    rope_in = pltpu.make_async_copy(
        rope_ref.at[:, pl.ds(pl.multiple_of(p.k * BLOCK, BLOCK), BLOCK)], rope_own, loc.at[4]
    )
    rope_in.start()
    gains_o[p.s] = gain_ref[...]
    position = lax.broadcasted_iota(jnp.int32, (1, 1024), 1)
    for i in range(4):
        tag = jnp.zeros((1, 1024), jnp.int32)
        for n in range(2):
            first = starts[i, n]
            inside = (position >= first) & (position < first + PIECE)
            tag += jnp.where(inside, ids[i, n] + 1, 0)
        meta[p.c, i : i + 1, :] = tag - 1
    meta[p.c, 4:8, :] = valid[...]
    meta_out = remote(meta.at[p.c], meta.at[p.c], misc_send.at[1], misc_recv.at[1], p.sib())
    meta_out.start()
    own_row = jnp.zeros((1, 1024), jnp.int32)
    for i in range(4):
        own_row = jnp.where(p.x == i, valid[i : i + 1, :], own_row)
    own_valid = own_row[:, 0:BLOCK]
    for b in range(1, 8):
        own_valid = jnp.where(p.k == b, own_row[:, b * BLOCK : (b + 1) * BLOCK], own_valid)
    keep_o[...] = jnp.broadcast_to(own_valid.astype(F32), (BLOCK, BLOCK)).T
    cot_in = pltpu.make_async_copy(cot_ref, stage_cot, loc.at[3])
    cot_in.start()
    cot_own = pltpu.make_async_copy(stage_cot, cot_o.at[:, 0], loc.at[3])
    cot_out = remote(cot_ref, cot_o.at[:, 1], misc_send.at[2], misc_recv.at[2], p.sib())
    cot_out.start()

    for i in range(3):
        block = p.yl * 2 + 1 - p.c if i == 0 else (1 - p.yl) * 2 + (i - 1)
        here = gains_o.at[block]
        remote(here, here, gain_send.at[i], gain_recv.at[i], p.sib()).wait_recv()
    x_own.wait()
    x_out.wait_recv()
    gain = jnp.concatenate([gains_o[b, 0:1, :] for b in range(4)], axis=1)

    def norm_step(i, carry):
        v = x_all[i // 2, i % 2].astype(F32).reshape(BLOCK, MODEL)
        r = lax.rsqrt(jnp.mean(v * v, axis=1, keepdims=True) + NORM_EPS)
        v = (v * r * gain).astype(BF)
        attn_in[i // 2, pl.ds((i % 2) * BLOCK, BLOCK), :] = v
        attn_in_t_o[:, pl.ds(pl.multiple_of(i * BLOCK, BLOCK), BLOCK)] = v.T
        return carry

    lax.fori_loop(0, 8, norm_step, 0)
    rope_in.wait()
    for i in range(4):
        g.pass_on(i)
    cot_in.wait()
    cot_own.start()
    meta_out.wait_send()
    here = meta.at[1 - p.c]
    remote(here, here, misc_send.at[1], misc_recv.at[1], p.sib()).wait_recv()
    pieces = meta[p.k % 2, pl.ds(p.k // 2, 1), :]
    info_o[...] = jnp.zeros_like(info_o)
    info_o[0:1, :] = pieces
    info_o[1:2, :] = meta[p.k % 2, pl.ds(4 + p.k // 2, 1), :]
    for b in range(8):
        rows = slice(b * BLOCK, (b + 1) * BLOCK)
        pcol_o[rows, :] = jnp.broadcast_to(pieces[:, rows], (BLOCK, BLOCK)).T

    def send_block(j, q):
        other = p.c if q == 0 else 1 - p.c
        k = j * 2 + other
        slot = j * 2 + q
        return (
            k,
            remote(
                qkv_send.at[slot],
                qkv_o.at[p.k],
                a2a_send.at[slot],
                a2a_recv.at[p.k],
                p.member(k),
            ),
            pltpu.make_async_copy(qkv_send.at[slot], qkv_o.at[p.k], a2a_send.at[slot]),
        )

    for i in range(3):
        g.arrive(i)

    def wide(v):
        v = jnp.concatenate([v, v], axis=1)
        return jnp.concatenate([v, v], axis=0)

    def qkv_step(n, carry):
        j = (p.k // 2 + 1 + n) % 4
        a = attn_in[j]
        for part in range(3):
            cols = pl.ds(part * 256, 256)
            w = wqkv_o[:, :, cols].reshape(MODEL, 256)
            v = jnp.dot(a, w, preferred_element_type=F32)
            if part < 2:
                v = v * wide(rope_own[0]) + swap_halves(v) * wide(rope_own[1])
            v = v.reshape(32, 8, 256).astype(BF)
            qkv_send[j * 2, :, :, cols] = v[:16]
            qkv_send[j * 2 + 1, :, :, cols] = v[16:]
        for q in (0, 1):
            k, out, here = send_block(j, q)

            @pl.when(k != p.k)
            def _():
                out.start()

            @pl.when(k == p.k)
            def _():
                here.start()

        return carry

    lax.fori_loop(0, 4, qkv_step, 0)
    g.arrive(3)
    for i in range(4):
        g.sent(i)
    x_out.wait_send()
    cot_own.wait()
    cot_out.wait()
    for c in gain_copies:
        c.wait_send()
    for j in range(4):
        for q in (0, 1):
            k, out, here = send_block(j, q)

            @pl.when(k != p.k)
            def _():
                out.wait_send()

            @pl.when(k == p.k)
            def _():
                here.wait()

    for i in range(8):

        @pl.when(i != p.k)
        def _():
            here = qkv_o.at[i]
            remote(here, here, a2a_send.at[i], a2a_recv.at[i], p.member(i)).wait_recv()


def start_call(x, cot, weights, attn_gain, ffn_gain, starts, ids, valid, rope):
    shapes = (
        jax.ShapeDtypeStruct((256, 8, 768), BF),
        jax.ShapeDtypeStruct((32, 8, 2048), BF),
        jax.ShapeDtypeStruct((4, 8, 512), F32),
        jax.ShapeDtypeStruct((8, 1024), jnp.int32),
        jax.ShapeDtypeStruct((1024, 128), jnp.int32),
        jax.ShapeDtypeStruct((BLOCK, BLOCK), F32),
        jax.ShapeDtypeStruct((4, 2, 16, 8, MODEL), BF),
        jax.ShapeDtypeStruct((MODEL, 1024), BF),
        jax.ShapeDtypeStruct((8, 16, 8, 768), BF),
    )
    return pl.pallas_call(
        start_kernel,
        out_shape=shapes,
        in_specs=[ANY] * 6 + [VM] * 2 + [pl.BlockSpec(memory_space=pltpu.SMEM)] * 2 + [VM, ANY],
        out_specs=[VM, ANY, VM, VM, VM, VM, ANY, VM, ANY],
        scratch_shapes=[
            pltpu.VMEM((4, 256, MODEL), BF),
            pltpu.VMEM((2, BLOCK, 128), F32),
            pltpu.VMEM((8, 512), F32),
            pltpu.VMEM((2, 8, 1024), jnp.int32),
            pltpu.VMEM((4, 2, 16, 8, MODEL), BF),
            pltpu.VMEM((8, 16, 8, 768), BF),
            pltpu.VMEM((32, 8, 512), BF),
            pltpu.VMEM((4, 16, 8, MODEL), BF),
            DMA((5,)),
            DMA((3,)),
            DMA((3,)),
            DMA((3,)),
            DMA((3,)),
            DMA((8,)),
            DMA((8,)),
        ]
        + Gather.sems(4),
        compiler_params=params(1),
    )(
        tiles(x),
        tiles(cot),
        *[tiles(w) for w in weights],
        attn_gain[None],
        ffn_gain[None],
        starts,
        ids,
        valid,
        rope,
    )


def bias_rows(qb, rows, prow, vrow, pcol):
    i = qb * rows + lax.broadcasted_iota(jnp.int32, (rows, 1024), 0)
    j = lax.broadcasted_iota(jnp.int32, (rows, 1024), 1)
    same = (pcol >= 0) & (pcol == prow)
    ok = ((j <= i) | same) & ((vrow > 0) | (i == j))
    return jnp.where(ok, 0.0, MASK_FILL)


def attend_kernel(
    qkv, info, pcol, out_o, lse_o, o_send, a2a_send, a2a_recv
):
    p = Place()
    greet(context_peers(p))
    mine = p.slot(p.k)
    rows = 256

    def sends(i):
        return (
            remote(o_send.at[i], out_o.at[mine], a2a_send.at[i], a2a_recv.at[p.k], p.member(i)),
            pltpu.make_async_copy(o_send.at[i], out_o.at[mine], a2a_send.at[i]),
        )

    def step(n, carry):
        qb = (p.k // 2 + 1 + n) % 4
        at = pl.ds(pl.multiple_of(qb * rows, rows), rows)
        bias = bias_rows(qb, rows, info[0:1, :], info[1:2, :], pcol[at, 0:1])
        lane = lax.broadcasted_iota(jnp.int32, (rows, 128), 1)
        totals = jnp.zeros((rows, 128), F32)
        outs = []
        for h in range(4):
            q = qkv[at, pl.ds(h * 64, 64)]
            k = qkv[:, pl.ds(256 + h * 64, 64)]
            v = qkv[:, pl.ds(512 + h * 64, 64)]
            sc = lax.dot_general(q, k, (((1,), (1,)), ((), ())), preferred_element_type=F32)
            sc = sc * (HEAD_DIM**-0.5) + bias
            top = jnp.max(sc, axis=1, keepdims=True)
            e = jnp.exp(sc - top)
            total = jnp.sum(e, axis=1, keepdims=True)
            prob = (e * (1.0 / total)).astype(BF)
            totals = jnp.where(lane == h, top + jnp.log(total), totals)
            outs.append(jnp.dot(prob, v, preferred_element_type=F32))
        lse_o[at, :] = totals
        o = jnp.concatenate(outs, axis=1).reshape(32, 8, 256).astype(BF)
        for half in (0, 1):
            i = qb * 2 + half
            o_send[i] = o[half * 16 : (half + 1) * 16]
            out, here = sends(i)

            @pl.when(i != p.k)
            def _():
                out.start()

            @pl.when(i == p.k)
            def _():
                here.start()

        return carry

    lax.fori_loop(0, 4, step, 0)
    for i in range(8):
        out, here = sends(i)

        @pl.when(i != p.k)
        def _():
            out.wait_send()
            spot = out_o.at[p.slot(i)]
            remote(spot, spot, a2a_send.at[i], a2a_recv.at[i], p.member(i)).wait_recv()

        @pl.when(i == p.k)
        def _():
            here.wait()


def attend_call(qkv, info, pcol):
    return pl.pallas_call(
        attend_kernel,
        out_shape=(
            jax.ShapeDtypeStruct((8, 16, 8, 256), BF),
            jax.ShapeDtypeStruct((1024, 128), F32),
        ),
        in_specs=[VM] * 3,
        out_specs=[ANY, VM],
        scratch_shapes=[pltpu.VMEM((8, 16, 8, 256), BF), DMA((8,)), DMA((8,))],
        compiler_params=params(2),
    )(qkv, info, pcol)


X_SCRATCH = [
    pltpu.VMEM((4, BLOCK, MODEL), F32),
    pltpu.VMEM((4, BLOCK, MODEL), BF),
    pltpu.VMEM((4, BLOCK, MODEL), BF),
    pltpu.VMEM((3, BLOCK, MODEL), BF),
    pltpu.VMEM((3, BLOCK, MODEL), BF),
    DMA((4,)),
    DMA((4,)),
    DMA((6,)),
    DMA((6,)),
    DMA((10,)),
    DMA((10,)),
]


def x_peers(p):
    return [p.sib(), p.dev(dx=1), p.dev(dx=-1)]


def multiplier(lhs, rhs, transposed):
    def multiply(n, j, first):
        cols = pl.ds(pl.multiple_of(first, TILE), TILE)
        if transposed:
            return lax.dot_general(
                lhs[j], rhs[cols, :], (((1,), (1,)), ((), ())), preferred_element_type=F32
            )
        return jnp.dot(lhs[j], rhs[:, cols], preferred_element_type=F32)

    return multiply


def x_phase(p, multiply, scratch, out, both, finish, prepare=None, arrived=None):
    acc, sib_out, sib_in, x_out, x_in, s_send, s_recv, x_send, x_recv, g_send, g_recv = scratch
    half = BLOCK // 2
    top, low = pl.ds(0, half), pl.ds(half, half)
    to_right, to_left = p.dev(dx=1), p.dev(dx=-1)

    def sib_copy(r):
        return remote(sib_out.at[r], sib_in.at[r], s_send.at[r], s_recv.at[r], p.sib())

    def product(r):
        j = (p.x + r) % 4
        n = (2, 1, 3, 0).index(r)
        if prepare is not None:
            prepare(n, j)

        def step(i, carry):
            cols = pl.ds(pl.multiple_of(i * TILE, TILE), TILE)
            v = multiply(n, j, i * TILE)
            acc[r, :, cols] = v[:BLOCK]
            sib_out[r, :, cols] = v[BLOCK:].astype(BF)
            return carry

        lax.fori_loop(0, MODEL // TILE, step, 0)
        sib_copy(r).start()

    def along(n, slot, rows, device):
        return remote(
            x_out.at[slot, rows], x_in.at[slot, rows], x_send.at[n], x_recv.at[n], device
        )

    far_right, far_left = along(0, 0, top, to_right), along(1, 0, low, to_left)
    right_low, right_top = along(2, 1, low, to_right), along(3, 1, top, to_right)
    left_top, left_low = along(4, 2, top, to_left), along(5, 2, low, to_left)
    product(2)
    yield
    product(1)
    sib_copy(2).wait_recv()
    x_out[0] = (acc[2] + sib_in[2].astype(F32)).astype(BF)
    far_right.start()
    far_left.start()
    yield
    product(3)
    sib_copy(1).wait_recv()
    x_out[1, half:] = (acc[1, half:] + sib_in[1, half:].astype(F32)).astype(BF)
    right_low.start()
    sib_copy(3).wait_recv()
    x_out[2, 0:half] = (acc[3, 0:half] + sib_in[3, 0:half].astype(F32)).astype(BF)
    left_top.start()
    yield
    product(0)
    yield
    far_right.wait_recv()
    x_out[1, 0:half] = (
        acc[1, 0:half] + sib_in[1, 0:half].astype(F32) + x_in[0, 0:half].astype(F32)
    ).astype(BF)
    right_top.start()
    far_left.wait_recv()
    x_out[2, half:] = (
        acc[3, half:] + sib_in[3, half:].astype(F32) + x_in[0, half:].astype(F32)
    ).astype(BF)
    left_low.start()
    yield
    sib_copy(0).wait_recv()
    acc[0] += sib_in[0].astype(F32)
    for c in (right_low, left_top, right_top, left_low):
        c.wait_recv()
    total = acc[0] + x_in[1].astype(F32) + x_in[2].astype(F32)
    for r in range(4):
        sib_copy(r).wait_send()
    for c in (far_right, far_left, right_low, right_top, left_top, left_low):
        c.wait_send()

    me, right, left, far = p.x, (p.x + 1) % 4, (p.x + 3) % 4, (p.x + 2) % 4
    out[me, 0] = finish(total)
    sent = []

    def copy(n, j, rows, d):
        src = out.at[j, 0, rows]
        return remote(src, src, g_send.at[n], g_recv.at[n], d)

    def go(c):
        c.start()
        sent.append(c)

    def to_sib(n, j):
        return remote(out.at[j, 0], out.at[j, 1], g_send.at[n], g_recv.at[n], p.sib())

    go(copy(0, me, top, to_right))
    go(copy(1, me, low, to_left))
    go(copy(2, me, low, to_right))
    go(copy(3, me, top, to_left))
    if both:
        go(to_sib(6, me))
    yield
    copy(0, left, top, to_left).wait_recv()
    go(copy(4, left, top, to_right))
    copy(1, right, low, to_right).wait_recv()
    go(copy(5, right, low, to_left))
    yield
    copy(2, left, low, to_left).wait_recv()
    copy(3, right, top, to_right).wait_recv()
    if both:
        go(to_sib(7, left))
        go(to_sib(8, right))
    yield
    copy(4, far, top, to_left).wait_recv()
    copy(5, far, low, to_right).wait_recv()
    if both:
        go(to_sib(9, far))
        yield
        for n, j in ((6, me), (7, left), (8, right), (9, far)):
            to_sib(n, j).wait_recv()
            if arrived is not None:
                arrived(j)
    for c in sent:
        c.wait_send()


def rms(v):
    return lax.rsqrt(jnp.mean(v * v, axis=1, keepdims=True) + NORM_EPS)


def full_row(gains, row):
    return jnp.concatenate([gains[b, row : row + 1, :] for b in range(4)], axis=1)


def norm_back(grad, normed, gain, inv):
    w = grad * gain
    return inv * (w - normed * jnp.mean(w * normed, axis=1, keepdims=True))


UNITS = {
    "down_a": (64, 512, "col", 0, ()),
    "down_b": (64, 512, "col", 64, ()),
    "gate_a": (64, 512, "row", 0, (1024,)),
    "gate_b": (64, 512, "row", 512, (1024,)),
    "up_a": (64, 512, "row", 0, (512,)),
    "up_b": (64, 512, "row", 512, (512,)),
    "out": (32, 512, "col", 0, ()),
    "qkv": (64, 768, "row", 0, (256, 256, 256)),
}
UNIT_SCRATCH = 8
DOWN_OUT = jax.ShapeDtypeStruct((2, 2, 2, 32, 8, 512), BF)
OUT_OUT = jax.ShapeDtypeStruct((2, 1, 2, 16, 8, 512), BF)
FFN_OUT = jax.ShapeDtypeStruct((2, 32, 8, 2048), BF)
UP_OUT = jax.ShapeDtypeStruct((2, 32, 8, 1024), BF)
QKV_OUT = jax.ShapeDtypeStruct((2, 32, 8, 512), BF)


def unit_scratch(name):
    r, c, _, _, _ = UNITS[name]
    return [
        pltpu.VMEM((2, 2, r // 2, 8, c), BF),
        pltpu.VMEM((2, 2, r // 2, 8, c), BF),
        pltpu.VMEM((2, 2, 2, r // 8, 8, c), BF),
        pltpu.VMEM((3, 2, 2, r // 8, 8, c), BF),
        pltpu.VMEM((2, 2, r // 8, 8, c), BF),
        DMA((4,)),
        DMA((18,)),
        DMA((18,)),
    ]


def unit_peers(p):
    return [p.sib(), p.dev(dy=1), p.dev(dy=-1), p.dev(dy=2), p.dev(dz=1), p.dev(dz=-1)]


def unit(p, name, src, outs, scratch):
    rows, cols, kind, first, widths = UNITS[name]
    own, yin, zout, zin, yhin, loc, send, recv = scratch
    part = rows // 8
    half = rows // 2
    z_of = {0: p.dev(dz=1), 1: p.dev(dz=-1)}
    me, zr, zl, zf = p.z, (p.z + 1) % 4, (p.z + 3) % 4, (p.z + 2) % 4

    def cp(n, src, dst, d):
        return remote(src, dst, send.at[n], recv.at[n], d)

    def fetch(yl, h, dst, make):
        if kind == "row":
            return [
                make(
                    h * 2,
                    src.at[pl.ds(yl * 2, 2), pl.ds(h * half, half), :, pl.ds(first, cols)],
                    dst.at[:, h],
                )
            ]
        return [
            make(
                h * 2 + core,
                src.at[pl.ds(first + h * half, half), :, pl.ds((yl * 2 + core) * cols, cols)],
                dst.at[core, h],
            )
            for core in (0, 1)
        ]

    along_y, local = [], []
    for h in (0, 1):
        d = p.dev(dy=1 if h == 0 else -1)
        along_y += fetch(1 - p.yl, h, yin, lambda n, a, b, d=d: cp(n, a, b, d))
        local += fetch(p.yl, h, own, lambda n, a, b: pltpu.make_async_copy(a, b, loc.at[n]))
    for c in along_y + local:
        c.start()
    yield
    for c in local:
        c.wait()
    for c in along_y:
        c.wait_recv()
    own[...] = (own[...].astype(F32) + yin[...].astype(F32)).astype(BF)

    def chunk(h, zc):
        return own.at[:, h, pl.ds(zc * part, part)]

    far = [cp(4 + h, chunk(h, zf), zin.at[0, :, h], z_of[h]) for h in (0, 1)]
    for c in far:
        c.start()
    yield
    for c in far:
        c.wait_send()
    near = []
    for side, zc in ((0, zr), (1, zl)):
        zout[side, :, 1 - side] = own[:, 1 - side, pl.ds(zc * part, part)]
        far[side].wait_recv()
        zout[side, :, side] = (
            own[:, side, pl.ds(zc * part, part)].astype(F32) + zin[0, :, side].astype(F32)
        ).astype(BF)
        c = cp(6 + side, zout.at[side], zin.at[1 + side], z_of[side])
        c.start()
        near.append(c)
    yield
    for c in near:
        c.wait_recv()
    for c in near:
        c.wait_send()
    v = own[:, :, pl.ds(me * part, part)].astype(F32)
    zout[0] = (v + zin[1].astype(F32) + zin[2].astype(F32)).astype(BF)
    yh = cp(8, zout.at[0], yhin, p.dev(dy=2))
    yh.start()
    yield
    yh.wait_recv()
    own[:, :, pl.ds(me * part, part)] = (zout[0].astype(F32) + yhin[...].astype(F32)).astype(BF)
    back = [cp(9 + side * 2 + h, chunk(h, me), chunk(h, me), z_of[side]) for side, h in ((0, 0), (1, 1), (0, 1), (1, 0))]
    for c in back:
        c.start()
    yield
    for side, zc in ((0, zl), (1, zr)):
        here = chunk(side, zc)
        cp(9 + side * 3, here, here, z_of[1 - side]).wait_recv()
        c = cp(13 + side, here, here, z_of[side])
        c.start()
        back.append(c)
    yield
    for side, zc in ((0, zl), (1, zr)):
        here = chunk(1 - side, zc)
        cp(9 + side * 2 + 1 - side, here, here, z_of[1 - side]).wait_recv()
    for h in (0, 1):
        here = chunk(h, zf)
        cp(13 + h, here, here, z_of[1 - h]).wait_recv()
    for c in back + along_y + [yh]:
        c.wait_send()
    done = []
    if kind == "col":
        spot = outs[0].at[p.c, first // rows]
        done.append(cp(15, own.at[1 - p.c], spot, p.sib()))
        done.append(pltpu.make_async_copy(own.at[p.c], spot, loc.at[0]))
    else:
        for i, width in enumerate(widths):
            take = min(cols, width)
            spot = outs[i].at[:, :, :, pl.ds(p.c * width + (first if width > cols else 0), take)]
            piece = pl.ds(i * take, take)
            done.append(cp(15 + i, own.at[1 - p.c, :, :, :, piece], spot, p.sib()))
            done.append(pltpu.make_async_copy(own.at[p.c, :, :, :, piece], spot, loc.at[i]))
    for c in done:
        c.start()
    yield
    for c in done:
        c.wait()


def out_proj_kernel(
    lhs,
    rhs,
    keep,
    gains,
    x_ref,
    wg,
    wu,
    wd,
    ffn_in_o,
    resid_o,
    stat_o,
    wgu_o,
    wd_o,
    stage_g,
    stage_u,
    stage_d,
    x_rows,
    x_sem,
    *scratch,
):
    p = Place()
    nx = len(X_SCRATCH)
    g = Gather(
        p,
        (4, 5, 6),
        (wg, wu, wd),
        (wgu_o, wgu_o, wd_o),
        (stage_g, stage_u, stage_d),
        scratch[nx:],
    )
    greet(Gather.peers(p) + [p.dev(dx=1), p.dev(dx=-1)])
    x_read = own_rows(p, x_ref, (x_rows, x_sem))

    def finish(attn_out):
        stat_o[...] = jnp.full((8, 128), jnp.sum(keep[:, 0:1] * attn_out * attn_out), F32)
        resid = x_read() + attn_out
        resid_o[...] = resid
        return (resid * rms(resid) * full_row(gains, 1)).astype(BF)

    run(
        PROJ_ORDER,
        g=g.steps(),
        x=x_phase(p, multiplier(lhs, rhs, False), scratch[:nx], ffn_in_o, True, finish),
    )


def out_proj_call(lhs, rhs, keep, gains, x, weights):
    return pl.pallas_call(
        out_proj_kernel,
        out_shape=(
            jax.ShapeDtypeStruct((4, 2, BLOCK, MODEL), BF),
            jax.ShapeDtypeStruct((BLOCK, MODEL), F32),
            jax.ShapeDtypeStruct((8, 128), F32),
            jax.ShapeDtypeStruct((256, 8, 2048), BF),
            jax.ShapeDtypeStruct((128, 8, 2048), BF),
        ),
        in_specs=[VM] * 4 + [ANY] * 4,
        out_specs=[VM] * 3 + [ANY] * 2,
        scratch_shapes=[
            pltpu.VMEM((64, 8, 1024), BF),
            pltpu.VMEM((64, 8, 1024), BF),
            pltpu.VMEM((128, 8, 512), BF),
        ]
        + OWN_ROWS
        + X_SCRATCH
        + Gather.sems(3),
        compiler_params=params(3),
    )(lhs, rhs, keep, gains, tiles(x), *[tiles(w) for w in weights])


def ffn_kernel(a_ref, c_ref, wg, wu, wd, h_o, gg_o, gu_o, dd_o, dg_o, du_o, a_t):
    rows = FFN_ROWS

    @pl.when(pl.program_id(0) == 0)
    def _():
        def turn(i, carry):
            at = pl.ds(pl.multiple_of(i * 256, 256), 256)
            a_t[:, at] = a_ref[at, :].T
            return carry

        lax.fori_loop(0, 4, turn, 0)

    def step(i, carry):
        at = pl.ds(pl.multiple_of(i * rows, rows), rows)
        a = a_ref[at, :]
        gate = jnp.dot(a, wg[...], preferred_element_type=F32)
        up = jnp.dot(a, wu[...], preferred_element_type=F32)
        grad = lax.dot_general(
            c_ref[at, :], wd[...], (((1,), (1,)), ((), ())), preferred_element_type=F32
        )
        sig = 1.0 / (1.0 + jnp.exp(-gate))
        silu = gate * sig
        h_o[at, :] = (silu * up).astype(BF)
        gg_o[at, :] = (grad * up * sig * (1.0 + gate * (1.0 - sig))).astype(BF)
        gu_o[at, :] = (grad * silu).astype(BF)
        return carry

    lax.fori_loop(0, 1024 // rows, step, 0)
    h_t = h_o[...].T

    def down(n, carry):
        cols = pl.ds(pl.multiple_of(n * 256, 256), 256)
        dd_o[:, cols] = jnp.dot(h_t, c_ref[:, cols], preferred_element_type=F32).astype(BF)
        return carry

    lax.fori_loop(0, MODEL // 256, down, 0)

    def back(n, carry):
        at = pl.ds(pl.multiple_of(n * FFN_BACK, FFN_BACK), FFN_BACK)
        t = a_t[at, :]
        dg_o[at, :] = jnp.dot(t, gg_o[...], preferred_element_type=F32).astype(BF)
        du_o[at, :] = jnp.dot(t, gu_o[...], preferred_element_type=F32).astype(BF)
        return carry

    lax.fori_loop(0, MODEL // FFN_BACK, back, 0)


def ffn_call(ffn_in, cot, wgu, wd):
    tile = FFN_TILE
    n = 1024 // tile
    whole = pl.BlockSpec((1024, MODEL), lambda i: (0, 0), pipeline_mode=pl.Buffered(1))
    cols = pl.BlockSpec((1024, tile), lambda i: (0, i))
    tall = pl.BlockSpec((MODEL, tile), lambda i: (0, i))
    wide = pl.BlockSpec((tile, MODEL), lambda i: (i, 0))
    tokens = jax.ShapeDtypeStruct((1024, 1024), BF)
    grads = jax.ShapeDtypeStruct((MODEL, 1024), BF)
    return pl.pallas_call(
        ffn_kernel,
        grid=(n,),
        out_shape=(tokens, tokens, tokens, jax.ShapeDtypeStruct((1024, MODEL), BF), grads, grads),
        in_specs=[whole, whole, tall, pl.BlockSpec((MODEL, tile), lambda i: (0, i + n)), wide],
        out_specs=[cols, cols, cols, wide, tall, tall],
        scratch_shapes=[pltpu.VMEM((MODEL, 1024), BF)],
        compiler_params=params(),
    )(ffn_in, cot, wgu, wgu, wd)


MID = ("down_a", "down_b", "gate_a", "gate_b", "up_a")


def mid_kernel(*refs):
    gate, up, hidden, wgu, wd, dd, dgate, dup, cot_ref = refs[:9]
    wo, resid_ref, gains, keep, qkv, info, pcol, lse, rope = refs[9:18]
    grad_o, resid_grad_o, gain_o, final_o, stat_o, d_o, dd_o, dgate_o, dup_o = refs[18:27]
    lhs, rhs, g_out, g_in, d_out, dk, dv = refs[27:34]
    loc, g_send, g_recv, a2a_send, a2a_recv = refs[34:39]
    cot_scratch = refs[39:41]
    at = 41
    nx = len(X_SCRATCH)
    xs = refs[at : at + nx]
    at += nx
    us = [refs[at + i * UNIT_SCRATCH : at + (i + 1) * UNIT_SCRATCH] for i in range(len(MID))]
    p = Place()
    greet(context_peers(p) + x_peers(p) + [p.dev(dy=1), p.dev(dy=-1)])
    rows = ATTEND_ROWS
    each = rows // 8
    scale = HEAD_DIM**-0.5
    mine = p.slot(p.k)
    cot_read = own_rows(p, cot_ref, cot_scratch)

    def fetch(n, sources):
        j = (p.x + (2, 1, 3, 0)[n]) % 4
        return [
            pltpu.make_async_copy(v.at[j], lhs.at[n % 2, i], loc.at[(n % 2) * 2 + i])
            for i, v in enumerate(sources)
        ]

    def preparer(sources, right):
        def prepare(n, j):
            if n == 0:
                for c in fetch(0, sources):
                    c.start()
            if n < 3:
                for c in fetch(n + 1, sources):
                    c.start()
            if n == 0:
                right.wait()
            for c in fetch(n, sources):
                c.wait()

        return prepare

    def flat(v):
        return v.reshape(v.shape[0] * 8, v.shape[2])

    wgu_in = pltpu.make_async_copy(wgu, rhs, loc.at[4])
    wgu_in.start()
    wd_in = pltpu.make_async_copy(wd, rhs.at[pl.ds(0, 128)], loc.at[4])

    def multiply_back(n, j, first):
        v = 0.0
        for i in (0, 1):
            w = rhs[pl.ds(first // 8, TILE // 8), :, pl.ds(i * 1024, 1024)]
            v += lax.dot_general(
                flat(lhs[n % 2, i]), flat(w), (((1,), (1,)), ((), ())), preferred_element_type=F32
            )
        return v

    def multiply_out(n, j, first):
        w = rhs[pl.ds(0, 128), :, pl.ds(pl.multiple_of(first, TILE), TILE)]
        return jnp.dot(flat(lhs[n % 2, 0]), flat(w), preferred_element_type=F32)

    def finish_back(g):
        wd_in.start()
        resid = resid_ref[...]
        inv = rms(resid)
        normed = resid * inv
        gain_o[...] = jnp.broadcast_to(jnp.sum(g * normed, axis=0, keepdims=True), (8, MODEL))
        grad_resid = cot_read() + norm_back(g, normed, full_row(gains, 1), inv)
        resid_grad_o[...] = grad_resid
        return grad_resid.astype(BF)

    def finish_out(ffn_out):
        final = resid_ref[...] + ffn_out
        kp = keep[:, 0:1]
        stat_o[0] = jnp.full((8, 128), jnp.sum(kp * ffn_out * ffn_out), F32)
        stat_o[1] = jnp.full((8, 128), jnp.sum(kp * final * final), F32)
        return final.astype(BF)

    def g_copy(j, q):
        k = j * 2 + (p.c if q == 0 else 1 - p.c)
        slot = j * 2 + q
        return (
            k,
            remote(g_out.at[slot], g_in.at[p.k], g_send.at[slot], g_recv.at[p.k], p.member(k)),
            pltpu.make_async_copy(g_out.at[slot], g_in.at[p.k], g_send.at[slot]),
        )

    def arrived(j):
        v = lax.dot_general(
            grad_o[j].reshape(256, MODEL), wo[...], (((1,), (1,)), ((), ())), preferred_element_type=F32
        )
        v = v.reshape(32, 8, 256).astype(BF)
        for q in (0, 1):
            g_out[j * 2 + q] = v[q * 16 : (q + 1) * 16]
            k, out, here = g_copy(j, q)

            @pl.when(k != p.k)
            def _():
                out.start()

            @pl.when(k == p.k)
            def _():
                here.start()

    def sends(i):
        return (
            remote(d_out.at[i], d_o.at[mine], a2a_send.at[i], a2a_recv.at[p.k], p.member(i)),
            pltpu.make_async_copy(d_out.at[i], d_o.at[mine], a2a_send.at[i]),
        )

    def wide(v):
        return jnp.concatenate([v, v], axis=1)

    def query_block(qb):
        spot = pl.ds(qb * rows, rows)
        bias = bias_rows(qb, rows, info[0:1, :], info[1:2, :], pcol[spot, 0:1])
        blocks = pl.ds(qb * (rows // BLOCK), rows // BLOCK)
        g2 = g_in[blocks].astype(F32).reshape(rows, 256).astype(BF)
        dqs = []
        for h in range(4):
            lanes = pl.ds(h * 64, 64)
            q = qkv[spot, lanes]
            k = qkv[:, pl.ds(256 + h * 64, 64)]
            v = qkv[:, pl.ds(512 + h * 64, 64)]
            g = g2[:, h * 64 : (h + 1) * 64]
            sc = lax.dot_general(q, k, (((1,), (1,)), ((), ())), preferred_element_type=F32)
            prob = jnp.exp(sc * scale + bias - lse[spot, h : h + 1])
            gp = lax.dot_general(g, v, (((1,), (1,)), ((), ())), preferred_element_type=F32)
            inner = jnp.sum(prob * gp, axis=1, keepdims=True)
            gs = (prob * (gp - inner)).astype(BF)
            dqs.append(jnp.dot(gs, k, preferred_element_type=F32))
            dk[:, lanes] += lax.dot_general(
                gs, q, (((0,), (0,)), ((), ())), preferred_element_type=F32
            )
            dv[:, lanes] += lax.dot_general(
                prob.astype(BF), g, (((0,), (0,)), ((), ())), preferred_element_type=F32
            )
        dq = jnp.concatenate(dqs, axis=1) * scale
        dq = dq * wide(rope[0, spot]) - swap_halves(dq) * wide(rope[1, spot])
        dq = dq.reshape(each, 8, 256).astype(BF)
        for b in range(rows // BLOCK):
            d_out[qb * (rows // BLOCK) + b, :, :, 0:256] = dq[b * 16 : (b + 1) * 16]

    def give(n, carry):
        i = (p.k + 1 + n) % 8
        spot = pl.ds(pl.multiple_of(i * BLOCK, BLOCK), BLOCK)
        w = dk[spot, :] * scale
        w = w * wide(rope[0, spot]) - swap_halves(w) * wide(rope[1, spot])
        d_out[i, :, :, 256:512] = w.reshape(16, 8, 256).astype(BF)
        d_out[i, :, :, 512:768] = dv[spot, :].reshape(16, 8, 256).astype(BF)
        out, here = sends(i)

        @pl.when(i != p.k)
        def _():
            out.start()

        @pl.when(i == p.k)
        def _():
            here.start()

        return carry

    def main():
        yield from x_phase(
            p,
            multiply_back,
            xs,
            grad_o,
            True,
            finish_back,
            preparer((gate, up), wgu_in),
            arrived,
        )
        dk[...] = jnp.zeros_like(dk)
        dv[...] = jnp.zeros_like(dv)
        yield
        for j in range(4):
            for q in (0, 1):
                k, out, here = g_copy(j, q)

                @pl.when(k != p.k)
                def _():
                    out.wait_send()

                @pl.when(k == p.k)
                def _():
                    here.wait()

        for i in range(8):

            @pl.when(i != p.k)
            def _():
                spot = g_in.at[i]
                remote(spot, spot, g_send.at[i], g_recv.at[i], p.member(i)).wait_recv()

        for qb in range(1024 // rows):
            query_block(qb)
            yield
        lax.fori_loop(0, 8, give, 0)
        yield
        for i in range(8):
            out, here = sends(i)

            @pl.when(i != p.k)
            def _():
                out.wait_send()
                spot = d_o.at[p.slot(i)]
                remote(spot, spot, a2a_send.at[i], a2a_recv.at[i], p.member(i)).wait_recv()

            @pl.when(i == p.k)
            def _():
                here.wait()

    x = x_phase(
        p, multiply_out, xs, final_o, False, finish_out, preparer((hidden,), wd_in)
    )
    sources = (dd, dd, dgate, dgate, dup)
    results = (dd_o, dd_o, dgate_o, dgate_o, dup_o)
    a, b, c, d, e = [
        unit(p, name, src, (o,), scr) for name, src, o, scr in zip(MID, sources, results, us)
    ]
    run(MID_ORDER, m=main(), x=x, a=a, b=b, c=c, d=d, e=e)


def mid_call(gate, up, hidden, wgu, wd, dd, dgate, dup, cot, wo, *rest):
    scratch = list(X_SCRATCH)
    for name in MID:
        scratch += unit_scratch(name)
    blocks = [tiles(v.reshape(4, 256, 1024)) for v in (gate, up, hidden)]
    return pl.pallas_call(
        mid_kernel,
        out_shape=(
            jax.ShapeDtypeStruct((4, 2, BLOCK, MODEL), BF),
            jax.ShapeDtypeStruct((BLOCK, MODEL), F32),
            jax.ShapeDtypeStruct((8, MODEL), F32),
            jax.ShapeDtypeStruct((4, 1, BLOCK, MODEL), BF),
            jax.ShapeDtypeStruct((2, 8, 128), F32),
            jax.ShapeDtypeStruct((8, 16, 8, 768), BF),
            DOWN_OUT,
            FFN_OUT,
            UP_OUT,
        ),
        in_specs=[ANY] * 9 + [VM] * 9,
        out_specs=[VM] * 5 + [ANY] * 4,
        scratch_shapes=[
            pltpu.VMEM((2, 2, 32, 8, 1024), BF),
            pltpu.VMEM((256, 8, 2048), BF),
            pltpu.VMEM((8, 16, 8, 256), BF),
            pltpu.VMEM((8, 16, 8, 256), BF),
            pltpu.VMEM((8, 16, 8, 768), BF),
            pltpu.VMEM((1024, 256), F32),
            pltpu.VMEM((1024, 256), F32),
            DMA((5,)),
            DMA((8,)),
            DMA((8,)),
            DMA((8,)),
            DMA((8,)),
        ]
        + OWN_ROWS
        + scratch,
        compiler_params=params(5),
    )(
        *blocks,
        wgu,
        wd,
        tiles(dd),
        tiles(dgate).reshape(4, 64, 8, 1024),
        tiles(dup).reshape(4, 64, 8, 1024),
        tiles(cot),
        wo,
        *rest,
    )


LAST = ("up_b", "out", "qkv")


def last_kernel(
    lhs,
    rhs,
    grad_resid,
    gains,
    ffn_gain,
    stat_attn,
    stat_ffn,
    keep,
    attn_in_t,
    attended,
    grad_attn,
    dup,
    x_ref,
    *refs,
):
    out_o, small_o, up_o, do_o = refs[:4]
    qkv_o = refs[4:7]
    at = 7
    nx = len(X_SCRATCH)
    xs = refs[at : at + nx]
    at += nx
    us = []
    for _ in LAST:
        us.append(refs[at : at + UNIT_SCRATCH])
        at += UNIT_SCRATCH
    core_in, ring_in, s_send, s_recv, do, dw = refs[at : at + 6]
    x_scratch = refs[at + 6 :]
    p = Place()
    greet(unit_peers(p) + [p.dev(dx=1), p.dev(dx=-1), p.dev(dx=2), p.dev(dz=2)])
    x_read = own_rows(p, x_ref, x_scratch)

    def finish(g):
        v = x_read()
        inv = rms(v)
        normed = v * inv
        few = slice(0, 128)
        small_o[...] = jnp.zeros_like(small_o)
        small_o[0:1, :] = jnp.sum(g * normed, axis=0, keepdims=True)
        small_o[1:2, :] = ffn_gain[0:1, :]
        small_o[2:3, few] = jnp.sum(keep[...], axis=0, keepdims=True)
        small_o[3:4, few] = stat_attn[0:1, :]
        small_o[4:5, few] = stat_ffn[0, 0:1, :]
        small_o[5:6, few] = stat_ffn[1, 0:1, :]
        grad_in = grad_resid[...] + norm_back(g, normed, full_row(gains, 0), inv)
        return grad_in.astype(BF)

    def small():
        core_in[p.c] = small_o[...]
        c = remote(core_in.at[p.c], core_in.at[p.c], s_send.at[0], s_recv.at[0], p.sib())
        c.start()
        yield
        here = core_in.at[1 - p.c]
        remote(here, here, s_send.at[0], s_recv.at[0], p.sib()).wait_recv()
        c.wait_send()
        total = core_in[0] + core_in[1]
        for axis, me, move in (
            (0, p.x, lambda d: p.dev(dx=d)),
            (1, p.y, lambda d: p.dev(dy=d)),
            (2, p.z, lambda d: p.dev(dz=d)),
        ):
            ring_in[axis, me] = total
            here = ring_in.at[axis, me]
            out = [
                remote(
                    here, here, s_send.at[axis * 3 + d], s_recv.at[axis * 3 + d], move(d)
                )
                for d in (1, 2, 3)
            ]
            for c in out:
                c.start()
            yield
            for d in (1, 2, 3):
                there = ring_in.at[axis, (me + 4 - d) % 4]
                remote(
                    there, there, s_send.at[axis * 3 + d], s_recv.at[axis * 3 + d], move(4 - d)
                ).wait_recv()
            for c in out:
                c.wait_send()
            total = (ring_in[axis, 0] + ring_in[axis, 1]) + (ring_in[axis, 2] + ring_in[axis, 3])
        small_o[...] = total

    def out_unit():
        left = attended[...].reshape(1024, 256).T

        def step(n, carry):
            cols = pl.ds(pl.multiple_of(n * 512, 512), 512)
            v = jnp.dot(left, grad_attn[:, cols], preferred_element_type=F32)
            do[:, :, cols] = v.reshape(32, 8, 512).astype(BF)
            return carry

        lax.fori_loop(0, 4, step, 0)
        yield from unit(p, LAST[1], do, (do_o,), us[1])

    def qkv_unit():
        def step(n, carry):
            v = jnp.dot(
                attn_in_t[pl.ds(pl.multiple_of(n * 512, 512), 512), :],
                lhs[...].reshape(1024, 768),
                preferred_element_type=F32,
            )
            dw[n] = v.reshape(64, 8, 768).astype(BF)
            return carry

        lax.fori_loop(0, 4, step, 0)
        yield from unit(p, LAST[2], dw, qkv_o, us[2])

    run(
        LAST_ORDER,
        x=x_phase(p, multiplier(lhs, rhs, True), xs, out_o, False, finish),
        b=unit(p, LAST[0], dup, (up_o,), us[0]),
        c=out_unit(),
        d=qkv_unit(),
        s=small(),
    )


def last_call(lhs, rhs, grad_resid, gains, small_parts, attn_in_t, attended, grad_attn, dup, x):
    scratch = list(X_SCRATCH)
    for name in LAST:
        scratch += unit_scratch(name)
    outs = [UP_OUT, OUT_OUT, QKV_OUT, QKV_OUT, QKV_OUT]
    return pl.pallas_call(
        last_kernel,
        out_shape=(
            jax.ShapeDtypeStruct((4, 1, BLOCK, MODEL), BF),
            jax.ShapeDtypeStruct((8, MODEL), F32),
            *outs,
        ),
        in_specs=[VM] * 11 + [ANY] * 2,
        out_specs=[VM] * 2 + [ANY] * len(outs),
        scratch_shapes=scratch
        + [
            pltpu.VMEM((2, 8, MODEL), F32),
            pltpu.VMEM((3, 4, 8, MODEL), F32),
            DMA((10,)),
            DMA((10,)),
            pltpu.VMEM((32, 8, MODEL), BF),
            pltpu.VMEM((4, 64, 8, 768), BF),
        ]
        + OWN_ROWS,
        compiler_params=params(6),
    )(
        lhs,
        rhs,
        grad_resid,
        gains,
        *small_parts,
        attn_in_t,
        attended,
        grad_attn,
        tiles(dup).reshape(4, 64, 8, 1024),
        tiles(x),
    )


def results_kernel(small, output, grad, q, k, v, o, gate, up_a, up_b, down, *outs):
    own = pl.ds(
        pl.multiple_of((lax.axis_index("shard") * 4 + lax.axis_index("tensor")) * BLOCK, BLOCK), BLOCK
    )
    outs[9][...] = small[0:1, own]
    outs[10][...] = small[1:2, own]
    tokens = jnp.maximum(small[2:3, 0:BLOCK], 1.0) * MODEL
    means = [jnp.sqrt(small[i : i + 1, 0:BLOCK] / tokens) for i in (3, 4, 5)]
    lane = lax.broadcasted_iota(jnp.int32, (1, BLOCK), 1)
    outs[11][...] = jnp.where(lane == 0, means[0], jnp.where(lane == 1, means[1], means[2]))
    for src, dst in zip((output, grad, q, k, v, o, gate), outs[:7]):
        dst[...] = src[...].astype(dst.dtype)
    for h in (0, 1):
        here = slice(h * 512, (h + 1) * 512)
        outs[7][:, h * 1024 : h * 1024 + 512] = up_a[:, here].astype(F32)
        outs[7][:, h * 1024 + 512 : (h + 1) * 1024] = up_b[:, here].astype(F32)
    outs[8][...] = down[...].astype(F32)


def results_call(small, *arrays):
    arrays = [a.reshape(-1, a.shape[-1]) for a in arrays]
    steps = 4

    def block(shape):
        return pl.BlockSpec((shape[0] // steps, shape[1]), lambda i: (i, 0))

    types = [BF, BF] + [F32] * 7
    shapes = [(512, 2048)] * 2 + [(512, 512)] * 4 + [(512, 2048)] * 2 + [(2048, 512)]
    return pl.pallas_call(
        results_kernel,
        grid=(steps,),
        out_shape=[jax.ShapeDtypeStruct(sh, t) for sh, t in zip(shapes, types)]
        + [jax.ShapeDtypeStruct((1, BLOCK), F32)] * 3,
        in_specs=[pl.BlockSpec((8, MODEL), lambda i: (0, 0))] + [block(a.shape) for a in arrays],
        out_specs=[block(sh) for sh in shapes] + [pl.BlockSpec((1, BLOCK), lambda i: (0, 0))] * 3,
        compiler_params=params(),
    )(small, *arrays)


def rope_table():
    half_dim = HEAD_DIM // 2
    inv_freq = ROPE_BASE ** (-np.arange(half_dim) * 2.0 / HEAD_DIM)
    angles = np.arange(1024)[:, None] * inv_freq[None, :]
    cosine, sine = np.cos(angles), np.sin(angles)
    cosine = np.concatenate([cosine, cosine], axis=1)
    sine = np.concatenate([-sine, sine], axis=1)
    return np.stack([np.tile(cosine, (1, 2)), np.tile(sine, (1, 2))]).astype(np.float32)


def per_device(
    inputs,
    cotangent,
    q_weight,
    k_weight,
    v_weight,
    o_weight,
    gate_weight,
    up_weight,
    down_weight,
    attn_gain,
    ffn_gain,
    piece_starts,
    piece_ids,
    valid_mask,
):
    rope = jnp.asarray(rope_table())
    wqkv, wo, gains, info, pcol, keep, cot_all, attn_in_t, qkv = start_call(
        inputs,
        cotangent,
        (q_weight, k_weight, v_weight, o_weight),
        attn_gain,
        ffn_gain,
        piece_starts,
        piece_ids,
        valid_mask,
        rope,
    )
    wqkv, wo = rows_of(wqkv), rows_of(wo)
    cot_all = rows_of(cot_all)
    qkv = qkv.reshape(1024, 768)
    attended, lse = attend_call(qkv, info, pcol)
    attended = attended.reshape(4, 256, 256)
    ffn_in, resid, stat_attn, wgu, wd = out_proj_call(
        attended, wo, keep, gains, inputs, (gate_weight, up_weight, down_weight)
    )
    ffn_in = ffn_in.reshape(1024, MODEL)
    cot_rows = cot_all.reshape(1024, MODEL)
    hidden, grad_gate, grad_up, dd, dgate, dup = ffn_call(
        ffn_in, cot_rows, rows_of(wgu), rows_of(wd)
    )

    grad_attn, grad_resid, ffn_gain_part, output, stat_ffn, d_seq, sd, sgate, sup_a = mid_call(
        grad_gate,
        grad_up,
        hidden,
        wgu,
        wd,
        dd,
        dgate,
        dup,
        cotangent,
        wo,
        resid,
        gains,
        keep,
        qkv,
        info,
        pcol,
        lse,
        rope,
    )
    dqkv = d_seq.reshape(4, 256, 768)
    input_grad, small, sup_b, so, sq, sk, sv = last_call(
        dqkv,
        wqkv,
        grad_resid,
        gains,
        (ffn_gain_part, stat_attn, stat_ffn, keep),
        attn_in_t,
        attended,
        grad_attn.reshape(1024, MODEL),
        dup,
        inputs,
    )
    output, input_grad, *grads, attn_gain_out, ffn_gain_out, means = results_call(
        small, output, input_grad, sq, sk, sv, so, sgate, sup_a, sup_b, sd
    )
    return (
        output.reshape(4, BLOCK, MODEL),
        input_grad.reshape(4, BLOCK, MODEL),
        *grads,
        attn_gain_out[0],
        ffn_gain_out[0],
        means[0, 0:3],
    )


def solution(mesh):
    return jax.shard_map(
        per_device,
        mesh=mesh,
        in_specs=(
            P("shard", "context", None),
            P("shard", "context", None),
            P("shard", "tensor"),
            P("shard", "tensor"),
            P("shard", "tensor"),
            P("tensor", "shard"),
            P("shard", "tensor"),
            P("shard", "tensor"),
            P("tensor", "shard"),
            P("shard"),
            P("shard"),
            P("shard", None),
            P("shard", None),
            P("shard", None),
        ),
        out_specs=(
            P("shard", "context", None),
            P("shard", "context", None),
            P("shard", "tensor"),
            P("shard", "tensor"),
            P("shard", "tensor"),
            P("tensor", "shard"),
            P("shard", "tensor"),
            P("shard", "tensor"),
            P("tensor", "shard"),
            P(("shard", "tensor")),
            P(("shard", "tensor")),
            P(),
        ),
        check_vma=False,
    )
```

```python
import functools

import jax
import jax.numpy as jnp
import numpy as np
from jax import lax
from jax.experimental import pallas as pl
from jax.experimental.pallas import tpu as pltpu
from jax.sharding import PartitionSpec as P

HEAD_DIM = 64
PIECE = 256
NORM_EPS = 1e-05
ROPE_BASE = 130000.0
MASK_FILL = -1e30
BF = jnp.bfloat16
F32 = jnp.float32
ANY = pl.BlockSpec(memory_space=pl.ANY)
VM = pl.BlockSpec(memory_space=pltpu.VMEM)
DMA = pltpu.SemaphoreType.DMA
PROJ_ORDER = "gxxxxxggxgxgxgxggx"
MID_ORDER = (
    "amecmmmbmaemaemdcambemcbmxcdxxdambedcmx"
    "bxambdcexmdmxbacdeaxcxbdmdmmcbxxaeem"
)
ATTEND_ROWS = 256
LAST_ORDER = "bxdxxbxcbdxbdcbxdbcdscbsbxcxdscbsxdcsxdccd"
FFN_TILE, FFN_ROWS, FFN_BACK = 512, 1024, 2048
VMEM_LIMIT = 60 * 1024 * 1024
MODEL = 2048
TILE = 256
BLOCK = 128
MESH_ID = pl.DeviceIdType.MESH


class Place:
    def __init__(self):
        self.s = lax.axis_index("shard")
        self.k = lax.axis_index("context")
        self.x = lax.axis_index("tensor")
        self.yl = self.s // 2
        self.c = self.s % 2
        self.y = (self.k // 4) * 2 + self.yl
        self.z = self.k % 4

    def dev(self, dx=0, dy=0, dz=0, core=None):
        x = (self.x + dx + 4) % 4
        y = (self.y + dy + 4) % 4
        z = (self.z + dz + 4) % 4
        c = self.c if core is None else core
        return {"shard": (y % 2) * 2 + c, "context": (y // 2) * 4 + z, "tensor": x}

    def member(self, k):
        return {"shard": self.s, "context": k, "tensor": self.x}

    def slot(self, k):
        return (k // 2) * 2 + (k % 2 + self.c) % 2

    def sib(self):
        return self.dev(core=1 - self.c)


def remote(src, dst, send_sem, recv_sem, device):
    return pltpu.make_async_remote_copy(
        src_ref=src,
        dst_ref=dst,
        send_sem=send_sem,
        recv_sem=recv_sem,
        device_id=device,
        device_id_type=MESH_ID,
    )


def greet(devices):
    barrier = pltpu.get_barrier_semaphore()
    for d in devices:
        pl.semaphore_signal(barrier, inc=1, device_id=d, device_id_type=MESH_ID)
    pl.semaphore_wait(barrier, len(devices))


def params(collective_id=None):
    if collective_id is None:
        return pltpu.CompilerParams(vmem_limit_bytes=VMEM_LIMIT)
    return pltpu.CompilerParams(
        vmem_limit_bytes=VMEM_LIMIT, collective_id=collective_id, has_side_effects=True
    )


def tiles(v):
    return v.reshape(*v.shape[:-2], v.shape[-2] // 8, 8, v.shape[-1])


def rows_of(v):
    return v.reshape(*v.shape[:-3], v.shape[-3] * 8, v.shape[-1])


def context_peers(p):
    return [p.member((p.k + d) % 8) for d in range(1, 8)]


def swap_halves(v):
    width = v.shape[1]
    lane = lax.broadcasted_iota(jnp.int32, v.shape, 1) % HEAD_DIM
    return jnp.where(
        lane < HEAD_DIM // 2,
        pltpu.roll(v, width - HEAD_DIM // 2, 1),
        pltpu.roll(v, HEAD_DIM // 2, 1),
    )


WEIGHTS = (
    (256, "row", 0),
    (256, "row", 256),
    (256, "row", 512),
    (256, "col", 0),
    (1024, "row", 0),
    (1024, "row", 1024),
    (1024, "col", 0),
)


OWN_ROWS = [pltpu.VMEM((16, 8, MODEL), BF), DMA((1,))]


def own_rows(p, ref, scratch):
    rows, sem = scratch
    copy = pltpu.make_async_copy(ref.at[p.x], rows, sem.at[0])
    copy.start()

    def read():
        copy.wait()
        return rows[...].astype(F32).reshape(BLOCK, MODEL)

    return read


class Gather:
    def __init__(self, p, ws, srcs, dsts, stages, sems):
        self.p, self.ws, self.srcs, self.dsts, self.stages = p, ws, srcs, dsts, stages
        self.y_send, self.y_recv, self.z_send, self.z_recv, self.s_send, self.s_recv, self.loc = sems
        self.qa = 2 * (p.z % 2)

    @staticmethod
    def sems(n):
        return [DMA((n, 2, 2))] * 4 + [DMA((n,))] * 3

    @staticmethod
    def peers(p):
        return (
            [p.sib()]
            + [p.dev(dy=dy, core=core) for dy in (-1, 1) for core in (0, 1)]
            + [p.dev(dz=1), p.dev(dz=-1)]
        )

    def src(self, i, half, quarter):
        size, kind, _ = WEIGHTS[self.ws[i]]
        if kind == "row":
            rows = pl.ds(0, 64) if quarter is None else pl.ds(quarter * 16, 16)
            return self.srcs[i].at[rows, :, pl.ds(half * size, size)]
        size = size // 8
        if quarter is None:
            return self.srcs[i].at[pl.ds(half * size, size)]
        return self.srcs[i].at[pl.ds(half * size + quarter * (size // 4), size // 4)]

    def dst(self, i, block, quarter):
        size, kind, off = WEIGHTS[self.ws[i]]
        if kind == "row":
            rows = (
                pl.ds(block * 64, 64)
                if quarter is None
                else pl.ds(block * 64 + quarter * 16, 16)
            )
            return self.dsts[i].at[rows, :, pl.ds(off, size)]
        size = size // 8
        cols = pl.ds(block * 512, 512)
        if quarter is None:
            return self.dsts[i].at[:, :, cols]
        return self.dsts[i].at[pl.ds(quarter * (size // 4), size // 4), :, cols]

    def y_copy(self, i, side, core):
        p = self.p
        quarter = self.qa + side
        return remote(
            self.src(i, core, quarter),
            self.dst(i, p.s, quarter),
            self.y_send.at[i, side, core],
            self.y_recv.at[i, side, p.c],
            p.dev(dy=-1 if side == 0 else 1, core=core),
        )

    def y_arrival(self, i, side, core):
        p = self.p
        here = self.dst(i, (1 - p.yl) * 2 + core, self.qa + side)
        return remote(
            here,
            here,
            self.y_send.at[i, side, core],
            self.y_recv.at[i, side, core],
            p.dev(dy=1 if side == 0 else -1, core=core),
        )

    def z_copy(self, i, side, core, arrival=False):
        p = self.p
        quarter = 2 - self.qa + side if arrival else self.qa + side
        here = self.dst(i, (1 - p.yl) * 2 + core, quarter)
        return remote(
            here,
            here,
            self.z_send.at[i, side, core],
            self.z_recv.at[i, side, core],
            p.dev(dz=1 if (side == 0) == arrival else -1),
        )

    def sib_copy(self, i, arrival=False):
        p = self.p
        there = self.dst(i, p.yl * 2 + 1 - p.c if arrival else p.s, None)
        return remote(
            there if arrival else self.src(i, 1 - p.c, None),
            there,
            self.s_send.at[i],
            self.s_recv.at[i],
            p.sib(),
        )

    def own_copy(self, i, step):
        stage = self.stages[i]
        here = self.dst(i, self.p.s, None)
        if step == 1:
            return pltpu.make_async_copy(stage, here, self.loc.at[i])
        return pltpu.make_async_copy(
            self.src(i, self.p.c, None), here if stage is None else stage, self.loc.at[i]
        )

    def start(self):
        for i in range(len(self.ws)):
            for core in (0, 1):
                for side in (0, 1):
                    self.y_copy(i, side, core).start()
        for i in range(len(self.ws)):
            self.sib_copy(i).start()
            self.own_copy(i, 0).start()

    def pass_on(self, i):
        for side in (0, 1):
            for core in (0, 1):
                self.y_arrival(i, side, core).wait_recv()
                self.z_copy(i, side, core).start()
        if self.stages[i] is not None:
            self.own_copy(i, 0).wait()
            self.own_copy(i, 1).start()

    def arrive(self, i):
        for side in (0, 1):
            for core in (0, 1):
                self.z_copy(i, side, core, True).wait_recv()
        self.sib_copy(i, True).wait_recv()
        self.own_copy(i, 0 if self.stages[i] is None else 1).wait()

    def sent(self, i):
        self.sib_copy(i).wait_send()
        for side in (0, 1):
            for core in (0, 1):
                self.y_copy(i, side, core).wait_send()
                self.z_copy(i, side, core).wait_send()

    def steps(self):
        self.start()
        yield
        for i in range(len(self.ws)):
            self.pass_on(i)
            yield
        for i in range(len(self.ws)):
            self.arrive(i)
            self.sent(i)
            yield


def run(order, **gens):
    alive = dict(gens)

    def step(name):
        if name in alive:
            try:
                next(alive[name])
            except StopIteration:
                del alive[name]

    for name in order:
        step(name)
    while alive:
        for name in list(alive):
            step(name)


def start_kernel(
    x_ref,
    cot_ref,
    wq,
    wk,
    wv,
    wo,
    attn_gain,
    ffn_gain,
    pieces_ref,
    valid,
    rope_ref,
    wqkv_o,
    wo_o,
    gains_o,
    info_o,
    pcol_o,
    keep_o,
    cot_o,
    attn_in_t_o,
    qkv_o,
    attn_in,
    rope_own,
    gain_ref,
    meta,
    x_all,
    qkv_send,
    stage_o,
    stage_cot,
    loc,
    misc_send,
    misc_recv,
    gain_send,
    gain_recv,
    a2a_send,
    a2a_recv,
    *sems,
):
    p = Place()
    g = Gather(
        p,
        (0, 1, 2, 3),
        (wq, wk, wv, wo),
        (wqkv_o, wqkv_o, wqkv_o, wo_o),
        (None, None, None, stage_o),
        sems,
    )
    greet(
        [p.sib()]
        + [p.dev(dy=dy, core=core) for dy in (-1, 1) for core in (0, 1)]
        + context_peers(p)
    )
    gain_ref[...] = jnp.zeros_like(gain_ref)
    gain_ref[0:1, :] = attn_gain[...].astype(F32)
    gain_ref[1:2, :] = ffn_gain[...].astype(F32)
    gain_targets = [p.sib()] + [p.dev(dy=1, core=core) for core in (0, 1)]
    gain_copies = [
        remote(gain_ref, gains_o.at[p.s], gain_send.at[i], gain_recv.at[i if i == 0 else 1 + p.c], d)
        for i, d in enumerate(gain_targets)
    ]
    for c in gain_copies:
        c.start()
    x_own = pltpu.make_async_copy(x_ref, x_all.at[:, 0], loc.at[0])
    x_own.start()
    x_out = remote(x_ref, x_all.at[:, 1], misc_send.at[0], misc_recv.at[0], p.sib())
    x_out.start()
    g.start()
    rope_in = pltpu.make_async_copy(
        rope_ref.at[:, pl.ds(pl.multiple_of(p.k * BLOCK, BLOCK), BLOCK)], rope_own, loc.at[4]
    )
    rope_in.start()
    gains_o[p.s] = gain_ref[...]
    position = lax.broadcasted_iota(jnp.int32, (1, 1024), 1)
    for i in range(4):
        tag = jnp.zeros((1, 1024), jnp.int32)
        for n in range(2):
            first = pieces_ref[i, n]
            inside = (position >= first) & (position < first + PIECE)
            tag += jnp.where(inside, pieces_ref[i, 2 + n] + 1, 0)
        meta[p.c, i : i + 1, :] = tag - 1
    meta[p.c, 4:8, :] = valid[...]
    meta_out = remote(meta.at[p.c], meta.at[p.c], misc_send.at[1], misc_recv.at[1], p.sib())
    meta_out.start()
    own_row = jnp.zeros((1, 1024), jnp.int32)
    for i in range(4):
        own_row = jnp.where(p.x == i, valid[i : i + 1, :], own_row)
    own_valid = own_row[:, 0:BLOCK]
    for b in range(1, 8):
        own_valid = jnp.where(p.k == b, own_row[:, b * BLOCK : (b + 1) * BLOCK], own_valid)
    keep_o[...] = jnp.broadcast_to(own_valid.astype(F32), (BLOCK, BLOCK)).T
    cot_in = pltpu.make_async_copy(cot_ref, stage_cot, loc.at[3])
    cot_in.start()
    cot_own = pltpu.make_async_copy(stage_cot, cot_o.at[:, 0], loc.at[3])
    cot_out = remote(cot_ref, cot_o.at[:, 1], misc_send.at[2], misc_recv.at[2], p.sib())
    cot_out.start()

    for i in range(3):
        block = p.yl * 2 + 1 - p.c if i == 0 else (1 - p.yl) * 2 + (i - 1)
        here = gains_o.at[block]
        remote(here, here, gain_send.at[i], gain_recv.at[i], p.sib()).wait_recv()
    x_own.wait()
    x_out.wait_recv()
    gain = jnp.concatenate([gains_o[b, 0:1, :] for b in range(4)], axis=1)

    def norm_step(i, carry):
        v = x_all[i // 2, i % 2].astype(F32).reshape(BLOCK, MODEL)
        r = lax.rsqrt(jnp.mean(v * v, axis=1, keepdims=True) + NORM_EPS)
        v = (v * r * gain).astype(BF)
        attn_in[i // 2, pl.ds((i % 2) * BLOCK, BLOCK), :] = v
        attn_in_t_o[:, pl.ds(pl.multiple_of(i * BLOCK, BLOCK), BLOCK)] = v.T
        return carry

    lax.fori_loop(0, 8, norm_step, 0)
    rope_in.wait()
    for i in range(4):
        g.pass_on(i)
    cot_in.wait()
    cot_own.start()
    meta_out.wait_send()
    here = meta.at[1 - p.c]
    remote(here, here, misc_send.at[1], misc_recv.at[1], p.sib()).wait_recv()
    pieces = meta[p.k % 2, pl.ds(p.k // 2, 1), :]
    info_o[...] = jnp.zeros_like(info_o)
    info_o[0:1, :] = pieces
    info_o[1:2, :] = meta[p.k % 2, pl.ds(4 + p.k // 2, 1), :]
    for b in range(8):
        rows = slice(b * BLOCK, (b + 1) * BLOCK)
        pcol_o[rows, :] = jnp.broadcast_to(pieces[:, rows], (BLOCK, BLOCK)).T

    def send_block(j, q):
        other = p.c if q == 0 else 1 - p.c
        k = j * 2 + other
        slot = j * 2 + q
        return (
            k,
            remote(
                qkv_send.at[slot],
                qkv_o.at[p.k],
                a2a_send.at[slot],
                a2a_recv.at[p.k],
                p.member(k),
            ),
            pltpu.make_async_copy(qkv_send.at[slot], qkv_o.at[p.k], a2a_send.at[slot]),
        )

    for i in range(3):
        g.arrive(i)

    def wide(v):
        v = jnp.concatenate([v, v], axis=1)
        return jnp.concatenate([v, v], axis=0)

    def qkv_step(n, carry):
        j = (p.k // 2 + 1 + n) % 4
        a = attn_in[j]
        for part in range(3):
            cols = pl.ds(part * 256, 256)
            w = wqkv_o[:, :, cols].reshape(MODEL, 256)
            v = jnp.dot(a, w, preferred_element_type=F32)
            if part < 2:
                v = v * wide(rope_own[0]) + swap_halves(v) * wide(rope_own[1])
            v = v.reshape(32, 8, 256).astype(BF)
            qkv_send[j * 2, :, :, cols] = v[:16]
            qkv_send[j * 2 + 1, :, :, cols] = v[16:]
        for q in (0, 1):
            k, out, here = send_block(j, q)

            @pl.when(k != p.k)
            def _():
                out.start()

            @pl.when(k == p.k)
            def _():
                here.start()

        return carry

    lax.fori_loop(0, 4, qkv_step, 0)
    g.arrive(3)
    for i in range(4):
        g.sent(i)
    x_out.wait_send()
    cot_own.wait()
    cot_out.wait()
    for c in gain_copies:
        c.wait_send()
    for j in range(4):
        for q in (0, 1):
            k, out, here = send_block(j, q)

            @pl.when(k != p.k)
            def _():
                out.wait_send()

            @pl.when(k == p.k)
            def _():
                here.wait()

    for i in range(8):

        @pl.when(i != p.k)
        def _():
            here = qkv_o.at[i]
            remote(here, here, a2a_send.at[i], a2a_recv.at[i], p.member(i)).wait_recv()


def start_call(x, cot, weights, attn_gain, ffn_gain, starts, ids, valid, rope):
    shapes = (
        jax.ShapeDtypeStruct((256, 8, 768), BF),
        jax.ShapeDtypeStruct((32, 8, 2048), BF),
        jax.ShapeDtypeStruct((4, 8, 512), F32),
        jax.ShapeDtypeStruct((8, 1024), jnp.int32),
        jax.ShapeDtypeStruct((1024, 128), jnp.int32),
        jax.ShapeDtypeStruct((BLOCK, BLOCK), F32),
        jax.ShapeDtypeStruct((4, 2, 16, 8, MODEL), BF),
        jax.ShapeDtypeStruct((MODEL, 1024), BF),
        jax.ShapeDtypeStruct((8, 16, 8, 768), BF),
    )
    return pl.pallas_call(
        start_kernel,
        out_shape=shapes,
        in_specs=[ANY] * 6 + [VM] * 2 + [pl.BlockSpec(memory_space=pltpu.SMEM), VM, ANY],
        out_specs=[VM, ANY, VM, VM, VM, VM, ANY, VM, ANY],
        scratch_shapes=[
            pltpu.VMEM((4, 256, MODEL), BF),
            pltpu.VMEM((2, BLOCK, 128), F32),
            pltpu.VMEM((8, 512), F32),
            pltpu.VMEM((2, 8, 1024), jnp.int32),
            pltpu.VMEM((4, 2, 16, 8, MODEL), BF),
            pltpu.VMEM((8, 16, 8, 768), BF),
            pltpu.VMEM((32, 8, 512), BF),
            pltpu.VMEM((4, 16, 8, MODEL), BF),
            DMA((5,)),
            DMA((3,)),
            DMA((3,)),
            DMA((3,)),
            DMA((3,)),
            DMA((8,)),
            DMA((8,)),
        ]
        + Gather.sems(4),
        compiler_params=params(1),
    )(
        tiles(x),
        tiles(cot),
        *[tiles(w) for w in weights],
        attn_gain[None],
        ffn_gain[None],
        jnp.concatenate([starts, ids], axis=1),
        valid,
        rope,
    )


def bias_rows(qb, rows, prow, vrow, pcol):
    i = qb * rows + lax.broadcasted_iota(jnp.int32, (rows, 1024), 0)
    j = lax.broadcasted_iota(jnp.int32, (rows, 1024), 1)
    same = (pcol >= 0) & (pcol == prow)
    ok = ((j <= i) | same) & ((vrow > 0) | (i == j))
    return jnp.where(ok, 0.0, MASK_FILL)


def attend_kernel(
    qkv, info, pcol, out_o, lse_o, o_send, a2a_send, a2a_recv
):
    p = Place()
    greet(context_peers(p))
    mine = p.slot(p.k)
    rows = 256

    def sends(i):
        return (
            remote(o_send.at[i], out_o.at[mine], a2a_send.at[i], a2a_recv.at[p.k], p.member(i)),
            pltpu.make_async_copy(o_send.at[i], out_o.at[mine], a2a_send.at[i]),
        )

    def step(n, carry):
        qb = (p.k // 2 + 1 + n) % 4
        at = pl.ds(pl.multiple_of(qb * rows, rows), rows)
        bias = bias_rows(qb, rows, info[0:1, :], info[1:2, :], pcol[at, 0:1])
        lane = lax.broadcasted_iota(jnp.int32, (rows, 128), 1)
        totals = jnp.zeros((rows, 128), F32)
        outs = []
        for h in range(4):
            q = qkv[at, pl.ds(h * 64, 64)]
            k = qkv[:, pl.ds(256 + h * 64, 64)]
            v = qkv[:, pl.ds(512 + h * 64, 64)]
            sc = lax.dot_general(q, k, (((1,), (1,)), ((), ())), preferred_element_type=F32)
            sc = sc * (HEAD_DIM**-0.5) + bias
            top = jnp.max(sc, axis=1, keepdims=True)
            e = jnp.exp(sc - top)
            total = jnp.sum(e, axis=1, keepdims=True)
            prob = (e * (1.0 / total)).astype(BF)
            totals = jnp.where(lane == h, top + jnp.log(total), totals)
            outs.append(jnp.dot(prob, v, preferred_element_type=F32))
        lse_o[at, :] = totals
        o = jnp.concatenate(outs, axis=1).reshape(32, 8, 256).astype(BF)
        for half in (0, 1):
            i = qb * 2 + half
            o_send[i] = o[half * 16 : (half + 1) * 16]
            out, here = sends(i)

            @pl.when(i != p.k)
            def _():
                out.start()

            @pl.when(i == p.k)
            def _():
                here.start()

        return carry

    lax.fori_loop(0, 4, step, 0)
    for i in range(8):
        out, here = sends(i)

        @pl.when(i != p.k)
        def _():
            out.wait_send()
            spot = out_o.at[p.slot(i)]
            remote(spot, spot, a2a_send.at[i], a2a_recv.at[i], p.member(i)).wait_recv()

        @pl.when(i == p.k)
        def _():
            here.wait()


def attend_call(qkv, info, pcol):
    return pl.pallas_call(
        attend_kernel,
        out_shape=(
            jax.ShapeDtypeStruct((8, 16, 8, 256), BF),
            jax.ShapeDtypeStruct((1024, 128), F32),
        ),
        in_specs=[VM] * 3,
        out_specs=[ANY, VM],
        scratch_shapes=[pltpu.VMEM((8, 16, 8, 256), BF), DMA((8,)), DMA((8,))],
        compiler_params=params(2),
    )(qkv, info, pcol)


X_SCRATCH = [
    pltpu.VMEM((4, BLOCK, MODEL), F32),
    pltpu.VMEM((4, BLOCK, MODEL), BF),
    pltpu.VMEM((4, BLOCK, MODEL), BF),
    pltpu.VMEM((3, BLOCK, MODEL), BF),
    pltpu.VMEM((3, BLOCK, MODEL), BF),
    DMA((4,)),
    DMA((4,)),
    DMA((6,)),
    DMA((6,)),
    DMA((10,)),
    DMA((10,)),
]


def x_peers(p):
    return [p.sib(), p.dev(dx=1), p.dev(dx=-1)]


def multiplier(lhs, rhs, transposed):
    def multiply(n, j, first):
        cols = pl.ds(pl.multiple_of(first, TILE), TILE)
        if transposed:
            return lax.dot_general(
                lhs[j], rhs[cols, :], (((1,), (1,)), ((), ())), preferred_element_type=F32
            )
        return jnp.dot(lhs[j], rhs[:, cols], preferred_element_type=F32)

    return multiply


def x_phase(p, multiply, scratch, out, both, finish, prepare=None, arrived=None):
    acc, sib_out, sib_in, x_out, x_in, s_send, s_recv, x_send, x_recv, g_send, g_recv = scratch
    half = BLOCK // 2
    top, low = pl.ds(0, half), pl.ds(half, half)
    to_right, to_left = p.dev(dx=1), p.dev(dx=-1)

    def sib_copy(r):
        return remote(sib_out.at[r], sib_in.at[r], s_send.at[r], s_recv.at[r], p.sib())

    def product(r):
        j = (p.x + r) % 4
        n = (2, 1, 3, 0).index(r)
        if prepare is not None:
            prepare(n, j)

        def step(i, carry):
            cols = pl.ds(pl.multiple_of(i * TILE, TILE), TILE)
            v = multiply(n, j, i * TILE)
            acc[r, :, cols] = v[:BLOCK]
            sib_out[r, :, cols] = v[BLOCK:].astype(BF)
            return carry

        lax.fori_loop(0, MODEL // TILE, step, 0)
        sib_copy(r).start()

    def along(n, slot, rows, device):
        return remote(
            x_out.at[slot, rows], x_in.at[slot, rows], x_send.at[n], x_recv.at[n], device
        )

    far_right, far_left = along(0, 0, top, to_right), along(1, 0, low, to_left)
    right_low, right_top = along(2, 1, low, to_right), along(3, 1, top, to_right)
    left_top, left_low = along(4, 2, top, to_left), along(5, 2, low, to_left)
    product(2)
    yield
    product(1)
    sib_copy(2).wait_recv()
    x_out[0] = (acc[2] + sib_in[2].astype(F32)).astype(BF)
    far_right.start()
    far_left.start()
    yield
    product(3)
    sib_copy(1).wait_recv()
    x_out[1, half:] = (acc[1, half:] + sib_in[1, half:].astype(F32)).astype(BF)
    right_low.start()
    sib_copy(3).wait_recv()
    x_out[2, 0:half] = (acc[3, 0:half] + sib_in[3, 0:half].astype(F32)).astype(BF)
    left_top.start()
    yield
    product(0)
    yield
    far_right.wait_recv()
    x_out[1, 0:half] = (
        acc[1, 0:half] + sib_in[1, 0:half].astype(F32) + x_in[0, 0:half].astype(F32)
    ).astype(BF)
    right_top.start()
    far_left.wait_recv()
    x_out[2, half:] = (
        acc[3, half:] + sib_in[3, half:].astype(F32) + x_in[0, half:].astype(F32)
    ).astype(BF)
    left_low.start()
    yield
    sib_copy(0).wait_recv()
    acc[0] += sib_in[0].astype(F32)
    for c in (right_low, left_top, right_top, left_low):
        c.wait_recv()
    total = acc[0] + x_in[1].astype(F32) + x_in[2].astype(F32)
    for r in range(4):
        sib_copy(r).wait_send()
    for c in (far_right, far_left, right_low, right_top, left_top, left_low):
        c.wait_send()

    me, right, left, far = p.x, (p.x + 1) % 4, (p.x + 3) % 4, (p.x + 2) % 4
    out[me, 0] = finish(total)
    sent = []

    def copy(n, j, rows, d):
        src = out.at[j, 0, rows]
        return remote(src, src, g_send.at[n], g_recv.at[n], d)

    def go(c):
        c.start()
        sent.append(c)

    def to_sib(n, j):
        return remote(out.at[j, 0], out.at[j, 1], g_send.at[n], g_recv.at[n], p.sib())

    go(copy(0, me, top, to_right))
    go(copy(1, me, low, to_left))
    go(copy(2, me, low, to_right))
    go(copy(3, me, top, to_left))
    if both:
        go(to_sib(6, me))
    yield
    copy(0, left, top, to_left).wait_recv()
    go(copy(4, left, top, to_right))
    copy(1, right, low, to_right).wait_recv()
    go(copy(5, right, low, to_left))
    yield
    copy(2, left, low, to_left).wait_recv()
    copy(3, right, top, to_right).wait_recv()
    if both:
        go(to_sib(7, left))
        go(to_sib(8, right))
    yield
    copy(4, far, top, to_left).wait_recv()
    copy(5, far, low, to_right).wait_recv()
    if both:
        go(to_sib(9, far))
        yield
        for n, j in ((6, me), (7, left), (8, right), (9, far)):
            to_sib(n, j).wait_recv()
            if arrived is not None:
                arrived(j)
    for c in sent:
        c.wait_send()


def rms(v):
    return lax.rsqrt(jnp.mean(v * v, axis=1, keepdims=True) + NORM_EPS)


def full_row(gains, row):
    return jnp.concatenate([gains[b, row : row + 1, :] for b in range(4)], axis=1)


def norm_back(grad, normed, gain, inv):
    w = grad * gain
    return inv * (w - normed * jnp.mean(w * normed, axis=1, keepdims=True))


UNITS = {
    "down_a": (64, 512, "col", 0, ()),
    "down_b": (64, 512, "col", 64, ()),
    "gate_a": (64, 512, "row", 0, (1024,)),
    "gate_b": (64, 512, "row", 512, (1024,)),
    "up_a": (64, 512, "row", 0, (512,)),
    "up_b": (64, 512, "row", 512, (512,)),
    "out": (32, 512, "col", 0, ()),
    "qkv": (64, 768, "row", 0, (256, 256, 256)),
}
UNIT_SCRATCH = 9
DOWN_OUT = jax.ShapeDtypeStruct((2, 2, 2, 32, 8, 512), BF)
OUT_OUT = jax.ShapeDtypeStruct((2, 1, 2, 16, 8, 512), BF)
FFN_OUT = jax.ShapeDtypeStruct((2, 32, 8, 2048), BF)
UP_OUT = jax.ShapeDtypeStruct((2, 32, 8, 1024), BF)
QKV_OUT = jax.ShapeDtypeStruct((2, 32, 8, 512), BF)


def unit_scratch(name):
    r, c, _, _, _ = UNITS[name]
    return [
        pltpu.VMEM((2, 2, r // 2, 8, c), BF),
        pltpu.VMEM((2, 2, r // 2, 8, c), BF),
        pltpu.VMEM((2, 2, 2, r // 8, 8, c), BF),
        pltpu.VMEM((3, 2, 2, r // 8, 8, c), BF),
        pltpu.VMEM((2, 2, r // 8, 8, c), BF),
        DMA((4,)),
        DMA((18,)),
        DMA((18,)),
        pltpu.SemaphoreType.REGULAR,
    ]


def unit_peers(p):
    return [p.sib(), p.dev(dy=1), p.dev(dy=-1), p.dev(dy=2), p.dev(dz=1), p.dev(dz=-1)]


def unit(p, name, src, outs, scratch, pace=False):
    rows, cols, kind, first, widths = UNITS[name]
    own, yin, zout, zin, yhin, loc, send, recv, beside = scratch
    part = rows // 8
    half = rows // 2
    z_of = {0: p.dev(dz=1), 1: p.dev(dz=-1)}
    me, zr, zl, zf = p.z, (p.z + 1) % 4, (p.z + 3) % 4, (p.z + 2) % 4

    def cp(n, src, dst, d):
        return remote(src, dst, send.at[n], recv.at[n], d)

    def fetch(yl, h, dst, make):
        if kind == "row":
            return [
                make(
                    h * 2,
                    src.at[pl.ds(yl * 2, 2), pl.ds(h * half, half), :, pl.ds(first, cols)],
                    dst.at[:, h],
                )
            ]
        return [
            make(
                h * 2 + core,
                src.at[pl.ds(first + h * half, half), :, pl.ds((yl * 2 + core) * cols, cols)],
                dst.at[core, h],
            )
            for core in (0, 1)
        ]

    along_y, local = [], []
    for h in (0, 1):
        d = p.dev(dy=1 if h == 0 else -1)
        along_y += fetch(1 - p.yl, h, yin, lambda n, a, b, d=d: cp(n, a, b, d))
        local += fetch(p.yl, h, own, lambda n, a, b: pltpu.make_async_copy(a, b, loc.at[n]))
    for c in along_y + local:
        c.start()
    yield
    for c in local:
        c.wait()
    for c in along_y:
        c.wait_recv()
    own[...] = own[...] + yin[...]

    def chunk(h, zc):
        return own.at[:, h, pl.ds(zc * part, part)]

    far = [cp(4 + h, chunk(h, zf), zin.at[0, :, h], z_of[h]) for h in (0, 1)]
    for c in far:
        c.start()
    yield
    for c in far:
        c.wait_send()
    near = []
    for side, zc in ((0, zr), (1, zl)):
        zout[side, :, 1 - side] = own[:, 1 - side, pl.ds(zc * part, part)]
        far[side].wait_recv()
        zout[side, :, side] = own[:, side, pl.ds(zc * part, part)] + zin[0, :, side]
        c = cp(6 + side, zout.at[side], zin.at[1 + side], z_of[side])
        c.start()
        near.append(c)
    yield
    for c in near:
        c.wait_recv()
    for c in near:
        c.wait_send()
    v = own[:, :, pl.ds(me * part, part)].astype(F32)
    zout[0] = (v + zin[1].astype(F32) + zin[2].astype(F32)).astype(BF)
    if pace:
        for dy in (-1, 1):
            pl.semaphore_signal(beside, inc=1, device_id=p.dev(dy=dy), device_id_type=MESH_ID)
        pl.semaphore_wait(beside, 2)
    yh = cp(8, zout.at[0], yhin, p.dev(dy=2))
    yh.start()
    yield
    yh.wait_recv()
    own[:, :, pl.ds(me * part, part)] = zout[0] + yhin[...]
    back = [cp(9 + side * 2 + h, chunk(h, me), chunk(h, me), z_of[side]) for side, h in ((0, 0), (1, 1), (0, 1), (1, 0))]
    for c in back:
        c.start()
    yield
    for side, zc in ((0, zl), (1, zr)):
        here = chunk(side, zc)
        cp(9 + side * 3, here, here, z_of[1 - side]).wait_recv()
        c = cp(13 + side, here, here, z_of[side])
        c.start()
        back.append(c)
    yield
    for side, zc in ((0, zl), (1, zr)):
        here = chunk(1 - side, zc)
        cp(9 + side * 2 + 1 - side, here, here, z_of[1 - side]).wait_recv()
    for h in (0, 1):
        here = chunk(h, zf)
        cp(13 + h, here, here, z_of[1 - h]).wait_recv()
    for c in back + along_y + [yh]:
        c.wait_send()
    done = []
    if kind == "col":
        spot = outs[0].at[p.c, first // rows]
        done.append(cp(15, own.at[1 - p.c], spot, p.sib()))
        done.append(pltpu.make_async_copy(own.at[p.c], spot, loc.at[0]))
    else:
        for i, width in enumerate(widths):
            take = min(cols, width)
            spot = outs[i].at[:, :, :, pl.ds(p.c * width + (first if width > cols else 0), take)]
            piece = pl.ds(i * take, take)
            done.append(cp(15 + i, own.at[1 - p.c, :, :, :, piece], spot, p.sib()))
            done.append(pltpu.make_async_copy(own.at[p.c, :, :, :, piece], spot, loc.at[i]))
    for c in done:
        c.start()
    yield
    for c in done:
        c.wait()


def out_proj_kernel(
    lhs,
    rhs,
    keep,
    gains,
    x_ref,
    wg,
    wu,
    wd,
    ffn_in_o,
    resid_o,
    stat_o,
    wgu_o,
    wd_o,
    stage_g,
    stage_u,
    stage_d,
    x_rows,
    x_sem,
    *scratch,
):
    p = Place()
    nx = len(X_SCRATCH)
    g = Gather(
        p,
        (4, 5, 6),
        (wg, wu, wd),
        (wgu_o, wgu_o, wd_o),
        (stage_g, stage_u, stage_d),
        scratch[nx:],
    )
    greet(Gather.peers(p) + [p.dev(dx=1), p.dev(dx=-1)])
    x_read = own_rows(p, x_ref, (x_rows, x_sem))

    def finish(attn_out):
        stat_o[...] = jnp.full((8, 128), jnp.sum(keep[:, 0:1] * attn_out * attn_out), F32)
        resid = x_read() + attn_out
        resid_o[...] = resid
        return (resid * rms(resid) * full_row(gains, 1)).astype(BF)

    run(
        PROJ_ORDER,
        g=g.steps(),
        x=x_phase(p, multiplier(lhs, rhs, False), scratch[:nx], ffn_in_o, True, finish),
    )


def out_proj_call(lhs, rhs, keep, gains, x, weights):
    return pl.pallas_call(
        out_proj_kernel,
        out_shape=(
            jax.ShapeDtypeStruct((4, 2, BLOCK, MODEL), BF),
            jax.ShapeDtypeStruct((BLOCK, MODEL), F32),
            jax.ShapeDtypeStruct((8, 128), F32),
            jax.ShapeDtypeStruct((256, 8, 2048), BF),
            jax.ShapeDtypeStruct((128, 8, 2048), BF),
        ),
        in_specs=[VM] * 4 + [ANY] * 4,
        out_specs=[VM] * 3 + [ANY] * 2,
        scratch_shapes=[
            pltpu.VMEM((64, 8, 1024), BF),
            pltpu.VMEM((64, 8, 1024), BF),
            pltpu.VMEM((128, 8, 512), BF),
        ]
        + OWN_ROWS
        + X_SCRATCH
        + Gather.sems(3),
        compiler_params=params(3),
    )(lhs, rhs, keep, gains, tiles(x), *[tiles(w) for w in weights])


def ffn_kernel(a_ref, c_ref, wg, wu, wd, h_o, gg_o, gu_o, dd_o, dg_o, du_o, a_t):
    rows = FFN_ROWS

    @pl.when(pl.program_id(0) == 0)
    def _():
        def turn(i, carry):
            at = pl.ds(pl.multiple_of(i * 256, 256), 256)
            a_t[:, at] = a_ref[at, :].T
            return carry

        lax.fori_loop(0, 4, turn, 0)

    def step(i, carry):
        at = pl.ds(pl.multiple_of(i * rows, rows), rows)
        a = a_ref[at, :]
        gate = jnp.dot(a, wg[...], preferred_element_type=F32)
        up = jnp.dot(a, wu[...], preferred_element_type=F32)
        grad = lax.dot_general(
            c_ref[at, :], wd[...], (((1,), (1,)), ((), ())), preferred_element_type=F32
        )
        sig = 1.0 / (1.0 + jnp.exp(-gate))
        silu = gate * sig
        h_o[at, :] = (silu * up).astype(BF)
        gg_o[at, :] = (grad * up * sig * (1.0 + gate * (1.0 - sig))).astype(BF)
        gu_o[at, :] = (grad * silu).astype(BF)
        return carry

    lax.fori_loop(0, 1024 // rows, step, 0)
    h_t = h_o[...].T

    def down(n, carry):
        cols = pl.ds(pl.multiple_of(n * 256, 256), 256)
        dd_o[:, cols] = jnp.dot(h_t, c_ref[:, cols], preferred_element_type=F32).astype(BF)
        return carry

    lax.fori_loop(0, MODEL // 256, down, 0)

    def back(n, carry):
        at = pl.ds(pl.multiple_of(n * FFN_BACK, FFN_BACK), FFN_BACK)
        t = a_t[at, :]
        dg_o[at, :] = jnp.dot(t, gg_o[...], preferred_element_type=F32).astype(BF)
        du_o[at, :] = jnp.dot(t, gu_o[...], preferred_element_type=F32).astype(BF)
        return carry

    lax.fori_loop(0, MODEL // FFN_BACK, back, 0)


def ffn_call(ffn_in, cot, wgu, wd):
    tile = FFN_TILE
    n = 1024 // tile
    whole = pl.BlockSpec((1024, MODEL), lambda i: (0, 0), pipeline_mode=pl.Buffered(1))
    cols = pl.BlockSpec((1024, tile), lambda i: (0, i))
    tall = pl.BlockSpec((MODEL, tile), lambda i: (0, i))
    wide = pl.BlockSpec((tile, MODEL), lambda i: (i, 0))
    tokens = jax.ShapeDtypeStruct((1024, 1024), BF)
    grads = jax.ShapeDtypeStruct((MODEL, 1024), BF)
    return pl.pallas_call(
        ffn_kernel,
        grid=(n,),
        out_shape=(tokens, tokens, tokens, jax.ShapeDtypeStruct((1024, MODEL), BF), grads, grads),
        in_specs=[whole, whole, tall, pl.BlockSpec((MODEL, tile), lambda i: (0, i + n)), wide],
        out_specs=[cols, cols, cols, wide, tall, tall],
        scratch_shapes=[pltpu.VMEM((MODEL, 1024), BF)],
        compiler_params=params(),
    )(ffn_in, cot, wgu, wgu, wd)


MID = ("down_a", "down_b", "gate_a", "gate_b", "up_a")


def mid_kernel(*refs):
    gate, up, hidden, wgu, wd, dd, dgate, dup, cot_ref = refs[:9]
    wo, resid_ref, gains, keep, qkv, info, pcol, lse, rope = refs[9:18]
    grad_o, resid_grad_o, gain_o, final_o, stat_o, d_o, dd_o, dgate_o, dup_o = refs[18:27]
    lhs, rhs, g_out, g_in, d_out, dk, dv = refs[27:34]
    loc, g_send, g_recv, a2a_send, a2a_recv = refs[34:39]
    cot_scratch = refs[39:41]
    at = 41
    nx = len(X_SCRATCH)
    xs = refs[at : at + nx]
    at += nx
    us = [refs[at + i * UNIT_SCRATCH : at + (i + 1) * UNIT_SCRATCH] for i in range(len(MID))]
    p = Place()
    greet(context_peers(p) + x_peers(p) + [p.dev(dy=1), p.dev(dy=-1)])
    rows = ATTEND_ROWS
    each = rows // 8
    scale = HEAD_DIM**-0.5
    mine = p.slot(p.k)
    cot_read = own_rows(p, cot_ref, cot_scratch)

    def fetch(n, sources):
        j = (p.x + (2, 1, 3, 0)[n]) % 4
        return [
            pltpu.make_async_copy(v.at[j], lhs.at[n % 2, i], loc.at[(n % 2) * 2 + i])
            for i, v in enumerate(sources)
        ]

    def preparer(sources, right):
        def prepare(n, j):
            if n == 0:
                for c in fetch(0, sources):
                    c.start()
            if n < 3:
                for c in fetch(n + 1, sources):
                    c.start()
            if n == 0:
                right.wait()
            for c in fetch(n, sources):
                c.wait()

        return prepare

    def flat(v):
        return v.reshape(v.shape[0] * 8, v.shape[2])

    wgu_in = pltpu.make_async_copy(wgu, rhs, loc.at[4])
    wgu_in.start()
    wd_in = pltpu.make_async_copy(wd, rhs.at[pl.ds(0, 128)], loc.at[4])

    def multiply_back(n, j, first):
        v = 0.0
        for i in (0, 1):
            w = rhs[pl.ds(first // 8, TILE // 8), :, pl.ds(i * 1024, 1024)]
            v += lax.dot_general(
                flat(lhs[n % 2, i]), flat(w), (((1,), (1,)), ((), ())), preferred_element_type=F32
            )
        return v

    def multiply_out(n, j, first):
        w = rhs[pl.ds(0, 128), :, pl.ds(pl.multiple_of(first, TILE), TILE)]
        return jnp.dot(flat(lhs[n % 2, 0]), flat(w), preferred_element_type=F32)

    def finish_back(g):
        wd_in.start()
        resid = resid_ref[...]
        inv = rms(resid)
        normed = resid * inv
        gain_o[...] = jnp.broadcast_to(jnp.sum(g * normed, axis=0, keepdims=True), (8, MODEL))
        grad_resid = cot_read() + norm_back(g, normed, full_row(gains, 1), inv)
        resid_grad_o[...] = grad_resid
        return grad_resid.astype(BF)

    def finish_out(ffn_out):
        final = resid_ref[...] + ffn_out
        kp = keep[:, 0:1]
        stat_o[0] = jnp.full((8, 128), jnp.sum(kp * ffn_out * ffn_out), F32)
        stat_o[1] = jnp.full((8, 128), jnp.sum(kp * final * final), F32)
        return final.astype(BF)

    def g_copy(j, q):
        k = j * 2 + (p.c if q == 0 else 1 - p.c)
        slot = j * 2 + q
        return (
            k,
            remote(g_out.at[slot], g_in.at[p.k], g_send.at[slot], g_recv.at[p.k], p.member(k)),
            pltpu.make_async_copy(g_out.at[slot], g_in.at[p.k], g_send.at[slot]),
        )

    def arrived(j):
        v = lax.dot_general(
            grad_o[j].reshape(256, MODEL), wo[...], (((1,), (1,)), ((), ())), preferred_element_type=F32
        )
        v = v.reshape(32, 8, 256).astype(BF)
        for q in (0, 1):
            g_out[j * 2 + q] = v[q * 16 : (q + 1) * 16]
            k, out, here = g_copy(j, q)

            @pl.when(k != p.k)
            def _():
                out.start()

            @pl.when(k == p.k)
            def _():
                here.start()

    def sends(i):
        return (
            remote(d_out.at[i], d_o.at[mine], a2a_send.at[i], a2a_recv.at[p.k], p.member(i)),
            pltpu.make_async_copy(d_out.at[i], d_o.at[mine], a2a_send.at[i]),
        )

    def wide(v):
        return jnp.concatenate([v, v], axis=1)

    def query_block(qb):
        spot = pl.ds(qb * rows, rows)
        bias = bias_rows(qb, rows, info[0:1, :], info[1:2, :], pcol[spot, 0:1])
        blocks = pl.ds(qb * (rows // BLOCK), rows // BLOCK)
        g2 = g_in[blocks].astype(F32).reshape(rows, 256).astype(BF)
        dqs = []
        for h in range(4):
            lanes = pl.ds(h * 64, 64)
            q = qkv[spot, lanes]
            k = qkv[:, pl.ds(256 + h * 64, 64)]
            v = qkv[:, pl.ds(512 + h * 64, 64)]
            g = g2[:, h * 64 : (h + 1) * 64]
            sc = lax.dot_general(q, k, (((1,), (1,)), ((), ())), preferred_element_type=F32)
            prob = jnp.exp(sc * scale + bias - lse[spot, h : h + 1])
            gp = lax.dot_general(g, v, (((1,), (1,)), ((), ())), preferred_element_type=F32)
            inner = jnp.sum(prob * gp, axis=1, keepdims=True)
            gs = (prob * (gp - inner)).astype(BF)
            dqs.append(jnp.dot(gs, k, preferred_element_type=F32))
            dk[:, lanes] += lax.dot_general(
                gs, q, (((0,), (0,)), ((), ())), preferred_element_type=F32
            )
            dv[:, lanes] += lax.dot_general(
                prob.astype(BF), g, (((0,), (0,)), ((), ())), preferred_element_type=F32
            )
        dq = jnp.concatenate(dqs, axis=1) * scale
        dq = dq * wide(rope[0, spot]) - swap_halves(dq) * wide(rope[1, spot])
        dq = dq.reshape(each, 8, 256).astype(BF)
        for b in range(rows // BLOCK):
            d_out[qb * (rows // BLOCK) + b, :, :, 0:256] = dq[b * 16 : (b + 1) * 16]

    def give(i, carry):
        spot = pl.ds(pl.multiple_of(i * BLOCK, BLOCK), BLOCK)
        w = dk[spot, :] * scale
        w = w * wide(rope[0, spot]) - swap_halves(w) * wide(rope[1, spot])
        d_out[i, :, :, 256:512] = w.reshape(16, 8, 256).astype(BF)
        d_out[i, :, :, 512:768] = dv[spot, :].reshape(16, 8, 256).astype(BF)
        out, here = sends(i)

        @pl.when(i != p.k)
        def _():
            out.start()

        @pl.when(i == p.k)
        def _():
            here.start()

        return carry

    def main():
        yield from x_phase(
            p,
            multiply_back,
            xs,
            grad_o,
            True,
            finish_back,
            preparer((gate, up), wgu_in),
            arrived,
        )
        dk[...] = jnp.zeros_like(dk)
        dv[...] = jnp.zeros_like(dv)
        yield
        for j in range(4):
            for q in (0, 1):
                k, out, here = g_copy(j, q)

                @pl.when(k != p.k)
                def _():
                    out.wait_send()

                @pl.when(k == p.k)
                def _():
                    here.wait()

        for i in range(8):

            @pl.when(i != p.k)
            def _():
                spot = g_in.at[i]
                remote(spot, spot, g_send.at[i], g_recv.at[i], p.member(i)).wait_recv()

        for qb in range(1024 // rows):
            query_block(qb)
            yield
        lax.fori_loop(0, 8, give, 0)
        yield
        for i in range(8):
            out, here = sends(i)

            @pl.when(i != p.k)
            def _():
                out.wait_send()
                spot = d_o.at[p.slot(i)]
                remote(spot, spot, a2a_send.at[i], a2a_recv.at[i], p.member(i)).wait_recv()

            @pl.when(i == p.k)
            def _():
                here.wait()

    x = x_phase(
        p, multiply_out, xs, final_o, False, finish_out, preparer((hidden,), wd_in)
    )
    sources = (dd, dd, dgate, dgate, dup)
    results = (dd_o, dd_o, dgate_o, dgate_o, dup_o)
    a, b, c, d, e = [
        unit(p, name, src, (o,), scr, True)
        for name, src, o, scr in zip(MID, sources, results, us)
    ]
    run(MID_ORDER, m=main(), x=x, a=a, b=b, c=c, d=d, e=e)


def mid_call(gate, up, hidden, wgu, wd, dd, dgate, dup, cot, wo, *rest):
    scratch = list(X_SCRATCH)
    for name in MID:
        scratch += unit_scratch(name)
    blocks = [tiles(v.reshape(4, 256, 1024)) for v in (gate, up, hidden)]
    return pl.pallas_call(
        mid_kernel,
        out_shape=(
            jax.ShapeDtypeStruct((4, 2, BLOCK, MODEL), BF),
            jax.ShapeDtypeStruct((BLOCK, MODEL), F32),
            jax.ShapeDtypeStruct((8, MODEL), F32),
            jax.ShapeDtypeStruct((4, 1, BLOCK, MODEL), BF),
            jax.ShapeDtypeStruct((2, 8, 128), F32),
            jax.ShapeDtypeStruct((8, 16, 8, 768), BF),
            DOWN_OUT,
            FFN_OUT,
            UP_OUT,
        ),
        in_specs=[ANY] * 9 + [VM] * 9,
        out_specs=[VM] * 5 + [ANY] * 4,
        scratch_shapes=[
            pltpu.VMEM((2, 2, 32, 8, 1024), BF),
            pltpu.VMEM((256, 8, 2048), BF),
            pltpu.VMEM((8, 16, 8, 256), BF),
            pltpu.VMEM((8, 16, 8, 256), BF),
            pltpu.VMEM((8, 16, 8, 768), BF),
            pltpu.VMEM((1024, 256), F32),
            pltpu.VMEM((1024, 256), F32),
            DMA((5,)),
            DMA((8,)),
            DMA((8,)),
            DMA((8,)),
            DMA((8,)),
        ]
        + OWN_ROWS
        + scratch,
        compiler_params=params(5),
    )(
        *blocks,
        wgu,
        wd,
        tiles(dd),
        tiles(dgate).reshape(4, 64, 8, 1024),
        tiles(dup).reshape(4, 64, 8, 1024),
        tiles(cot),
        wo,
        *rest,
    )


LAST = ("up_b", "out", "qkv")


def last_kernel(
    lhs,
    rhs,
    grad_resid,
    gains,
    ffn_gain,
    stat_attn,
    stat_ffn,
    keep,
    attn_in_t,
    attended,
    grad_attn,
    dup,
    x_ref,
    *refs,
):
    out_o, small_o, up_o, do_o = refs[:4]
    qkv_o = refs[4:7]
    at = 7
    nx = len(X_SCRATCH)
    xs = refs[at : at + nx]
    at += nx
    us = []
    for _ in LAST:
        us.append(refs[at : at + UNIT_SCRATCH])
        at += UNIT_SCRATCH
    core_in, ring_in, s_send, s_recv, do, dw = refs[at : at + 6]
    x_scratch = refs[at + 6 :]
    p = Place()
    greet(unit_peers(p) + [p.dev(dx=1), p.dev(dx=-1), p.dev(dx=2), p.dev(dz=2)])
    x_read = own_rows(p, x_ref, x_scratch)

    def finish(g):
        v = x_read()
        inv = rms(v)
        normed = v * inv
        few = slice(0, 128)
        small_o[...] = jnp.zeros_like(small_o)
        small_o[0:1, :] = jnp.sum(g * normed, axis=0, keepdims=True)
        small_o[1:2, :] = ffn_gain[0:1, :]
        small_o[2:3, few] = jnp.sum(keep[...], axis=0, keepdims=True)
        small_o[3:4, few] = stat_attn[0:1, :]
        small_o[4:5, few] = stat_ffn[0, 0:1, :]
        small_o[5:6, few] = stat_ffn[1, 0:1, :]
        grad_in = grad_resid[...] + norm_back(g, normed, full_row(gains, 0), inv)
        return grad_in.astype(BF)

    def small():
        core_in[p.c] = small_o[...]
        c = remote(core_in.at[p.c], core_in.at[p.c], s_send.at[0], s_recv.at[0], p.sib())
        c.start()
        yield
        here = core_in.at[1 - p.c]
        remote(here, here, s_send.at[0], s_recv.at[0], p.sib()).wait_recv()
        c.wait_send()
        total = core_in[0] + core_in[1]
        for axis, me, move in (
            (0, p.x, lambda d: p.dev(dx=d)),
            (1, p.y, lambda d: p.dev(dy=d)),
            (2, p.z, lambda d: p.dev(dz=d)),
        ):
            ring_in[axis, me] = total
            here = ring_in.at[axis, me]
            out = [
                remote(
                    here, here, s_send.at[axis * 3 + d], s_recv.at[axis * 3 + d], move(d)
                )
                for d in (1, 2, 3)
            ]
            for c in out:
                c.start()
            yield
            for d in (1, 2, 3):
                there = ring_in.at[axis, (me + 4 - d) % 4]
                remote(
                    there, there, s_send.at[axis * 3 + d], s_recv.at[axis * 3 + d], move(4 - d)
                ).wait_recv()
            for c in out:
                c.wait_send()
            total = (ring_in[axis, 0] + ring_in[axis, 1]) + (ring_in[axis, 2] + ring_in[axis, 3])
        small_o[...] = total

    def out_unit():
        left = attended[...].reshape(1024, 256).T

        def step(n, carry):
            cols = pl.ds(pl.multiple_of(n * 512, 512), 512)
            v = jnp.dot(left, grad_attn[:, cols], preferred_element_type=F32)
            do[:, :, cols] = v.reshape(32, 8, 512).astype(BF)
            return carry

        lax.fori_loop(0, 4, step, 0)
        yield from unit(p, LAST[1], do, (do_o,), us[1])

    def qkv_unit():
        def step(n, carry):
            v = jnp.dot(
                attn_in_t[pl.ds(pl.multiple_of(n * 512, 512), 512), :],
                lhs[...].reshape(1024, 768),
                preferred_element_type=F32,
            )
            dw[n] = v.reshape(64, 8, 768).astype(BF)
            return carry

        lax.fori_loop(0, 4, step, 0)
        yield from unit(p, LAST[2], dw, qkv_o, us[2])

    run(
        LAST_ORDER,
        x=x_phase(p, multiplier(lhs, rhs, True), xs, out_o, False, finish),
        b=unit(p, LAST[0], dup, (up_o,), us[0]),
        c=out_unit(),
        d=qkv_unit(),
        s=small(),
    )


def last_call(lhs, rhs, grad_resid, gains, small_parts, attn_in_t, attended, grad_attn, dup, x):
    scratch = list(X_SCRATCH)
    for name in LAST:
        scratch += unit_scratch(name)
    outs = [UP_OUT, OUT_OUT, QKV_OUT, QKV_OUT, QKV_OUT]
    return pl.pallas_call(
        last_kernel,
        out_shape=(
            jax.ShapeDtypeStruct((4, 1, BLOCK, MODEL), BF),
            jax.ShapeDtypeStruct((8, MODEL), F32),
            *outs,
        ),
        in_specs=[VM] * 11 + [ANY] * 2,
        out_specs=[VM] * 2 + [ANY] * len(outs),
        scratch_shapes=scratch
        + [
            pltpu.VMEM((2, 8, MODEL), F32),
            pltpu.VMEM((3, 4, 8, MODEL), F32),
            DMA((10,)),
            DMA((10,)),
            pltpu.VMEM((32, 8, MODEL), BF),
            pltpu.VMEM((4, 64, 8, 768), BF),
        ]
        + OWN_ROWS,
        compiler_params=params(6),
    )(
        lhs,
        rhs,
        grad_resid,
        gains,
        *small_parts,
        attn_in_t,
        attended,
        grad_attn,
        tiles(dup).reshape(4, 64, 8, 1024),
        tiles(x),
    )


def results_kernel(small, output, grad, q, k, v, o, gate, up_a, up_b, down, *outs):
    own = pl.ds(
        pl.multiple_of((lax.axis_index("shard") * 4 + lax.axis_index("tensor")) * BLOCK, BLOCK), BLOCK
    )
    outs[9][...] = small[0:1, own]
    outs[10][...] = small[1:2, own]
    tokens = jnp.maximum(small[2:3, 0:BLOCK], 1.0) * MODEL
    means = [jnp.sqrt(small[i : i + 1, 0:BLOCK] / tokens) for i in (3, 4, 5)]
    lane = lax.broadcasted_iota(jnp.int32, (1, BLOCK), 1)
    outs[11][...] = jnp.where(lane == 0, means[0], jnp.where(lane == 1, means[1], means[2]))
    for src, dst in zip((output, grad, q, k, v, o, gate), outs[:7]):
        dst[...] = src[...].astype(dst.dtype)
    for h in (0, 1):
        here = slice(h * 512, (h + 1) * 512)
        outs[7][:, h * 1024 : h * 1024 + 512] = up_a[:, here].astype(F32)
        outs[7][:, h * 1024 + 512 : (h + 1) * 1024] = up_b[:, here].astype(F32)
    outs[8][...] = down[...].astype(F32)


def results_call(small, *arrays):
    arrays = [a.reshape(-1, a.shape[-1]) for a in arrays]
    steps = 4

    def block(shape):
        return pl.BlockSpec((shape[0] // steps, shape[1]), lambda i: (i, 0))

    types = [BF, BF] + [F32] * 7
    shapes = [(512, 2048)] * 2 + [(512, 512)] * 4 + [(512, 2048)] * 2 + [(2048, 512)]
    return pl.pallas_call(
        results_kernel,
        grid=(steps,),
        out_shape=[jax.ShapeDtypeStruct(sh, t) for sh, t in zip(shapes, types)]
        + [jax.ShapeDtypeStruct((1, BLOCK), F32)] * 3,
        in_specs=[pl.BlockSpec((8, MODEL), lambda i: (0, 0))] + [block(a.shape) for a in arrays],
        out_specs=[block(sh) for sh in shapes] + [pl.BlockSpec((1, BLOCK), lambda i: (0, 0))] * 3,
        compiler_params=params(),
    )(small, *arrays)


def rope_table():
    half_dim = HEAD_DIM // 2
    inv_freq = ROPE_BASE ** (-np.arange(half_dim) * 2.0 / HEAD_DIM)
    angles = np.arange(1024)[:, None] * inv_freq[None, :]
    cosine, sine = np.cos(angles), np.sin(angles)
    cosine = np.concatenate([cosine, cosine], axis=1)
    sine = np.concatenate([-sine, sine], axis=1)
    return np.stack([np.tile(cosine, (1, 2)), np.tile(sine, (1, 2))]).astype(np.float32)


def per_device(
    inputs,
    cotangent,
    q_weight,
    k_weight,
    v_weight,
    o_weight,
    gate_weight,
    up_weight,
    down_weight,
    attn_gain,
    ffn_gain,
    piece_starts,
    piece_ids,
    valid_mask,
):
    rope = jnp.asarray(rope_table())
    wqkv, wo, gains, info, pcol, keep, cot_all, attn_in_t, qkv = start_call(
        inputs,
        cotangent,
        (q_weight, k_weight, v_weight, o_weight),
        attn_gain,
        ffn_gain,
        piece_starts,
        piece_ids,
        valid_mask,
        rope,
    )
    wqkv, wo = rows_of(wqkv), rows_of(wo)
    cot_all = rows_of(cot_all)
    qkv = qkv.reshape(1024, 768)
    attended, lse = attend_call(qkv, info, pcol)
    attended = attended.reshape(4, 256, 256)
    ffn_in, resid, stat_attn, wgu, wd = out_proj_call(
        attended, wo, keep, gains, inputs, (gate_weight, up_weight, down_weight)
    )
    ffn_in = ffn_in.reshape(1024, MODEL)
    cot_rows = cot_all.reshape(1024, MODEL)
    hidden, grad_gate, grad_up, dd, dgate, dup = ffn_call(
        ffn_in, cot_rows, rows_of(wgu), rows_of(wd)
    )

    grad_attn, grad_resid, ffn_gain_part, output, stat_ffn, d_seq, sd, sgate, sup_a = mid_call(
        grad_gate,
        grad_up,
        hidden,
        wgu,
        wd,
        dd,
        dgate,
        dup,
        cotangent,
        wo,
        resid,
        gains,
        keep,
        qkv,
        info,
        pcol,
        lse,
        rope,
    )
    dqkv = d_seq.reshape(4, 256, 768)
    input_grad, small, sup_b, so, sq, sk, sv = last_call(
        dqkv,
        wqkv,
        grad_resid,
        gains,
        (ffn_gain_part, stat_attn, stat_ffn, keep),
        attn_in_t,
        attended,
        grad_attn.reshape(1024, MODEL),
        dup,
        inputs,
    )
    output, input_grad, *grads, attn_gain_out, ffn_gain_out, means = results_call(
        small, output, input_grad, sq, sk, sv, so, sgate, sup_a, sup_b, sd
    )
    return (
        output.reshape(4, BLOCK, MODEL),
        input_grad.reshape(4, BLOCK, MODEL),
        *grads,
        attn_gain_out[0],
        ffn_gain_out[0],
        means[0, 0:3],
    )


def solution(mesh):
    return jax.shard_map(
        per_device,
        mesh=mesh,
        in_specs=(
            P("shard", "context", None),
            P("shard", "context", None),
            P("shard", "tensor"),
            P("shard", "tensor"),
            P("shard", "tensor"),
            P("tensor", "shard"),
            P("shard", "tensor"),
            P("shard", "tensor"),
            P("tensor", "shard"),
            P("shard"),
            P("shard"),
            P("shard", None),
            P("shard", None),
            P("shard", None),
        ),
        out_specs=(
            P("shard", "context", None),
            P("shard", "context", None),
            P("shard", "tensor"),
            P("shard", "tensor"),
            P("shard", "tensor"),
            P("tensor", "shard"),
            P("shard", "tensor"),
            P("shard", "tensor"),
            P("tensor", "shard"),
            P(("shard", "tensor")),
            P(("shard", "tensor")),
            P(),
        ),
        check_vma=False,
    )
```

```python
import functools

import jax
import jax.numpy as jnp
import numpy as np
from jax import lax
from jax.experimental import pallas as pl
from jax.experimental.pallas import tpu as pltpu
from jax.sharding import PartitionSpec as P

HEAD_DIM = 64
PIECE = 256
NORM_EPS = 1e-05
ROPE_BASE = 130000.0
MASK_FILL = -1e30
BF = jnp.bfloat16
F32 = jnp.float32
ANY = pl.BlockSpec(memory_space=pl.ANY)
VM = pl.BlockSpec(memory_space=pltpu.VMEM)
DMA = pltpu.SemaphoreType.DMA
PROJ_ORDER = "gxxxxxggxgxgxgxggx"
MID_ORDER = (
    "amecmmmbmaemaemdcambemcbmxcdxxdambedcmx"
    "bxambdcexmdmxbacdeaxcxbdmdmmcbxxaeem"
)
ATTEND_ROWS = 256
LAST_ORDER = "bxdxxbxcbdxbdcbxdbcdscbsbxcxdscbsxdcsxdccd"
FFN_TILE, FFN_ROWS, FFN_BACK = 512, 1024, 2048
VMEM_LIMIT = 60 * 1024 * 1024
MODEL = 2048
TILE = 256
BLOCK = 128
MESH_ID = pl.DeviceIdType.MESH


class Place:
    def __init__(self):
        self.s = lax.axis_index("shard")
        self.k = lax.axis_index("context")
        self.x = lax.axis_index("tensor")
        self.yl = self.s // 2
        self.c = self.s % 2
        self.y = (self.k // 4) * 2 + self.yl
        self.z = self.k % 4

    def dev(self, dx=0, dy=0, dz=0, core=None):
        x = (self.x + dx + 4) % 4
        y = (self.y + dy + 4) % 4
        z = (self.z + dz + 4) % 4
        c = self.c if core is None else core
        return {"shard": (y % 2) * 2 + c, "context": (y // 2) * 4 + z, "tensor": x}

    def member(self, k):
        return {"shard": self.s, "context": k, "tensor": self.x}

    def slot(self, k):
        return (k // 2) * 2 + (k % 2 + self.c) % 2

    def sib(self):
        return self.dev(core=1 - self.c)


def remote(src, dst, send_sem, recv_sem, device):
    return pltpu.make_async_remote_copy(
        src_ref=src,
        dst_ref=dst,
        send_sem=send_sem,
        recv_sem=recv_sem,
        device_id=device,
        device_id_type=MESH_ID,
    )


def greet(devices):
    barrier = pltpu.get_barrier_semaphore()
    for d in devices:
        pl.semaphore_signal(barrier, inc=1, device_id=d, device_id_type=MESH_ID)
    pl.semaphore_wait(barrier, len(devices))


def params(collective_id=None):
    if collective_id is None:
        return pltpu.CompilerParams(vmem_limit_bytes=VMEM_LIMIT)
    return pltpu.CompilerParams(
        vmem_limit_bytes=VMEM_LIMIT, collective_id=collective_id, has_side_effects=True
    )


def tiles(v):
    return v.reshape(*v.shape[:-2], v.shape[-2] // 8, 8, v.shape[-1])


def rows_of(v):
    return v.reshape(*v.shape[:-3], v.shape[-3] * 8, v.shape[-1])


def context_peers(p):
    return [p.member((p.k + d) % 8) for d in range(1, 8)]


def swap_halves(v):
    width = v.shape[1]
    lane = lax.broadcasted_iota(jnp.int32, v.shape, 1) % HEAD_DIM
    return jnp.where(
        lane < HEAD_DIM // 2,
        pltpu.roll(v, width - HEAD_DIM // 2, 1),
        pltpu.roll(v, HEAD_DIM // 2, 1),
    )


WEIGHTS = (
    (256, "row", 0),
    (256, "row", 256),
    (256, "row", 512),
    (256, "col", 0),
    (1024, "row", 0),
    (1024, "row", 1024),
    (1024, "col", 0),
)


OWN_ROWS = [pltpu.VMEM((16, 8, MODEL), BF), DMA((1,))]


def own_rows(p, ref, scratch):
    rows, sem = scratch
    copy = pltpu.make_async_copy(ref.at[p.x], rows, sem.at[0])
    copy.start()

    def read():
        copy.wait()
        return rows[...].astype(F32).reshape(BLOCK, MODEL)

    return read


class Gather:
    def __init__(self, p, ws, srcs, dsts, stages, sems):
        self.p, self.ws, self.srcs, self.dsts, self.stages = p, ws, srcs, dsts, stages
        self.y_send, self.y_recv, self.z_send, self.z_recv, self.s_send, self.s_recv, self.loc = sems
        self.qa = 2 * (p.z % 2)

    @staticmethod
    def sems(n):
        return [DMA((n, 2, 2))] * 4 + [DMA((n,))] * 3

    @staticmethod
    def peers(p):
        return (
            [p.sib()]
            + [p.dev(dy=dy, core=core) for dy in (-1, 1) for core in (0, 1)]
            + [p.dev(dz=1), p.dev(dz=-1)]
        )

    def src(self, i, half, quarter):
        size, kind, _ = WEIGHTS[self.ws[i]]
        if kind == "row":
            rows = pl.ds(0, 64) if quarter is None else pl.ds(quarter * 16, 16)
            return self.srcs[i].at[rows, :, pl.ds(half * size, size)]
        size = size // 8
        if quarter is None:
            return self.srcs[i].at[pl.ds(half * size, size)]
        return self.srcs[i].at[pl.ds(half * size + quarter * (size // 4), size // 4)]

    def dst(self, i, block, quarter):
        size, kind, off = WEIGHTS[self.ws[i]]
        if kind == "row":
            rows = (
                pl.ds(block * 64, 64)
                if quarter is None
                else pl.ds(block * 64 + quarter * 16, 16)
            )
            return self.dsts[i].at[rows, :, pl.ds(off, size)]
        size = size // 8
        cols = pl.ds(block * 512, 512)
        if quarter is None:
            return self.dsts[i].at[:, :, cols]
        return self.dsts[i].at[pl.ds(quarter * (size // 4), size // 4), :, cols]

    def y_copy(self, i, side, core):
        p = self.p
        quarter = self.qa + side
        return remote(
            self.src(i, core, quarter),
            self.dst(i, p.s, quarter),
            self.y_send.at[i, side, core],
            self.y_recv.at[i, side, p.c],
            p.dev(dy=-1 if side == 0 else 1, core=core),
        )

    def y_arrival(self, i, side, core):
        p = self.p
        here = self.dst(i, (1 - p.yl) * 2 + core, self.qa + side)
        return remote(
            here,
            here,
            self.y_send.at[i, side, core],
            self.y_recv.at[i, side, core],
            p.dev(dy=1 if side == 0 else -1, core=core),
        )

    def z_copy(self, i, side, core, arrival=False):
        p = self.p
        quarter = 2 - self.qa + side if arrival else self.qa + side
        here = self.dst(i, (1 - p.yl) * 2 + core, quarter)
        return remote(
            here,
            here,
            self.z_send.at[i, side, core],
            self.z_recv.at[i, side, core],
            p.dev(dz=1 if (side == 0) == arrival else -1),
        )

    def sib_copy(self, i, arrival=False):
        p = self.p
        there = self.dst(i, p.yl * 2 + 1 - p.c if arrival else p.s, None)
        return remote(
            there if arrival else self.src(i, 1 - p.c, None),
            there,
            self.s_send.at[i],
            self.s_recv.at[i],
            p.sib(),
        )

    def own_copy(self, i, step):
        stage = self.stages[i]
        here = self.dst(i, self.p.s, None)
        if step == 1:
            return pltpu.make_async_copy(stage, here, self.loc.at[i])
        return pltpu.make_async_copy(
            self.src(i, self.p.c, None), here if stage is None else stage, self.loc.at[i]
        )

    def start(self):
        for i in range(len(self.ws)):
            for core in (0, 1):
                for side in (0, 1):
                    self.y_copy(i, side, core).start()
        for i in range(len(self.ws)):
            self.sib_copy(i).start()
            self.own_copy(i, 0).start()

    def pass_on(self, i):
        for side in (0, 1):
            for core in (0, 1):
                self.y_arrival(i, side, core).wait_recv()
                self.z_copy(i, side, core).start()
        if self.stages[i] is not None:
            self.own_copy(i, 0).wait()
            self.own_copy(i, 1).start()

    def arrive(self, i):
        for side in (0, 1):
            for core in (0, 1):
                self.z_copy(i, side, core, True).wait_recv()
        self.sib_copy(i, True).wait_recv()
        self.own_copy(i, 0 if self.stages[i] is None else 1).wait()

    def sent(self, i):
        self.sib_copy(i).wait_send()
        for side in (0, 1):
            for core in (0, 1):
                self.y_copy(i, side, core).wait_send()
                self.z_copy(i, side, core).wait_send()

    def steps(self):
        self.start()
        yield
        for i in range(len(self.ws)):
            self.pass_on(i)
            yield
        for i in range(len(self.ws)):
            self.arrive(i)
            self.sent(i)
            yield


def run(order, **gens):
    alive = dict(gens)

    def step(name):
        if name in alive:
            try:
                next(alive[name])
            except StopIteration:
                del alive[name]

    for name in order:
        step(name)
    while alive:
        for name in list(alive):
            step(name)


def start_kernel(
    x_ref,
    cot_ref,
    wq,
    wk,
    wv,
    wo,
    gains_ref,
    pieces_ref,
    valid,
    rope_ref,
    wqkv_o,
    wo_o,
    gains_o,
    info_o,
    pcol_o,
    keep_o,
    cot_o,
    attn_in_t_o,
    qkv_o,
    attn_in,
    rope_own,
    gain_ref,
    meta,
    x_all,
    qkv_send,
    stage_o,
    stage_cot,
    loc,
    misc_send,
    misc_recv,
    gain_send,
    gain_recv,
    a2a_send,
    a2a_recv,
    *sems,
):
    p = Place()
    g = Gather(
        p,
        (0, 1, 2, 3),
        (wq, wk, wv, wo),
        (wqkv_o, wqkv_o, wqkv_o, wo_o),
        (None, None, None, stage_o),
        sems,
    )
    greet(
        [p.sib()]
        + [p.dev(dy=dy, core=core) for dy in (-1, 1) for core in (0, 1)]
        + context_peers(p)
    )
    gain_ref[...] = jnp.zeros_like(gain_ref)
    gain_ref[0:2, :] = gains_ref[...]
    gain_targets = [p.sib()] + [p.dev(dy=1, core=core) for core in (0, 1)]
    gain_copies = [
        remote(gain_ref, gains_o.at[p.s], gain_send.at[i], gain_recv.at[i if i == 0 else 1 + p.c], d)
        for i, d in enumerate(gain_targets)
    ]
    for c in gain_copies:
        c.start()
    x_own = pltpu.make_async_copy(x_ref, x_all.at[:, 0], loc.at[0])
    x_own.start()
    x_out = remote(x_ref, x_all.at[:, 1], misc_send.at[0], misc_recv.at[0], p.sib())
    x_out.start()
    g.start()
    rope_in = pltpu.make_async_copy(
        rope_ref.at[:, pl.ds(pl.multiple_of(p.k * BLOCK, BLOCK), BLOCK)], rope_own, loc.at[4]
    )
    rope_in.start()
    gains_o[p.s] = gain_ref[...]
    position = lax.broadcasted_iota(jnp.int32, (1, 1024), 1)
    for i in range(4):
        tag = jnp.zeros((1, 1024), jnp.int32)
        for n in range(2):
            first = pieces_ref[i, n]
            inside = (position >= first) & (position < first + PIECE)
            tag += jnp.where(inside, pieces_ref[i, 2 + n] + 1, 0)
        meta[p.c, i : i + 1, :] = tag - 1
    meta[p.c, 4:8, :] = valid[...]
    meta_out = remote(meta.at[p.c], meta.at[p.c], misc_send.at[1], misc_recv.at[1], p.sib())
    meta_out.start()
    own_row = jnp.zeros((1, 1024), jnp.int32)
    for i in range(4):
        own_row = jnp.where(p.x == i, valid[i : i + 1, :], own_row)
    own_valid = own_row[:, 0:BLOCK]
    for b in range(1, 8):
        own_valid = jnp.where(p.k == b, own_row[:, b * BLOCK : (b + 1) * BLOCK], own_valid)
    keep_o[...] = jnp.broadcast_to(own_valid.astype(F32), (BLOCK, BLOCK)).T
    cot_in = pltpu.make_async_copy(cot_ref, stage_cot, loc.at[3])
    cot_in.start()
    cot_own = pltpu.make_async_copy(stage_cot, cot_o.at[:, 0], loc.at[3])
    cot_out = remote(cot_ref, cot_o.at[:, 1], misc_send.at[2], misc_recv.at[2], p.sib())
    cot_out.start()

    for i in range(3):
        block = p.yl * 2 + 1 - p.c if i == 0 else (1 - p.yl) * 2 + (i - 1)
        here = gains_o.at[block]
        remote(here, here, gain_send.at[i], gain_recv.at[i], p.sib()).wait_recv()
    x_own.wait()
    x_out.wait_recv()
    gain = jnp.concatenate([gains_o[b, 0:1, :] for b in range(4)], axis=1)

    def norm_step(i, carry):
        v = x_all[i // 2, i % 2].astype(F32).reshape(BLOCK, MODEL)
        r = lax.rsqrt(jnp.mean(v * v, axis=1, keepdims=True) + NORM_EPS)
        v = (v * r * gain).astype(BF)
        attn_in[i // 2, pl.ds((i % 2) * BLOCK, BLOCK), :] = v
        return carry

    lax.fori_loop(0, 3, norm_step, 0)
    g.pass_on(0)
    lax.fori_loop(3, 6, norm_step, 0)
    g.pass_on(1)
    lax.fori_loop(6, 8, norm_step, 0)
    g.pass_on(2)
    g.pass_on(3)
    rope_in.wait()
    cot_in.wait()
    cot_own.start()
    def send_block(j, q):
        other = p.c if q == 0 else 1 - p.c
        k = j * 2 + other
        slot = j * 2 + q
        return (
            k,
            remote(
                qkv_send.at[slot],
                qkv_o.at[p.k],
                a2a_send.at[slot],
                a2a_recv.at[p.k],
                p.member(k),
            ),
            pltpu.make_async_copy(qkv_send.at[slot], qkv_o.at[p.k], a2a_send.at[slot]),
        )

    for i in range(3):
        g.arrive(i)

    def wide(v):
        v = jnp.concatenate([v, v], axis=1)
        return jnp.concatenate([v, v], axis=0)

    def qkv_step(n, carry):
        j = (p.k // 2 + 1 + n) % 4
        a = attn_in[j]
        for part in range(3):
            cols = pl.ds(part * 256, 256)
            w = wqkv_o[:, :, cols].reshape(MODEL, 256)
            v = jnp.dot(a, w, preferred_element_type=F32)
            if part < 2:
                v = v * wide(rope_own[0]) + swap_halves(v) * wide(rope_own[1])
            v = v.reshape(32, 8, 256).astype(BF)
            qkv_send[j * 2, :, :, cols] = v[:16]
            qkv_send[j * 2 + 1, :, :, cols] = v[16:]
        for q in (0, 1):
            k, out, here = send_block(j, q)

            @pl.when(k != p.k)
            def _():
                out.start()

            @pl.when(k == p.k)
            def _():
                here.start()

        return carry

    lax.fori_loop(0, 4, qkv_step, 0)

    def turn_step(i, carry):
        cols = pl.ds(pl.multiple_of(i * 256, 256), 256)
        attn_in_t_o[:, cols] = attn_in[i].T
        return carry

    lax.fori_loop(0, 4, turn_step, 0)
    meta_out.wait_send()
    here = meta.at[1 - p.c]
    remote(here, here, misc_send.at[1], misc_recv.at[1], p.sib()).wait_recv()
    pieces = meta[p.k % 2, pl.ds(p.k // 2, 1), :]
    info_o[...] = jnp.zeros_like(info_o)
    info_o[0:1, :] = pieces
    info_o[1:2, :] = meta[p.k % 2, pl.ds(4 + p.k // 2, 1), :]
    for b in range(8):
        rows = slice(b * BLOCK, (b + 1) * BLOCK)
        pcol_o[rows, :] = jnp.broadcast_to(pieces[:, rows], (BLOCK, BLOCK)).T
    g.arrive(3)
    for i in range(4):
        g.sent(i)
    x_out.wait_send()
    cot_own.wait()
    cot_out.wait()
    for c in gain_copies:
        c.wait_send()
    for j in range(4):
        for q in (0, 1):
            k, out, here = send_block(j, q)

            @pl.when(k != p.k)
            def _():
                out.wait_send()

            @pl.when(k == p.k)
            def _():
                here.wait()

    for i in range(8):

        @pl.when(i != p.k)
        def _():
            here = qkv_o.at[i]
            remote(here, here, a2a_send.at[i], a2a_recv.at[i], p.member(i)).wait_recv()


def start_call(x, cot, weights, attn_gain, ffn_gain, starts, ids, valid, rope):
    shapes = (
        jax.ShapeDtypeStruct((256, 8, 768), BF),
        jax.ShapeDtypeStruct((32, 8, 2048), BF),
        jax.ShapeDtypeStruct((4, 8, 512), F32),
        jax.ShapeDtypeStruct((8, 1024), jnp.int32),
        jax.ShapeDtypeStruct((1024, 128), jnp.int32),
        jax.ShapeDtypeStruct((BLOCK, BLOCK), F32),
        jax.ShapeDtypeStruct((4, 2, 16, 8, MODEL), BF),
        jax.ShapeDtypeStruct((MODEL, 1024), BF),
        jax.ShapeDtypeStruct((8, 16, 8, 768), BF),
    )
    return pl.pallas_call(
        start_kernel,
        out_shape=shapes,
        in_specs=[ANY] * 6 + [VM] + [pl.BlockSpec(memory_space=pltpu.SMEM), VM, ANY],
        out_specs=[VM, ANY, VM, VM, VM, VM, ANY, VM, ANY],
        scratch_shapes=[
            pltpu.VMEM((4, 256, MODEL), BF),
            pltpu.VMEM((2, BLOCK, 128), F32),
            pltpu.VMEM((8, 512), F32),
            pltpu.VMEM((2, 8, 1024), jnp.int32),
            pltpu.VMEM((4, 2, 16, 8, MODEL), BF),
            pltpu.VMEM((8, 16, 8, 768), BF),
            pltpu.VMEM((32, 8, 512), BF),
            pltpu.VMEM((4, 16, 8, MODEL), BF),
            DMA((5,)),
            DMA((3,)),
            DMA((3,)),
            DMA((3,)),
            DMA((3,)),
            DMA((8,)),
            DMA((8,)),
        ]
        + Gather.sems(4),
        compiler_params=params(1),
    )(
        tiles(x),
        tiles(cot),
        *[tiles(w) for w in weights],
        jnp.stack([attn_gain, ffn_gain]).astype(F32),
        jnp.concatenate([starts, ids], axis=1),
        valid,
        rope,
    )


def bias_rows(qb, rows, prow, vrow, pcol):
    i = qb * rows + lax.broadcasted_iota(jnp.int32, (rows, 1024), 0)
    j = lax.broadcasted_iota(jnp.int32, (rows, 1024), 1)
    same = (pcol >= 0) & (pcol == prow)
    ok = ((j <= i) | same) & ((vrow > 0) | (i == j))
    return jnp.where(ok, 0.0, MASK_FILL)


def attend_kernel(
    qkv, info, pcol, out_o, lse_o, o_send, a2a_send, a2a_recv
):
    p = Place()
    greet(context_peers(p))
    mine = p.slot(p.k)
    rows = 256

    def sends(i):
        return (
            remote(o_send.at[i], out_o.at[mine], a2a_send.at[i], a2a_recv.at[p.k], p.member(i)),
            pltpu.make_async_copy(o_send.at[i], out_o.at[mine], a2a_send.at[i]),
        )

    def step(n, carry):
        qb = (p.k // 2 + 1 + n) % 4
        at = pl.ds(pl.multiple_of(qb * rows, rows), rows)
        bias = bias_rows(qb, rows, info[0:1, :], info[1:2, :], pcol[at, 0:1])
        lane = lax.broadcasted_iota(jnp.int32, (rows, 128), 1)
        totals = jnp.zeros((rows, 128), F32)
        outs = []
        for h in range(4):
            q = qkv[at, pl.ds(h * 64, 64)]
            k = qkv[:, pl.ds(256 + h * 64, 64)]
            v = qkv[:, pl.ds(512 + h * 64, 64)]
            sc = lax.dot_general(q, k, (((1,), (1,)), ((), ())), preferred_element_type=F32)
            sc = sc * (HEAD_DIM**-0.5) + bias
            top = jnp.max(sc, axis=1, keepdims=True)
            e = jnp.exp(sc - top)
            total = jnp.sum(e, axis=1, keepdims=True)
            prob = (e * (1.0 / total)).astype(BF)
            totals = jnp.where(lane == h, top + jnp.log(total), totals)
            outs.append(jnp.dot(prob, v, preferred_element_type=F32))
        lse_o[at, :] = totals
        o = jnp.concatenate(outs, axis=1).reshape(32, 8, 256).astype(BF)
        for half in (0, 1):
            i = qb * 2 + half
            o_send[i] = o[half * 16 : (half + 1) * 16]
            out, here = sends(i)

            @pl.when(i != p.k)
            def _():
                out.start()

            @pl.when(i == p.k)
            def _():
                here.start()

        return carry

    lax.fori_loop(0, 4, step, 0)
    for i in range(8):
        out, here = sends(i)

        @pl.when(i != p.k)
        def _():
            out.wait_send()
            spot = out_o.at[p.slot(i)]
            remote(spot, spot, a2a_send.at[i], a2a_recv.at[i], p.member(i)).wait_recv()

        @pl.when(i == p.k)
        def _():
            here.wait()


def attend_call(qkv, info, pcol):
    return pl.pallas_call(
        attend_kernel,
        out_shape=(
            jax.ShapeDtypeStruct((8, 16, 8, 256), BF),
            jax.ShapeDtypeStruct((1024, 128), F32),
        ),
        in_specs=[VM] * 3,
        out_specs=[ANY, VM],
        scratch_shapes=[pltpu.VMEM((8, 16, 8, 256), BF), DMA((8,)), DMA((8,))],
        compiler_params=params(2),
    )(qkv, info, pcol)


X_SCRATCH = [
    pltpu.VMEM((4, BLOCK, MODEL), F32),
    pltpu.VMEM((4, BLOCK, MODEL), BF),
    pltpu.VMEM((4, BLOCK, MODEL), BF),
    pltpu.VMEM((3, BLOCK, MODEL), BF),
    pltpu.VMEM((3, BLOCK, MODEL), BF),
    DMA((4,)),
    DMA((4,)),
    DMA((6,)),
    DMA((6,)),
    DMA((10,)),
    DMA((10,)),
]


def x_peers(p):
    return [p.sib(), p.dev(dx=1), p.dev(dx=-1)]


def multiplier(lhs, rhs, transposed):
    def multiply(n, j, first):
        cols = pl.ds(pl.multiple_of(first, TILE), TILE)
        if transposed:
            return lax.dot_general(
                lhs[j], rhs[cols, :], (((1,), (1,)), ((), ())), preferred_element_type=F32
            )
        return jnp.dot(lhs[j], rhs[:, cols], preferred_element_type=F32)

    return multiply


def x_phase(p, multiply, scratch, out, both, finish, prepare=None, arrived=None):
    acc, sib_out, sib_in, x_out, x_in, s_send, s_recv, x_send, x_recv, g_send, g_recv = scratch
    half = BLOCK // 2
    top, low = pl.ds(0, half), pl.ds(half, half)
    to_right, to_left = p.dev(dx=1), p.dev(dx=-1)

    def sib_copy(r):
        return remote(sib_out.at[r], sib_in.at[r], s_send.at[r], s_recv.at[r], p.sib())

    def product(r):
        j = (p.x + r) % 4
        n = (2, 1, 3, 0).index(r)
        if prepare is not None:
            prepare(n, j)

        def step(i, carry):
            cols = pl.ds(pl.multiple_of(i * TILE, TILE), TILE)
            v = multiply(n, j, i * TILE)
            acc[r, :, cols] = v[:BLOCK]
            sib_out[r, :, cols] = v[BLOCK:].astype(BF)
            return carry

        lax.fori_loop(0, MODEL // TILE, step, 0)
        sib_copy(r).start()

    def along(n, slot, rows, device):
        return remote(
            x_out.at[slot, rows], x_in.at[slot, rows], x_send.at[n], x_recv.at[n], device
        )

    far_right, far_left = along(0, 0, top, to_right), along(1, 0, low, to_left)
    right_low, right_top = along(2, 1, low, to_right), along(3, 1, top, to_right)
    left_top, left_low = along(4, 2, top, to_left), along(5, 2, low, to_left)
    product(2)
    yield
    product(1)
    sib_copy(2).wait_recv()
    x_out[0] = (acc[2] + sib_in[2].astype(F32)).astype(BF)
    far_right.start()
    far_left.start()
    yield
    product(3)
    sib_copy(1).wait_recv()
    x_out[1, half:] = (acc[1, half:] + sib_in[1, half:].astype(F32)).astype(BF)
    right_low.start()
    sib_copy(3).wait_recv()
    x_out[2, 0:half] = (acc[3, 0:half] + sib_in[3, 0:half].astype(F32)).astype(BF)
    left_top.start()
    yield
    product(0)
    yield
    far_right.wait_recv()
    x_out[1, 0:half] = (
        acc[1, 0:half] + sib_in[1, 0:half].astype(F32) + x_in[0, 0:half].astype(F32)
    ).astype(BF)
    right_top.start()
    far_left.wait_recv()
    x_out[2, half:] = (
        acc[3, half:] + sib_in[3, half:].astype(F32) + x_in[0, half:].astype(F32)
    ).astype(BF)
    left_low.start()
    yield
    sib_copy(0).wait_recv()
    acc[0] += sib_in[0].astype(F32)
    for c in (right_low, left_top, right_top, left_low):
        c.wait_recv()
    total = acc[0] + x_in[1].astype(F32) + x_in[2].astype(F32)
    for r in range(4):
        sib_copy(r).wait_send()
    for c in (far_right, far_left, right_low, right_top, left_top, left_low):
        c.wait_send()

    me, right, left, far = p.x, (p.x + 1) % 4, (p.x + 3) % 4, (p.x + 2) % 4
    out[me, 0] = finish(total)
    sent = []

    def copy(n, j, rows, d):
        src = out.at[j, 0, rows]
        return remote(src, src, g_send.at[n], g_recv.at[n], d)

    def go(c):
        c.start()
        sent.append(c)

    def to_sib(n, j):
        return remote(out.at[j, 0], out.at[j, 1], g_send.at[n], g_recv.at[n], p.sib())

    go(copy(0, me, top, to_right))
    go(copy(1, me, low, to_left))
    go(copy(2, me, low, to_right))
    go(copy(3, me, top, to_left))
    if both:
        go(to_sib(6, me))
    yield
    copy(0, left, top, to_left).wait_recv()
    go(copy(4, left, top, to_right))
    copy(1, right, low, to_right).wait_recv()
    go(copy(5, right, low, to_left))
    yield
    copy(2, left, low, to_left).wait_recv()
    copy(3, right, top, to_right).wait_recv()
    if both:
        go(to_sib(7, left))
        go(to_sib(8, right))
    yield
    copy(4, far, top, to_left).wait_recv()
    copy(5, far, low, to_right).wait_recv()
    if both:
        go(to_sib(9, far))
        yield
        for n, j in ((6, me), (7, left), (8, right), (9, far)):
            to_sib(n, j).wait_recv()
            if arrived is not None:
                arrived(j)
    for c in sent:
        c.wait_send()


def rms(v):
    return lax.rsqrt(jnp.mean(v * v, axis=1, keepdims=True) + NORM_EPS)


def full_row(gains, row):
    return jnp.concatenate([gains[b, row : row + 1, :] for b in range(4)], axis=1)


def norm_back(grad, normed, gain, inv):
    w = grad * gain
    return inv * (w - normed * jnp.mean(w * normed, axis=1, keepdims=True))


UNITS = {
    "down_a": (64, 512, "col", 0, ()),
    "down_b": (64, 512, "col", 64, ()),
    "gate_a": (64, 512, "row", 0, (1024,)),
    "gate_b": (64, 512, "row", 512, (1024,)),
    "up_a": (64, 512, "row", 0, (512,)),
    "up_b": (64, 512, "row", 512, (512,)),
    "out": (32, 512, "col", 0, ()),
    "qkv": (64, 768, "row", 0, (256, 256, 256)),
}
UNIT_SCRATCH = 9
DOWN_OUT = jax.ShapeDtypeStruct((2, 2, 2, 32, 8, 512), BF)
OUT_OUT = jax.ShapeDtypeStruct((2, 1, 2, 16, 8, 512), BF)
FFN_OUT = jax.ShapeDtypeStruct((2, 32, 8, 2048), BF)
UP_OUT = jax.ShapeDtypeStruct((2, 32, 8, 1024), BF)
QKV_OUT = jax.ShapeDtypeStruct((2, 32, 8, 512), BF)


def unit_scratch(name):
    r, c, _, _, _ = UNITS[name]
    return [
        pltpu.VMEM((2, 2, r // 2, 8, c), BF),
        pltpu.VMEM((2, 2, r // 2, 8, c), BF),
        pltpu.VMEM((2, 2, 2, r // 8, 8, c), BF),
        pltpu.VMEM((3, 2, 2, r // 8, 8, c), BF),
        pltpu.VMEM((2, 2, r // 8, 8, c), BF),
        DMA((4,)),
        DMA((18,)),
        DMA((18,)),
        pltpu.SemaphoreType.REGULAR,
    ]


def unit_peers(p):
    return [p.sib(), p.dev(dy=1), p.dev(dy=-1), p.dev(dy=2), p.dev(dz=1), p.dev(dz=-1)]


def unit(p, name, src, outs, scratch, pace=False):
    rows, cols, kind, first, widths = UNITS[name]
    own, yin, zout, zin, yhin, loc, send, recv, beside = scratch
    part = rows // 8
    half = rows // 2
    z_of = {0: p.dev(dz=1), 1: p.dev(dz=-1)}
    me, zr, zl, zf = p.z, (p.z + 1) % 4, (p.z + 3) % 4, (p.z + 2) % 4

    def cp(n, src, dst, d):
        return remote(src, dst, send.at[n], recv.at[n], d)

    def fetch(yl, h, dst, make):
        if kind == "row":
            return [
                make(
                    h * 2,
                    src.at[pl.ds(yl * 2, 2), pl.ds(h * half, half), :, pl.ds(first, cols)],
                    dst.at[:, h],
                )
            ]
        return [
            make(
                h * 2 + core,
                src.at[pl.ds(first + h * half, half), :, pl.ds((yl * 2 + core) * cols, cols)],
                dst.at[core, h],
            )
            for core in (0, 1)
        ]

    along_y, local = [], []
    for h in (0, 1):
        d = p.dev(dy=1 if h == 0 else -1)
        along_y += fetch(1 - p.yl, h, yin, lambda n, a, b, d=d: cp(n, a, b, d))
        local += fetch(p.yl, h, own, lambda n, a, b: pltpu.make_async_copy(a, b, loc.at[n]))
    for c in along_y + local:
        c.start()
    yield
    for c in local:
        c.wait()
    for c in along_y:
        c.wait_recv()
    own[...] = own[...] + yin[...]

    def chunk(h, zc):
        return own.at[:, h, pl.ds(zc * part, part)]

    far = [cp(4 + h, chunk(h, zf), zin.at[0, :, h], z_of[h]) for h in (0, 1)]
    for c in far:
        c.start()
    yield
    for c in far:
        c.wait_send()
    near = []
    for side, zc in ((0, zr), (1, zl)):
        zout[side, :, 1 - side] = own[:, 1 - side, pl.ds(zc * part, part)]
        far[side].wait_recv()
        zout[side, :, side] = own[:, side, pl.ds(zc * part, part)] + zin[0, :, side]
        c = cp(6 + side, zout.at[side], zin.at[1 + side], z_of[side])
        c.start()
        near.append(c)
    yield
    for c in near:
        c.wait_recv()
    for c in near:
        c.wait_send()
    v = own[:, :, pl.ds(me * part, part)].astype(F32)
    zout[0] = (v + zin[1].astype(F32) + zin[2].astype(F32)).astype(BF)
    if pace:
        for dy in (-1, 1):
            pl.semaphore_signal(beside, inc=1, device_id=p.dev(dy=dy), device_id_type=MESH_ID)
        pl.semaphore_wait(beside, 2)
    yh = cp(8, zout.at[0], yhin, p.dev(dy=2))
    yh.start()
    yield
    yh.wait_recv()
    own[:, :, pl.ds(me * part, part)] = zout[0] + yhin[...]
    back = [cp(9 + side * 2 + h, chunk(h, me), chunk(h, me), z_of[side]) for side, h in ((0, 0), (1, 1), (0, 1), (1, 0))]
    for c in back:
        c.start()
    yield
    for side, zc in ((0, zl), (1, zr)):
        here = chunk(side, zc)
        cp(9 + side * 3, here, here, z_of[1 - side]).wait_recv()
        c = cp(13 + side, here, here, z_of[side])
        c.start()
        back.append(c)
    yield
    for side, zc in ((0, zl), (1, zr)):
        here = chunk(1 - side, zc)
        cp(9 + side * 2 + 1 - side, here, here, z_of[1 - side]).wait_recv()
    for h in (0, 1):
        here = chunk(h, zf)
        cp(13 + h, here, here, z_of[1 - h]).wait_recv()
    for c in back + along_y + [yh]:
        c.wait_send()
    done = []
    if kind == "col":
        spot = outs[0].at[p.c, first // rows]
        done.append(cp(15, own.at[1 - p.c], spot, p.sib()))
        done.append(pltpu.make_async_copy(own.at[p.c], spot, loc.at[0]))
    else:
        for i, width in enumerate(widths):
            take = min(cols, width)
            spot = outs[i].at[:, :, :, pl.ds(p.c * width + (first if width > cols else 0), take)]
            piece = pl.ds(i * take, take)
            done.append(cp(15 + i, own.at[1 - p.c, :, :, :, piece], spot, p.sib()))
            done.append(pltpu.make_async_copy(own.at[p.c, :, :, :, piece], spot, loc.at[i]))
    for c in done:
        c.start()
    yield
    for c in done:
        c.wait()


def out_proj_kernel(
    lhs,
    rhs,
    keep,
    gains,
    x_ref,
    wg,
    wu,
    wd,
    ffn_in_o,
    resid_o,
    stat_o,
    wgu_o,
    wd_o,
    stage_g,
    stage_u,
    stage_d,
    x_rows,
    x_sem,
    *scratch,
):
    p = Place()
    nx = len(X_SCRATCH)
    g = Gather(
        p,
        (4, 5, 6),
        (wg, wu, wd),
        (wgu_o, wgu_o, wd_o),
        (stage_g, stage_u, stage_d),
        scratch[nx:],
    )
    greet(Gather.peers(p) + [p.dev(dx=1), p.dev(dx=-1)])
    x_read = own_rows(p, x_ref, (x_rows, x_sem))

    def finish(attn_out):
        stat_o[...] = jnp.full((8, 128), jnp.sum(keep[:, 0:1] * attn_out * attn_out), F32)
        resid = x_read() + attn_out
        resid_o[...] = resid
        return (resid * rms(resid) * full_row(gains, 1)).astype(BF)

    run(
        PROJ_ORDER,
        g=g.steps(),
        x=x_phase(p, multiplier(lhs, rhs, False), scratch[:nx], ffn_in_o, True, finish),
    )


def out_proj_call(lhs, rhs, keep, gains, x, weights):
    return pl.pallas_call(
        out_proj_kernel,
        out_shape=(
            jax.ShapeDtypeStruct((4, 2, BLOCK, MODEL), BF),
            jax.ShapeDtypeStruct((BLOCK, MODEL), F32),
            jax.ShapeDtypeStruct((8, 128), F32),
            jax.ShapeDtypeStruct((256, 8, 2048), BF),
            jax.ShapeDtypeStruct((128, 8, 2048), BF),
        ),
        in_specs=[VM] * 4 + [ANY] * 4,
        out_specs=[VM] * 3 + [ANY] * 2,
        scratch_shapes=[
            pltpu.VMEM((64, 8, 1024), BF),
            pltpu.VMEM((64, 8, 1024), BF),
            pltpu.VMEM((128, 8, 512), BF),
        ]
        + OWN_ROWS
        + X_SCRATCH
        + Gather.sems(3),
        compiler_params=params(3),
    )(lhs, rhs, keep, gains, tiles(x), *[tiles(w) for w in weights])


def ffn_kernel(a_ref, c_ref, wg, wu, wd, h_o, gg_o, gu_o, dd_o, dg_o, du_o, a_t):
    rows = FFN_ROWS

    @pl.when(pl.program_id(0) == 0)
    def _():
        def turn(i, carry):
            at = pl.ds(pl.multiple_of(i * 256, 256), 256)
            a_t[:, at] = a_ref[at, :].T
            return carry

        lax.fori_loop(0, 4, turn, 0)

    def step(i, carry):
        at = pl.ds(pl.multiple_of(i * rows, rows), rows)
        a = a_ref[at, :]
        gate = jnp.dot(a, wg[...], preferred_element_type=F32)
        up = jnp.dot(a, wu[...], preferred_element_type=F32)
        grad = lax.dot_general(
            c_ref[at, :], wd[...], (((1,), (1,)), ((), ())), preferred_element_type=F32
        )
        sig = 1.0 / (1.0 + jnp.exp(-gate))
        silu = gate * sig
        h_o[at, :] = (silu * up).astype(BF)
        gg_o[at, :] = (grad * up * sig * (1.0 + gate * (1.0 - sig))).astype(BF)
        gu_o[at, :] = (grad * silu).astype(BF)
        return carry

    lax.fori_loop(0, 1024 // rows, step, 0)
    h_t = h_o[...].T

    def down(n, carry):
        cols = pl.ds(pl.multiple_of(n * 256, 256), 256)
        dd_o[:, cols] = jnp.dot(h_t, c_ref[:, cols], preferred_element_type=F32).astype(BF)
        return carry

    lax.fori_loop(0, MODEL // 256, down, 0)

    def back(n, carry):
        at = pl.ds(pl.multiple_of(n * FFN_BACK, FFN_BACK), FFN_BACK)
        t = a_t[at, :]
        dg_o[at, :] = jnp.dot(t, gg_o[...], preferred_element_type=F32).astype(BF)
        du_o[at, :] = jnp.dot(t, gu_o[...], preferred_element_type=F32).astype(BF)
        return carry

    lax.fori_loop(0, MODEL // FFN_BACK, back, 0)


def ffn_call(ffn_in, cot, wgu, wd):
    tile = FFN_TILE
    n = 1024 // tile
    whole = pl.BlockSpec((1024, MODEL), lambda i: (0, 0), pipeline_mode=pl.Buffered(1))
    cols = pl.BlockSpec((1024, tile), lambda i: (0, i))
    tall = pl.BlockSpec((MODEL, tile), lambda i: (0, i))
    wide = pl.BlockSpec((tile, MODEL), lambda i: (i, 0))
    tokens = jax.ShapeDtypeStruct((1024, 1024), BF)
    grads = jax.ShapeDtypeStruct((MODEL, 1024), BF)
    return pl.pallas_call(
        ffn_kernel,
        grid=(n,),
        out_shape=(tokens, tokens, tokens, jax.ShapeDtypeStruct((1024, MODEL), BF), grads, grads),
        in_specs=[whole, whole, tall, pl.BlockSpec((MODEL, tile), lambda i: (0, i + n)), wide],
        out_specs=[cols, cols, cols, wide, tall, tall],
        scratch_shapes=[pltpu.VMEM((MODEL, 1024), BF)],
        compiler_params=params(),
    )(ffn_in, cot, wgu, wgu, wd)


MID = ("down_a", "down_b", "gate_a", "gate_b", "up_a")


def mid_kernel(*refs):
    gate, up, hidden, wgu, wd, dd, dgate, dup, cot_ref = refs[:9]
    wo, resid_ref, gains, keep, qkv, info, pcol, lse, rope = refs[9:18]
    grad_o, resid_grad_o, gain_o, final_o, stat_o, d_o, dd_o, dgate_o, dup_o = refs[18:27]
    lhs, rhs, g_out, g_in, d_out, dk, dv = refs[27:34]
    loc, g_send, g_recv, a2a_send, a2a_recv = refs[34:39]
    cot_scratch = refs[39:41]
    at = 41
    nx = len(X_SCRATCH)
    xs = refs[at : at + nx]
    at += nx
    us = [refs[at + i * UNIT_SCRATCH : at + (i + 1) * UNIT_SCRATCH] for i in range(len(MID))]
    p = Place()
    greet(context_peers(p) + x_peers(p) + [p.dev(dy=1), p.dev(dy=-1)])
    rows = ATTEND_ROWS
    each = rows // 8
    scale = HEAD_DIM**-0.5
    mine = p.slot(p.k)
    cot_read = own_rows(p, cot_ref, cot_scratch)

    def fetch(n, sources):
        j = (p.x + (2, 1, 3, 0)[n]) % 4
        return [
            pltpu.make_async_copy(v.at[j], lhs.at[n % 2, i], loc.at[(n % 2) * 2 + i])
            for i, v in enumerate(sources)
        ]

    def preparer(sources, right):
        def prepare(n, j):
            if n == 0:
                for c in fetch(0, sources):
                    c.start()
            if n < 3:
                for c in fetch(n + 1, sources):
                    c.start()
            if n == 0:
                right.wait()
            for c in fetch(n, sources):
                c.wait()

        return prepare

    def flat(v):
        return v.reshape(v.shape[0] * 8, v.shape[2])

    wgu_in = pltpu.make_async_copy(wgu, rhs, loc.at[4])
    wgu_in.start()
    wd_in = pltpu.make_async_copy(wd, rhs.at[pl.ds(0, 128)], loc.at[4])

    def multiply_back(n, j, first):
        v = 0.0
        for i in (0, 1):
            w = rhs[pl.ds(first // 8, TILE // 8), :, pl.ds(i * 1024, 1024)]
            v += lax.dot_general(
                flat(lhs[n % 2, i]), flat(w), (((1,), (1,)), ((), ())), preferred_element_type=F32
            )
        return v

    def multiply_out(n, j, first):
        w = rhs[pl.ds(0, 128), :, pl.ds(pl.multiple_of(first, TILE), TILE)]
        return jnp.dot(flat(lhs[n % 2, 0]), flat(w), preferred_element_type=F32)

    def finish_back(g):
        wd_in.start()
        resid = resid_ref[...]
        inv = rms(resid)
        normed = resid * inv
        gain_o[...] = jnp.broadcast_to(jnp.sum(g * normed, axis=0, keepdims=True), (8, MODEL))
        grad_resid = cot_read() + norm_back(g, normed, full_row(gains, 1), inv)
        resid_grad_o[...] = grad_resid
        return grad_resid.astype(BF)

    def finish_out(ffn_out):
        final = resid_ref[...] + ffn_out
        kp = keep[:, 0:1]
        stat_o[0] = jnp.full((8, 128), jnp.sum(kp * ffn_out * ffn_out), F32)
        stat_o[1] = jnp.full((8, 128), jnp.sum(kp * final * final), F32)
        return final.astype(BF)

    def g_copy(j, q):
        k = j * 2 + (p.c if q == 0 else 1 - p.c)
        slot = j * 2 + q
        return (
            k,
            remote(g_out.at[slot], g_in.at[p.k], g_send.at[slot], g_recv.at[p.k], p.member(k)),
            pltpu.make_async_copy(g_out.at[slot], g_in.at[p.k], g_send.at[slot]),
        )

    def arrived(j):
        v = lax.dot_general(
            grad_o[j].reshape(256, MODEL), wo[...], (((1,), (1,)), ((), ())), preferred_element_type=F32
        )
        v = v.reshape(32, 8, 256).astype(BF)
        for q in (0, 1):
            g_out[j * 2 + q] = v[q * 16 : (q + 1) * 16]
            k, out, here = g_copy(j, q)

            @pl.when(k != p.k)
            def _():
                out.start()

            @pl.when(k == p.k)
            def _():
                here.start()

    def sends(i):
        return (
            remote(d_out.at[i], d_o.at[mine], a2a_send.at[i], a2a_recv.at[p.k], p.member(i)),
            pltpu.make_async_copy(d_out.at[i], d_o.at[mine], a2a_send.at[i]),
        )

    def wide(v):
        return jnp.concatenate([v, v], axis=1)

    def query_block(qb):
        spot = pl.ds(qb * rows, rows)
        bias = bias_rows(qb, rows, info[0:1, :], info[1:2, :], pcol[spot, 0:1])
        blocks = pl.ds(qb * (rows // BLOCK), rows // BLOCK)
        g2 = g_in[blocks].astype(F32).reshape(rows, 256).astype(BF)
        dqs = []
        for h in range(4):
            lanes = pl.ds(h * 64, 64)
            q = qkv[spot, lanes]
            k = qkv[:, pl.ds(256 + h * 64, 64)]
            v = qkv[:, pl.ds(512 + h * 64, 64)]
            g = g2[:, h * 64 : (h + 1) * 64]
            sc = lax.dot_general(q, k, (((1,), (1,)), ((), ())), preferred_element_type=F32)
            prob = jnp.exp(sc * scale + bias - lse[spot, h : h + 1])
            gp = lax.dot_general(g, v, (((1,), (1,)), ((), ())), preferred_element_type=F32)
            inner = jnp.sum(prob * gp, axis=1, keepdims=True)
            gs = (prob * (gp - inner)).astype(BF)
            dqs.append(jnp.dot(gs, k, preferred_element_type=F32))
            dk[:, lanes] += lax.dot_general(
                gs, q, (((0,), (0,)), ((), ())), preferred_element_type=F32
            )
            dv[:, lanes] += lax.dot_general(
                prob.astype(BF), g, (((0,), (0,)), ((), ())), preferred_element_type=F32
            )
        dq = jnp.concatenate(dqs, axis=1) * scale
        dq = dq * wide(rope[0, spot]) - swap_halves(dq) * wide(rope[1, spot])
        dq = dq.reshape(each, 8, 256).astype(BF)
        for b in range(rows // BLOCK):
            d_out[qb * (rows // BLOCK) + b, :, :, 0:256] = dq[b * 16 : (b + 1) * 16]

    def give(i, carry):
        spot = pl.ds(pl.multiple_of(i * BLOCK, BLOCK), BLOCK)
        w = dk[spot, :] * scale
        w = w * wide(rope[0, spot]) - swap_halves(w) * wide(rope[1, spot])
        d_out[i, :, :, 256:512] = w.reshape(16, 8, 256).astype(BF)
        d_out[i, :, :, 512:768] = dv[spot, :].reshape(16, 8, 256).astype(BF)
        out, here = sends(i)

        @pl.when(i != p.k)
        def _():
            out.start()

        @pl.when(i == p.k)
        def _():
            here.start()

        return carry

    def main():
        yield from x_phase(
            p,
            multiply_back,
            xs,
            grad_o,
            True,
            finish_back,
            preparer((gate, up), wgu_in),
            arrived,
        )
        dk[...] = jnp.zeros_like(dk)
        dv[...] = jnp.zeros_like(dv)
        yield
        for j in range(4):
            for q in (0, 1):
                k, out, here = g_copy(j, q)

                @pl.when(k != p.k)
                def _():
                    out.wait_send()

                @pl.when(k == p.k)
                def _():
                    here.wait()

        for i in range(8):

            @pl.when(i != p.k)
            def _():
                spot = g_in.at[i]
                remote(spot, spot, g_send.at[i], g_recv.at[i], p.member(i)).wait_recv()

        for qb in range(1024 // rows):
            query_block(qb)
            yield
        lax.fori_loop(0, 8, give, 0)
        yield
        for i in range(8):
            out, here = sends(i)

            @pl.when(i != p.k)
            def _():
                out.wait_send()
                spot = d_o.at[p.slot(i)]
                remote(spot, spot, a2a_send.at[i], a2a_recv.at[i], p.member(i)).wait_recv()

            @pl.when(i == p.k)
            def _():
                here.wait()

    x = x_phase(
        p, multiply_out, xs, final_o, False, finish_out, preparer((hidden,), wd_in)
    )
    sources = (dd, dd, dgate, dgate, dup)
    results = (dd_o, dd_o, dgate_o, dgate_o, dup_o)
    a, b, c, d, e = [
        unit(p, name, src, (o,), scr, True)
        for name, src, o, scr in zip(MID, sources, results, us)
    ]
    run(MID_ORDER, m=main(), x=x, a=a, b=b, c=c, d=d, e=e)


def mid_call(gate, up, hidden, wgu, wd, dd, dgate, dup, cot, wo, *rest):
    scratch = list(X_SCRATCH)
    for name in MID:
        scratch += unit_scratch(name)
    blocks = [tiles(v.reshape(4, 256, 1024)) for v in (gate, up, hidden)]
    return pl.pallas_call(
        mid_kernel,
        out_shape=(
            jax.ShapeDtypeStruct((4, 2, BLOCK, MODEL), BF),
            jax.ShapeDtypeStruct((BLOCK, MODEL), F32),
            jax.ShapeDtypeStruct((8, MODEL), F32),
            jax.ShapeDtypeStruct((4, 1, BLOCK, MODEL), BF),
            jax.ShapeDtypeStruct((2, 8, 128), F32),
            jax.ShapeDtypeStruct((8, 16, 8, 768), BF),
            DOWN_OUT,
            FFN_OUT,
            UP_OUT,
        ),
        in_specs=[ANY] * 9 + [VM] * 9,
        out_specs=[VM] * 5 + [ANY] * 4,
        scratch_shapes=[
            pltpu.VMEM((2, 2, 32, 8, 1024), BF),
            pltpu.VMEM((256, 8, 2048), BF),
            pltpu.VMEM((8, 16, 8, 256), BF),
            pltpu.VMEM((8, 16, 8, 256), BF),
            pltpu.VMEM((8, 16, 8, 768), BF),
            pltpu.VMEM((1024, 256), F32),
            pltpu.VMEM((1024, 256), F32),
            DMA((5,)),
            DMA((8,)),
            DMA((8,)),
            DMA((8,)),
            DMA((8,)),
        ]
        + OWN_ROWS
        + scratch,
        compiler_params=params(5),
    )(
        *blocks,
        wgu,
        wd,
        tiles(dd),
        tiles(dgate).reshape(4, 64, 8, 1024),
        tiles(dup).reshape(4, 64, 8, 1024),
        tiles(cot),
        wo,
        *rest,
    )


LAST = ("up_b", "out", "qkv")


def last_kernel(
    lhs,
    rhs,
    grad_resid,
    gains,
    ffn_gain,
    stat_attn,
    stat_ffn,
    keep,
    attn_in_t,
    attended,
    grad_attn,
    dup,
    x_ref,
    *refs,
):
    out_o, small_o, up_o, do_o = refs[:4]
    qkv_o = refs[4:7]
    at = 7
    nx = len(X_SCRATCH)
    xs = refs[at : at + nx]
    at += nx
    us = []
    for _ in LAST:
        us.append(refs[at : at + UNIT_SCRATCH])
        at += UNIT_SCRATCH
    core_in, ring_in, s_send, s_recv, do, dw = refs[at : at + 6]
    x_scratch = refs[at + 6 :]
    p = Place()
    greet(unit_peers(p) + [p.dev(dx=1), p.dev(dx=-1), p.dev(dx=2), p.dev(dz=2)])
    x_read = own_rows(p, x_ref, x_scratch)

    def finish(g):
        v = x_read()
        inv = rms(v)
        normed = v * inv
        few = slice(0, 128)
        small_o[...] = jnp.zeros_like(small_o)
        small_o[0:1, :] = jnp.sum(g * normed, axis=0, keepdims=True)
        small_o[1:2, :] = ffn_gain[0:1, :]
        small_o[2:3, few] = jnp.sum(keep[...], axis=0, keepdims=True)
        small_o[3:4, few] = stat_attn[0:1, :]
        small_o[4:5, few] = stat_ffn[0, 0:1, :]
        small_o[5:6, few] = stat_ffn[1, 0:1, :]
        grad_in = grad_resid[...] + norm_back(g, normed, full_row(gains, 0), inv)
        return grad_in.astype(BF)

    def small():
        core_in[p.c] = small_o[...]
        c = remote(core_in.at[p.c], core_in.at[p.c], s_send.at[0], s_recv.at[0], p.sib())
        c.start()
        yield
        here = core_in.at[1 - p.c]
        remote(here, here, s_send.at[0], s_recv.at[0], p.sib()).wait_recv()
        c.wait_send()
        total = core_in[0] + core_in[1]
        for axis, me, move in (
            (0, p.x, lambda d: p.dev(dx=d)),
            (1, p.y, lambda d: p.dev(dy=d)),
            (2, p.z, lambda d: p.dev(dz=d)),
        ):
            ring_in[axis, me] = total
            here = ring_in.at[axis, me]
            out = [
                remote(
                    here, here, s_send.at[axis * 3 + d], s_recv.at[axis * 3 + d], move(d)
                )
                for d in (1, 2, 3)
            ]
            for c in out:
                c.start()
            yield
            for d in (1, 2, 3):
                there = ring_in.at[axis, (me + 4 - d) % 4]
                remote(
                    there, there, s_send.at[axis * 3 + d], s_recv.at[axis * 3 + d], move(4 - d)
                ).wait_recv()
            for c in out:
                c.wait_send()
            total = (ring_in[axis, 0] + ring_in[axis, 1]) + (ring_in[axis, 2] + ring_in[axis, 3])
        small_o[...] = total

    def out_unit():
        left = attended[...].reshape(1024, 256).T

        def step(n, carry):
            cols = pl.ds(pl.multiple_of(n * 512, 512), 512)
            v = jnp.dot(left, grad_attn[:, cols], preferred_element_type=F32)
            do[:, :, cols] = v.reshape(32, 8, 512).astype(BF)
            return carry

        lax.fori_loop(0, 4, step, 0)
        yield from unit(p, LAST[1], do, (do_o,), us[1])

    def qkv_unit():
        def step(n, carry):
            v = jnp.dot(
                attn_in_t[pl.ds(pl.multiple_of(n * 512, 512), 512), :],
                lhs[...].reshape(1024, 768),
                preferred_element_type=F32,
            )
            dw[n] = v.reshape(64, 8, 768).astype(BF)
            return carry

        lax.fori_loop(0, 4, step, 0)
        yield from unit(p, LAST[2], dw, qkv_o, us[2])

    run(
        LAST_ORDER,
        x=x_phase(p, multiplier(lhs, rhs, True), xs, out_o, False, finish),
        b=unit(p, LAST[0], dup, (up_o,), us[0]),
        c=out_unit(),
        d=qkv_unit(),
        s=small(),
    )


def last_call(lhs, rhs, grad_resid, gains, small_parts, attn_in_t, attended, grad_attn, dup, x):
    scratch = list(X_SCRATCH)
    for name in LAST:
        scratch += unit_scratch(name)
    outs = [UP_OUT, OUT_OUT, QKV_OUT, QKV_OUT, QKV_OUT]
    return pl.pallas_call(
        last_kernel,
        out_shape=(
            jax.ShapeDtypeStruct((4, 1, BLOCK, MODEL), BF),
            jax.ShapeDtypeStruct((8, MODEL), F32),
            *outs,
        ),
        in_specs=[VM] * 11 + [ANY] * 2,
        out_specs=[VM] * 2 + [ANY] * len(outs),
        scratch_shapes=scratch
        + [
            pltpu.VMEM((2, 8, MODEL), F32),
            pltpu.VMEM((3, 4, 8, MODEL), F32),
            DMA((10,)),
            DMA((10,)),
            pltpu.VMEM((32, 8, MODEL), BF),
            pltpu.VMEM((4, 64, 8, 768), BF),
        ]
        + OWN_ROWS,
        compiler_params=params(6),
    )(
        lhs,
        rhs,
        grad_resid,
        gains,
        *small_parts,
        attn_in_t,
        attended,
        grad_attn,
        tiles(dup).reshape(4, 64, 8, 1024),
        tiles(x),
    )


def results_kernel(small, output, grad, q, k, v, o, gate, up_a, up_b, down, *outs):
    own = pl.ds(
        pl.multiple_of((lax.axis_index("shard") * 4 + lax.axis_index("tensor")) * BLOCK, BLOCK), BLOCK
    )
    outs[9][...] = small[0:1, own]
    outs[10][...] = small[1:2, own]
    tokens = jnp.maximum(small[2:3, 0:BLOCK], 1.0) * MODEL
    means = [jnp.sqrt(small[i : i + 1, 0:BLOCK] / tokens) for i in (3, 4, 5)]
    lane = lax.broadcasted_iota(jnp.int32, (1, BLOCK), 1)
    outs[11][...] = jnp.where(lane == 0, means[0], jnp.where(lane == 1, means[1], means[2]))
    for src, dst in zip((output, grad, q, k, v, o, gate), outs[:7]):
        dst[...] = src[...].astype(dst.dtype)
    for h in (0, 1):
        here = slice(h * 512, (h + 1) * 512)
        outs[7][:, h * 1024 : h * 1024 + 512] = up_a[:, here].astype(F32)
        outs[7][:, h * 1024 + 512 : (h + 1) * 1024] = up_b[:, here].astype(F32)
    outs[8][...] = down[...].astype(F32)


def results_call(small, *arrays):
    arrays = [a.reshape(-1, a.shape[-1]) for a in arrays]
    steps = 4

    def block(shape):
        return pl.BlockSpec((shape[0] // steps, shape[1]), lambda i: (i, 0))

    types = [BF, BF] + [F32] * 7
    shapes = [(512, 2048)] * 2 + [(512, 512)] * 4 + [(512, 2048)] * 2 + [(2048, 512)]
    return pl.pallas_call(
        results_kernel,
        grid=(steps,),
        out_shape=[jax.ShapeDtypeStruct(sh, t) for sh, t in zip(shapes, types)]
        + [jax.ShapeDtypeStruct((1, BLOCK), F32)] * 3,
        in_specs=[pl.BlockSpec((8, MODEL), lambda i: (0, 0))] + [block(a.shape) for a in arrays],
        out_specs=[block(sh) for sh in shapes] + [pl.BlockSpec((1, BLOCK), lambda i: (0, 0))] * 3,
        compiler_params=params(),
    )(small, *arrays)


def rope_table():
    half_dim = HEAD_DIM // 2
    inv_freq = ROPE_BASE ** (-np.arange(half_dim) * 2.0 / HEAD_DIM)
    angles = np.arange(1024)[:, None] * inv_freq[None, :]
    cosine, sine = np.cos(angles), np.sin(angles)
    cosine = np.concatenate([cosine, cosine], axis=1)
    sine = np.concatenate([-sine, sine], axis=1)
    return np.stack([np.tile(cosine, (1, 2)), np.tile(sine, (1, 2))]).astype(np.float32)


def per_device(
    inputs,
    cotangent,
    q_weight,
    k_weight,
    v_weight,
    o_weight,
    gate_weight,
    up_weight,
    down_weight,
    attn_gain,
    ffn_gain,
    piece_starts,
    piece_ids,
    valid_mask,
):
    rope = jnp.asarray(rope_table())
    wqkv, wo, gains, info, pcol, keep, cot_all, attn_in_t, qkv = start_call(
        inputs,
        cotangent,
        (q_weight, k_weight, v_weight, o_weight),
        attn_gain,
        ffn_gain,
        piece_starts,
        piece_ids,
        valid_mask,
        rope,
    )
    wqkv, wo = rows_of(wqkv), rows_of(wo)
    cot_all = rows_of(cot_all)
    qkv = qkv.reshape(1024, 768)
    attended, lse = attend_call(qkv, info, pcol)
    attended = attended.reshape(4, 256, 256)
    ffn_in, resid, stat_attn, wgu, wd = out_proj_call(
        attended, wo, keep, gains, inputs, (gate_weight, up_weight, down_weight)
    )
    ffn_in = ffn_in.reshape(1024, MODEL)
    cot_rows = cot_all.reshape(1024, MODEL)
    hidden, grad_gate, grad_up, dd, dgate, dup = ffn_call(
        ffn_in, cot_rows, rows_of(wgu), rows_of(wd)
    )

    grad_attn, grad_resid, ffn_gain_part, output, stat_ffn, d_seq, sd, sgate, sup_a = mid_call(
        grad_gate,
        grad_up,
        hidden,
        wgu,
        wd,
        dd,
        dgate,
        dup,
        cotangent,
        wo,
        resid,
        gains,
        keep,
        qkv,
        info,
        pcol,
        lse,
        rope,
    )
    dqkv = d_seq.reshape(4, 256, 768)
    input_grad, small, sup_b, so, sq, sk, sv = last_call(
        dqkv,
        wqkv,
        grad_resid,
        gains,
        (ffn_gain_part, stat_attn, stat_ffn, keep),
        attn_in_t,
        attended,
        grad_attn.reshape(1024, MODEL),
        dup,
        inputs,
    )
    output, input_grad, *grads, attn_gain_out, ffn_gain_out, means = results_call(
        small, output, input_grad, sq, sk, sv, so, sgate, sup_a, sup_b, sd
    )
    return (
        output.reshape(4, BLOCK, MODEL),
        input_grad.reshape(4, BLOCK, MODEL),
        *grads,
        attn_gain_out[0],
        ffn_gain_out[0],
        means[0, 0:3],
    )


def solution(mesh):
    return jax.shard_map(
        per_device,
        mesh=mesh,
        in_specs=(
            P("shard", "context", None),
            P("shard", "context", None),
            P("shard", "tensor"),
            P("shard", "tensor"),
            P("shard", "tensor"),
            P("tensor", "shard"),
            P("shard", "tensor"),
            P("shard", "tensor"),
            P("tensor", "shard"),
            P("shard"),
            P("shard"),
            P("shard", None),
            P("shard", None),
            P("shard", None),
        ),
        out_specs=(
            P("shard", "context", None),
            P("shard", "context", None),
            P("shard", "tensor"),
            P("shard", "tensor"),
            P("shard", "tensor"),
            P("tensor", "shard"),
            P("shard", "tensor"),
            P("shard", "tensor"),
            P("tensor", "shard"),
            P(("shard", "tensor")),
            P(("shard", "tensor")),
            P(),
        ),
        check_vma=False,
    )
```
